32 devices in a mesh: grp: 2 (over y), sp: 16 (over z, x, core).
Axes of the slice: x: 2, y: 2, z: 4, core: 2. Of those that a mesh axis runs over, the one named last changes fastest.
Arguments:
- tokens: bfloat16 [128, 256, 512], P(('grp', 'sp')), may hold values from -6 to 6
- frame_slot: int32 [16, 8], P('grp'), may hold values from 0 to 7, each once within a row
- norm_gain: float32 [4, 512], replicated, may hold values from 0.1 to 1.9
- norm_shift: float32 [4, 512], replicated, may hold values from -4 to 4
- w_qkv: bfloat16 [2, 512, 1536], replicated, may hold values from -0.375 to 0.375
- w_out: bfloat16 [2, 512, 512], replicated, may hold values from -0.75 to 0.75
- w_up: bfloat16 [2, 512, 2048], replicated, may hold values from -0.25 to 0.25
- b_up: float32 [2, 2048], replicated, may hold values from -4 to 4
- w_down: bfloat16 [2, 2048, 512], replicated, may hold values from -0.125 to 0.125
- b_down: float32 [2, 512], replicated, may hold values from -4 to 4
- cotangent: bfloat16 [128, 256, 512], P(('grp', 'sp')), may hold values from -6 to 6
Outputs:
- output: bfloat16 [128, 256, 512], P(('grp', 'sp'))
- grad_tokens: bfloat16 [128, 256, 512], P(('grp', 'sp'))
- grad_norm_gain: float32 [4, 512], P(None, 'sp')
- grad_norm_shift: float32 [4, 512], P(None, 'sp')
- grad_w_qkv: float32 [2, 512, 1536], P(None, 'sp')
- grad_w_out: float32 [2, 512, 512], P(None, 'sp')
- grad_w_up: float32 [2, 512, 2048], P(None, 'sp')
- grad_b_up: float32 [2, 2048], P(None, 'sp')
- grad_w_down: float32 [2, 2048, 512], P(None, 'sp')
- grad_b_down: float32 [2, 512], P(None, 'sp')
The draws below stay inside these ranges and needn't reach their ends.
Inputs may be any that keep to these rules, and one draw needn't show every extreme that they name: `frame_slot`: each row names every slot of a group once; slots 0 to 5 are the video's time steps, the others are images.
All inputs are finite; a program needn't handle non-finite values.
Results may differ from the reference program's by a relative error of at most 0.028.
Values may be sent and summed in bfloat16 or wider, within the bound.
No kernel may reach another device: no remote copies, remote signals or barrier semaphores. Data moves between devices by JAX's collectives and lax.ppermute only.
A program may use at most 192 MiB of HBM per device.

```python
import jax
import jax.numpy as jnp
from jax import lax

D = 512
HEADS = 8
HEAD = 64
FF = 2048
PATCHES = 256
VIDEO_STEPS = 6
GROUP_FRAMES = 8
FRAMES = 128
GROUPS = 16


def block_levels(key, shape, cuts, smallest, top_value):
    level, own = 1.0, jax.random.fold_in(key, 6)
    for position, shards_of in cuts:
        draws = jnp.exp(jax.random.uniform(jax.random.fold_in(own, position), (shards_of,), jnp.float32, smallest / len(cuts), top_value / len(cuts)))
        level = level * jnp.repeat(draws, shape[position] // shards_of).reshape([-1 if axis == position else 1 for axis in range(len(shape))])
    return level


def normal_values(key, dims, width, most, shards=(), held_as=jnp.bfloat16):
    values = width * jax.random.normal(key, dims, jnp.float32)
    if shards:
        values = values * block_levels(key, dims, shards, -0.22, 0.18)
    return jnp.clip(values, -most, most).astype(held_as)


def setup_inputs(seed: int = 0) -> dict:
    key_list = jax.random.split(jax.random.key(seed), 12)
    return {
        "tokens": normal_values(key_list[0], (FRAMES, PATCHES, D), 1.0, 6.0, ((0, 32),)),
        "frame_slot": jax.vmap(lambda own: jax.random.permutation(own, GROUP_FRAMES))(jax.random.split(key_list[1], GROUPS)).reshape((GROUPS, GROUP_FRAMES)).astype(jnp.int32),
        "norm_gain": jnp.clip(1.0 + 0.18 * jax.random.normal(key_list[2], (4, D), jnp.float32), 0.1, 1.9),
        "norm_shift": normal_values(key_list[3], (4, D), 0.3, 4.0, (), jnp.float32),
        "w_qkv": normal_values(key_list[4], (2, D, 3 * D), (D // 2) ** -0.5, 0.375),
        "w_out": normal_values(key_list[5], (2, D, D), (D // 8) ** -0.5, 0.75),
        "w_up": normal_values(key_list[6], (2, D, FF), D ** -0.5, 0.25),
        "b_up": normal_values(key_list[7], (2, FF), 0.3, 4.0, (), jnp.float32),
        "w_down": normal_values(key_list[8], (2, FF, D), FF ** -0.5, 0.125),
        "b_down": normal_values(key_list[9], (2, D), 0.3, 4.0, (), jnp.float32),
        "cotangent": normal_values(key_list[10], (FRAMES, PATCHES, D), 1.0, 6.0, ((0, 32),)),
    }


FAR = -1e+30
NORM_EPS = 1e-05

@jax.custom_vjp
def low(v):
    return lax.optimization_barrier(v.astype(jnp.bfloat16)).astype(jnp.float32)

@jax.custom_vjp
def low_back(v):
    return v

def low_keep(v):
    return (low(v), None)

def low_pass(kept, grad):
    return (grad,)

def back_keep(v):
    return (v, None)

def back_low(kept, grad):
    return (low(grad),)
low.defvjp(low_keep, low_pass)
low_back.defvjp(back_keep, back_low)

def product(left, right):
    return jnp.dot(left, right, precision=lax.Precision.HIGHEST)

def layer_norm(values, gain, shift):
    average = lax.optimization_barrier(jnp.mean(values, axis=-1, keepdims=True))
    centred = values - average
    spread = lax.optimization_barrier(jnp.mean(centred * centred, axis=-1, keepdims=True))
    return centred * lax.rsqrt(spread + NORM_EPS) * gain + shift

def attention(values_in, gain, shift, weight_qkv, weight_out, score_form, mix_form, allowed):
    normed = low(layer_norm(values_in, gain, shift))
    joined = low_back(low(product(normed, weight_qkv)))
    joined = joined.reshape(values_in.shape[:-1] + (3, HEADS, HEAD))
    query = joined[..., 0, :, :]
    keys = joined[..., 1, :, :]
    vals = joined[..., 2, :, :]
    scores = low_back(jnp.einsum(score_form, query, keys, precision=lax.Precision.HIGHEST) * HEAD ** (-0.5))
    if allowed is not None:
        scores = jnp.where(allowed, scores, FAR)
    probs = low(jax.nn.softmax(scores, axis=-1))
    mixed = low_back(low(jnp.einsum(mix_form, probs, vals, precision=lax.Precision.HIGHEST)))
    mixed = mixed.reshape(values_in.shape)
    return product(mixed, weight_out)

def feed_forward(values_in, gain, shift, weight_up, bias_up, weight_down, bias_down):
    normed = low(layer_norm(values_in, gain, shift))
    preact = low_back(product(normed, weight_up) + bias_up)
    activated = low(jax.nn.gelu(preact))
    branch = low_back(product(activated, weight_down) + bias_down)
    return values_in + branch

def layer_block(frames_in, slots, gain, shift, w_qkv, w_out, w_up, b_up, w_down, b_down):
    after_space = frames_in + low_back(attention(frames_in, gain[0], shift[0], w_qkv[0], w_out[0], 'fqhe,fkhe->fhqk', 'fhqk,fkhe->fqhe', None))
    first = feed_forward(after_space, gain[1], shift[1], w_up[0], b_up[0], w_down[0], b_down[0])
    groups_here = slots.shape[0]
    placed = low_back(low(first)).reshape(groups_here, GROUP_FRAMES, PATCHES, D)
    query_slot = slots[:, :, None]
    key_slot = slots[:, None, :]
    allowed = (key_slot <= query_slot) & ((query_slot < VIDEO_STEPS) | (key_slot == query_slot))
    allowed = allowed[:, None, None, :, :]
    temporal = attention(placed, gain[2], shift[2], w_qkv[1], w_out[1], 'gtphe,gsphe->gphts', 'gphts,gsphe->gtphe', allowed)
    temporal = low_back(low(temporal)).reshape(first.shape)
    return feed_forward(first + temporal, gain[3], shift[3], w_up[1], b_up[1], w_down[1], b_down[1])

def forward(tokens_in, gain, shift, w_qkv, w_out, w_up, b_up, w_down, b_down, slots):
    blocks = tokens_in.reshape(GROUPS // 2, 2 * GROUP_FRAMES, PATCHES, D)
    slot_blocks = slots.reshape(GROUPS // 2, 2, GROUP_FRAMES)

    def one_block(pair):
        return layer_block(pair[0], pair[1], gain, shift, w_qkv, w_out, w_up, b_up, w_down, b_down)
    results = lax.map(jax.checkpoint(one_block), (blocks, slot_blocks))
    return results.reshape(tokens_in.shape)

def reference(tokens, frame_slot, norm_gain, norm_shift, w_qkv, w_out, w_up, b_up, w_down, b_down, cotangent):
    floats = (tokens.astype(jnp.float32), norm_gain.astype(jnp.float32), norm_shift.astype(jnp.float32), w_qkv.astype(jnp.float32), w_out.astype(jnp.float32), w_up.astype(jnp.float32), b_up.astype(jnp.float32), w_down.astype(jnp.float32), b_down.astype(jnp.float32))

    def whole(*params):
        return forward(*params, frame_slot)
    result, pullback = jax.vjp(whole, *floats)
    grads = pullback(cotangent.astype(jnp.float32))
    return (result.astype(jnp.bfloat16), grads[0].astype(jnp.bfloat16), grads[1], grads[2], grads[3], grads[4], grads[5], grads[6], grads[7], grads[8])
```

```python
import functools

import jax
import jax.numpy as jnp
from jax import lax
from jax.experimental import pallas as pl
from jax.experimental.pallas import tpu as pltpu
from jax.sharding import PartitionSpec as P

HEADS = 8
HEAD = 64
VIDEO_STEPS = 6
GROUP_FRAMES = 8
NORM_EPS = 1e-05
TILE = 512
SCALE = HEAD**-0.5
TANH_A = 0.7978845608028654
TANH_B = TANH_A * 0.044715
PAIRS = [(t, s) for t in range(VIDEO_STEPS) for s in range(t + 1)]
F32 = jnp.float32
BF16 = jnp.bfloat16
MIB = 1024 * 1024


def dot(left, right):
    return jnp.dot(left, right, preferred_element_type=F32)


def dot_nt(left, right):
    return lax.dot_general(left, right, (((1,), (1,)), ((), ())), preferred_element_type=F32)


def dot_tn(left, right):
    return lax.dot_general(left, right, (((0,), (0,)), ((), ())), preferred_element_type=F32)


def norm(rows, gain, shift):
    centred = rows - jnp.mean(rows, axis=-1, keepdims=True)
    inv = lax.rsqrt(jnp.mean(centred * centred, axis=-1, keepdims=True) + NORM_EPS)
    unit = centred * inv
    return unit * gain + shift, unit, inv


def norm_back(grad, unit, inv, gain):
    grad_unit = grad * gain
    mean_grad = jnp.mean(grad_unit, axis=-1, keepdims=True)
    mean_both = jnp.mean(grad_unit * unit, axis=-1, keepdims=True)
    return inv * (grad_unit - mean_grad - unit * mean_both)


def column_sum(rows):
    return jnp.sum(rows, axis=0, keepdims=True)


def gelu_pair(u):
    square = u * u
    t = jnp.tanh(u * (TANH_A + TANH_B * square))
    half = 0.5 * u
    act = half + half * t
    slope = 0.5 + 0.5 * t + half * (1.0 - t * t) * (TANH_A + 3.0 * TANH_B * square)
    return act.astype(BF16), slope.astype(BF16)


def head_mask(lanes, which):
    lane = lax.broadcasted_iota(jnp.int32, lanes.shape, 1)
    return (lane < HEAD) if which == 0 else (lane >= HEAD)


def qkv_rows(normed, weight):
    out = []
    for part in range(3):
        piece = dot(normed, weight[:, part * TILE : (part + 1) * TILE])
        if part == 0:
            out.append(piece.astype(BF16) * BF16(SCALE))
        else:
            out.append(piece.astype(BF16))
    return out


def mlp_forward(normed, w_up, b_up, w_down, act_ref, slope_ref):
    total = None
    for j in range(w_up.shape[1] // TILE):
        cols = slice(j * TILE, (j + 1) * TILE)
        u = dot(normed, w_up[:, cols]) + b_up[:, cols]
        act, slope = gelu_pair(u)
        act_ref[:, cols] = act
        slope_ref[:, cols] = slope
        piece = dot(act, w_down[cols, :])
        total = piece if total is None else total + piece
    return total


def mlp_backward(grad_low, w_up, w_down, slope_ref, du_ref, small_ref):
    total = None
    for j in range(w_up.shape[1] // TILE):
        cols = slice(j * TILE, (j + 1) * TILE)
        du = (dot_nt(grad_low, w_down[cols, :]) * slope_ref[:, cols].astype(F32)).astype(BF16)
        du_ref[:, cols] = du
        small_ref[4 + j : 5 + j, :] += column_sum(du.astype(F32))
        piece = dot_nt(du, w_up[:, cols])
        total = piece if total is None else total + piece
    return total


def clear_first(small_ref):
    @pl.when(pl.program_id(0) == 0)
    def _():
        small_ref[...] = jnp.zeros_like(small_ref)


def space_forward_kernel(
    tok_ref, gain_ref, shift_ref, wqkv_ref, wout_ref, wup_ref, bup_ref, wdown_ref, bdown_ref,
    keep_ref, send_ref, h0_ref, qkv_ref, lse_ref, o_ref, xa_ref, h1_ref, act_ref, slope_ref,
    x1_scr,
):
    part = lax.rem(lax.axis_index("sp"), 2)
    x0 = tok_ref[0].astype(F32)
    rows = x0.shape[0]
    h0 = norm(x0, gain_ref[0:1, :], shift_ref[0:1, :])[0].astype(BF16)
    h0_ref[0] = h0
    q, k, v = qkv_rows(h0, wqkv_ref[0])
    qkv_ref[0, :, 0:TILE] = q
    qkv_ref[0, :, TILE : 2 * TILE] = k
    qkv_ref[0, :, 2 * TILE :] = v
    lane = lax.broadcasted_iota(jnp.int32, (rows, 128), 1)
    lse_all = jnp.zeros((rows, 128), F32)
    mixed = []
    for pair in range(HEADS // 2):
        cols = slice(pair * 128, (pair + 1) * 128)
        qp, kp, vp = q[:, cols], k[:, cols], v[:, cols]
        both = []
        for e in range(2):
            s = dot_nt(jnp.where(head_mask(qp, e), qp, jnp.zeros_like(qp)), kp)
            top = jnp.max(s, axis=-1, keepdims=True)
            p = jnp.exp(s - top)
            total = jnp.sum(p, axis=-1, keepdims=True)
            both.append(dot(p.astype(BF16), vp) * (1.0 / total))
            lse_all = jnp.where(lane == 2 * pair + e, top + jnp.log(total), lse_all)
        mixed.append(jnp.where(head_mask(both[0], 0), both[0], both[1]).astype(BF16))
    lse_ref[0] = jnp.transpose(lse_all)[0:HEADS, :]
    o = jnp.concatenate(mixed, axis=1)
    o_ref[0] = o
    xa = x0 + dot(o, wout_ref[0])
    xa_ref[0] = xa
    h1 = norm(xa, gain_ref[1:2, :], shift_ref[1:2, :])[0].astype(BF16)
    h1_ref[0] = h1
    branch = mlp_forward(h1, wup_ref[0], bup_ref[0:1, :], wdown_ref[0], act_ref.at[0], slope_ref.at[0])
    x1_scr[...] = xa + branch + bdown_ref[0:1, :]
    half = rows // 2
    keep_ref[0] = x1_scr[pl.ds(pl.multiple_of(part * half, half), half), :].astype(BF16)
    send_ref[0] = x1_scr[pl.ds(pl.multiple_of((1 - part) * half, half), half), :].astype(BF16)


def pick_rows(where_ref, both_scr, step_rows):
    return jnp.concatenate([both_scr[where_ref[s]] for s in range(GROUP_FRAMES)], axis=0)


def lane_heads(dtype):
    c = lax.broadcasted_iota(jnp.int32, (TILE, 128), 0)
    h = lax.broadcasted_iota(jnp.int32, (TILE, 128), 1)
    return (c // HEAD == h).astype(dtype)


def slot_places(slots_ref, where_scr, frames):
    sp = lax.axis_index("sp")
    group = (sp * frames) // GROUP_FRAMES
    part = lax.rem(sp, GROUP_FRAMES // frames)
    for t in range(GROUP_FRAMES):
        where_scr[slots_ref[group, t]] = lax.rem(t + GROUP_FRAMES - part * frames, GROUP_FRAMES)


def time_scores(q, k, spread, count):
    parts = []
    for t, s in PAIRS:
        parts.append((q[t] * k[s]).astype(BF16))
    return dot(jnp.concatenate(parts, axis=0), spread)


def time_probs(scores, count):
    blocks = [scores[i * count : (i + 1) * count] for i in range(len(PAIRS))]
    probs = []
    at = 0
    for t in range(VIDEO_STEPS):
        mine = blocks[at : at + t + 1]
        at += t + 1
        top = functools.reduce(jnp.maximum, mine)
        raw = [jnp.exp(b - top) for b in mine]
        inv = 1.0 / functools.reduce(lambda a, b: a + b, raw)
        probs.extend([r * inv for r in raw])
    return probs


def time_forward_kernel(
    slots_ref, keep_ref, recv_ref, cot_ref, cotr_ref, gain_ref, shift_ref,
    wqkv_ref, wout_ref, wup_ref, bup_ref, wdown_ref, bdown_ref,
    own_ref, send_ref, x_ref, h2_ref, qkv_ref, o_ref, h3_ref, act_ref, du_ref, gr_ref, dxb_ref,
    small_ref,
    where_scr, both_scr, slope_scr,
):
    frames = keep_ref.shape[0]
    count = keep_ref.shape[1]
    step = pl.program_id(0)
    part = lax.rem(lax.axis_index("sp"), GROUP_FRAMES // frames)
    clear_first(small_ref)

    @pl.when(step == 0)
    def _():
        slot_places(slots_ref, where_scr, frames)

    both_scr[0:frames] = keep_ref[...]
    both_scr[frames:] = recv_ref[...]
    x_low = pick_rows(where_scr, both_scr, count)
    x_ref[...] = x_low
    x = x_low.astype(F32)
    h2 = norm(x, gain_ref[2:3, :], shift_ref[2:3, :])[0].astype(BF16)
    h2_ref[...] = h2
    q, k, v = qkv_rows(h2, wqkv_ref[0])
    qkv_ref[:, 0:TILE] = q
    qkv_ref[:, TILE : 2 * TILE] = k
    qkv_ref[:, 2 * TILE :] = v

    def split(rows):
        return [rows[s * count : (s + 1) * count].astype(F32) for s in range(GROUP_FRAMES)]

    qs, ks, vs = split(q), split(k), split(v)
    spread = lane_heads(BF16)
    probs = time_probs(time_scores(qs, ks, spread, count), count)
    wide = dot_nt(jnp.concatenate([p.astype(BF16) for p in probs], axis=0), spread)
    mixed = []
    at = 0
    for t in range(VIDEO_STEPS):
        total = None
        for s in range(t + 1):
            piece = wide[at * count : (at + 1) * count] * vs[s]
            total = piece if total is None else total + piece
            at += 1
        mixed.append(total)
    mixed.extend(vs[VIDEO_STEPS:])
    o = jnp.concatenate([m.astype(BF16) for m in mixed], axis=0)
    o_ref[...] = o
    xb = x + dot(o, wout_ref[0]).astype(BF16).astype(F32)
    h3, unit, inv = norm(xb, gain_ref[3:4, :], shift_ref[3:4, :])
    h3 = h3.astype(BF16)
    h3_ref[...] = h3
    branch = mlp_forward(h3, wup_ref[0], bup_ref[1:2, :], wdown_ref[0], act_ref, slope_scr)
    out = (xb + branch + bdown_ref[1:2, :]).astype(BF16)
    for s in range(GROUP_FRAMES):
        both_scr[where_scr[s]] = out[s * count : (s + 1) * count]
    own_ref[...] = both_scr[0:frames]
    send_ref[...] = both_scr[frames:]

    places = pl.ds(pl.multiple_of(part * (cot_ref.shape[1] // 2) + step * count, count), count)
    both_scr[0:frames] = cot_ref[:, places, :]
    both_scr[frames:] = cotr_ref[:, places, :]
    grad_low = pick_rows(where_scr, both_scr, count)
    gr_ref[...] = grad_low
    grad = grad_low.astype(F32)
    dh = mlp_backward(grad_low, wup_ref[0], wdown_ref[0], slope_scr, du_ref, small_ref)
    small_ref[0:1, :] += column_sum(dh * unit)
    small_ref[1:2, :] += column_sum(dh)
    small_ref[2:3, :] += column_sum(grad)
    dxb_ref[...] = grad + norm_back(dh, unit, inv, gain_ref[3:4, :])


def time_backward_kernel(
    slots_ref, x_ref, qkv_ref, dxb_ref, gain_ref, shift_ref, wqkv_ref, wout_ref,
    own_ref, send_ref, ar_ref, dqkv_ref, small_ref,
    where_scr, both_scr,
):
    frames = own_ref.shape[0]
    count = own_ref.shape[1]
    clear_first(small_ref)

    @pl.when(pl.program_id(0) == 0)
    def _():
        slot_places(slots_ref, where_scr, frames)

    def split(rows):
        return [rows[s * count : (s + 1) * count].astype(F32) for s in range(GROUP_FRAMES)]

    dxb = dxb_ref[...]
    ar = dxb.astype(BF16)
    ar_ref[...] = ar
    do = split(dot_nt(ar, wout_ref[0]).astype(BF16))
    qs = split(qkv_ref[:, 0:TILE])
    ks = split(qkv_ref[:, TILE : 2 * TILE])
    vs = split(qkv_ref[:, 2 * TILE :])
    spread = lane_heads(BF16)
    probs = time_probs(time_scores(qs, ks, spread, count), count)
    dps = time_scores(do, vs, spread, count)
    dps = [dps[i * count : (i + 1) * count] for i in range(len(PAIRS))]
    dss = []
    at = 0
    for t in range(VIDEO_STEPS):
        centre = functools.reduce(
            lambda a, b: a + b, [probs[at + s] * dps[at + s] for s in range(t + 1)]
        )
        dss.extend([probs[at + s] * (dps[at + s] - centre) for s in range(t + 1)])
        at += t + 1
    wide_p = dot_nt(jnp.concatenate([p.astype(BF16) for p in probs], axis=0), spread)
    wide_ds = dot_nt(jnp.concatenate([d.astype(BF16) for d in dss], axis=0), spread)
    dq = [None] * GROUP_FRAMES
    dk = [None] * GROUP_FRAMES
    dv = [None] * GROUP_FRAMES

    def add(table, index, piece):
        table[index] = piece if table[index] is None else table[index] + piece

    for i, (t, s) in enumerate(PAIRS):
        rows = slice(i * count, (i + 1) * count)
        add(dq, t, wide_ds[rows] * ks[s])
        add(dk, s, wide_ds[rows] * qs[t])
        add(dv, s, wide_p[rows] * do[t])
    for t in range(VIDEO_STEPS, GROUP_FRAMES):
        dq[t] = jnp.zeros_like(do[t])
        dk[t] = jnp.zeros_like(do[t])
        dv[t] = do[t]
    dq = jnp.concatenate([(d * SCALE).astype(BF16) for d in dq], axis=0)
    dk = jnp.concatenate([d.astype(BF16) for d in dk], axis=0)
    dv = jnp.concatenate([d.astype(BF16) for d in dv], axis=0)
    dqkv_ref[:, 0:TILE] = dq
    dqkv_ref[:, TILE : 2 * TILE] = dk
    dqkv_ref[:, 2 * TILE :] = dv
    dh = (
        dot_nt(dq, wqkv_ref[0, :, 0:TILE])
        + dot_nt(dk, wqkv_ref[0, :, TILE : 2 * TILE])
        + dot_nt(dv, wqkv_ref[0, :, 2 * TILE :])
    )
    gain = gain_ref[2:3, :]
    unit, inv = norm(x_ref[...].astype(F32), gain, shift_ref[2:3, :])[1:]
    small_ref[0:1, :] += column_sum(dh * unit)
    small_ref[1:2, :] += column_sum(dh)
    dxp = norm_back(dh, unit, inv, gain).astype(BF16).astype(F32)
    dx1 = (dxb + dxp).astype(BF16)
    for s in range(GROUP_FRAMES):
        both_scr[where_scr[s]] = dx1[s * count : (s + 1) * count]
    own_ref[...] = both_scr[0:frames]
    send_ref[...] = both_scr[frames:]


def space_mlp_back_kernel(
    own_ref, recv_ref, xa_ref, slope_ref, gain_ref, shift_ref, wup_ref, wdown_ref,
    gr_ref, du_ref, dxa_ref, small_ref,
):
    part = lax.rem(lax.axis_index("sp"), 2)
    clear_first(small_ref)
    half = own_ref.shape[1]
    gr_ref[0, pl.ds(pl.multiple_of(part * half, half), half), :] = own_ref[0]
    gr_ref[0, pl.ds(pl.multiple_of((1 - part) * half, half), half), :] = recv_ref[0]
    grad_low = gr_ref[0]
    grad = grad_low.astype(F32)
    dh = mlp_backward(grad_low, wup_ref[0], wdown_ref[0], slope_ref.at[0], du_ref.at[0], small_ref)
    gain = gain_ref[1:2, :]
    unit, inv = norm(xa_ref[0], gain, shift_ref[1:2, :])[1:]
    small_ref[0:1, :] += column_sum(dh * unit)
    small_ref[1:2, :] += column_sum(dh)
    small_ref[2:3, :] += column_sum(grad)
    dxa_ref[0] = grad + norm_back(dh, unit, inv, gain)


def space_attn_back_kernel(
    tok_ref, dxa_ref, qkv_ref, lse_ref, o_ref, own_ref, recv_ref, gain_ref, shift_ref, wqkv_ref,
    wout_ref, ar_ref, dqkv_ref, gtok_ref, out_ref, small_ref,
):
    part = lax.rem(lax.axis_index("sp"), 2)
    clear_first(small_ref)
    half = own_ref.shape[1]
    out_ref[0, pl.ds(pl.multiple_of(part * half, half), half), :] = own_ref[0]
    out_ref[0, pl.ds(pl.multiple_of((1 - part) * half, half), half), :] = recv_ref[0]
    dxa = dxa_ref[0]
    ar = dxa.astype(BF16)
    ar_ref[0] = ar
    do = dot_nt(ar, wout_ref[0]).astype(BF16)
    both = do.astype(F32) * o_ref[0].astype(F32)
    high = both.astype(BF16)
    rest = (both - high.astype(F32)).astype(BF16)
    h = lax.broadcasted_iota(jnp.int32, (HEADS, TILE), 0)
    c = lax.broadcasted_iota(jnp.int32, (HEADS, TILE), 1)
    pick = (c // HEAD == h).astype(BF16)
    centre = dot_nt(pick, high) + dot_nt(pick, rest)
    dq, dk, dv = [], [], []
    for pair in range(HEADS // 2):
        cols = slice(pair * 128, (pair + 1) * 128)
        qp = qkv_ref[0, :, pair * 128 : (pair + 1) * 128]
        kp = qkv_ref[0, :, TILE + pair * 128 : TILE + (pair + 1) * 128]
        vp = qkv_ref[0, :, 2 * TILE + pair * 128 : 2 * TILE + (pair + 1) * 128]
        dop = do[:, cols]
        parts = []
        for e in range(2):
            row = slice(2 * pair + e, 2 * pair + e + 1)
            mask = head_mask(kp, e)
            zero = jnp.zeros_like(kp)
            st = dot_nt(jnp.where(mask, kp, zero), qp)
            pt = jnp.exp(st - lse_ref[0, row, :])
            dpt = dot_nt(jnp.where(mask, vp, zero), dop)
            dst = (pt * (dpt - centre[row, :])).astype(BF16)
            parts.append((dot_tn(dst, kp) * SCALE, dot(dst, qp), dot(pt.astype(BF16), dop)))
        mask = head_mask(parts[0][0], 0)
        for table, index in ((dq, 0), (dk, 1), (dv, 2)):
            table.append(jnp.where(mask, parts[0][index], parts[1][index]).astype(BF16))
    dh = None
    for index, table in enumerate((dq, dk, dv)):
        whole = jnp.concatenate(table, axis=1)
        cols = slice(index * TILE, (index + 1) * TILE)
        dqkv_ref[0, :, cols] = whole
        piece = dot_nt(whole, wqkv_ref[0, :, cols])
        dh = piece if dh is None else dh + piece
    gain = gain_ref[0:1, :]
    unit, inv = norm(tok_ref[0].astype(F32), gain, shift_ref[0:1, :])[1:]
    small_ref[0:1, :] += column_sum(dh * unit)
    small_ref[1:2, :] += column_sum(dh)
    gtok_ref[0] = (dxa + norm_back(dh, unit, inv, gain)).astype(BF16)


def place_of(block, order, sp):
    bits = len(order)
    mixed = jnp.bitwise_xor(block, sp)
    slot = jnp.int32(0)
    for i, b in enumerate(order):
        bit = jnp.bitwise_and(lax.shift_right_logical(mixed, jnp.int32(b)), 1)
        slot = slot + lax.shift_left(bit, jnp.int32(bits - 1 - i))
    return slot


def put_blocks(result, first, size, at, order, keep_ref, send_ref):
    sp = lax.axis_index("sp")
    part = lax.rem(sp, 2)
    low = result.astype(BF16)
    for j in range(result.shape[0] // (2 * size)):
        even = low[2 * j * size : (2 * j + 1) * size]
        odd = low[(2 * j + 1) * size : (2 * j + 2) * size]
        slot = place_of(first + 2 * j, order[1:], sp)
        keep_ref[slot, at : at + size, :] = jnp.where(part == 0, even, odd)
        send_ref[slot, at : at + size, :] = jnp.where(part == 0, odd, even)


def mlp_weights_kernel(order, h_ref, du_ref, act_ref, gr_ref, keep_ref, send_ref):
    slots = 2 * keep_ref.shape[0]
    up_size = h_ref.shape[1] // slots
    chunks = 4
    down_size = chunks * TILE // slots
    j = pl.program_id(0)
    up = dot_tn(h_ref[...], du_ref[...])
    at = pl.multiple_of(j * up_size, up_size)
    sp = lax.axis_index("sp")
    part = lax.rem(sp, 2)
    low = up.astype(BF16)
    for i in range(slots // 2):
        even = low[2 * i * up_size : (2 * i + 1) * up_size]
        odd = low[(2 * i + 1) * up_size : (2 * i + 2) * up_size]
        slot = place_of(jnp.int32(2 * i), order[1:], sp)
        keep_ref[slot, pl.ds(at, up_size), :] = jnp.where(part == 0, even, odd)
        send_ref[slot, pl.ds(at, up_size), :] = jnp.where(part == 0, odd, even)
    down = dot_tn(act_ref[...], gr_ref[...])
    put_blocks(down, j * (TILE // down_size), down_size, chunks * up_size, order, keep_ref, send_ref)


def attn_weights_kernel(order, h_ref, dqkv_ref, o_ref, ar_ref, keep_ref, send_ref):
    size = h_ref.shape[1] // (2 * keep_ref.shape[0])
    zero = jnp.int32(0)
    for j in range(3):
        cols = slice(j * TILE, (j + 1) * TILE)
        put_blocks(dot_tn(h_ref[...], dqkv_ref[:, cols]), zero, size, j * size, order, keep_ref, send_ref)
    put_blocks(dot_tn(o_ref[...], ar_ref[...]), zero, size, 3 * size, order, keep_ref, send_ref)


def whole_spec(array):
    rank = len(array.shape)
    return pl.BlockSpec(array.shape, lambda i: (0,) * rank)


def layer_spec(array, layer):
    return pl.BlockSpec((1,) + array.shape[1:], lambda i: (layer,) + (0,) * (len(array.shape) - 1))


def step_spec(shape, axis=0):
    rank = len(shape)
    return pl.BlockSpec(shape, lambda i: (0,) * axis + (i,) + (0,) * (rank - axis - 1))


def params(limit_mib):
    return pltpu.CompilerParams(dimension_semantics=("arbitrary",), vmem_limit_bytes=limit_mib * MIB)


def cost(flops, read):
    return pl.CostEstimate(flops=int(flops), bytes_accessed=int(read), transcendentals=0)


def sds(shape, dtype):
    return jax.ShapeDtypeStruct(shape, dtype)


def add_low(a, b):
    return (a.astype(F32) + b.astype(F32)).astype(BF16)


def swap(array, axis, size, bit):
    return lax.ppermute(array, axis, [(i, i ^ (1 << bit)) for i in range(size)])


def sum_scatter(keep, send, order, sp_size, grp_size):
    recv = swap(send, "sp", sp_size, order[0])
    for b in order[1:]:
        half = keep.shape[0] // 2
        send = add_low(keep[half:], recv[half:])
        keep = add_low(keep[:half], recv[:half])
        recv = swap(send, "sp", sp_size, b)
    now = add_low(keep, recv)
    for b in range(grp_size.bit_length() - 1):
        now = add_low(now, swap(now, "grp", grp_size, b))
    return now[0].astype(F32)


def shards(sizes, tokens, frame_slot, norm_gain, norm_shift, w_qkv, w_out, w_up, b_up, w_down, b_down, cotangent):
    grp_size, sp_size = sizes
    frames, patches, width = tokens.shape
    hidden = w_up.shape[2]
    assert GROUP_FRAMES == 2 * frames
    half = patches // 2
    rows = frames * patches
    sp_bits = sp_size.bit_length() - 1
    core_swap = functools.partial(swap, axis="sp", size=sp_size, bit=0)
    macs = rows * width

    cot_recv = core_swap(cotangent)

    def frame_out(cols, dtype):
        return sds((frames, patches, cols), dtype)

    frame_block = lambda cols: step_spec((1, patches, cols))
    half_block = step_spec((1, half, width))
    (x_keep, x_send, h0, qkv0, lse0, o0, xa, h1, act0, slope0) = pl.pallas_call(
        space_forward_kernel,
        grid=(frames,),
        in_specs=[
            frame_block(width), whole_spec(norm_gain), whole_spec(norm_shift), layer_spec(w_qkv, 0),
            layer_spec(w_out, 0), layer_spec(w_up, 0), whole_spec(b_up), layer_spec(w_down, 0),
            whole_spec(b_down),
        ],
        out_specs=[
            half_block, half_block, frame_block(width), frame_block(3 * width),
            step_spec((1, HEADS, patches)), frame_block(width), frame_block(width),
            frame_block(width), frame_block(hidden), frame_block(hidden),
        ],
        out_shape=[
            sds((frames, half, width), BF16), sds((frames, half, width), BF16), frame_out(width, BF16),
            frame_out(3 * width, BF16), sds((frames, HEADS, patches), F32), frame_out(width, BF16),
            frame_out(width, F32), frame_out(width, BF16), frame_out(hidden, BF16),
            frame_out(hidden, BF16),
        ],
        scratch_shapes=[pltpu.VMEM((patches, width), F32)],
        compiler_params=params(56),
        cost_estimate=cost(2 * macs * (4 * width + 2 * hidden), 30e6),
    )(tokens, norm_gain, norm_shift, w_qkv, w_out, w_up, b_up, w_down, b_down)
    x_recv = core_swap(x_send)

    steps = 4
    count = half // steps
    step_rows = GROUP_FRAMES * count
    place_block = step_spec((frames, count, width), 1)
    row_block = lambda cols: step_spec((step_rows, cols))
    smem = pl.BlockSpec(memory_space=pltpu.SMEM)
    place_scratch = [
        pltpu.SMEM((GROUP_FRAMES,), jnp.int32),
        pltpu.VMEM((GROUP_FRAMES, count, width), BF16),
    ]
    small_shape = sds((8, TILE), F32)
    small_spec = pl.BlockSpec((8, TILE), lambda i: (0, 0))
    half_shape = sds((frames, half, width), BF16)
    (out_own, out_send, xt, h2, qkv1, o1, h3, act1, du1, gr1, dxb, small3) = pl.pallas_call(
        time_forward_kernel,
        grid=(steps,),
        in_specs=[
            smem, place_block, place_block, whole_spec(cotangent), whole_spec(cotangent),
            whole_spec(norm_gain), whole_spec(norm_shift), layer_spec(w_qkv, 1), layer_spec(w_out, 1),
            layer_spec(w_up, 1), whole_spec(b_up), layer_spec(w_down, 1), whole_spec(b_down),
        ],
        out_specs=[
            place_block, place_block, row_block(width), row_block(width), row_block(3 * width),
            row_block(width), row_block(width), row_block(hidden), row_block(hidden), row_block(width),
            row_block(width), small_spec,
        ],
        out_shape=[
            half_shape, half_shape, sds((rows, width), BF16), sds((rows, width), BF16),
            sds((rows, 3 * width), BF16), sds((rows, width), BF16), sds((rows, width), BF16),
            sds((rows, hidden), BF16), sds((rows, hidden), BF16), sds((rows, width), BF16),
            sds((rows, width), F32), small_shape,
        ],
        scratch_shapes=place_scratch + [pltpu.VMEM((step_rows, hidden), BF16)],
        compiler_params=params(56),
        cost_estimate=cost(2 * macs * (4 * width + 4 * hidden), 30e6),
    )(
        frame_slot, x_keep, x_recv, cotangent, cot_recv, norm_gain, norm_shift, w_qkv, w_out, w_up,
        b_up, w_down, b_down,
    )
    out_recv = core_swap(out_send)

    def mlp_weights(order, h, du, act, gr):
        slots = sp_size // 2
        shape = sds((slots, 4 * (width // sp_size) + hidden // sp_size, TILE), BF16)
        return pl.pallas_call(
            functools.partial(mlp_weights_kernel, order),
            grid=(hidden // TILE,),
            in_specs=[
                whole_spec(h), pl.BlockSpec((rows, TILE), lambda i: (0, i)),
                pl.BlockSpec((rows, TILE), lambda i: (0, i)), whole_spec(gr),
            ],
            out_specs=[pl.BlockSpec(shape.shape, lambda i: (0, 0, 0))] * 2,
            out_shape=[shape, shape],
            compiler_params=params(40),
            cost_estimate=cost(2 * macs * 2 * hidden, 14e6),
        )(h, du, act, gr)

    def attn_weights(order, h, dqkv, o, ar):
        slots = sp_size // 2
        shape = sds((slots, 4 * (width // sp_size), TILE), BF16)
        return pl.pallas_call(
            functools.partial(attn_weights_kernel, order),
            grid=(1,),
            in_specs=[whole_spec(h), whole_spec(dqkv), whole_spec(o), whole_spec(ar)],
            out_specs=[pl.BlockSpec(shape.shape, lambda i: (0, 0, 0))] * 2,
            out_shape=[shape, shape],
            compiler_params=params(40),
            cost_estimate=cost(2 * macs * 4 * width, 8e6),
        )(h, dqkv, o, ar)

    order_a = list(range(sp_bits))
    order_b = [0, 2, 1] + list(range(3, sp_bits))
    mlp1 = sum_scatter(*mlp_weights(order_a, h3, du1, act1, gr1), order_a, sp_size, grp_size)

    (dx_own, dx_send, ar1, dqkv1, small2) = pl.pallas_call(
        time_backward_kernel,
        grid=(steps,),
        in_specs=[
            smem, row_block(width), row_block(3 * width), row_block(width), whole_spec(norm_gain),
            whole_spec(norm_shift), layer_spec(w_qkv, 1), layer_spec(w_out, 1),
        ],
        out_specs=[place_block, place_block, row_block(width), row_block(3 * width), small_spec],
        out_shape=[
            half_shape, half_shape, sds((rows, width), BF16), sds((rows, 3 * width), BF16), small_shape,
        ],
        scratch_shapes=place_scratch,
        compiler_params=params(56),
        cost_estimate=cost(2 * macs * 4 * width, 15e6),
    )(frame_slot, xt, qkv1, dxb, norm_gain, norm_shift, w_qkv, w_out)
    dx_recv = core_swap(dx_send)
    attn1 = sum_scatter(*attn_weights(order_b, h2, dqkv1, o1, ar1), order_b, sp_size, grp_size)

    (gr0, du0, dxa, small1) = pl.pallas_call(
        space_mlp_back_kernel,
        grid=(frames,),
        in_specs=[
            half_block, half_block, frame_block(width), frame_block(hidden), whole_spec(norm_gain),
            whole_spec(norm_shift), layer_spec(w_up, 0), layer_spec(w_down, 0),
        ],
        out_specs=[frame_block(width), frame_block(hidden), frame_block(width), small_spec],
        out_shape=[frame_out(width, BF16), frame_out(hidden, BF16), frame_out(width, F32), small_shape],
        compiler_params=params(56),
        cost_estimate=cost(2 * macs * 2 * hidden, 20e6),
    )(dx_own, dx_recv, xa, slope0, norm_gain, norm_shift, w_up, w_down)
    flat = lambda a: a.reshape(rows, a.shape[-1])
    mlp0 = sum_scatter(
        *mlp_weights(order_b, flat(h1), flat(du0), flat(act0), flat(gr0)), order_b, sp_size, grp_size
    )

    (ar0, dqkv0, grad_tokens, output, small0) = pl.pallas_call(
        space_attn_back_kernel,
        grid=(frames,),
        in_specs=[
            frame_block(width), frame_block(width), frame_block(3 * width),
            step_spec((1, HEADS, patches)), frame_block(width), half_block, half_block,
            whole_spec(norm_gain), whole_spec(norm_shift), layer_spec(w_qkv, 0), layer_spec(w_out, 0),
        ],
        out_specs=[
            frame_block(width), frame_block(3 * width), frame_block(width), frame_block(width),
            small_spec,
        ],
        out_shape=[
            frame_out(width, BF16), frame_out(3 * width, BF16), frame_out(width, BF16),
            frame_out(width, BF16), small_shape,
        ],
        compiler_params=params(56),
        cost_estimate=cost(2 * macs * 6 * width, 20e6),
    )(tokens, dxa, qkv0, lse0, o0, out_own, out_recv, norm_gain, norm_shift, w_qkv, w_out)
    attn0 = sum_scatter(
        *attn_weights(order_a, flat(h0), flat(dqkv0), flat(o0), flat(ar0)), order_a, sp_size, grp_size
    )

    small = jnp.concatenate([small0, small1, small2, small3], axis=0).astype(BF16)
    for b in range(sp_bits):
        small = add_low(small, swap(small, "sp", sp_size, b))
    for b in range(grp_size.bit_length() - 1):
        small = add_low(small, swap(small, "grp", grp_size, b))
    small = small.astype(F32).reshape(4, 8, TILE)
    sp = lax.axis_index("sp")

    def mine(array):
        size = array.shape[1] // sp_size
        return lax.dynamic_slice_in_dim(array, sp * size, size, axis=1)

    def up_part(a):
        size = width // sp_size
        return a[: 4 * size].reshape(4, size, TILE).transpose(1, 0, 2).reshape(size, hidden)

    def qkv_part(a):
        size = width // sp_size
        return a[: 3 * size].reshape(3, size, TILE).transpose(1, 0, 2).reshape(size, 3 * width)

    size = width // sp_size
    return (
        output,
        grad_tokens,
        mine(small[:, 0]),
        mine(small[:, 1]),
        jnp.stack([qkv_part(attn0), qkv_part(attn1)]),
        jnp.stack([attn0[3 * size :], attn1[3 * size :]]),
        jnp.stack([up_part(mlp0), up_part(mlp1)]),
        mine(small[1::2, 4:].reshape(2, hidden)),
        jnp.stack([mlp0[4 * size :], mlp1[4 * size :]]),
        mine(small[1::2, 2]),
    )


def solution(mesh):
    rows = P(("grp", "sp"), None, None)
    in_specs = (rows, P("grp", None), P(), P(), P(), P(), P(), P(), P(), P(), rows)
    out_specs = (
        rows, rows, P(None, "sp"), P(None, "sp"), P(None, "sp", None), P(None, "sp", None),
        P(None, "sp", None), P(None, "sp"), P(None, "sp", None), P(None, "sp"),
    )
    body = functools.partial(shards, (mesh.shape["grp"], mesh.shape["sp"]))
    return jax.shard_map(body, mesh=mesh, in_specs=in_specs, out_specs=out_specs, check_vma=False)
```

```python
import functools

import jax
import jax.numpy as jnp
from jax import lax
from jax.experimental import pallas as pl
from jax.experimental.pallas import tpu as pltpu
from jax.sharding import PartitionSpec as P

HEADS = 8
HEAD = 64
VIDEO_STEPS = 6
GROUP_FRAMES = 8
NORM_EPS = 1e-05
TILE = 512
SCALE = HEAD**-0.5
TANH_A = 0.7978845608028654
TANH_B = TANH_A * 0.044715
PAIRS = [(t, s) for t in range(VIDEO_STEPS) for s in range(t + 1)]
F32 = jnp.float32
BF16 = jnp.bfloat16
MIB = 1024 * 1024


def dot(left, right):
    return jnp.dot(left, right, preferred_element_type=F32)


def dot_nt(left, right):
    return lax.dot_general(left, right, (((1,), (1,)), ((), ())), preferred_element_type=F32)


def dot_tn(left, right):
    return lax.dot_general(left, right, (((0,), (0,)), ((), ())), preferred_element_type=F32)


def norm(rows, gain, shift):
    centred = rows - jnp.mean(rows, axis=-1, keepdims=True)
    inv = lax.rsqrt(jnp.mean(centred * centred, axis=-1, keepdims=True) + NORM_EPS)
    unit = centred * inv
    return unit * gain + shift, unit, inv


def norm_back(grad, unit, inv, gain):
    grad_unit = grad * gain
    mean_grad = jnp.mean(grad_unit, axis=-1, keepdims=True)
    mean_both = jnp.mean(grad_unit * unit, axis=-1, keepdims=True)
    return inv * (grad_unit - mean_grad - unit * mean_both)


def column_sum(rows):
    return jnp.sum(rows, axis=0, keepdims=True)


def gelu_pair(u):
    square = u * u
    t = jnp.tanh(u * (TANH_A + TANH_B * square))
    half = 0.5 * u
    act = half + half * t
    slope = 0.5 + 0.5 * t + half * (1.0 - t * t) * (TANH_A + 3.0 * TANH_B * square)
    return act.astype(BF16), slope.astype(BF16)


def head_mask(lanes, which):
    lane = lax.broadcasted_iota(jnp.int32, lanes.shape, 1)
    return (lane < HEAD) if which == 0 else (lane >= HEAD)


def qkv_rows(normed, weight):
    out = []
    for part in range(3):
        piece = dot(normed, weight[:, part * TILE : (part + 1) * TILE])
        if part == 0:
            out.append(piece.astype(BF16) * BF16(SCALE))
        else:
            out.append(piece.astype(BF16))
    return out


def mlp_forward(normed, w_up, b_up, w_down, act_ref, slope_ref):
    total = None
    for j in range(w_up.shape[1] // TILE):
        cols = slice(j * TILE, (j + 1) * TILE)
        u = dot(normed, w_up[:, cols]) + b_up[:, cols]
        act, slope = gelu_pair(u)
        act_ref[:, cols] = act
        slope_ref[:, cols] = slope
        piece = dot(act, w_down[cols, :])
        total = piece if total is None else total + piece
    return total


def mlp_backward(grad_low, w_up, w_down, slope_ref, du_ref, small_ref):
    total = None
    for j in range(w_up.shape[1] // TILE):
        cols = slice(j * TILE, (j + 1) * TILE)
        du = (dot_nt(grad_low, w_down[cols, :]) * slope_ref[:, cols].astype(F32)).astype(BF16)
        du_ref[:, cols] = du
        small_ref[4 + j : 5 + j, :] += column_sum(du.astype(F32))
        piece = dot_nt(du, w_up[:, cols])
        total = piece if total is None else total + piece
    return total


def clear_first(small_ref):
    @pl.when(pl.program_id(0) == 0)
    def _():
        small_ref[...] = jnp.zeros_like(small_ref)


def space_forward_kernel(
    tok_ref, gain_ref, shift_ref, wqkv_ref, wout_ref, wup_ref, bup_ref, wdown_ref, bdown_ref,
    keep_ref, send_ref, h0_ref, qkv_ref, lse_ref, o_ref, xa_ref, h1_ref, act_ref, slope_ref,
    x1_scr,
):
    part = lax.rem(lax.axis_index("sp"), 2)
    x0 = tok_ref[0].astype(F32)
    rows = x0.shape[0]
    h0 = norm(x0, gain_ref[0:1, :], shift_ref[0:1, :])[0].astype(BF16)
    h0_ref[0] = h0
    q, k, v = qkv_rows(h0, wqkv_ref[0])
    qkv_ref[0, :, 0:TILE] = q
    qkv_ref[0, :, TILE : 2 * TILE] = k
    qkv_ref[0, :, 2 * TILE :] = v
    lane = lax.broadcasted_iota(jnp.int32, (rows, 128), 1)
    lse_all = jnp.zeros((rows, 128), F32)
    mixed = []
    for pair in range(HEADS // 2):
        cols = slice(pair * 128, (pair + 1) * 128)
        qp, kp, vp = q[:, cols], k[:, cols], v[:, cols]
        both = []
        for e in range(2):
            s = dot_nt(jnp.where(head_mask(qp, e), qp, jnp.zeros_like(qp)), kp)
            top = jnp.max(s, axis=-1, keepdims=True)
            p = jnp.exp(s - top)
            total = jnp.sum(p, axis=-1, keepdims=True)
            both.append(dot(p.astype(BF16), vp) * (1.0 / total))
            lse_all = jnp.where(lane == 2 * pair + e, top + jnp.log(total), lse_all)
        mixed.append(jnp.where(head_mask(both[0], 0), both[0], both[1]).astype(BF16))
    lse_ref[0] = jnp.transpose(lse_all)[0:HEADS, :]
    o = jnp.concatenate(mixed, axis=1)
    o_ref[0] = o
    xa = x0 + dot(o, wout_ref[0])
    xa_ref[0] = xa
    h1 = norm(xa, gain_ref[1:2, :], shift_ref[1:2, :])[0].astype(BF16)
    h1_ref[0] = h1
    branch = mlp_forward(h1, wup_ref[0], bup_ref[0:1, :], wdown_ref[0], act_ref.at[0], slope_ref.at[0])
    x1_scr[...] = xa + branch + bdown_ref[0:1, :]
    half = rows // 2
    keep_ref[0] = x1_scr[pl.ds(pl.multiple_of(part * half, half), half), :].astype(BF16)
    send_ref[0] = x1_scr[pl.ds(pl.multiple_of((1 - part) * half, half), half), :].astype(BF16)


def pick_rows(where_ref, both_scr, step_rows):
    return jnp.concatenate([both_scr[where_ref[s]] for s in range(GROUP_FRAMES)], axis=0)


def lane_heads(dtype):
    c = lax.broadcasted_iota(jnp.int32, (TILE, 128), 0)
    h = lax.broadcasted_iota(jnp.int32, (TILE, 128), 1)
    return (c // HEAD == h).astype(dtype)


def slot_places(slots_ref, where_scr, frames):
    sp = lax.axis_index("sp")
    group = (sp * frames) // GROUP_FRAMES
    part = lax.rem(sp, GROUP_FRAMES // frames)
    for t in range(GROUP_FRAMES):
        where_scr[slots_ref[group, t]] = lax.rem(t + GROUP_FRAMES - part * frames, GROUP_FRAMES)


def time_scores(q, k, spread, count):
    parts = []
    for t, s in PAIRS:
        parts.append((q[t] * k[s]).astype(BF16))
    return dot(jnp.concatenate(parts, axis=0), spread)


def time_probs(scores, count):
    blocks = [scores[i * count : (i + 1) * count] for i in range(len(PAIRS))]
    probs = []
    at = 0
    for t in range(VIDEO_STEPS):
        mine = blocks[at : at + t + 1]
        at += t + 1
        top = functools.reduce(jnp.maximum, mine)
        raw = [jnp.exp(b - top) for b in mine]
        inv = 1.0 / functools.reduce(lambda a, b: a + b, raw)
        probs.extend([r * inv for r in raw])
    return probs


def time_forward_kernel(
    slots_ref, keep_ref, recv_ref, cot_ref, cotr_ref, gain_ref, shift_ref,
    wqkv_ref, wout_ref, wup_ref, bup_ref, wdown_ref, bdown_ref,
    own_ref, send_ref, x_ref, h2_ref, qkv_ref, o_ref, h3_ref, act_ref, du_ref, gr_ref, dxb_ref,
    small_ref,
    where_scr, both_scr, slope_scr,
):
    frames = keep_ref.shape[0]
    count = keep_ref.shape[1]
    step = pl.program_id(0)
    part = lax.rem(lax.axis_index("sp"), GROUP_FRAMES // frames)
    clear_first(small_ref)

    @pl.when(step == 0)
    def _():
        slot_places(slots_ref, where_scr, frames)

    both_scr[0:frames] = keep_ref[...]
    both_scr[frames:] = recv_ref[...]
    x_low = pick_rows(where_scr, both_scr, count)
    x_ref[...] = x_low
    x = x_low.astype(F32)
    h2 = norm(x, gain_ref[2:3, :], shift_ref[2:3, :])[0].astype(BF16)
    h2_ref[...] = h2
    q, k, v = qkv_rows(h2, wqkv_ref[0])
    qkv_ref[:, 0:TILE] = q
    qkv_ref[:, TILE : 2 * TILE] = k
    qkv_ref[:, 2 * TILE :] = v

    def split(rows):
        return [rows[s * count : (s + 1) * count].astype(F32) for s in range(GROUP_FRAMES)]

    qs, ks, vs = split(q), split(k), split(v)
    spread = lane_heads(BF16)
    probs = time_probs(time_scores(qs, ks, spread, count), count)
    wide = dot_nt(jnp.concatenate([p.astype(BF16) for p in probs], axis=0), spread)
    mixed = []
    at = 0
    for t in range(VIDEO_STEPS):
        total = None
        for s in range(t + 1):
            piece = wide[at * count : (at + 1) * count] * vs[s]
            total = piece if total is None else total + piece
            at += 1
        mixed.append(total)
    mixed.extend(vs[VIDEO_STEPS:])
    o = jnp.concatenate([m.astype(BF16) for m in mixed], axis=0)
    o_ref[...] = o
    xb = x + dot(o, wout_ref[0]).astype(BF16).astype(F32)
    h3, unit, inv = norm(xb, gain_ref[3:4, :], shift_ref[3:4, :])
    h3 = h3.astype(BF16)
    h3_ref[...] = h3
    branch = mlp_forward(h3, wup_ref[0], bup_ref[1:2, :], wdown_ref[0], act_ref, slope_scr)
    out = (xb + branch + bdown_ref[1:2, :]).astype(BF16)
    for s in range(GROUP_FRAMES):
        both_scr[where_scr[s]] = out[s * count : (s + 1) * count]
    own_ref[...] = both_scr[0:frames]
    send_ref[...] = both_scr[frames:]

    places = pl.ds(pl.multiple_of(part * (cot_ref.shape[1] // 2) + step * count, count), count)
    both_scr[0:frames] = cot_ref[:, places, :]
    both_scr[frames:] = cotr_ref[:, places, :]
    grad_low = pick_rows(where_scr, both_scr, count)
    gr_ref[...] = grad_low
    grad = grad_low.astype(F32)
    dh = mlp_backward(grad_low, wup_ref[0], wdown_ref[0], slope_scr, du_ref, small_ref)
    small_ref[0:1, :] += column_sum(dh * unit)
    small_ref[1:2, :] += column_sum(dh)
    small_ref[2:3, :] += column_sum(grad)
    dxb_ref[...] = grad + norm_back(dh, unit, inv, gain_ref[3:4, :])


def time_backward_kernel(
    after_ref, slots_ref, x_ref, qkv_ref, dxb_ref, gain_ref, shift_ref, wqkv_ref, wout_ref,
    own_ref, send_ref, ar_ref, dqkv_ref, small_ref,
    where_scr, both_scr,
):
    frames = own_ref.shape[0]
    count = own_ref.shape[1]
    clear_first(small_ref)

    @pl.when(pl.program_id(0) == 0)
    def _():
        slot_places(slots_ref, where_scr, frames)

    def split(rows):
        return [rows[s * count : (s + 1) * count].astype(F32) for s in range(GROUP_FRAMES)]

    dxb = dxb_ref[...]
    ar = dxb.astype(BF16)
    ar_ref[...] = ar
    do = split(dot_nt(ar, wout_ref[0]).astype(BF16))
    qs = split(qkv_ref[:, 0:TILE])
    ks = split(qkv_ref[:, TILE : 2 * TILE])
    vs = split(qkv_ref[:, 2 * TILE :])
    spread = lane_heads(BF16)
    probs = time_probs(time_scores(qs, ks, spread, count), count)
    dps = time_scores(do, vs, spread, count)
    dps = [dps[i * count : (i + 1) * count] for i in range(len(PAIRS))]
    dss = []
    at = 0
    for t in range(VIDEO_STEPS):
        centre = functools.reduce(
            lambda a, b: a + b, [probs[at + s] * dps[at + s] for s in range(t + 1)]
        )
        dss.extend([probs[at + s] * (dps[at + s] - centre) for s in range(t + 1)])
        at += t + 1
    wide_p = dot_nt(jnp.concatenate([p.astype(BF16) for p in probs], axis=0), spread)
    wide_ds = dot_nt(jnp.concatenate([d.astype(BF16) for d in dss], axis=0), spread)
    dq = [None] * GROUP_FRAMES
    dk = [None] * GROUP_FRAMES
    dv = [None] * GROUP_FRAMES

    def add(table, index, piece):
        table[index] = piece if table[index] is None else table[index] + piece

    for i, (t, s) in enumerate(PAIRS):
        rows = slice(i * count, (i + 1) * count)
        add(dq, t, wide_ds[rows] * ks[s])
        add(dk, s, wide_ds[rows] * qs[t])
        add(dv, s, wide_p[rows] * do[t])
    for t in range(VIDEO_STEPS, GROUP_FRAMES):
        dq[t] = jnp.zeros_like(do[t])
        dk[t] = jnp.zeros_like(do[t])
        dv[t] = do[t]
    dq = jnp.concatenate([(d * SCALE).astype(BF16) for d in dq], axis=0)
    dk = jnp.concatenate([d.astype(BF16) for d in dk], axis=0)
    dv = jnp.concatenate([d.astype(BF16) for d in dv], axis=0)
    dqkv_ref[:, 0:TILE] = dq
    dqkv_ref[:, TILE : 2 * TILE] = dk
    dqkv_ref[:, 2 * TILE :] = dv
    dh = (
        dot_nt(dq, wqkv_ref[0, :, 0:TILE])
        + dot_nt(dk, wqkv_ref[0, :, TILE : 2 * TILE])
        + dot_nt(dv, wqkv_ref[0, :, 2 * TILE :])
    )
    gain = gain_ref[2:3, :]
    unit, inv = norm(x_ref[...].astype(F32), gain, shift_ref[2:3, :])[1:]
    small_ref[0:1, :] += column_sum(dh * unit)
    small_ref[1:2, :] += column_sum(dh)
    dxp = norm_back(dh, unit, inv, gain).astype(BF16).astype(F32)
    dx1 = (dxb + dxp).astype(BF16)
    for s in range(GROUP_FRAMES):
        both_scr[where_scr[s]] = dx1[s * count : (s + 1) * count]
    own_ref[...] = both_scr[0:frames]
    send_ref[...] = both_scr[frames:]


def space_mlp_back_kernel(
    after_ref, own_ref, recv_ref, xa_ref, slope_ref, gain_ref, shift_ref, wup_ref, wdown_ref,
    gr_ref, du_ref, dxa_ref, ar_ref, small_ref,
):
    part = lax.rem(lax.axis_index("sp"), 2)
    clear_first(small_ref)
    half = own_ref.shape[1]
    gr_ref[0, pl.ds(pl.multiple_of(part * half, half), half), :] = own_ref[0]
    gr_ref[0, pl.ds(pl.multiple_of((1 - part) * half, half), half), :] = recv_ref[0]
    grad_low = gr_ref[0]
    grad = grad_low.astype(F32)
    dh = mlp_backward(grad_low, wup_ref[0], wdown_ref[0], slope_ref.at[0], du_ref.at[0], small_ref)
    gain = gain_ref[1:2, :]
    unit, inv = norm(xa_ref[0], gain, shift_ref[1:2, :])[1:]
    small_ref[0:1, :] += column_sum(dh * unit)
    small_ref[1:2, :] += column_sum(dh)
    small_ref[2:3, :] += column_sum(grad)
    dxa = grad + norm_back(dh, unit, inv, gain)
    dxa_ref[0] = dxa
    ar_ref[0] = dxa.astype(BF16)


def space_attn_back_kernel(
    after_ref, dxa_ref, qkv_ref, lse_ref, o_ref, wout_ref, dqkv_ref,
):
    do = dot_nt(dxa_ref[0].astype(BF16), wout_ref[0]).astype(BF16)
    both = do.astype(F32) * o_ref[0].astype(F32)
    high = both.astype(BF16)
    rest = (both - high.astype(F32)).astype(BF16)
    h = lax.broadcasted_iota(jnp.int32, (HEADS, TILE), 0)
    c = lax.broadcasted_iota(jnp.int32, (HEADS, TILE), 1)
    pick = (c // HEAD == h).astype(BF16)
    centre = dot_nt(pick, high) + dot_nt(pick, rest)
    for pair in range(HEADS // 2):
        cols = slice(pair * 128, (pair + 1) * 128)
        qp = qkv_ref[0, :, pair * 128 : (pair + 1) * 128]
        kp = qkv_ref[0, :, TILE + pair * 128 : TILE + (pair + 1) * 128]
        vp = qkv_ref[0, :, 2 * TILE + pair * 128 : 2 * TILE + (pair + 1) * 128]
        dop = do[:, cols]
        parts = []
        for e in range(2):
            row = slice(2 * pair + e, 2 * pair + e + 1)
            mask = head_mask(kp, e)
            zero = jnp.zeros_like(kp)
            st = dot_nt(jnp.where(mask, kp, zero), qp)
            pt = jnp.exp(st - lse_ref[0, row, :])
            dpt = dot_nt(jnp.where(mask, vp, zero), dop)
            dst = (pt * (dpt - centre[row, :])).astype(BF16)
            parts.append((dot_tn(dst, kp) * SCALE, dot(dst, qp), dot(pt.astype(BF16), dop)))
        mask = head_mask(parts[0][0], 0)
        for index in range(3):
            at = index * TILE + pair * 128
            dqkv_ref[0, :, at : at + 128] = jnp.where(mask, parts[0][index], parts[1][index]).astype(BF16)


def finish_kernel(
    after_ref, tok_ref, dxa_ref, dqkv_ref, own_ref, recv_ref, gain_ref, shift_ref, wqkv_ref,
    gtok_ref, out_ref, small_ref,
):
    part = lax.rem(lax.axis_index("sp"), 2)
    clear_first(small_ref)
    half = own_ref.shape[1]
    out_ref[0, pl.ds(pl.multiple_of(part * half, half), half), :] = own_ref[0]
    out_ref[0, pl.ds(pl.multiple_of((1 - part) * half, half), half), :] = recv_ref[0]
    dh = dot_nt(dqkv_ref[0], wqkv_ref[0])
    gain = gain_ref[0:1, :]
    unit, inv = norm(tok_ref[0].astype(F32), gain, shift_ref[0:1, :])[1:]
    small_ref[0:1, :] += column_sum(dh * unit)
    small_ref[1:2, :] += column_sum(dh)
    gtok_ref[0] = (dxa_ref[0] + norm_back(dh, unit, inv, gain)).astype(BF16)


def place_of(block, order, sp):
    bits = len(order)
    mixed = jnp.bitwise_xor(block, sp)
    slot = jnp.int32(0)
    for i, b in enumerate(order):
        bit = jnp.bitwise_and(lax.shift_right_logical(mixed, jnp.int32(b)), 1)
        slot = slot + lax.shift_left(bit, jnp.int32(bits - 1 - i))
    return slot


def put_blocks(result, first, size, at, order, keep_ref, send_ref, cut=None):
    sp = lax.axis_index("sp")
    part = lax.rem(sp, 2)
    low = result.astype(BF16)
    take = slice(0, size) if cut is None else cut
    width = take.stop - take.start
    for j in range(result.shape[0] // (2 * size)):
        even = low[2 * j * size : (2 * j + 1) * size][take]
        odd = low[(2 * j + 1) * size : (2 * j + 2) * size][take]
        slot = place_of(first + 2 * j, order[1:], sp)
        keep_ref[slot, pl.ds(at, width), :] = jnp.where(part == 0, even, odd)
        send_ref[slot, pl.ds(at, width), :] = jnp.where(part == 0, odd, even)


def mlp_weights_kernel(orders, *refs):
    h_ref, du_ref, act_ref, gr_ref = refs[:4]
    extra = refs[4:-4]
    keep_a, send_a, keep_b, send_b = refs[-4:]
    slots = 2 * keep_a.shape[0]
    up_size = h_ref.shape[1] // slots
    down_size = 4 * TILE // slots
    zero = jnp.int32(0)
    j = pl.program_id(0)
    up = dot_tn(h_ref[...], du_ref[...])
    put_blocks(up, zero, up_size, pl.multiple_of(j * up_size, up_size), orders[0], keep_a, send_a)
    down = dot_tn(act_ref[...], gr_ref[...])
    put_blocks(down, j * (TILE // down_size), down_size, 0, orders[1], keep_b, send_b)
    if extra:

        @pl.when(j == 0)
        def _():
            out = dot_tn(extra[0][...], extra[1][...])
            put_blocks(out, zero, up_size, down_size, orders[1], keep_b, send_b)


def attn_weights_kernel(order, h_ref, dqkv_ref, o_ref, ar_ref, keep_ref, send_ref):
    size = h_ref.shape[1] // (2 * keep_ref.shape[0])
    zero = jnp.int32(0)
    for j in range(3):
        cols = slice(j * TILE, (j + 1) * TILE)
        put_blocks(dot_tn(h_ref[...], dqkv_ref[:, cols]), zero, size, j * size, order, keep_ref, send_ref)
    put_blocks(dot_tn(o_ref[...], ar_ref[...]), zero, size, 3 * size, order, keep_ref, send_ref)


def qkv_weights_kernel(orders, h_ref, dqkv_ref, keep_a, send_a, keep_b, send_b):
    size = h_ref.shape[1] // (2 * keep_a.shape[0])
    zero = jnp.int32(0)
    half = size // 2
    put_blocks(dot_tn(h_ref[...], dqkv_ref[:, :TILE]), zero, size, 0, orders[0], keep_a, send_a)
    put_blocks(dot_tn(h_ref[...], dqkv_ref[:, TILE : 2 * TILE]), zero, size, 0, orders[1], keep_b, send_b)
    last = dot_tn(h_ref[...], dqkv_ref[:, 2 * TILE :])
    put_blocks(last, zero, size, size, orders[0], keep_a, send_a, slice(0, half))
    put_blocks(last, zero, size, size, orders[1], keep_b, send_b, slice(half, size))


def whole_spec(array):
    rank = len(array.shape)
    return pl.BlockSpec(array.shape, lambda i: (0,) * rank)


def layer_spec(array, layer):
    return pl.BlockSpec((1,) + array.shape[1:], lambda i: (layer,) + (0,) * (len(array.shape) - 1))


def step_spec(shape, axis=0):
    rank = len(shape)
    return pl.BlockSpec(shape, lambda i: (0,) * axis + (i,) + (0,) * (rank - axis - 1))


def params(limit_mib):
    return pltpu.CompilerParams(dimension_semantics=("arbitrary",), vmem_limit_bytes=limit_mib * MIB)


def cost(flops, read):
    return pl.CostEstimate(flops=int(flops), bytes_accessed=int(read), transcendentals=0)


def sds(shape, dtype):
    return jax.ShapeDtypeStruct(shape, dtype)


def add_low(a, b):
    return (a.astype(F32) + b.astype(F32)).astype(BF16)


def swap(array, axis, size, bit):
    return lax.ppermute(array, axis, [(i, i ^ (1 << bit)) for i in range(size)])


def sum_scatter(keep, send, order, sp_size, grp_size):
    recv = swap(send, "sp", sp_size, order[0])
    for b in order[1:]:
        half = keep.shape[0] // 2
        send = add_low(keep[half:], recv[half:])
        keep = add_low(keep[:half], recv[:half])
        recv = swap(send, "sp", sp_size, b)
    now = add_low(keep, recv)
    for b in range(grp_size.bit_length() - 1):
        now = add_low(now, swap(now, "grp", grp_size, b))
    return now[0].astype(F32)


def shards(sizes, tokens, frame_slot, norm_gain, norm_shift, w_qkv, w_out, w_up, b_up, w_down, b_down, cotangent):
    grp_size, sp_size = sizes
    frames, patches, width = tokens.shape
    hidden = w_up.shape[2]
    assert GROUP_FRAMES == 2 * frames
    half = patches // 2
    rows = frames * patches
    sp_bits = sp_size.bit_length() - 1
    core_swap = functools.partial(swap, axis="sp", size=sp_size, bit=0)
    macs = rows * width

    cot_recv = core_swap(cotangent)

    def frame_out(cols, dtype):
        return sds((frames, patches, cols), dtype)

    frame_block = lambda cols: step_spec((1, patches, cols))
    half_block = step_spec((1, half, width))
    (x_keep, x_send, h0, qkv0, lse0, o0, xa, h1, act0, slope0) = pl.pallas_call(
        space_forward_kernel,
        grid=(frames,),
        in_specs=[
            frame_block(width), whole_spec(norm_gain), whole_spec(norm_shift), layer_spec(w_qkv, 0),
            layer_spec(w_out, 0), layer_spec(w_up, 0), whole_spec(b_up), layer_spec(w_down, 0),
            whole_spec(b_down),
        ],
        out_specs=[
            half_block, half_block, frame_block(width), frame_block(3 * width),
            step_spec((1, HEADS, patches)), frame_block(width), frame_block(width),
            frame_block(width), frame_block(hidden), frame_block(hidden),
        ],
        out_shape=[
            sds((frames, half, width), BF16), sds((frames, half, width), BF16), frame_out(width, BF16),
            frame_out(3 * width, BF16), sds((frames, HEADS, patches), F32), frame_out(width, BF16),
            frame_out(width, F32), frame_out(width, BF16), frame_out(hidden, BF16),
            frame_out(hidden, BF16),
        ],
        scratch_shapes=[pltpu.VMEM((patches, width), F32)],
        compiler_params=params(56),
        cost_estimate=cost(2 * macs * (4 * width + 2 * hidden), 30e6),
    )(tokens, norm_gain, norm_shift, w_qkv, w_out, w_up, b_up, w_down, b_down)
    x_recv = core_swap(x_send)

    steps = 4
    count = half // steps
    step_rows = GROUP_FRAMES * count
    place_block = step_spec((frames, count, width), 1)
    row_block = lambda cols: step_spec((step_rows, cols))
    smem = pl.BlockSpec(memory_space=pltpu.SMEM)
    place_scratch = [
        pltpu.SMEM((GROUP_FRAMES,), jnp.int32),
        pltpu.VMEM((GROUP_FRAMES, count, width), BF16),
    ]
    small_shape = sds((8, TILE), F32)
    small_spec = pl.BlockSpec((8, TILE), lambda i: (0, 0))
    half_shape = sds((frames, half, width), BF16)
    (out_own, out_send, xt, h2, qkv1, o1, h3, act1, du1, gr1, dxb, small3) = pl.pallas_call(
        time_forward_kernel,
        grid=(steps,),
        in_specs=[
            smem, place_block, place_block, whole_spec(cotangent), whole_spec(cotangent),
            whole_spec(norm_gain), whole_spec(norm_shift), layer_spec(w_qkv, 1), layer_spec(w_out, 1),
            layer_spec(w_up, 1), whole_spec(b_up), layer_spec(w_down, 1), whole_spec(b_down),
        ],
        out_specs=[
            place_block, place_block, row_block(width), row_block(width), row_block(3 * width),
            row_block(width), row_block(width), row_block(hidden), row_block(hidden), row_block(width),
            row_block(width), small_spec,
        ],
        out_shape=[
            half_shape, half_shape, sds((rows, width), BF16), sds((rows, width), BF16),
            sds((rows, 3 * width), BF16), sds((rows, width), BF16), sds((rows, width), BF16),
            sds((rows, hidden), BF16), sds((rows, hidden), BF16), sds((rows, width), BF16),
            sds((rows, width), F32), small_shape,
        ],
        scratch_shapes=place_scratch + [pltpu.VMEM((step_rows, hidden), BF16)],
        compiler_params=params(56),
        cost_estimate=cost(2 * macs * (4 * width + 4 * hidden), 30e6),
    )(
        frame_slot, x_keep, x_recv, cotangent, cot_recv, norm_gain, norm_shift, w_qkv, w_out, w_up,
        b_up, w_down, b_down,
    )
    out_recv = core_swap(out_send)

    slots = sp_size // 2
    size = width // sp_size
    down_size = hidden // sp_size

    def buffer_specs(*heights):
        shapes = []
        for height in heights:
            shapes += [sds((slots, height, TILE), BF16)] * 2
        return [pl.BlockSpec(s.shape, lambda i: (0, 0, 0)) for s in shapes], shapes

    def mlp_weights(h, du, act, gr, *extra):
        specs, shapes = buffer_specs(4 * size, down_size + (size if extra else 0))
        return pl.pallas_call(
            functools.partial(mlp_weights_kernel, (order_a, order_b)),
            grid=(hidden // TILE,),
            in_specs=[
                whole_spec(h), pl.BlockSpec((rows, TILE), lambda i: (0, i)),
                pl.BlockSpec((rows, TILE), lambda i: (0, i)), whole_spec(gr),
            ] + [whole_spec(e) for e in extra],
            out_specs=specs,
            out_shape=shapes,
            compiler_params=params(40),
            cost_estimate=cost(2 * macs * 2 * hidden, 14e6),
        )(h, du, act, gr, *extra)

    order_a = list(range(sp_bits))
    order_b = [0, 2, 1] + list(range(3, sp_bits))
    any_spec = pl.BlockSpec(memory_space=pl.ANY)
    collect = functools.partial(sum_scatter, sp_size=sp_size, grp_size=grp_size)

    up1_keep, up1_send, down1_keep, down1_send = mlp_weights(h3, du1, act1, gr1)
    up1 = collect(up1_keep, up1_send, order_a)
    down1 = collect(down1_keep, down1_send, order_b)

    (dx_own, dx_send, ar1, dqkv1, small2) = pl.pallas_call(
        time_backward_kernel,
        grid=(steps,),
        in_specs=[
            any_spec, smem, row_block(width), row_block(3 * width), row_block(width),
            whole_spec(norm_gain), whole_spec(norm_shift), layer_spec(w_qkv, 1), layer_spec(w_out, 1),
        ],
        out_specs=[place_block, place_block, row_block(width), row_block(3 * width), small_spec],
        out_shape=[
            half_shape, half_shape, sds((rows, width), BF16), sds((rows, 3 * width), BF16), small_shape,
        ],
        scratch_shapes=place_scratch,
        compiler_params=params(56),
        cost_estimate=cost(2 * macs * 4 * width, 15e6),
    )(up1_keep, frame_slot, xt, qkv1, dxb, norm_gain, norm_shift, w_qkv, w_out)
    dx_recv = core_swap(dx_send)
    specs, shapes = buffer_specs(4 * size)
    attn1_keep, attn1_send = pl.pallas_call(
        functools.partial(attn_weights_kernel, order_a),
        grid=(1,),
        in_specs=[whole_spec(h2), whole_spec(dqkv1), whole_spec(o1), whole_spec(ar1)],
        out_specs=specs,
        out_shape=shapes,
        compiler_params=params(40),
        cost_estimate=cost(2 * macs * 4 * width, 8e6),
    )(h2, dqkv1, o1, ar1)
    attn1 = collect(attn1_keep, attn1_send, order_a)

    (gr0, du0, dxa, ar0, small1) = pl.pallas_call(
        space_mlp_back_kernel,
        grid=(frames,),
        in_specs=[
            any_spec, half_block, half_block, frame_block(width), frame_block(hidden),
            whole_spec(norm_gain), whole_spec(norm_shift), layer_spec(w_up, 0), layer_spec(w_down, 0),
        ],
        out_specs=[
            frame_block(width), frame_block(hidden), frame_block(width), frame_block(width), small_spec,
        ],
        out_shape=[
            frame_out(width, BF16), frame_out(hidden, BF16), frame_out(width, F32),
            frame_out(width, BF16), small_shape,
        ],
        compiler_params=params(56),
        cost_estimate=cost(2 * macs * 2 * hidden, 20e6),
    )(attn1_keep, dx_own, dx_recv, xa, slope0, norm_gain, norm_shift, w_up, w_down)
    flat = lambda a: a.reshape(rows, a.shape[-1])
    up0_keep, up0_send, down0_keep, down0_send = mlp_weights(
        flat(h1), flat(du0), flat(act0), flat(gr0), flat(o0), flat(ar0)
    )
    up0 = collect(up0_keep, up0_send, order_a)
    down0 = collect(down0_keep, down0_send, order_b)

    dqkv0 = pl.pallas_call(
        space_attn_back_kernel,
        grid=(frames,),
        in_specs=[
            any_spec, frame_block(width), frame_block(3 * width), step_spec((1, HEADS, patches)),
            frame_block(width), layer_spec(w_out, 0),
        ],
        out_specs=frame_block(3 * width),
        out_shape=frame_out(3 * width, BF16),
        compiler_params=params(56),
        cost_estimate=cost(2 * macs * 6 * width, 20e6),
    )(up0_keep, dxa, qkv0, lse0, o0, w_out)

    specs, shapes = buffer_specs(size + size // 2, size + size // 2)
    qkva_keep, qkva_send, qkvb_keep, qkvb_send = pl.pallas_call(
        functools.partial(qkv_weights_kernel, (order_a, order_b)),
        grid=(1,),
        in_specs=[whole_spec(flat(h0)), whole_spec(flat(dqkv0))],
        out_specs=specs,
        out_shape=shapes,
        compiler_params=params(40),
        cost_estimate=cost(2 * macs * 3 * width, 8e6),
    )(flat(h0), flat(dqkv0))
    qkva = collect(qkva_keep, qkva_send, order_a)
    qkvb = collect(qkvb_keep, qkvb_send, order_b)

    grad_tokens, output, small0 = pl.pallas_call(
        finish_kernel,
        grid=(frames,),
        in_specs=[
            any_spec, frame_block(width), frame_block(width), frame_block(3 * width), half_block,
            half_block, whole_spec(norm_gain), whole_spec(norm_shift), layer_spec(w_qkv, 0),
        ],
        out_specs=[frame_block(width), frame_block(width), small_spec],
        out_shape=[frame_out(width, BF16), frame_out(width, BF16), small_shape],
        compiler_params=params(56),
        cost_estimate=cost(2 * macs * 3 * width, 8e6),
    )(qkva_keep, tokens, dxa, dqkv0, out_own, out_recv, norm_gain, norm_shift, w_qkv)

    small = jnp.concatenate([small0, small1, small2, small3], axis=0).astype(BF16)
    for b in range(sp_bits):
        small = add_low(small, swap(small, "sp", sp_size, b))
    for b in range(grp_size.bit_length() - 1):
        small = add_low(small, swap(small, "grp", grp_size, b))
    small = small.astype(F32).reshape(4, 8, TILE)
    sp = lax.axis_index("sp")

    def mine(array):
        size = array.shape[1] // sp_size
        return lax.dynamic_slice_in_dim(array, sp * size, size, axis=1)

    def columns(parts):
        return jnp.concatenate(parts, axis=1)

    def blocks(a, count):
        return columns([a[i * size : (i + 1) * size] for i in range(count)])

    third = jnp.concatenate([qkva[size:], qkvb[size:]], axis=0)
    return (
        output,
        grad_tokens,
        mine(small[:, 0]),
        mine(small[:, 1]),
        jnp.stack([columns([qkva[:size], qkvb[:size], third]), blocks(attn1, 3)]),
        jnp.stack([down0[down_size:], attn1[3 * size :]]),
        jnp.stack([blocks(up0, 4), blocks(up1, 4)]),
        mine(small[1::2, 4:].reshape(2, hidden)),
        jnp.stack([down0[:down_size], down1]),
        mine(small[1::2, 2]),
    )


def solution(mesh):
    rows = P(("grp", "sp"), None, None)
    in_specs = (rows, P("grp", None), P(), P(), P(), P(), P(), P(), P(), P(), rows)
    out_specs = (
        rows, rows, P(None, "sp"), P(None, "sp"), P(None, "sp", None), P(None, "sp", None),
        P(None, "sp", None), P(None, "sp"), P(None, "sp", None), P(None, "sp"),
    )
    body = functools.partial(shards, (mesh.shape["grp"], mesh.shape["sp"]))
    return jax.shard_map(body, mesh=mesh, in_specs=in_specs, out_specs=out_specs, check_vma=False)
```

```python
import functools

import jax
import jax.numpy as jnp
from jax import lax
from jax.experimental import pallas as pl
from jax.experimental.pallas import tpu as pltpu
from jax.sharding import PartitionSpec as P

HEADS = 8
HEAD = 64
VIDEO_STEPS = 6
GROUP_FRAMES = 8
NORM_EPS = 1e-05
TILE = 512
SCALE = HEAD**-0.5
TANH_A = 0.7978845608028654
TANH_B = TANH_A * 0.044715
PAIRS = [(t, s) for t in range(VIDEO_STEPS) for s in range(t + 1)]
F32 = jnp.float32
BF16 = jnp.bfloat16
MIB = 1024 * 1024


def dot(left, right):
    return jnp.dot(left, right, preferred_element_type=F32)


def dot_nt(left, right):
    return lax.dot_general(left, right, (((1,), (1,)), ((), ())), preferred_element_type=F32)


def dot_tn(left, right):
    return lax.dot_general(left, right, (((0,), (0,)), ((), ())), preferred_element_type=F32)


def norm(rows, gain, shift):
    centred = rows - jnp.mean(rows, axis=-1, keepdims=True)
    inv = lax.rsqrt(jnp.mean(centred * centred, axis=-1, keepdims=True) + NORM_EPS)
    unit = centred * inv
    return unit * gain + shift, unit, inv


def norm_back(grad, unit, inv, gain):
    grad_unit = grad * gain
    mean_grad = jnp.mean(grad_unit, axis=-1, keepdims=True)
    mean_both = jnp.mean(grad_unit * unit, axis=-1, keepdims=True)
    return inv * (grad_unit - mean_grad - unit * mean_both)


def column_sum(rows):
    return jnp.sum(rows, axis=0, keepdims=True)


def gelu_pair(u):
    square = u * u
    t = jnp.tanh(u * (TANH_A + TANH_B * square))
    half = 0.5 * u
    act = half + half * t
    slope = 0.5 + 0.5 * t + half * (1.0 - t * t) * (TANH_A + 3.0 * TANH_B * square)
    return act.astype(BF16), slope.astype(BF16)


def head_mask(lanes, which):
    lane = lax.broadcasted_iota(jnp.int32, lanes.shape, 1)
    return (lane < HEAD) if which == 0 else (lane >= HEAD)


def qkv_rows(normed, weight):
    out = []
    for part in range(3):
        piece = dot(normed, weight[:, part * TILE : (part + 1) * TILE])
        if part == 0:
            out.append(piece.astype(BF16) * BF16(SCALE))
        else:
            out.append(piece.astype(BF16))
    return out


def mlp_forward(normed, w_up, b_up, w_down, act_ref, slope_ref):
    total = None
    for j in range(w_up.shape[1] // TILE):
        cols = slice(j * TILE, (j + 1) * TILE)
        u = dot(normed, w_up[:, cols]) + b_up[:, cols]
        act, slope = gelu_pair(u)
        act_ref[:, cols] = act
        slope_ref[:, cols] = slope
        piece = dot(act, w_down[cols, :])
        total = piece if total is None else total + piece
    return total


def mlp_backward(grad_low, w_up, w_down, slope_ref, du_ref, small_ref):
    total = None
    for j in range(w_up.shape[1] // TILE):
        cols = slice(j * TILE, (j + 1) * TILE)
        du = (dot_nt(grad_low, w_down[cols, :]) * slope_ref[:, cols].astype(F32)).astype(BF16)
        du_ref[:, cols] = du
        small_ref[4 + j : 5 + j, :] += column_sum(du.astype(F32))
        piece = dot_nt(du, w_up[:, cols])
        total = piece if total is None else total + piece
    return total


def clear_first(small_ref):
    @pl.when(pl.program_id(0) == 0)
    def _():
        small_ref[...] = jnp.zeros_like(small_ref)


def space_forward_kernel(
    tok_ref, gain_ref, shift_ref, wqkv_ref, wout_ref, wup_ref, bup_ref, wdown_ref, bdown_ref,
    keep_ref, send_ref, h0_ref, qkv_ref, lse_ref, o_ref, xa_ref, h1_ref, act_ref, slope_ref,
    x1_scr,
):
    part = lax.rem(lax.axis_index("sp"), 2)
    x0 = tok_ref[0].astype(F32)
    rows = x0.shape[0]
    h0 = norm(x0, gain_ref[0:1, :], shift_ref[0:1, :])[0].astype(BF16)
    h0_ref[0] = h0
    q, k, v = qkv_rows(h0, wqkv_ref[0])
    qkv_ref[0, :, 0:TILE] = q
    qkv_ref[0, :, TILE : 2 * TILE] = k
    qkv_ref[0, :, 2 * TILE :] = v
    lane = lax.broadcasted_iota(jnp.int32, (rows, 128), 1)
    lse_all = jnp.zeros((rows, 128), F32)
    mixed = []
    for pair in range(HEADS // 2):
        cols = slice(pair * 128, (pair + 1) * 128)
        qp, kp, vp = q[:, cols], k[:, cols], v[:, cols]
        both = []
        for e in range(2):
            s = dot_nt(jnp.where(head_mask(qp, e), qp, jnp.zeros_like(qp)), kp)
            top = jnp.max(s, axis=-1, keepdims=True)
            p = jnp.exp(s - top)
            total = jnp.sum(p, axis=-1, keepdims=True)
            both.append(dot(p.astype(BF16), vp) * (1.0 / total))
            lse_all = jnp.where(lane == 2 * pair + e, top + jnp.log(total), lse_all)
        mixed.append(jnp.where(head_mask(both[0], 0), both[0], both[1]).astype(BF16))
    lse_ref[0] = jnp.transpose(lse_all)[0:HEADS, :]
    o = jnp.concatenate(mixed, axis=1)
    o_ref[0] = o
    xa = x0 + dot(o, wout_ref[0])
    xa_ref[0] = xa
    h1 = norm(xa, gain_ref[1:2, :], shift_ref[1:2, :])[0].astype(BF16)
    h1_ref[0] = h1
    branch = mlp_forward(h1, wup_ref[0], bup_ref[0:1, :], wdown_ref[0], act_ref.at[0], slope_ref.at[0])
    x1_scr[...] = xa + branch + bdown_ref[0:1, :]
    half = rows // 2
    keep_ref[0] = x1_scr[pl.ds(pl.multiple_of(part * half, half), half), :].astype(BF16)
    send_ref[0] = x1_scr[pl.ds(pl.multiple_of((1 - part) * half, half), half), :].astype(BF16)


def pick_rows(where_ref, both_scr, step_rows):
    return jnp.concatenate([both_scr[where_ref[s]] for s in range(GROUP_FRAMES)], axis=0)


def lane_heads(dtype):
    c = lax.broadcasted_iota(jnp.int32, (TILE, 128), 0)
    h = lax.broadcasted_iota(jnp.int32, (TILE, 128), 1)
    return (c // HEAD == h).astype(dtype)


def slot_places(slots_ref, where_scr, frames):
    sp = lax.axis_index("sp")
    group = (sp * frames) // GROUP_FRAMES
    part = lax.rem(sp, GROUP_FRAMES // frames)
    for t in range(GROUP_FRAMES):
        where_scr[slots_ref[group, t]] = lax.rem(t + GROUP_FRAMES - part * frames, GROUP_FRAMES)


def time_scores(q, k, spread, count):
    parts = []
    for t, s in PAIRS:
        parts.append((q[t] * k[s]).astype(BF16))
    return dot(jnp.concatenate(parts, axis=0), spread)


def time_probs(scores, count):
    blocks = [scores[i * count : (i + 1) * count] for i in range(len(PAIRS))]
    probs = []
    at = 0
    for t in range(VIDEO_STEPS):
        mine = blocks[at : at + t + 1]
        at += t + 1
        top = functools.reduce(jnp.maximum, mine)
        raw = [jnp.exp(b - top) for b in mine]
        inv = 1.0 / functools.reduce(lambda a, b: a + b, raw)
        probs.extend([r * inv for r in raw])
    return probs


def time_forward_kernel(
    slots_ref, keep_ref, recv_ref, cot_ref, cotr_ref, gain_ref, shift_ref,
    wqkv_ref, wout_ref, wup_ref, bup_ref, wdown_ref, bdown_ref,
    own_ref, send_ref, x_ref, h2_ref, qkv_ref, o_ref, h3_ref, act_ref, du_ref, gr_ref, dxb_ref,
    small_ref,
    where_scr, both_scr, slope_scr,
):
    frames = keep_ref.shape[0]
    count = keep_ref.shape[1]
    step = pl.program_id(0)
    part = lax.rem(lax.axis_index("sp"), GROUP_FRAMES // frames)
    clear_first(small_ref)

    @pl.when(step == 0)
    def _():
        slot_places(slots_ref, where_scr, frames)

    both_scr[0:frames] = keep_ref[...]
    both_scr[frames:] = recv_ref[...]
    x_low = pick_rows(where_scr, both_scr, count)
    x_ref[...] = x_low
    x = x_low.astype(F32)
    h2 = norm(x, gain_ref[2:3, :], shift_ref[2:3, :])[0].astype(BF16)
    h2_ref[...] = h2
    q, k, v = qkv_rows(h2, wqkv_ref[0])
    qkv_ref[:, 0:TILE] = q
    qkv_ref[:, TILE : 2 * TILE] = k
    qkv_ref[:, 2 * TILE :] = v

    def split(rows):
        return [rows[s * count : (s + 1) * count].astype(F32) for s in range(GROUP_FRAMES)]

    qs, ks, vs = split(q), split(k), split(v)
    spread = lane_heads(BF16)
    probs = time_probs(time_scores(qs, ks, spread, count), count)
    wide = dot_nt(jnp.concatenate([p.astype(BF16) for p in probs], axis=0), spread)
    mixed = []
    at = 0
    for t in range(VIDEO_STEPS):
        total = None
        for s in range(t + 1):
            piece = wide[at * count : (at + 1) * count] * vs[s]
            total = piece if total is None else total + piece
            at += 1
        mixed.append(total)
    mixed.extend(vs[VIDEO_STEPS:])
    o = jnp.concatenate([m.astype(BF16) for m in mixed], axis=0)
    o_ref[...] = o
    xb = x + dot(o, wout_ref[0]).astype(BF16).astype(F32)
    h3, unit, inv = norm(xb, gain_ref[3:4, :], shift_ref[3:4, :])
    h3 = h3.astype(BF16)
    h3_ref[...] = h3
    branch = mlp_forward(h3, wup_ref[0], bup_ref[1:2, :], wdown_ref[0], act_ref, slope_scr)
    out = (xb + branch + bdown_ref[1:2, :]).astype(BF16)
    for s in range(GROUP_FRAMES):
        both_scr[where_scr[s]] = out[s * count : (s + 1) * count]
    own_ref[...] = both_scr[0:frames]
    send_ref[...] = both_scr[frames:]

    places = pl.ds(pl.multiple_of(part * (cot_ref.shape[1] // 2) + step * count, count), count)
    both_scr[0:frames] = cot_ref[:, places, :]
    both_scr[frames:] = cotr_ref[:, places, :]
    grad_low = pick_rows(where_scr, both_scr, count)
    gr_ref[...] = grad_low
    grad = grad_low.astype(F32)
    dh = mlp_backward(grad_low, wup_ref[0], wdown_ref[0], slope_scr, du_ref, small_ref)
    small_ref[0:1, :] += column_sum(dh * unit)
    small_ref[1:2, :] += column_sum(dh)
    small_ref[2:3, :] += column_sum(grad)
    dxb_ref[...] = grad + norm_back(dh, unit, inv, gain_ref[3:4, :])


def time_backward_kernel(
    slots_ref, x_ref, qkv_ref, dxb_ref, gain_ref, shift_ref, wqkv_ref, wout_ref,
    own_ref, send_ref, ar_ref, dqkv_ref, small_ref,
    where_scr, both_scr,
):
    frames = own_ref.shape[0]
    count = own_ref.shape[1]
    clear_first(small_ref)

    @pl.when(pl.program_id(0) == 0)
    def _():
        slot_places(slots_ref, where_scr, frames)

    def split(rows):
        return [rows[s * count : (s + 1) * count].astype(F32) for s in range(GROUP_FRAMES)]

    dxb = dxb_ref[...]
    ar = dxb.astype(BF16)
    ar_ref[...] = ar
    do = split(dot_nt(ar, wout_ref[0]).astype(BF16))
    qs = split(qkv_ref[:, 0:TILE])
    ks = split(qkv_ref[:, TILE : 2 * TILE])
    vs = split(qkv_ref[:, 2 * TILE :])
    spread = lane_heads(BF16)
    probs = time_probs(time_scores(qs, ks, spread, count), count)
    dps = time_scores(do, vs, spread, count)
    dps = [dps[i * count : (i + 1) * count] for i in range(len(PAIRS))]
    dss = []
    at = 0
    for t in range(VIDEO_STEPS):
        centre = functools.reduce(
            lambda a, b: a + b, [probs[at + s] * dps[at + s] for s in range(t + 1)]
        )
        dss.extend([probs[at + s] * (dps[at + s] - centre) for s in range(t + 1)])
        at += t + 1
    wide_p = dot_nt(jnp.concatenate([p.astype(BF16) for p in probs], axis=0), spread)
    wide_ds = dot_nt(jnp.concatenate([d.astype(BF16) for d in dss], axis=0), spread)
    dq = [None] * GROUP_FRAMES
    dk = [None] * GROUP_FRAMES
    dv = [None] * GROUP_FRAMES

    def add(table, index, piece):
        table[index] = piece if table[index] is None else table[index] + piece

    for i, (t, s) in enumerate(PAIRS):
        rows = slice(i * count, (i + 1) * count)
        add(dq, t, wide_ds[rows] * ks[s])
        add(dk, s, wide_ds[rows] * qs[t])
        add(dv, s, wide_p[rows] * do[t])
    for t in range(VIDEO_STEPS, GROUP_FRAMES):
        dq[t] = jnp.zeros_like(do[t])
        dk[t] = jnp.zeros_like(do[t])
        dv[t] = do[t]
    dq = jnp.concatenate([(d * SCALE).astype(BF16) for d in dq], axis=0)
    dk = jnp.concatenate([d.astype(BF16) for d in dk], axis=0)
    dv = jnp.concatenate([d.astype(BF16) for d in dv], axis=0)
    dqkv_ref[:, 0:TILE] = dq
    dqkv_ref[:, TILE : 2 * TILE] = dk
    dqkv_ref[:, 2 * TILE :] = dv
    dh = (
        dot_nt(dq, wqkv_ref[0, :, 0:TILE])
        + dot_nt(dk, wqkv_ref[0, :, TILE : 2 * TILE])
        + dot_nt(dv, wqkv_ref[0, :, 2 * TILE :])
    )
    gain = gain_ref[2:3, :]
    unit, inv = norm(x_ref[...].astype(F32), gain, shift_ref[2:3, :])[1:]
    small_ref[0:1, :] += column_sum(dh * unit)
    small_ref[1:2, :] += column_sum(dh)
    dxp = norm_back(dh, unit, inv, gain).astype(BF16).astype(F32)
    dx1 = (dxb + dxp).astype(BF16)
    for s in range(GROUP_FRAMES):
        both_scr[where_scr[s]] = dx1[s * count : (s + 1) * count]
    own_ref[...] = both_scr[0:frames]
    send_ref[...] = both_scr[frames:]


def space_mlp_back_kernel(
    own_ref, recv_ref, xa_ref, slope_ref, gain_ref, shift_ref, wup_ref, wdown_ref,
    gr_ref, du_ref, dxa_ref, ar_ref, small_ref,
):
    part = lax.rem(lax.axis_index("sp"), 2)
    clear_first(small_ref)
    half = own_ref.shape[1]
    gr_ref[0, pl.ds(pl.multiple_of(part * half, half), half), :] = own_ref[0]
    gr_ref[0, pl.ds(pl.multiple_of((1 - part) * half, half), half), :] = recv_ref[0]
    grad_low = gr_ref[0]
    grad = grad_low.astype(F32)
    dh = mlp_backward(grad_low, wup_ref[0], wdown_ref[0], slope_ref.at[0], du_ref.at[0], small_ref)
    gain = gain_ref[1:2, :]
    unit, inv = norm(xa_ref[0], gain, shift_ref[1:2, :])[1:]
    small_ref[0:1, :] += column_sum(dh * unit)
    small_ref[1:2, :] += column_sum(dh)
    small_ref[2:3, :] += column_sum(grad)
    dxa = grad + norm_back(dh, unit, inv, gain)
    dxa_ref[0] = dxa
    ar_ref[0] = dxa.astype(BF16)


def space_attn_back_kernel(
    dxa_ref, qkv_ref, lse_ref, o_ref, wout_ref, dqkv_ref,
):
    do = dot_nt(dxa_ref[0].astype(BF16), wout_ref[0]).astype(BF16)
    both = do.astype(F32) * o_ref[0].astype(F32)
    high = both.astype(BF16)
    rest = (both - high.astype(F32)).astype(BF16)
    h = lax.broadcasted_iota(jnp.int32, (HEADS, TILE), 0)
    c = lax.broadcasted_iota(jnp.int32, (HEADS, TILE), 1)
    pick = (c // HEAD == h).astype(BF16)
    centre = dot_nt(pick, high) + dot_nt(pick, rest)
    for pair in range(HEADS // 2):
        cols = slice(pair * 128, (pair + 1) * 128)
        qp = qkv_ref[0, :, pair * 128 : (pair + 1) * 128]
        kp = qkv_ref[0, :, TILE + pair * 128 : TILE + (pair + 1) * 128]
        vp = qkv_ref[0, :, 2 * TILE + pair * 128 : 2 * TILE + (pair + 1) * 128]
        dop = do[:, cols]
        parts = []
        for e in range(2):
            row = slice(2 * pair + e, 2 * pair + e + 1)
            mask = head_mask(kp, e)
            zero = jnp.zeros_like(kp)
            st = dot_nt(jnp.where(mask, kp, zero), qp)
            pt = jnp.exp(st - lse_ref[0, row, :])
            dpt = dot_nt(jnp.where(mask, vp, zero), dop)
            dst = (pt * (dpt - centre[row, :])).astype(BF16)
            parts.append((dot_tn(dst, kp) * SCALE, dot(dst, qp), dot(pt.astype(BF16), dop)))
        mask = head_mask(parts[0][0], 0)
        for index in range(3):
            at = index * TILE + pair * 128
            dqkv_ref[0, :, at : at + 128] = jnp.where(mask, parts[0][index], parts[1][index]).astype(BF16)


def finish_kernel(
    tok_ref, dxa_ref, dqkv_ref, own_ref, recv_ref, gain_ref, shift_ref, wqkv_ref,
    gtok_ref, out_ref, small_ref,
):
    part = lax.rem(lax.axis_index("sp"), 2)
    clear_first(small_ref)
    half = own_ref.shape[1]
    out_ref[0, pl.ds(pl.multiple_of(part * half, half), half), :] = own_ref[0]
    out_ref[0, pl.ds(pl.multiple_of((1 - part) * half, half), half), :] = recv_ref[0]
    dh = dot_nt(dqkv_ref[0], wqkv_ref[0])
    gain = gain_ref[0:1, :]
    unit, inv = norm(tok_ref[0].astype(F32), gain, shift_ref[0:1, :])[1:]
    small_ref[0:1, :] += column_sum(dh * unit)
    small_ref[1:2, :] += column_sum(dh)
    gtok_ref[0] = (dxa_ref[0] + norm_back(dh, unit, inv, gain)).astype(BF16)


def place_of(block, order, sp):
    bits = len(order)
    mixed = jnp.bitwise_xor(block, sp)
    slot = jnp.int32(0)
    for i, b in enumerate(order):
        bit = jnp.bitwise_and(lax.shift_right_logical(mixed, jnp.int32(b)), 1)
        slot = slot + lax.shift_left(bit, jnp.int32(bits - 1 - i))
    return slot


def put_blocks(result, first, size, at, order, keep_ref, send_ref, cut=None):
    sp = lax.axis_index("sp")
    part = lax.rem(sp, 2)
    low = result.astype(BF16)
    take = slice(0, size) if cut is None else cut
    width = take.stop - take.start
    for j in range(result.shape[0] // (2 * size)):
        even = low[2 * j * size : (2 * j + 1) * size][take]
        odd = low[(2 * j + 1) * size : (2 * j + 2) * size][take]
        slot = place_of(first + 2 * j, order[1:], sp)
        keep_ref[slot, pl.ds(at, width), :] = jnp.where(part == 0, even, odd)
        send_ref[slot, pl.ds(at, width), :] = jnp.where(part == 0, odd, even)


def mlp_weights_kernel(orders, *refs):
    h_ref, du_ref, act_ref, gr_ref = refs[:4]
    extra = refs[4:-4]
    keep_a, send_a, keep_b, send_b = refs[-4:]
    slots = 2 * keep_a.shape[0]
    up_size = h_ref.shape[1] // slots
    down_size = 4 * TILE // slots
    zero = jnp.int32(0)
    j = pl.program_id(0)
    up = dot_tn(h_ref[...], du_ref[...])
    put_blocks(up, zero, up_size, pl.multiple_of(j * up_size, up_size), orders[0], keep_a, send_a)
    down = dot_tn(act_ref[...], gr_ref[...])
    put_blocks(down, j * (TILE // down_size), down_size, 0, orders[1], keep_b, send_b)
    if extra:

        @pl.when(j == 0)
        def _():
            out = dot_tn(extra[0][...], extra[1][...])
            put_blocks(out, zero, up_size, down_size, orders[1], keep_b, send_b)


def attn_weights_kernel(order, h_ref, dqkv_ref, o_ref, ar_ref, keep_ref, send_ref):
    size = h_ref.shape[1] // (2 * keep_ref.shape[0])
    zero = jnp.int32(0)
    for j in range(3):
        cols = slice(j * TILE, (j + 1) * TILE)
        put_blocks(dot_tn(h_ref[...], dqkv_ref[:, cols]), zero, size, j * size, order, keep_ref, send_ref)
    put_blocks(dot_tn(o_ref[...], ar_ref[...]), zero, size, 3 * size, order, keep_ref, send_ref)


def qkv_weights_kernel(orders, h_ref, dqkv_ref, keep_a, send_a, keep_b, send_b):
    size = h_ref.shape[1] // (2 * keep_a.shape[0])
    zero = jnp.int32(0)
    half = size // 2
    put_blocks(dot_tn(h_ref[...], dqkv_ref[:, :TILE]), zero, size, 0, orders[0], keep_a, send_a)
    put_blocks(dot_tn(h_ref[...], dqkv_ref[:, TILE : 2 * TILE]), zero, size, 0, orders[1], keep_b, send_b)
    last = dot_tn(h_ref[...], dqkv_ref[:, 2 * TILE :])
    put_blocks(last, zero, size, size, orders[0], keep_a, send_a, slice(0, half))
    put_blocks(last, zero, size, size, orders[1], keep_b, send_b, slice(half, size))


def whole_spec(array):
    rank = len(array.shape)
    return pl.BlockSpec(array.shape, lambda i: (0,) * rank)


def layer_spec(array, layer):
    return pl.BlockSpec((1,) + array.shape[1:], lambda i: (layer,) + (0,) * (len(array.shape) - 1))


def step_spec(shape, axis=0):
    rank = len(shape)
    return pl.BlockSpec(shape, lambda i: (0,) * axis + (i,) + (0,) * (rank - axis - 1))


def params(limit_mib):
    return pltpu.CompilerParams(dimension_semantics=("arbitrary",), vmem_limit_bytes=limit_mib * MIB)


def cost(flops, read):
    return pl.CostEstimate(flops=int(flops), bytes_accessed=int(read), transcendentals=0)


def sds(shape, dtype):
    return jax.ShapeDtypeStruct(shape, dtype)


def run(kernel, after, in_specs, args, aliases=None, **rest):
    skip = len(after)
    extra = skip if aliases is None else skip + len(aliases)

    def body(*refs):
        kernel(*refs[extra:])

    alias_args = [] if aliases is None else aliases
    marks = [pl.BlockSpec(memory_space=pl.ANY)] * extra
    return pl.pallas_call(
        body,
        in_specs=marks + in_specs,
        input_output_aliases={skip + i: i for i in range(len(alias_args))},
        **rest,
    )(*after, *alias_args, *args)


class Chain:
    def __init__(self, keep, send, order, sizes):
        self.keep, self.send, self.sizes = keep, send, sizes
        grp_size, sp_size = sizes
        self.path = [("sp", sp_size, b) for b in order]
        self.path += [("grp", grp_size, b) for b in range(grp_size.bit_length() - 1)]
        self.swap()

    def swap(self):
        axis, size, bit = self.path.pop(0)
        self.recv = swap(self.send, axis, size, bit)

    def step(self):
        if self.path and self.path[0][0] == "sp":
            half = self.keep.shape[0] // 2
            self.send = add_low(self.keep[half:], self.recv[half:])
            self.keep = add_low(self.keep[:half], self.recv[:half])
        else:
            self.send = self.keep = add_low(self.keep, self.recv)
        self.swap()

    def finish(self):
        while self.path:
            self.step()
        return self.keep[0].astype(F32) + self.recv[0].astype(F32)


def add_low(a, b):
    return (a.astype(F32) + b.astype(F32)).astype(BF16)


def swap(array, axis, size, bit):
    return lax.ppermute(array, axis, [(i, i ^ (1 << bit)) for i in range(size)])


def shards(sizes, tokens, frame_slot, norm_gain, norm_shift, w_qkv, w_out, w_up, b_up, w_down, b_down, cotangent):
    grp_size, sp_size = sizes
    frames, patches, width = tokens.shape
    hidden = w_up.shape[2]
    assert GROUP_FRAMES == 2 * frames
    half = patches // 2
    rows = frames * patches
    sp_bits = sp_size.bit_length() - 1
    core_swap = functools.partial(swap, axis="sp", size=sp_size, bit=0)
    macs = rows * width

    cot_recv = core_swap(cotangent)

    def frame_out(cols, dtype):
        return sds((frames, patches, cols), dtype)

    frame_block = lambda cols: step_spec((1, patches, cols))
    half_block = step_spec((1, half, width))
    (x_keep, x_send, h0, qkv0, lse0, o0, xa, h1, act0, slope0) = pl.pallas_call(
        space_forward_kernel,
        grid=(frames,),
        in_specs=[
            frame_block(width), whole_spec(norm_gain), whole_spec(norm_shift), layer_spec(w_qkv, 0),
            layer_spec(w_out, 0), layer_spec(w_up, 0), whole_spec(b_up), layer_spec(w_down, 0),
            whole_spec(b_down),
        ],
        out_specs=[
            half_block, half_block, frame_block(width), frame_block(3 * width),
            step_spec((1, HEADS, patches)), frame_block(width), frame_block(width),
            frame_block(width), frame_block(hidden), frame_block(hidden),
        ],
        out_shape=[
            sds((frames, half, width), BF16), sds((frames, half, width), BF16), frame_out(width, BF16),
            frame_out(3 * width, BF16), sds((frames, HEADS, patches), F32), frame_out(width, BF16),
            frame_out(width, F32), frame_out(width, BF16), frame_out(hidden, BF16),
            frame_out(hidden, BF16),
        ],
        scratch_shapes=[pltpu.VMEM((patches, width), F32)],
        compiler_params=params(60),
        cost_estimate=cost(2 * macs * (4 * width + 2 * hidden), 30e6),
    )(tokens, norm_gain, norm_shift, w_qkv, w_out, w_up, b_up, w_down, b_down)
    x_recv = core_swap(x_send)

    steps = 4
    count = half // steps
    step_rows = GROUP_FRAMES * count
    place_block = step_spec((frames, count, width), 1)
    row_block = lambda cols: step_spec((step_rows, cols))
    smem = pl.BlockSpec(memory_space=pltpu.SMEM)
    place_scratch = [
        pltpu.SMEM((GROUP_FRAMES,), jnp.int32),
        pltpu.VMEM((GROUP_FRAMES, count, width), BF16),
    ]
    small_shape = sds((8, TILE), F32)
    small_spec = pl.BlockSpec((8, TILE), lambda i: (0, 0))
    half_shape = sds((frames, half, width), BF16)
    (out_own, out_send, xt, h2, qkv1, o1, h3, act1, du1, gr1, dxb, small3) = pl.pallas_call(
        time_forward_kernel,
        grid=(steps,),
        in_specs=[
            smem, place_block, place_block, whole_spec(cotangent), whole_spec(cotangent),
            whole_spec(norm_gain), whole_spec(norm_shift), layer_spec(w_qkv, 1), layer_spec(w_out, 1),
            layer_spec(w_up, 1), whole_spec(b_up), layer_spec(w_down, 1), whole_spec(b_down),
        ],
        out_specs=[
            place_block, place_block, row_block(width), row_block(width), row_block(3 * width),
            row_block(width), row_block(width), row_block(hidden), row_block(hidden), row_block(width),
            row_block(width), small_spec,
        ],
        out_shape=[
            half_shape, half_shape, sds((rows, width), BF16), sds((rows, width), BF16),
            sds((rows, 3 * width), BF16), sds((rows, width), BF16), sds((rows, width), BF16),
            sds((rows, hidden), BF16), sds((rows, hidden), BF16), sds((rows, width), BF16),
            sds((rows, width), F32), small_shape,
        ],
        scratch_shapes=place_scratch + [pltpu.VMEM((step_rows, hidden), BF16)],
        compiler_params=params(60),
        cost_estimate=cost(2 * macs * (4 * width + 4 * hidden), 30e6),
    )(
        frame_slot, x_keep, x_recv, cotangent, cot_recv, norm_gain, norm_shift, w_qkv, w_out, w_up,
        b_up, w_down, b_down,
    )
    out_recv = core_swap(out_send)

    slots = sp_size // 2
    size = width // sp_size
    down_size = hidden // sp_size

    def buffer_specs(*heights):
        shapes = []
        for height in heights:
            shapes += [sds((slots, height, TILE), BF16)] * 2
        return [pl.BlockSpec(s.shape, lambda i: (0, 0, 0)) for s in shapes], shapes

    order_a = list(range(sp_bits))
    order_b = [0, 2, 1] + list(range(3, sp_bits))
    chain = functools.partial(Chain, sizes=sizes)
    flat = lambda a: a.reshape(rows, a.shape[-1])

    def meet(chains, *arrays):
        out = lax.optimization_barrier(tuple(arrays) + tuple(c.recv for c in chains))
        for c, recv in zip(chains, out[len(arrays) :]):
            c.recv = recv
            c.step()
        return out[: len(arrays)]

    def mlp_weights(h, du, act, gr, *extra):
        specs, shapes = buffer_specs(4 * size, down_size + (size if extra else 0))
        tall = pl.BlockSpec((rows, TILE), lambda i: (0, i))
        out = pl.pallas_call(
            functools.partial(mlp_weights_kernel, (order_a, order_b)),
            in_specs=[whole_spec(h), tall, tall, whole_spec(gr)] + [whole_spec(e) for e in extra],
            grid=(hidden // TILE,),
            out_specs=specs,
            out_shape=shapes,
            compiler_params=params(60),
            cost_estimate=cost(2 * macs * 2 * hidden, 14e6),
        )(h, du, act, gr, *extra)
        return out

    out = mlp_weights(h3, du1, act1, gr1)
    out = lax.optimization_barrier(tuple(out) + (dxb,))
    up1, down1 = chain(out[0], out[1], order_a), chain(out[2], out[3], order_b)
    dxb = out[4]

    (dx_own, dx_send, ar1, dqkv1, small2) = pl.pallas_call(
        time_backward_kernel,
        in_specs=[
            smem, row_block(width), row_block(3 * width), row_block(width),
            whole_spec(norm_gain), whole_spec(norm_shift), layer_spec(w_qkv, 1), layer_spec(w_out, 1),
        ],
        grid=(steps,),
        out_specs=[place_block, place_block, row_block(width), row_block(3 * width), small_spec],
        out_shape=[
            half_shape, half_shape, sds((rows, width), BF16), sds((rows, 3 * width), BF16), small_shape,
        ],
        scratch_shapes=place_scratch,
        compiler_params=params(60),
        cost_estimate=cost(2 * macs * 4 * width, 15e6),
    )(frame_slot, xt, qkv1, dxb, norm_gain, norm_shift, w_qkv, w_out)
    dx_own, dx_send, dqkv1 = meet((up1, down1), dx_own, dx_send, dqkv1)
    dx_recv = core_swap(dx_send)

    specs, shapes = buffer_specs(4 * size)
    attn1 = pl.pallas_call(
        functools.partial(attn_weights_kernel, order_a),
        in_specs=[whole_spec(h2), whole_spec(dqkv1), whole_spec(o1), whole_spec(ar1)],
        grid=(1,),
        out_specs=specs,
        out_shape=shapes,
        compiler_params=params(60),
        cost_estimate=cost(2 * macs * 4 * width, 8e6),
    )(h2, dqkv1, o1, ar1)
    keep, send, dx_recv = lax.optimization_barrier((*attn1, dx_recv))
    attn1 = chain(keep, send, order_a)

    (gr0, du0, dxa, ar0, small1) = pl.pallas_call(
        space_mlp_back_kernel,
        in_specs=[
            half_block, half_block, frame_block(width), frame_block(hidden),
            whole_spec(norm_gain), whole_spec(norm_shift), layer_spec(w_up, 0), layer_spec(w_down, 0),
        ],
        grid=(frames,),
        out_specs=[
            frame_block(width), frame_block(hidden), frame_block(width), frame_block(width), small_spec,
        ],
        out_shape=[
            frame_out(width, BF16), frame_out(hidden, BF16), frame_out(width, F32),
            frame_out(width, BF16), small_shape,
        ],
        compiler_params=params(60),
        cost_estimate=cost(2 * macs * 2 * hidden, 20e6),
    )(dx_own, dx_recv, xa, slope0, norm_gain, norm_shift, w_up, w_down)
    gr0, du0, ar0 = meet((attn1, up1, down1), gr0, du0, ar0)
    out = mlp_weights(flat(h1), flat(du0), flat(act0), flat(gr0), flat(o0), flat(ar0))
    out = meet((), *out, dxa)
    dxa = out[4]
    up0, down0 = chain(out[0], out[1], order_a), chain(out[2], out[3], order_b)

    def attn_back(grad, first, count, before):
        offset_spec = lambda shape: pl.BlockSpec(shape, lambda i: (i + first,) + (0,) * (len(shape) - 1))
        return run(
            space_attn_back_kernel,
            [],
            [
                offset_spec((1, patches, width)), offset_spec((1, patches, 3 * width)),
                offset_spec((1, HEADS, patches)), offset_spec((1, patches, width)), layer_spec(w_out, 0),
            ],
            (grad, qkv0, lse0, o0, w_out),
            aliases=before,
            grid=(count,),
            out_specs=[offset_spec((1, patches, 3 * width))],
            out_shape=[frame_out(3 * width, BF16)],
            compiler_params=params(60),
            cost_estimate=cost(macs * 6 * width, 20e6),
        )

    (dqkv0,) = attn_back(dxa, 0, frames // 2, None)
    (dqkv0,) = meet((up0, down0, up1, down1, attn1), dqkv0)
    (dqkv0,) = attn_back(dxa, frames // 2, frames // 2, [dqkv0])
    (dqkv0,) = meet((up1, down1), dqkv0)
    specs, shapes = buffer_specs(size + size // 2, size + size // 2)
    out = pl.pallas_call(
        functools.partial(qkv_weights_kernel, (order_a, order_b)),
        in_specs=[whole_spec(flat(h0)), whole_spec(flat(dqkv0))],
        grid=(1,),
        out_specs=specs,
        out_shape=shapes,
        compiler_params=params(60),
        cost_estimate=cost(2 * macs * 3 * width, 8e6),
    )(flat(h0), flat(dqkv0))
    out = meet((attn1,), *out, dqkv0)
    qkva = chain(out[0], out[1], order_a)
    qkvb = chain(out[2], out[3], order_b)

    grad_tokens, output, small0 = pl.pallas_call(
        finish_kernel,
        in_specs=[
            frame_block(width), frame_block(width), frame_block(3 * width), half_block,
            half_block, whole_spec(norm_gain), whole_spec(norm_shift), layer_spec(w_qkv, 0),
        ],
        grid=(frames,),
        out_specs=[frame_block(width), frame_block(width), small_spec],
        out_shape=[frame_out(width, BF16), frame_out(width, BF16), small_shape],
        compiler_params=params(60),
        cost_estimate=cost(2 * macs * 3 * width, 8e6),
    )(tokens, dxa, out[4], out_own, out_recv, norm_gain, norm_shift, w_qkv)
    (small0,) = meet((qkva, qkvb, up0, down0, attn1), small0)
    meet((qkva, qkvb, up0, down0))
    meet((qkva, qkvb, up0, down0))
    up1, down1, attn1, up0, down0, qkva, qkvb = [
        c.finish() for c in (up1, down1, attn1, up0, down0, qkva, qkvb)
    ]

    small = jnp.concatenate([small0, small1, small2, small3], axis=0).astype(BF16)
    for b in range(sp_bits):
        small = add_low(small, swap(small, "sp", sp_size, b))
    for b in range(grp_size.bit_length() - 1):
        small = add_low(small, swap(small, "grp", grp_size, b))
    small = small.astype(F32).reshape(4, 8, TILE)
    sp = lax.axis_index("sp")

    def mine(array):
        size = array.shape[1] // sp_size
        return lax.dynamic_slice_in_dim(array, sp * size, size, axis=1)

    def columns(parts):
        return jnp.concatenate(parts, axis=1)

    def blocks(a, count):
        return columns([a[i * size : (i + 1) * size] for i in range(count)])

    third = jnp.concatenate([qkva[size:], qkvb[size:]], axis=0)
    return (
        output,
        grad_tokens,
        mine(small[:, 0]),
        mine(small[:, 1]),
        jnp.stack([columns([qkva[:size], qkvb[:size], third]), blocks(attn1, 3)]),
        jnp.stack([down0[down_size:], attn1[3 * size :]]),
        jnp.stack([blocks(up0, 4), blocks(up1, 4)]),
        mine(small[1::2, 4:].reshape(2, hidden)),
        jnp.stack([down0[:down_size], down1]),
        mine(small[1::2, 2]),
    )


def solution(mesh):
    rows = P(("grp", "sp"), None, None)
    in_specs = (rows, P("grp", None), P(), P(), P(), P(), P(), P(), P(), P(), rows)
    out_specs = (
        rows, rows, P(None, "sp"), P(None, "sp"), P(None, "sp", None), P(None, "sp", None),
        P(None, "sp", None), P(None, "sp"), P(None, "sp", None), P(None, "sp"),
    )
    body = functools.partial(shards, (mesh.shape["grp"], mesh.shape["sp"]))
    return jax.shard_map(body, mesh=mesh, in_specs=in_specs, out_specs=out_specs, check_vma=False)
```

```python
import functools

import jax
import jax.numpy as jnp
from jax import lax
from jax.experimental import pallas as pl
from jax.experimental.pallas import tpu as pltpu
from jax.sharding import PartitionSpec as P

HEADS = 8
HEAD = 64
VIDEO_STEPS = 6
GROUP_FRAMES = 8
NORM_EPS = 1e-05
TILE = 512
SCALE = HEAD**-0.5
TANH_A = 0.7978845608028654
TANH_B = TANH_A * 0.044715
PAIRS = [(t, s) for t in range(VIDEO_STEPS) for s in range(t + 1)]
F32 = jnp.float32
BF16 = jnp.bfloat16
MIB = 1024 * 1024


def dot(left, right):
    return jnp.dot(left, right, preferred_element_type=F32)


def dot_nt(left, right):
    return lax.dot_general(left, right, (((1,), (1,)), ((), ())), preferred_element_type=F32)


def dot_tn(left, right):
    return lax.dot_general(left, right, (((0,), (0,)), ((), ())), preferred_element_type=F32)


def norm(rows, gain, shift):
    centred = rows - jnp.mean(rows, axis=-1, keepdims=True)
    inv = lax.rsqrt(jnp.mean(centred * centred, axis=-1, keepdims=True) + NORM_EPS)
    unit = centred * inv
    return unit * gain + shift, unit, inv


def norm_back(grad, unit, inv, gain):
    grad_unit = grad * gain
    mean_grad = jnp.mean(grad_unit, axis=-1, keepdims=True)
    mean_both = jnp.mean(grad_unit * unit, axis=-1, keepdims=True)
    return inv * (grad_unit - mean_grad - unit * mean_both)


def column_sum(rows):
    return jnp.sum(rows, axis=0, keepdims=True)


def gelu_pair(u):
    square = u * u
    sigma = 0.5 + 0.5 * jnp.tanh(u * (TANH_A + TANH_B * square))
    act = u * sigma
    slope = sigma + act * (1.0 - sigma) * (2.0 * TANH_A + 6.0 * TANH_B * square)
    return act.astype(BF16), slope.astype(BF16)


def head_mask(lanes, which):
    lane = lax.broadcasted_iota(jnp.int32, lanes.shape, 1)
    return (lane < HEAD) if which == 0 else (lane >= HEAD)


def qkv_rows(normed, weight):
    out = []
    for part in range(3):
        piece = dot(normed, weight[:, part * TILE : (part + 1) * TILE])
        if part == 0:
            out.append(piece.astype(BF16) * BF16(SCALE))
        else:
            out.append(piece.astype(BF16))
    return out


def mlp_forward(normed, w_up, b_up, w_down, rows, act_ref, slope_ref):
    chunks = w_up.shape[1] // TILE
    up = lambda j: dot(normed, w_up[:, j * TILE : (j + 1) * TILE])
    total = None
    u = up(0)
    for j in range(chunks):
        cols = slice(j * TILE, (j + 1) * TILE)
        later = up(j + 1) if j + 1 < chunks else None
        act, slope = gelu_pair(u + b_up[:, cols])
        act_ref[rows, cols] = act
        slope_ref[rows, cols] = slope
        piece = dot(act, w_down[cols, :])
        total = piece if total is None else total + piece
        u = later
    return total


def mlp_backward(grad_low, w_up, w_down, rows, slope_ref, du_ref):
    chunks = w_up.shape[1] // TILE
    down = lambda j: dot_nt(grad_low, w_down[j * TILE : (j + 1) * TILE, :])
    total = None
    sums = []
    da = down(0)
    for j in range(chunks):
        cols = slice(j * TILE, (j + 1) * TILE)
        later = down(j + 1) if j + 1 < chunks else None
        du = (da * slope_ref[rows, cols].astype(F32)).astype(BF16)
        du_ref[rows, cols] = du
        sums.append(column_sum(du.astype(F32)))
        piece = dot_nt(du, w_up[:, cols])
        total = piece if total is None else total + piece
        da = later
    return total, sums


def add_small(small_ref, values, first):
    for i, value in enumerate(values):
        row = slice(i, i + 1) if i < 4 else slice(i, i + 1)
        if value is None:
            continue
        if first:
            small_ref[row, :] = value
        else:
            small_ref[row, :] += value


def half_rows(part, half):
    return pl.ds(pl.multiple_of(part * half, half), half)


def space_forward_kernel(
    tok_any, gain_ref, shift_ref, wqkv_any, wout_any, wup_any, bup_ref, wdown_any, bdown_ref,
    keep_ref, send_ref, h0_ref, qkv_ref, lse_ref, o_ref, xa_ref, h1_ref, act_ref, slope_ref,
    tok_ref, wqkv_ref, wout_ref, wup_ref, wdown_ref, x1_scr, sems,
):
    copies = [
        pltpu.make_async_copy(tok_any, tok_ref, sems.at[0]),
        pltpu.make_async_copy(wqkv_any.at[0], wqkv_ref, sems.at[1]),
        pltpu.make_async_copy(wout_any.at[0], wout_ref, sems.at[2]),
        pltpu.make_async_copy(wup_any.at[0], wup_ref, sems.at[3]),
        pltpu.make_async_copy(wdown_any.at[0], wdown_ref, sems.at[4]),
    ]
    for copy in copies:
        copy.start()
    part = lax.rem(lax.axis_index("sp"), 2)
    frames, rows = tok_ref.shape[0], tok_ref.shape[1]
    half = rows // 2
    lane = lax.broadcasted_iota(jnp.int32, (rows, 128), 1)
    copies[0].wait()
    for f in range(frames):
        span = slice(f * rows, (f + 1) * rows)
        x0 = tok_ref[f].astype(F32)
        h0 = norm(x0, gain_ref[0:1, :], shift_ref[0:1, :])[0].astype(BF16)
        h0_ref[span, :] = h0
        if f == 0:
            copies[1].wait()
        q, k, v = qkv_rows(h0, wqkv_ref)
        qkv_ref[span, 0:TILE] = q
        qkv_ref[span, TILE : 2 * TILE] = k
        qkv_ref[span, 2 * TILE :] = v
        lse_all = jnp.zeros((rows, 128), F32)
        mixed = []
        for pair in range(HEADS // 2):
            cols = slice(pair * 128, (pair + 1) * 128)
            qp, kp, vp = q[:, cols], k[:, cols], v[:, cols]
            zero = jnp.zeros_like(qp)
            mask = head_mask(qp, 0)
            s = dot_nt(jnp.concatenate([jnp.where(mask, qp, zero), jnp.where(mask, zero, qp)], axis=0), kp)
            top = jnp.max(s, axis=-1, keepdims=True)
            p = jnp.exp(s - top)
            total = jnp.sum(p, axis=-1, keepdims=True)
            both = dot(p.astype(BF16), vp) * (1.0 / total)
            lse = top + jnp.log(total)
            lse_all = jnp.where(lane == 2 * pair, lse[:rows], lse_all)
            lse_all = jnp.where(lane == 2 * pair + 1, lse[rows:], lse_all)
            mixed.append(jnp.where(mask, both[:rows], both[rows:]).astype(BF16))
        lse_ref[f] = jnp.transpose(lse_all)[0:HEADS, :]
        o = jnp.concatenate(mixed, axis=1)
        o_ref[span, :] = o
        if f == 0:
            copies[2].wait()
        xa = x0 + dot(o, wout_ref[...])
        xa_ref[span, :] = xa
        h1 = norm(xa, gain_ref[1:2, :], shift_ref[1:2, :])[0].astype(BF16)
        h1_ref[span, :] = h1
        if f == 0:
            copies[3].wait()
            copies[4].wait()
        branch = mlp_forward(h1, wup_ref, bup_ref[0:1, :], wdown_ref, span, act_ref, slope_ref)
        x1_scr[...] = xa + branch + bdown_ref[0:1, :]
        keep_ref[f] = x1_scr[half_rows(part, half), :].astype(BF16)
        send_ref[f] = x1_scr[half_rows(1 - part, half), :].astype(BF16)


def lane_heads(dtype):
    c = lax.broadcasted_iota(jnp.int32, (TILE, 128), 0)
    h = lax.broadcasted_iota(jnp.int32, (TILE, 128), 1)
    return (c // HEAD == h).astype(dtype)


def slot_places(slots_ref, where_scr, frames):
    sp = lax.axis_index("sp")
    group = (sp * frames) // GROUP_FRAMES
    part = lax.rem(sp, GROUP_FRAMES // frames)
    for t in range(GROUP_FRAMES):
        where_scr[slots_ref[group, t]] = lax.rem(t + GROUP_FRAMES - part * frames, GROUP_FRAMES)


def time_scores(q, k, spread):
    parts = []
    for t, s in PAIRS:
        parts.append((q[t] * k[s]).astype(BF16))
    return dot(jnp.concatenate(parts, axis=0), spread)


def time_probs(scores, count):
    blocks = [scores[i * count : (i + 1) * count] for i in range(len(PAIRS))]
    probs = []
    at = 0
    for t in range(VIDEO_STEPS):
        mine = blocks[at : at + t + 1]
        at += t + 1
        top = functools.reduce(jnp.maximum, mine)
        raw = [jnp.exp(b - top) for b in mine]
        inv = 1.0 / functools.reduce(lambda a, b: a + b, raw)
        probs.extend([r * inv for r in raw])
    return probs


def split_slots(rows):
    count = rows.shape[0] // GROUP_FRAMES
    return [rows[s * count : (s + 1) * count].astype(F32) for s in range(GROUP_FRAMES)]


def time_forward_kernel(
    slots_ref, keep_ref, recv_ref, cot_ref, cotr_ref, gain_ref, shift_ref,
    wqkv_ref, wout_ref, wup_ref, bup_ref, wdown_ref, bdown_ref,
    own_ref, send_ref, x_ref, h2_ref, qkv_ref, o_ref, h3_ref, act_ref, du_ref, gr_ref, dxb_ref,
    small_ref,
    where_scr, both_scr, slope_scr,
):
    frames, half = keep_ref.shape[0], keep_ref.shape[1]
    part = lax.rem(lax.axis_index("sp"), GROUP_FRAMES // frames)
    slot_places(slots_ref, where_scr, frames)
    small_ref[...] = jnp.zeros_like(small_ref)
    both_scr[0:frames] = keep_ref[...]
    both_scr[frames:] = recv_ref[...]
    spread = lane_heads(BF16)
    steps = 4
    count = half // steps
    step_rows = count * GROUP_FRAMES
    for i in range(steps):
        span = slice(i * step_rows, (i + 1) * step_rows)
        place = slice(i * count, (i + 1) * count)
        x_low = jnp.concatenate([both_scr[where_scr[s], place] for s in range(GROUP_FRAMES)], axis=0)
        x_ref[span, :] = x_low
        x = x_low.astype(F32)
        h2 = norm(x, gain_ref[2:3, :], shift_ref[2:3, :])[0].astype(BF16)
        h2_ref[span, :] = h2
        q, k, v = qkv_rows(h2, wqkv_ref.at[1])
        qkv_ref[span, 0:TILE] = q
        qkv_ref[span, TILE : 2 * TILE] = k
        qkv_ref[span, 2 * TILE :] = v
        qs, ks, vs = split_slots(q), split_slots(k), split_slots(v)
        probs = time_probs(time_scores(qs, ks, spread), count)
        wide = dot_nt(jnp.concatenate([p.astype(BF16) for p in probs], axis=0), spread)
        mixed = []
        at = 0
        for t in range(VIDEO_STEPS):
            total = None
            for s in range(t + 1):
                piece = wide[at * count : (at + 1) * count] * vs[s]
                total = piece if total is None else total + piece
                at += 1
            mixed.append(total)
        mixed.extend(vs[VIDEO_STEPS:])
        o = jnp.concatenate([m.astype(BF16) for m in mixed], axis=0)
        o_ref[span, :] = o
        xb = x + dot(o, wout_ref[1]).astype(BF16).astype(F32)
        h3, unit, inv = norm(xb, gain_ref[3:4, :], shift_ref[3:4, :])
        h3 = h3.astype(BF16)
        h3_ref[span, :] = h3
        whole = slice(0, step_rows)
        slope = slope_scr.at[i % 2]
        branch = mlp_forward(h3, wup_ref.at[1], bup_ref[1:2, :], wdown_ref.at[1], span, act_ref, SpanView(slope))
        out = (xb + branch + bdown_ref[1:2, :]).astype(BF16)
        for s in range(GROUP_FRAMES):
            both_scr[where_scr[s], place] = out[s * count : (s + 1) * count]
        grad_low = jnp.concatenate(
            [cot_slot(cot_ref, cotr_ref, where_scr[s], part * half + i * count, count) for s in range(GROUP_FRAMES)],
            axis=0,
        )
        gr_ref[span, :] = grad_low
        grad = grad_low.astype(F32)
        dh, sums = mlp_backward(grad_low, wup_ref.at[1], wdown_ref.at[1], span, SpanView(slope), du_ref)
        add_small(small_ref, [column_sum(dh * unit), column_sum(dh), column_sum(grad), None] + sums, False)
        dxb_ref[span, :] = grad + norm_back(dh, unit, inv, gain_ref[3:4, :])
    own_ref[...] = both_scr[0:frames]
    send_ref[...] = both_scr[frames:]


class SpanView:
    def __init__(self, ref):
        self.ref = ref

    def __getitem__(self, index):
        return self.ref[:, index[1]]

    def __setitem__(self, index, value):
        self.ref[:, index[1]] = value


def cot_slot(cot_ref, cotr_ref, frame, start, count):
    frames = cot_ref.shape[0]
    places = pl.ds(pl.multiple_of(start, count), count)
    mine = cot_ref[lax.rem(frame, frames), places, :]
    other = cotr_ref[lax.rem(frame, frames), places, :]
    return jnp.where(frame < frames, mine, other)


def time_backward_kernel(
    slots_ref, x_ref, qkv_ref, dxb_ref, gain_ref, shift_ref, wqkv_ref, wout_ref,
    own_ref, send_ref, ar_ref, dqkv_ref, small_ref,
    where_scr, both_scr,
):
    frames, half = own_ref.shape[0], own_ref.shape[1]
    slot_places(slots_ref, where_scr, frames)
    small_ref[...] = jnp.zeros_like(small_ref)
    spread = lane_heads(BF16)
    steps = 4
    count = half // steps
    step_rows = count * GROUP_FRAMES
    gain = gain_ref[2:3, :]
    for i in range(steps):
        span = slice(i * step_rows, (i + 1) * step_rows)
        place = slice(i * count, (i + 1) * count)
        dxb = dxb_ref[span, :]
        ar = dxb.astype(BF16)
        ar_ref[span, :] = ar
        do = split_slots(dot_nt(ar, wout_ref[1]).astype(BF16))
        qs = split_slots(qkv_ref[span, 0:TILE])
        ks = split_slots(qkv_ref[span, TILE : 2 * TILE])
        vs = split_slots(qkv_ref[span, 2 * TILE :])
        probs = time_probs(time_scores(qs, ks, spread), count)
        dps = time_scores(do, vs, spread)
        dps = [dps[j * count : (j + 1) * count] for j in range(len(PAIRS))]
        dss = []
        at = 0
        for t in range(VIDEO_STEPS):
            centre = functools.reduce(
                lambda a, b: a + b, [probs[at + s] * dps[at + s] for s in range(t + 1)]
            )
            dss.extend([probs[at + s] * (dps[at + s] - centre) for s in range(t + 1)])
            at += t + 1
        wide_p = dot_nt(jnp.concatenate([p.astype(BF16) for p in probs], axis=0), spread)
        wide_ds = dot_nt(jnp.concatenate([d.astype(BF16) for d in dss], axis=0), spread)
        dq = [None] * GROUP_FRAMES
        dk = [None] * GROUP_FRAMES
        dv = [None] * GROUP_FRAMES

        def add(table, index, piece):
            table[index] = piece if table[index] is None else table[index] + piece

        for j, (t, s) in enumerate(PAIRS):
            rows = slice(j * count, (j + 1) * count)
            add(dq, t, wide_ds[rows] * ks[s])
            add(dk, s, wide_ds[rows] * qs[t])
            add(dv, s, wide_p[rows] * do[t])
        for t in range(VIDEO_STEPS, GROUP_FRAMES):
            dq[t] = jnp.zeros_like(do[t])
            dk[t] = jnp.zeros_like(do[t])
            dv[t] = do[t]
        dq = jnp.concatenate([(d * SCALE).astype(BF16) for d in dq], axis=0)
        dk = jnp.concatenate([d.astype(BF16) for d in dk], axis=0)
        dv = jnp.concatenate([d.astype(BF16) for d in dv], axis=0)
        dqkv_ref[span, 0:TILE] = dq
        dqkv_ref[span, TILE : 2 * TILE] = dk
        dqkv_ref[span, 2 * TILE :] = dv
        dh = dot_nt(dqkv_ref[span, :], wqkv_ref[1])
        unit, inv = norm(x_ref[span, :].astype(F32), gain, shift_ref[2:3, :])[1:]
        add_small(small_ref, [column_sum(dh * unit), column_sum(dh)], False)
        dxp = norm_back(dh, unit, inv, gain).astype(BF16).astype(F32)
        dx1 = (dxb + dxp).astype(BF16)
        for s in range(GROUP_FRAMES):
            both_scr[where_scr[s], place] = dx1[s * count : (s + 1) * count]
    own_ref[...] = both_scr[0:frames]
    send_ref[...] = both_scr[frames:]


def space_mlp_back_kernel(
    own_ref, recv_ref, xa_ref, slope_ref, gain_ref, shift_ref, wup_ref, wdown_ref,
    gr_ref, du_ref, dxa_ref, ar_ref, small_ref,
):
    part = lax.rem(lax.axis_index("sp"), 2)
    small_ref[...] = jnp.zeros_like(small_ref)
    frames, half = own_ref.shape[0], own_ref.shape[1]
    rows = 2 * half
    gain = gain_ref[1:2, :]
    for f in range(frames):
        span = slice(f * rows, (f + 1) * rows)
        base = f * rows
        gr_ref[pl.ds(pl.multiple_of(base + part * half, half), half), :] = own_ref[f]
        gr_ref[pl.ds(pl.multiple_of(base + (1 - part) * half, half), half), :] = recv_ref[f]
        grad_low = gr_ref[span, :]
        grad = grad_low.astype(F32)
        dh, sums = mlp_backward(grad_low, wup_ref.at[0], wdown_ref.at[0], span, slope_ref, du_ref)
        unit, inv = norm(xa_ref[span, :], gain, shift_ref[1:2, :])[1:]
        add_small(small_ref, [column_sum(dh * unit), column_sum(dh), column_sum(grad), None] + sums, False)
        dxa = grad + norm_back(dh, unit, inv, gain)
        dxa_ref[span, :] = dxa
        ar_ref[span, :] = dxa.astype(BF16)


def space_attn_back_kernel(ar_ref, qkv_ref, lse_ref, o_ref, wout_ref, dqkv_ref):
    frames, rows = lse_ref.shape[0], lse_ref.shape[2]
    h = lax.broadcasted_iota(jnp.int32, (HEADS, TILE), 0)
    c = lax.broadcasted_iota(jnp.int32, (HEADS, TILE), 1)
    pick = (c // HEAD == h).astype(BF16)
    for f in range(frames):
        span = slice(f * rows, (f + 1) * rows)
        do = dot_nt(ar_ref[span, :], wout_ref[0]).astype(BF16)
        both = do.astype(F32) * o_ref[span, :].astype(F32)
        high = both.astype(BF16)
        rest = (both - high.astype(F32)).astype(BF16)
        centre = dot_nt(pick, high) + dot_nt(pick, rest)
        for pair in range(HEADS // 2):
            cols = slice(pair * 128, (pair + 1) * 128)
            qp = qkv_ref[span, pair * 128 : (pair + 1) * 128]
            kp = qkv_ref[span, TILE + pair * 128 : TILE + (pair + 1) * 128]
            vp = qkv_ref[span, 2 * TILE + pair * 128 : 2 * TILE + (pair + 1) * 128]
            dop = do[:, cols]
            zero = jnp.zeros_like(kp)
            mask = head_mask(kp, 0)
            st = dot_nt(jnp.concatenate([jnp.where(mask, kp, zero), jnp.where(mask, zero, kp)], axis=0), qp)
            dpt = dot_nt(jnp.concatenate([jnp.where(mask, vp, zero), jnp.where(mask, zero, vp)], axis=0), dop)
            pts, dsts, dqs = [], [], []
            for e in range(2):
                row = slice(2 * pair + e, 2 * pair + e + 1)
                keys = slice(e * rows, (e + 1) * rows)
                pt = jnp.exp(st[keys] - lse_ref[f, row, :])
                dst = (pt * (dpt[keys] - centre[row, :])).astype(BF16)
                pts.append(pt.astype(BF16))
                dsts.append(dst)
                dqs.append(dot_tn(dst, kp) * SCALE)
            dk = dot(jnp.concatenate(dsts, axis=0), qp)
            dv = dot(jnp.concatenate(pts, axis=0), dop)
            dq = jnp.where(mask, dqs[0], dqs[1])
            for index, value in enumerate((dq, jnp.where(mask, dk[:rows], dk[rows:]), jnp.where(mask, dv[:rows], dv[rows:]))):
                at = index * TILE + pair * 128
                dqkv_ref[span, at : at + 128] = value.astype(BF16)


def finish_kernel(
    tok_ref, dxa_ref, dqkv_ref, own_ref, recv_ref, gain_ref, shift_ref, wqkv_ref,
    gtok_ref, out_ref, small_ref,
):
    part = lax.rem(lax.axis_index("sp"), 2)
    small_ref[...] = jnp.zeros_like(small_ref)
    frames, half = own_ref.shape[0], own_ref.shape[1]
    rows = 2 * half
    gain = gain_ref[0:1, :]
    for f in range(frames):
        span = slice(f * rows, (f + 1) * rows)
        out_ref[f, half_rows(part, half), :] = own_ref[f]
        out_ref[f, half_rows(1 - part, half), :] = recv_ref[f]
        dh = dot_nt(dqkv_ref[span, :], wqkv_ref[0])
        unit, inv = norm(tok_ref[f].astype(F32), gain, shift_ref[0:1, :])[1:]
        add_small(small_ref, [column_sum(dh * unit), column_sum(dh)], False)
        gtok_ref[f] = (dxa_ref[span, :] + norm_back(dh, unit, inv, gain)).astype(BF16)


def place_of(block, order, sp):
    bits = len(order)
    mixed = jnp.bitwise_xor(block, sp)
    slot = jnp.int32(0)
    for i, b in enumerate(order):
        bit = jnp.bitwise_and(lax.shift_right_logical(mixed, jnp.int32(b)), 1)
        slot = slot + lax.shift_left(bit, jnp.int32(bits - 1 - i))
    return slot


def put_blocks(result, first, size, at, order, keep_ref, send_ref, cut=None):
    sp = lax.axis_index("sp")
    part = lax.rem(sp, 2)
    low = result.astype(BF16)
    take = slice(0, size) if cut is None else cut
    width = take.stop - take.start
    for j in range(result.shape[0] // (2 * size)):
        even = low[2 * j * size : (2 * j + 1) * size][take]
        odd = low[(2 * j + 1) * size : (2 * j + 2) * size][take]
        slot = place_of(first + 2 * j, order[1:], sp)
        keep_ref[slot, pl.ds(at, width), :] = jnp.where(part == 0, even, odd)
        send_ref[slot, pl.ds(at, width), :] = jnp.where(part == 0, odd, even)


def mlp_weights_kernel(orders, *refs):
    h_ref, du_ref, act_ref, gr_ref = refs[:4]
    extra = refs[4:-4]
    keep_a, send_a, keep_b, send_b = refs[-4:]
    slots = 2 * keep_a.shape[0]
    up_size = h_ref.shape[1] // slots
    chunks = du_ref.shape[1] // TILE
    down_size = chunks * TILE // slots
    zero = jnp.int32(0)
    turned = jnp.transpose(h_ref[...])
    for j in range(chunks):
        cols = slice(j * TILE, (j + 1) * TILE)
        put_blocks(dot(turned, du_ref[:, cols]), zero, up_size, j * up_size, orders[0], keep_a, send_a)
        down = dot_tn(act_ref[:, cols], gr_ref[...])
        put_blocks(down, jnp.int32(j * (TILE // down_size)), down_size, 0, orders[1], keep_b, send_b)
    if extra:
        put_blocks(dot_tn(extra[0][...], extra[1][...]), zero, up_size, down_size, orders[1], keep_b, send_b)


def attn_weights_kernel(order, h_ref, dqkv_ref, o_ref, ar_ref, keep_ref, send_ref):
    size = h_ref.shape[1] // (2 * keep_ref.shape[0])
    zero = jnp.int32(0)
    turned = jnp.transpose(h_ref[...])
    for j in range(3):
        cols = slice(j * TILE, (j + 1) * TILE)
        put_blocks(dot(turned, dqkv_ref[:, cols]), zero, size, j * size, order, keep_ref, send_ref)
    put_blocks(dot_tn(o_ref[...], ar_ref[...]), zero, size, 3 * size, order, keep_ref, send_ref)


def qkv_weights_kernel(orders, h_ref, dqkv_ref, keep_a, send_a, keep_b, send_b):
    size = h_ref.shape[1] // (2 * keep_a.shape[0])
    zero = jnp.int32(0)
    half = size // 2
    turned = jnp.transpose(h_ref[...])
    put_blocks(dot(turned, dqkv_ref[:, :TILE]), zero, size, 0, orders[0], keep_a, send_a)
    put_blocks(dot(turned, dqkv_ref[:, TILE : 2 * TILE]), zero, size, 0, orders[1], keep_b, send_b)
    last = dot(turned, dqkv_ref[:, 2 * TILE :])
    put_blocks(last, zero, size, size, orders[0], keep_a, send_a, slice(0, half))
    put_blocks(last, zero, size, size, orders[1], keep_b, send_b, slice(half, size))


VMEM = pl.BlockSpec(memory_space=pltpu.VMEM)
SMEM = pl.BlockSpec(memory_space=pltpu.SMEM)
ANY = pl.BlockSpec(memory_space=pl.ANY)


def sds(shape, dtype):
    return jax.ShapeDtypeStruct(shape, dtype)


def call(kernel, args, outs, flops, scratch=(), specs=None, limit=24):
    return pl.pallas_call(
        kernel,
        in_specs=[VMEM] * len(args) if specs is None else specs,
        out_specs=[VMEM] * len(outs),
        out_shape=outs,
        scratch_shapes=list(scratch),
        compiler_params=pltpu.CompilerParams(vmem_limit_bytes=limit * MIB),
        cost_estimate=pl.CostEstimate(flops=int(flops), bytes_accessed=int(flops // 400), transcendentals=0),
    )(*args)


class Chain:
    def __init__(self, keep, send, order, sizes):
        self.keep, self.send, self.sizes = keep, send, sizes
        grp_size, sp_size = sizes
        self.path = [("sp", sp_size, b) for b in order]
        self.path += [("grp", grp_size, b) for b in range(grp_size.bit_length() - 1)]
        self.swap()

    def swap(self):
        axis, size, bit = self.path.pop(0)
        self.recv = swap(self.send, axis, size, bit)

    def step(self):
        if self.path and self.path[0][0] == "sp":
            half = self.keep.shape[0] // 2
            self.send = add_low(self.keep[half:], self.recv[half:])
            self.keep = add_low(self.keep[:half], self.recv[:half])
        else:
            self.send = self.keep = add_low(self.keep, self.recv)
        self.swap()

    def finish(self):
        while self.path:
            self.step()
        return self.keep[0].astype(F32) + self.recv[0].astype(F32)


def add_low(a, b):
    return (a.astype(F32) + b.astype(F32)).astype(BF16)


def swap(array, axis, size, bit):
    return lax.ppermute(array, axis, [(i, i ^ (1 << bit)) for i in range(size)])


def shards(sizes, tokens, frame_slot, norm_gain, norm_shift, w_qkv, w_out, w_up, b_up, w_down, b_down, cotangent):
    grp_size, sp_size = sizes
    frames, patches, width = tokens.shape
    hidden = w_up.shape[2]
    assert GROUP_FRAMES == 2 * frames
    half = patches // 2
    rows = frames * patches
    sp_bits = sp_size.bit_length() - 1
    core_swap = functools.partial(swap, axis="sp", size=sp_size, bit=0)
    flops = 2 * rows * width
    slots = sp_size // 2
    size = width // sp_size
    down_size = hidden // sp_size
    order_a = list(range(sp_bits))
    order_b = [0, 2, 1] + list(range(3, sp_bits))
    chain = functools.partial(Chain, sizes=sizes)

    def row_out(cols, dtype=BF16):
        return sds((rows, cols), dtype)

    half_out = sds((frames, half, width), BF16)
    small_out = sds((8, TILE), F32)

    def meet(chains, *arrays):
        out = lax.optimization_barrier(tuple(arrays) + tuple(c.recv for c in chains))
        for c, recv in zip(chains, out[len(arrays) :]):
            c.recv = recv
            c.step()
        return out[: len(arrays)]

    cot_recv = core_swap(cotangent)
    (x_keep, x_send, h0, qkv0, lse0, o0, xa, h1, act0, slope0) = call(
        space_forward_kernel,
        (tokens, norm_gain, norm_shift, w_qkv, w_out, w_up, b_up, w_down, b_down),
        [
            half_out, half_out, row_out(width), row_out(3 * width), sds((frames, HEADS, patches), F32),
            row_out(width), row_out(width, F32), row_out(width), row_out(hidden), row_out(hidden),
        ],
        flops * (6 * width + 2 * hidden),
        scratch=[
            pltpu.VMEM(tokens.shape, BF16), pltpu.VMEM(w_qkv.shape[1:], BF16),
            pltpu.VMEM(w_out.shape[1:], BF16), pltpu.VMEM(w_up.shape[1:], BF16),
            pltpu.VMEM(w_down.shape[1:], BF16), pltpu.VMEM((patches, width), F32),
            pltpu.SemaphoreType.DMA((5,)),
        ],
        specs=[ANY, VMEM, VMEM, ANY, ANY, ANY, VMEM, ANY, VMEM],
    )
    x_recv = core_swap(x_send)

    place_scratch = [
        pltpu.SMEM((GROUP_FRAMES,), jnp.int32),
        pltpu.VMEM((GROUP_FRAMES, half, width), BF16),
    ]
    (out_own, out_send, xt, h2, qkv1, o1, h3, act1, du1, gr1, dxb, small3) = call(
        time_forward_kernel,
        (
            frame_slot, x_keep, x_recv, cotangent, cot_recv, norm_gain, norm_shift, w_qkv, w_out, w_up,
            b_up, w_down, b_down,
        ),
        [
            half_out, half_out, row_out(width), row_out(width), row_out(3 * width), row_out(width),
            row_out(width), row_out(hidden), row_out(hidden), row_out(width), row_out(width, F32),
            small_out,
        ],
        flops * (4 * width + 4 * hidden),
        scratch=place_scratch + [pltpu.VMEM((2, rows // 4, hidden), BF16)],
        specs=[SMEM] + [VMEM] * 12,
    )
    out_recv = core_swap(out_send)

    def buffers(*heights):
        return [sds((slots, height, TILE), BF16) for height in heights for _ in range(2)]

    def mlp_weights(h, du, act, gr, *extra):
        return call(
            functools.partial(mlp_weights_kernel, (order_a, order_b)),
            (h, du, act, gr) + extra,
            buffers(4 * size, down_size + (size if extra else 0)),
            flops * 2 * hidden,
        )

    out = mlp_weights(h3, du1, act1, gr1)
    out = lax.optimization_barrier(tuple(out) + (dxb,))
    up1, down1 = chain(out[0], out[1], order_a), chain(out[2], out[3], order_b)
    dxb = out[4]

    (dx_own, dx_send, ar1, dqkv1, small2) = call(
        time_backward_kernel,
        (frame_slot, xt, qkv1, dxb, norm_gain, norm_shift, w_qkv, w_out),
        [half_out, half_out, row_out(width), row_out(3 * width), small_out],
        flops * 4 * width,
        scratch=place_scratch,
        specs=[SMEM] + [VMEM] * 7,
    )
    dx_own, dx_send, dqkv1 = meet((up1, down1), dx_own, dx_send, dqkv1)
    dx_recv = core_swap(dx_send)
    attn1 = call(
        functools.partial(attn_weights_kernel, order_a), (h2, dqkv1, o1, ar1), buffers(4 * size),
        flops * 4 * width,
    )
    keep, send, dx_recv = lax.optimization_barrier((*attn1, dx_recv))
    attn1 = chain(keep, send, order_a)

    (gr0, du0, dxa, ar0, small1) = call(
        space_mlp_back_kernel,
        (dx_own, dx_recv, xa, slope0, norm_gain, norm_shift, w_up, w_down),
        [row_out(width), row_out(hidden), row_out(width, F32), row_out(width), small_out],
        flops * 2 * hidden,
    )
    gr0, du0, ar0 = meet((attn1, up1, down1), gr0, du0, ar0)
    out = mlp_weights(h1, du0, act0, gr0, o0, ar0)
    out = meet((), *out, ar0)
    ar0 = out[4]
    up0, down0 = chain(out[0], out[1], order_a), chain(out[2], out[3], order_b)

    (dqkv0,) = call(
        space_attn_back_kernel, (ar0, qkv0, lse0, o0, w_out), [row_out(3 * width)], flops * 8 * width
    )
    (dqkv0,) = meet((up0, down0, up1, down1, attn1), dqkv0)
    out = call(
        functools.partial(qkv_weights_kernel, (order_a, order_b)), (h0, dqkv0),
        buffers(size + size // 2, size + size // 2), flops * 3 * width,
    )
    out = meet((up1, down1), *out, dqkv0)
    qkva = chain(out[0], out[1], order_a)
    qkvb = chain(out[2], out[3], order_b)

    grad_tokens, output, small0 = call(
        finish_kernel,
        (tokens, dxa, out[4], out_own, out_recv, norm_gain, norm_shift, w_qkv),
        [sds(tokens.shape, BF16), sds(tokens.shape, BF16), small_out],
        flops * 3 * width,
    )
    (small0,) = meet((qkva, qkvb, up0, down0, attn1), small0)
    meet((qkva, qkvb, up0, down0))
    meet((qkva, qkvb, up0, down0))
    up1, down1, attn1, up0, down0, qkva, qkvb = [
        c.finish() for c in (up1, down1, attn1, up0, down0, qkva, qkvb)
    ]

    small = jnp.concatenate([small0, small1, small2, small3], axis=0).astype(BF16)
    for b in range(sp_bits):
        small = add_low(small, swap(small, "sp", sp_size, b))
    for b in range(grp_size.bit_length() - 1):
        small = add_low(small, swap(small, "grp", grp_size, b))
    small = small.astype(F32).reshape(4, 8, TILE)
    sp = lax.axis_index("sp")

    def mine(array):
        size = array.shape[1] // sp_size
        return lax.dynamic_slice_in_dim(array, sp * size, size, axis=1)

    def columns(parts):
        return jnp.concatenate(parts, axis=1)

    def blocks(a, count):
        return columns([a[i * size : (i + 1) * size] for i in range(count)])

    third = jnp.concatenate([qkva[size:], qkvb[size:]], axis=0)
    return (
        output,
        grad_tokens,
        mine(small[:, 0]),
        mine(small[:, 1]),
        jnp.stack([columns([qkva[:size], qkvb[:size], third]), blocks(attn1, 3)]),
        jnp.stack([down0[down_size:], attn1[3 * size :]]),
        jnp.stack([blocks(up0, 4), blocks(up1, 4)]),
        mine(small[1::2, 4:].reshape(2, hidden)),
        jnp.stack([down0[:down_size], down1]),
        mine(small[1::2, 2]),
    )


def solution(mesh):
    rows = P(("grp", "sp"), None, None)
    in_specs = (rows, P("grp", None), P(), P(), P(), P(), P(), P(), P(), P(), rows)
    out_specs = (
        rows, rows, P(None, "sp"), P(None, "sp"), P(None, "sp", None), P(None, "sp", None),
        P(None, "sp", None), P(None, "sp"), P(None, "sp", None), P(None, "sp"),
    )
    body = functools.partial(shards, (mesh.shape["grp"], mesh.shape["sp"]))
    return jax.shard_map(body, mesh=mesh, in_specs=in_specs, out_specs=out_specs, check_vma=False)
```

```python
import functools

import jax
import jax.numpy as jnp
from jax import lax
from jax.experimental import pallas as pl
from jax.experimental.pallas import tpu as pltpu
from jax.sharding import PartitionSpec as P

HEADS = 8
HEAD = 64
VIDEO_STEPS = 6
GROUP_FRAMES = 8
NORM_EPS = 1e-05
TILE = 512
SCALE = HEAD**-0.5
TANH_A = 0.7978845608028654
TANH_B = TANH_A * 0.044715
PAIRS = [(t, s) for t in range(VIDEO_STEPS) for s in range(t + 1)]
F32 = jnp.float32
BF16 = jnp.bfloat16
MIB = 1024 * 1024


def dot(left, right):
    return jnp.dot(left, right, preferred_element_type=F32)


def dot_nt(left, right):
    return lax.dot_general(left, right, (((1,), (1,)), ((), ())), preferred_element_type=F32)


def dot_tn(left, right):
    return lax.dot_general(left, right, (((0,), (0,)), ((), ())), preferred_element_type=F32)


def norm(rows, gain, shift):
    centred = rows - jnp.mean(rows, axis=-1, keepdims=True)
    inv = lax.rsqrt(jnp.mean(centred * centred, axis=-1, keepdims=True) + NORM_EPS)
    unit = centred * inv
    return unit * gain + shift, unit, inv


def norm_back(grad, unit, inv, gain):
    grad_unit = grad * gain
    mean_grad = jnp.mean(grad_unit, axis=-1, keepdims=True)
    mean_both = jnp.mean(grad_unit * unit, axis=-1, keepdims=True)
    return inv * (grad_unit - mean_grad - unit * mean_both)


def column_sum(rows):
    return jnp.sum(rows, axis=0, keepdims=True)


def gelu_pair(u):
    square = u * u
    sigma = 0.5 + 0.5 * jnp.tanh(u * (TANH_A + TANH_B * square))
    act = u * sigma
    slope = sigma + act * (1.0 - sigma) * (2.0 * TANH_A + 6.0 * TANH_B * square)
    return act.astype(BF16), slope.astype(BF16)


def head_mask(lanes, which):
    lane = lax.broadcasted_iota(jnp.int32, lanes.shape, 1)
    return (lane < HEAD) if which == 0 else (lane >= HEAD)


def qkv_rows(normed, weight):
    out = []
    for part in range(3):
        piece = dot(normed, weight[:, part * TILE : (part + 1) * TILE])
        if part == 0:
            out.append(piece.astype(BF16) * BF16(SCALE))
        else:
            out.append(piece.astype(BF16))
    return out


def mlp_forward(normed, w_up, b_up, w_down, rows, act_ref, slope_ref):
    chunks = w_up.shape[1] // TILE
    up = lambda j: dot(normed, w_up[:, j * TILE : (j + 1) * TILE])
    total = None
    u = up(0)
    for j in range(chunks):
        cols = slice(j * TILE, (j + 1) * TILE)
        later = up(j + 1) if j + 1 < chunks else None
        act, slope = gelu_pair(u + b_up[:, cols])
        act_ref[rows, cols] = act
        slope_ref[rows, cols] = slope
        piece = dot(act, w_down[cols, :])
        total = piece if total is None else total + piece
        u = later
    return total


def mlp_backward(grad_low, w_up, w_down, rows, slope_ref, du_ref):
    chunks = w_up.shape[1] // TILE
    down = lambda j: dot_nt(grad_low, w_down[j * TILE : (j + 1) * TILE, :])
    total = None
    sums = []
    da = down(0)
    for j in range(chunks):
        cols = slice(j * TILE, (j + 1) * TILE)
        later = down(j + 1) if j + 1 < chunks else None
        du = (da * slope_ref[rows, cols].astype(F32)).astype(BF16)
        du_ref[rows, cols] = du
        sums.append(column_sum(du.astype(F32)))
        piece = dot_nt(du, w_up[:, cols])
        total = piece if total is None else total + piece
        da = later
    return total, sums


def add_small(small_ref, values, first):
    for i, value in enumerate(values):
        row = slice(i, i + 1) if i < 4 else slice(i, i + 1)
        if value is None:
            continue
        if first:
            small_ref[row, :] = value
        else:
            small_ref[row, :] += value


def half_rows(part, half):
    return pl.ds(pl.multiple_of(part * half, half), half)


def space_forward_kernel(
    tok_hbm, gain_ref, shift_ref, wqkv_hbm, wout_hbm, wup_hbm, bup_ref, wdown_hbm, bdown_ref,
    keep_ref, send_ref, h0_ref, qkv_ref, lse_ref, o_ref, xa_ref, h1_ref, act_hbm, slope_hbm,
    tok_ref, wqkv_ref, wout_ref, wup_ref, wdown_ref, wqkv1_ref, wout1_ref, wup1_ref, wdown1_ref,
    act_scr, slope_scr, x1_scr, in_sems, out_sems,
):
    pairs = [
        (tok_hbm, tok_ref), (wqkv_hbm.at[0], wqkv_ref), (wout_hbm.at[0], wout_ref),
        (wup_hbm.at[0], wup_ref), (wdown_hbm.at[0], wdown_ref), (wqkv_hbm.at[1], wqkv1_ref),
        (wout_hbm.at[1], wout1_ref), (wup_hbm.at[1], wup1_ref), (wdown_hbm.at[1], wdown1_ref),
    ]
    copies = [pltpu.make_async_copy(src, dst, in_sems.at[i]) for i, (src, dst) in enumerate(pairs)]
    for copy in copies:
        copy.start()
    part = lax.rem(lax.axis_index("sp"), 2)
    frames, rows = tok_ref.shape[0], tok_ref.shape[1]
    half = rows // 2
    lane = lax.broadcasted_iota(jnp.int32, (rows, 128), 1)
    spills = []
    copies[0].wait()
    for f in range(frames):
        span = slice(f * rows, (f + 1) * rows)
        x0 = tok_ref[f].astype(F32)
        h0 = norm(x0, gain_ref[0:1, :], shift_ref[0:1, :])[0].astype(BF16)
        h0_ref[span, :] = h0
        if f == 0:
            copies[1].wait()
        q, k, v = qkv_rows(h0, wqkv_ref)
        qkv_ref[span, 0:TILE] = q
        qkv_ref[span, TILE : 2 * TILE] = k
        qkv_ref[span, 2 * TILE :] = v
        lse_all = jnp.zeros((rows, 128), F32)
        mixed = []
        for pair in range(HEADS // 2):
            cols = slice(pair * 128, (pair + 1) * 128)
            qp, kp, vp = q[:, cols], k[:, cols], v[:, cols]
            zero = jnp.zeros_like(qp)
            mask = head_mask(qp, 0)
            s = dot_nt(jnp.concatenate([jnp.where(mask, qp, zero), jnp.where(mask, zero, qp)], axis=0), kp)
            top = jnp.max(s, axis=-1, keepdims=True)
            p = jnp.exp(s - top)
            total = jnp.sum(p, axis=-1, keepdims=True)
            both = dot(p.astype(BF16), vp) * (1.0 / total)
            lse = top + jnp.log(total)
            lse_all = jnp.where(lane == 2 * pair, lse[:rows], lse_all)
            lse_all = jnp.where(lane == 2 * pair + 1, lse[rows:], lse_all)
            mixed.append(jnp.where(mask, both[:rows], both[rows:]).astype(BF16))
        lse_ref[f] = jnp.transpose(lse_all)[0:HEADS, :]
        o = jnp.concatenate(mixed, axis=1)
        o_ref[span, :] = o
        if f == 0:
            copies[2].wait()
        xa = x0 + dot(o, wout_ref[...])
        xa_ref[span, :] = xa
        h1 = norm(xa, gain_ref[1:2, :], shift_ref[1:2, :])[0].astype(BF16)
        h1_ref[span, :] = h1
        if f == 0:
            copies[3].wait()
            copies[4].wait()
        if f >= 2:
            for copy in spills[f - 2]:
                copy.wait()
        now = f % 2
        branch = mlp_forward(
            h1, wup_ref, bup_ref[0:1, :], wdown_ref, slice(None), act_scr.at[now], slope_scr.at[now]
        )
        spills.append([
            pltpu.make_async_copy(act_scr.at[now], act_hbm.at[span], out_sems.at[2 * f]),
            pltpu.make_async_copy(slope_scr.at[now], slope_hbm.at[span], out_sems.at[2 * f + 1]),
        ])
        for copy in spills[f]:
            copy.start()
        x1_scr[...] = xa + branch + bdown_ref[0:1, :]
        keep_ref[f] = x1_scr[half_rows(part, half), :].astype(BF16)
        send_ref[f] = x1_scr[half_rows(1 - part, half), :].astype(BF16)
    for copies_of in spills[-2:]:
        for copy in copies_of:
            copy.wait()
    for copy in copies[5:]:
        copy.wait()


def lane_heads(dtype):
    c = lax.broadcasted_iota(jnp.int32, (TILE, 128), 0)
    h = lax.broadcasted_iota(jnp.int32, (TILE, 128), 1)
    return (c // HEAD == h).astype(dtype)


def slot_places(slots_ref, where_scr, frames):
    sp = lax.axis_index("sp")
    group = (sp * frames) // GROUP_FRAMES
    part = lax.rem(sp, GROUP_FRAMES // frames)
    for t in range(GROUP_FRAMES):
        where_scr[slots_ref[group, t]] = lax.rem(t + GROUP_FRAMES - part * frames, GROUP_FRAMES)


def time_scores(q, k, spread):
    parts = []
    for t, s in PAIRS:
        parts.append((q[t] * k[s]).astype(BF16))
    return dot(jnp.concatenate(parts, axis=0), spread)


def time_probs(scores, count):
    blocks = [scores[i * count : (i + 1) * count] for i in range(len(PAIRS))]
    probs = []
    at = 0
    for t in range(VIDEO_STEPS):
        mine = blocks[at : at + t + 1]
        at += t + 1
        top = functools.reduce(jnp.maximum, mine)
        raw = [jnp.exp(b - top) for b in mine]
        inv = 1.0 / functools.reduce(lambda a, b: a + b, raw)
        probs.extend([r * inv for r in raw])
    return probs


def split_slots(rows):
    count = rows.shape[0] // GROUP_FRAMES
    return [rows[s * count : (s + 1) * count].astype(F32) for s in range(GROUP_FRAMES)]


def time_forward_kernel(
    slots_ref, keep_ref, recv_ref, cot_ref, cotr_ref, gain_ref, shift_ref,
    wqkv_ref, wout_ref, wup_ref, bup_ref, wdown_ref, bdown_ref,
    own_ref, send_ref, x_ref, h2_ref, qkv_ref, o_ref, h3_ref, act_ref, du_ref, gr_ref, dxb_ref,
    small_ref,
    where_scr, both_scr, slope_scr,
):
    frames, half = keep_ref.shape[0], keep_ref.shape[1]
    part = lax.rem(lax.axis_index("sp"), GROUP_FRAMES // frames)
    slot_places(slots_ref, where_scr, frames)
    small_ref[...] = jnp.zeros_like(small_ref)
    both_scr[0:frames] = keep_ref[...]
    both_scr[frames:] = recv_ref[...]
    spread = lane_heads(BF16)
    steps = 4
    count = half // steps
    step_rows = count * GROUP_FRAMES
    for i in range(steps):
        span = slice(i * step_rows, (i + 1) * step_rows)
        place = slice(i * count, (i + 1) * count)
        x_low = jnp.concatenate([both_scr[where_scr[s], place] for s in range(GROUP_FRAMES)], axis=0)
        x_ref[span, :] = x_low
        x = x_low.astype(F32)
        h2 = norm(x, gain_ref[2:3, :], shift_ref[2:3, :])[0].astype(BF16)
        h2_ref[span, :] = h2
        q, k, v = qkv_rows(h2, wqkv_ref)
        qkv_ref[span, 0:TILE] = q
        qkv_ref[span, TILE : 2 * TILE] = k
        qkv_ref[span, 2 * TILE :] = v
        qs, ks, vs = split_slots(q), split_slots(k), split_slots(v)
        probs = time_probs(time_scores(qs, ks, spread), count)
        wide = dot_nt(jnp.concatenate([p.astype(BF16) for p in probs], axis=0), spread)
        mixed = []
        at = 0
        for t in range(VIDEO_STEPS):
            total = None
            for s in range(t + 1):
                piece = wide[at * count : (at + 1) * count] * vs[s]
                total = piece if total is None else total + piece
                at += 1
            mixed.append(total)
        mixed.extend(vs[VIDEO_STEPS:])
        o = jnp.concatenate([m.astype(BF16) for m in mixed], axis=0)
        o_ref[span, :] = o
        xb = x + dot(o, wout_ref[...]).astype(BF16).astype(F32)
        h3, unit, inv = norm(xb, gain_ref[3:4, :], shift_ref[3:4, :])
        h3 = h3.astype(BF16)
        h3_ref[span, :] = h3
        whole = slice(0, step_rows)
        slope = slope_scr.at[i % 2]
        branch = mlp_forward(h3, wup_ref, bup_ref[1:2, :], wdown_ref, span, act_ref, SpanView(slope))
        out = (xb + branch + bdown_ref[1:2, :]).astype(BF16)
        for s in range(GROUP_FRAMES):
            both_scr[where_scr[s], place] = out[s * count : (s + 1) * count]
        grad_low = jnp.concatenate(
            [cot_slot(cot_ref, cotr_ref, where_scr[s], part * half + i * count, count) for s in range(GROUP_FRAMES)],
            axis=0,
        )
        gr_ref[span, :] = grad_low
        grad = grad_low.astype(F32)
        dh, sums = mlp_backward(grad_low, wup_ref, wdown_ref, span, SpanView(slope), du_ref)
        add_small(small_ref, [column_sum(dh * unit), column_sum(dh), column_sum(grad), None] + sums, False)
        dxb_ref[span, :] = grad + norm_back(dh, unit, inv, gain_ref[3:4, :])
    own_ref[...] = both_scr[0:frames]
    send_ref[...] = both_scr[frames:]


class SpanView:
    def __init__(self, ref):
        self.ref = ref

    def __getitem__(self, index):
        return self.ref[:, index[1]]

    def __setitem__(self, index, value):
        self.ref[:, index[1]] = value


def cot_slot(cot_ref, cotr_ref, frame, start, count):
    frames = cot_ref.shape[0]
    places = pl.ds(pl.multiple_of(start, count), count)
    mine = cot_ref[lax.rem(frame, frames), places, :]
    other = cotr_ref[lax.rem(frame, frames), places, :]
    return jnp.where(frame < frames, mine, other)


def time_backward_kernel(
    slots_ref, x_ref, qkv_ref, dxb_ref, gain_ref, shift_ref, wqkv_ref, wout_ref,
    own_ref, send_ref, ar_ref, dqkv_ref, small_ref,
    where_scr, both_scr,
):
    frames, half = own_ref.shape[0], own_ref.shape[1]
    slot_places(slots_ref, where_scr, frames)
    small_ref[...] = jnp.zeros_like(small_ref)
    spread = lane_heads(BF16)
    steps = 4
    count = half // steps
    step_rows = count * GROUP_FRAMES
    gain = gain_ref[2:3, :]
    for i in range(steps):
        span = slice(i * step_rows, (i + 1) * step_rows)
        place = slice(i * count, (i + 1) * count)
        dxb = dxb_ref[span, :]
        ar = dxb.astype(BF16)
        ar_ref[span, :] = ar
        do = split_slots(dot_nt(ar, wout_ref[...]).astype(BF16))
        qs = split_slots(qkv_ref[span, 0:TILE])
        ks = split_slots(qkv_ref[span, TILE : 2 * TILE])
        vs = split_slots(qkv_ref[span, 2 * TILE :])
        probs = time_probs(time_scores(qs, ks, spread), count)
        dps = time_scores(do, vs, spread)
        dps = [dps[j * count : (j + 1) * count] for j in range(len(PAIRS))]
        dss = []
        at = 0
        for t in range(VIDEO_STEPS):
            centre = functools.reduce(
                lambda a, b: a + b, [probs[at + s] * dps[at + s] for s in range(t + 1)]
            )
            dss.extend([probs[at + s] * (dps[at + s] - centre) for s in range(t + 1)])
            at += t + 1
        wide_p = dot_nt(jnp.concatenate([p.astype(BF16) for p in probs], axis=0), spread)
        wide_ds = dot_nt(jnp.concatenate([d.astype(BF16) for d in dss], axis=0), spread)
        dq = [None] * GROUP_FRAMES
        dk = [None] * GROUP_FRAMES
        dv = [None] * GROUP_FRAMES

        def add(table, index, piece):
            table[index] = piece if table[index] is None else table[index] + piece

        for j, (t, s) in enumerate(PAIRS):
            rows = slice(j * count, (j + 1) * count)
            add(dq, t, wide_ds[rows] * ks[s])
            add(dk, s, wide_ds[rows] * qs[t])
            add(dv, s, wide_p[rows] * do[t])
        for t in range(VIDEO_STEPS, GROUP_FRAMES):
            dq[t] = jnp.zeros_like(do[t])
            dk[t] = jnp.zeros_like(do[t])
            dv[t] = do[t]
        dq = jnp.concatenate([(d * SCALE).astype(BF16) for d in dq], axis=0)
        dk = jnp.concatenate([d.astype(BF16) for d in dk], axis=0)
        dv = jnp.concatenate([d.astype(BF16) for d in dv], axis=0)
        dqkv_ref[span, 0:TILE] = dq
        dqkv_ref[span, TILE : 2 * TILE] = dk
        dqkv_ref[span, 2 * TILE :] = dv
        dh = dot_nt(dqkv_ref[span, :], wqkv_ref[...])
        unit, inv = norm(x_ref[span, :].astype(F32), gain, shift_ref[2:3, :])[1:]
        add_small(small_ref, [column_sum(dh * unit), column_sum(dh)], False)
        dxp = norm_back(dh, unit, inv, gain).astype(BF16).astype(F32)
        dx1 = (dxb + dxp).astype(BF16)
        for s in range(GROUP_FRAMES):
            both_scr[where_scr[s], place] = dx1[s * count : (s + 1) * count]
    own_ref[...] = both_scr[0:frames]
    send_ref[...] = both_scr[frames:]


def space_mlp_back_kernel(
    own_ref, recv_ref, xa_ref, slope_ref, gain_ref, shift_ref, wup_ref, wdown_ref,
    gr_ref, du_ref, dxa_ref, ar_ref, small_ref,
):
    part = lax.rem(lax.axis_index("sp"), 2)
    small_ref[...] = jnp.zeros_like(small_ref)
    frames, half = own_ref.shape[0], own_ref.shape[1]
    rows = 2 * half
    gain = gain_ref[1:2, :]
    for f in range(frames):
        span = slice(f * rows, (f + 1) * rows)
        base = f * rows
        gr_ref[pl.ds(pl.multiple_of(base + part * half, half), half), :] = own_ref[f]
        gr_ref[pl.ds(pl.multiple_of(base + (1 - part) * half, half), half), :] = recv_ref[f]
        grad_low = gr_ref[span, :]
        grad = grad_low.astype(F32)
        dh, sums = mlp_backward(grad_low, wup_ref, wdown_ref, span, slope_ref, du_ref)
        unit, inv = norm(xa_ref[span, :], gain, shift_ref[1:2, :])[1:]
        add_small(small_ref, [column_sum(dh * unit), column_sum(dh), column_sum(grad), None] + sums, False)
        dxa = grad + norm_back(dh, unit, inv, gain)
        dxa_ref[span, :] = dxa
        ar_ref[span, :] = dxa.astype(BF16)


def head_picker():
    h = lax.broadcasted_iota(jnp.int32, (HEADS, TILE), 0)
    c = lax.broadcasted_iota(jnp.int32, (HEADS, TILE), 1)
    return (c // HEAD == h).astype(BF16)


def attn_back_frame(f, to, ar_ref, qkv_ref, lse_ref, o_ref, wout_ref, pick, dqkv_ref):
    rows = lse_ref.shape[2]
    span = slice(f * rows, (f + 1) * rows)
    dest = slice(to * rows, (to + 1) * rows)
    do = dot_nt(ar_ref[span, :], wout_ref[...]).astype(BF16)
    both = do.astype(F32) * o_ref[span, :].astype(F32)
    high = both.astype(BF16)
    rest = (both - high.astype(F32)).astype(BF16)
    centre = dot_nt(pick, high) + dot_nt(pick, rest)
    for pair in range(HEADS // 2):
        qp = qkv_ref[span, pair * 128 : (pair + 1) * 128]
        kp = qkv_ref[span, TILE + pair * 128 : TILE + (pair + 1) * 128]
        vp = qkv_ref[span, 2 * TILE + pair * 128 : 2 * TILE + (pair + 1) * 128]
        dop = do[:, pair * 128 : (pair + 1) * 128]
        zero = jnp.zeros_like(kp)
        mask = head_mask(kp, 0)
        st = dot_nt(jnp.concatenate([jnp.where(mask, kp, zero), jnp.where(mask, zero, kp)], axis=0), qp)
        dpt = dot_nt(jnp.concatenate([jnp.where(mask, vp, zero), jnp.where(mask, zero, vp)], axis=0), dop)
        pts, dsts, dqs = [], [], []
        for e in range(2):
            row = slice(2 * pair + e, 2 * pair + e + 1)
            keys = slice(e * rows, (e + 1) * rows)
            pt = jnp.exp(st[keys] - lse_ref[f, row, :])
            dst = (pt * (dpt[keys] - centre[row, :])).astype(BF16)
            pts.append(pt.astype(BF16))
            dsts.append(dst)
            dqs.append(dot_tn(dst, kp) * SCALE)
        dk = dot(jnp.concatenate(dsts, axis=0), qp)
        dv = dot(jnp.concatenate(pts, axis=0), dop)
        values = (
            jnp.where(mask, dqs[0], dqs[1]),
            jnp.where(mask, dk[:rows], dk[rows:]),
            jnp.where(mask, dv[:rows], dv[rows:]),
        )
        for index, value in enumerate(values):
            at = index * TILE + pair * 128
            dqkv_ref[dest, at : at + 128] = value.astype(BF16)


def space_attn_back_kernel(ar_ref, qkv_ref, lse_ref, o_ref, wout_ref, dqkv_ref):
    pick = head_picker()
    for f in range(lse_ref.shape[0] // 2):
        attn_back_frame(f, f, ar_ref, qkv_ref, lse_ref, o_ref, wout_ref, pick, dqkv_ref)


def finish_kernel(
    order, ar_ref, qkv_ref, lse_ref, o_ref, wout_ref, first_ref, tok_ref, dxa_ref, own_ref, recv_ref,
    gain_ref, shift_ref, wqkv_ref, h_ref, small1_ref, small2_ref, small3_ref,
    gtok_ref, out_ref, keep_ref, send_ref, dqkv_scr,
):
    sp = lax.axis_index("sp")
    part = lax.rem(sp, 2)
    frames, half = own_ref.shape[0], own_ref.shape[1]
    rows = 2 * half
    pick = head_picker()
    for f in range(frames // 2, frames):
        attn_back_frame(f, f - frames // 2, ar_ref, qkv_ref, lse_ref, o_ref, wout_ref, pick, dqkv_scr)
    gain = gain_ref[0:1, :]
    sums = []
    for f in range(frames):
        span = slice(f * rows, (f + 1) * rows)
        out_ref[f, half_rows(part, half), :] = own_ref[f]
        out_ref[f, half_rows(1 - part, half), :] = recv_ref[f]
        source = first_ref if f < frames // 2 else dqkv_scr
        at = (f % (frames // 2)) * rows
        dh = dot_nt(source[at : at + rows, :], wqkv_ref[...])
        unit, inv = norm(tok_ref[f].astype(F32), gain, shift_ref[0:1, :])[1:]
        sums.append((column_sum(dh * unit), column_sum(dh)))
        gtok_ref[f] = (dxa_ref[span, :] + norm_back(dh, unit, inv, gain)).astype(BF16)
    size = h_ref.shape[1] // lax.axis_size("sp")
    slots = lax.axis_size("sp") // 2
    turned = jnp.transpose(h_ref[...])
    middle = first_ref.shape[0]
    zero = jnp.int32(0)
    for j in range(3):
        cols = slice(j * TILE, (j + 1) * TILE)
        result = dot(turned[:, :middle], first_ref[:, cols]) + dot(turned[:, middle:], dqkv_scr[:, cols])
        put_blocks(result, zero, size, Place(0, 3 * size, j * size), order, keep_ref, send_ref)
    row = lax.broadcasted_iota(jnp.int32, (8, TILE), 0)
    total = [functools.reduce(lambda a, b: a + b, [x[i] for x in sums]) for i in range(2)]
    small0 = jnp.where(row == 0, total[0], jnp.where(row == 1, total[1], 0.0))
    small = jnp.concatenate([small0, small1_ref[...], small2_ref[...], small3_ref[...]], axis=0).astype(BF16)
    base = slots * 3 * size
    keep_ref[base:, :] = small
    send_ref[base:, :] = small


def place_of(block, order, sp):
    bits = len(order)
    mixed = jnp.bitwise_xor(block, sp)
    slot = jnp.int32(0)
    for i, b in enumerate(order):
        bit = jnp.bitwise_and(lax.shift_right_logical(mixed, jnp.int32(b)), 1)
        slot = slot + lax.shift_left(bit, jnp.int32(bits - 1 - i))
    return slot


class Place:
    def __init__(self, base, rows, at):
        self.base, self.rows, self.at = base, rows, at


def put_blocks(result, first, size, place, order, keep_ref, send_ref):
    sp = lax.axis_index("sp")
    part = lax.rem(sp, 2)
    low = result.astype(BF16)
    for j in range(result.shape[0] // (2 * size)):
        even = low[2 * j * size : (2 * j + 1) * size]
        odd = low[(2 * j + 1) * size : (2 * j + 2) * size]
        slot = place_of(first + 2 * j, order[1:], sp)
        rows = pl.ds(pl.multiple_of(place.base + slot * place.rows + place.at, 16), size)
        keep_ref[rows, :] = jnp.where(part == 0, even, odd)
        send_ref[rows, :] = jnp.where(part == 0, odd, even)


def mlp_weights_kernel(orders, *refs):
    h_ref, du_ref, act_ref, gr_ref = refs[:4]
    extra = refs[4:-2]
    keep_ref, send_ref = refs[-2:]
    sp_size = lax.axis_size("sp")
    slots = sp_size // 2
    up_size = h_ref.shape[1] // sp_size
    chunks = du_ref.shape[1] // TILE
    down_size = chunks * TILE // sp_size
    rows_a = chunks * up_size
    rows_b = down_size + (up_size if extra else 0)
    base = slots * rows_a
    zero = jnp.int32(0)
    turned = jnp.transpose(h_ref[...])
    for j in range(chunks):
        cols = slice(j * TILE, (j + 1) * TILE)
        up = dot(turned, du_ref[:, cols])
        put_blocks(up, zero, up_size, Place(0, rows_a, j * up_size), orders[0], keep_ref, send_ref)
        down = dot_tn(act_ref[:, cols], gr_ref[...])
        first = jnp.int32(j * (TILE // down_size))
        put_blocks(down, first, down_size, Place(base, rows_b, 0), orders[1], keep_ref, send_ref)
    if extra:
        out = dot_tn(extra[0][...], extra[1][...])
        put_blocks(out, zero, up_size, Place(base, rows_b, down_size), orders[1], keep_ref, send_ref)


def attn_weights_kernel(order, h_ref, dqkv_ref, o_ref, ar_ref, keep_ref, send_ref):
    size = h_ref.shape[1] // lax.axis_size("sp")
    zero = jnp.int32(0)
    turned = jnp.transpose(h_ref[...])
    for j in range(3):
        cols = slice(j * TILE, (j + 1) * TILE)
        result = dot(turned, dqkv_ref[:, cols])
        put_blocks(result, zero, size, Place(0, 4 * size, j * size), order, keep_ref, send_ref)
    result = dot_tn(o_ref[...], ar_ref[...])
    put_blocks(result, zero, size, Place(0, 4 * size, 3 * size), order, keep_ref, send_ref)


def fold_kernel(moves, count, summed, *refs):
    outs = refs[2 * count :]
    for source, at, rows, out, to, whole in moves:
        keep, recv = refs[2 * source], refs[2 * source + 1]
        if summed:
            outs[out][to : to + rows, :] = keep[at : at + rows, :] + recv[at : at + rows, :]
        elif whole:
            total = keep[at : at + rows, :] + recv[at : at + rows, :]
            outs[2 * out][to : to + rows, :] = total
            outs[2 * out + 1][to : to + rows, :] = total
        else:
            half = rows // 2
            for part in range(2):
                span = slice(at + part * half, at + (part + 1) * half)
                outs[2 * out + part][to : to + half, :] = keep[span, :] + recv[span, :]


class Group:
    def __init__(self, sizes, segments, split):
        grp_size, sp_size = sizes
        self.segments = segments
        names = tuple(segments)
        bits = sp_size.bit_length() - 1
        self.stages = [[("sp", sp_size, 0, names)]]
        for b in range(1, bits):
            if split and b < 3:
                self.stages.append([("sp", sp_size, b, names[:1]), ("sp", sp_size, 3 - b, names[1:])])
            else:
                self.stages.append([("sp", sp_size, b, names)])
        for b in range(grp_size.bit_length() - 1):
            self.stages.append([("grp", grp_size, b, names)])
        self.scatters = bits
        self.slots = sp_size // 2
        self.stage = 0

    def rows(self, name, slots):
        height, whole = self.segments[name]
        return height if whole else height * slots

    def start(self, sends):
        self.recvs = [
            swap(send, axis, size, bit) for send, (axis, size, bit, names) in zip(sends, self.stages[self.stage])
        ]

    def begin(self, keep, send):
        self.keeps = [keep]
        self.start([send])

    def step(self):
        now, later = self.stages[self.stage], self.stages[self.stage + 1]
        summed = self.slots == 1
        after = self.slots if summed else self.slots // 2
        where = {}
        shapes = []
        for out, entry in enumerate(later):
            at = 0
            for name in entry[3]:
                where[name] = (out, at)
                at += self.rows(name, after)
            shapes += [sds((at, TILE), BF16)] * (1 if summed else 2)
        moves = []
        for source, entry in enumerate(now):
            at = 0
            for name in entry[3]:
                rows = self.rows(name, self.slots)
                moves.append((source, at, rows) + where[name] + (self.segments[name][1],))
                at += rows
        args = [x for pair in zip(self.keeps, self.recvs) for x in pair]
        out = call(functools.partial(fold_kernel, moves, len(now), summed), args, shapes, 0.5, limit=4)
        self.keeps = out if summed else out[0::2]
        self.slots = after
        self.stage += 1
        self.start(out if summed else out[1::2])

    def left(self):
        return len(self.stages) - 1 - self.stage

    def pair(self):
        return self.keeps[0], self.recvs[0]


def result_kernel(sp_size, *refs):
    mlp1, attn1, mlp0, qkv0 = [(refs[2 * i], refs[2 * i + 1]) for i in range(4)]
    outs = refs[8:16]
    gain_scr, shift_scr, qkv_scr, out_scr, up_scr, bup_scr, down_scr, bdown_scr, small_scr, sems = refs[16:]
    size = TILE // sp_size
    chunks = up_scr.shape[2] // TILE
    down_size = chunks * size

    def total(pair, at, rows):
        return pair[0][at : at + rows, :].astype(F32) + pair[1][at : at + rows, :].astype(F32)

    for layer, (qkv, mlp) in enumerate(((qkv0, mlp0), (attn1, mlp1))):
        for j in range(3):
            qkv_scr[layer, :, j * TILE : (j + 1) * TILE] = total(qkv, j * size, size)
        for j in range(chunks):
            up_scr[layer, :, j * TILE : (j + 1) * TILE] = total(mlp, j * size, size)
        down_scr[layer] = total(mlp, chunks * size, down_size)
    out_scr[0] = total(mlp0, chunks * size + down_size, size)
    out_scr[1] = total(attn1, 3 * size, size)
    small_scr[...] = total(qkv0, 3 * size, 32)
    sp = lax.axis_index("sp")
    back = lax.rem(TILE - sp * size, TILE)
    turned = pltpu.roll(small_scr[...], back, 1)
    for i in range(4):
        gain_scr[i : i + 1, :] = turned[8 * i : 8 * i + 1, :size]
        shift_scr[i : i + 1, :] = turned[8 * i + 1 : 8 * i + 2, :size]
    start = sp * down_size
    line = start // TILE
    back = lax.rem(TILE - lax.rem(start, TILE), TILE)
    for layer in range(2):
        first = 8 + 16 * layer
        bdown_scr[layer : layer + 1, :] = turned[first + 2 : first + 3, :size]
        rows = small_scr[first : first + 8, :]
        lines = lax.broadcasted_iota(jnp.int32, rows.shape, 0)
        picked = jnp.sum(jnp.where(lines == 4 + line, rows, 0.0), axis=0, keepdims=True)
        picked = pltpu.roll(jnp.broadcast_to(picked, rows.shape), back, 1)
        bup_scr[layer : layer + 1, :] = picked[0:1, :down_size]
    scrs = (gain_scr, shift_scr, qkv_scr, out_scr, up_scr, bup_scr, down_scr, bdown_scr)
    copies = [pltpu.make_async_copy(scr, out, sems.at[i]) for i, (scr, out) in enumerate(zip(scrs, outs))]
    for copy in copies:
        copy.start()
    for copy in copies:
        copy.wait()


VMEM = pl.BlockSpec(memory_space=pltpu.VMEM)
SMEM = pl.BlockSpec(memory_space=pltpu.SMEM)
HBM = pl.BlockSpec(memory_space=pltpu.HBM)


def sds(shape, dtype):
    return jax.ShapeDtypeStruct(shape, dtype)


def call(kernel, args, outs, micros, scratch=(), specs=None, out_specs=None, limit=12):
    return pl.pallas_call(
        kernel,
        in_specs=[VMEM] * len(args) if specs is None else specs,
        out_specs=[VMEM] * len(outs) if out_specs is None else out_specs,
        out_shape=outs,
        scratch_shapes=list(scratch),
        compiler_params=pltpu.CompilerParams(vmem_limit_bytes=limit * MIB),
        cost_estimate=pl.CostEstimate(flops=int(micros * 1.15e9), bytes_accessed=0, transcendentals=0),
    )(*args)


def swap(array, axis, size, bit):
    return lax.ppermute(array, axis, [(i, i ^ (1 << bit)) for i in range(size)])


def shards(sizes, tokens, frame_slot, norm_gain, norm_shift, w_qkv, w_out, w_up, b_up, w_down, b_down, cotangent):
    grp_size, sp_size = sizes
    frames, patches, width = tokens.shape
    hidden = w_up.shape[2]
    assert GROUP_FRAMES == 2 * frames and sp_size >= 8
    half = patches // 2
    rows = frames * patches
    sp_bits = sp_size.bit_length() - 1
    core_swap = functools.partial(swap, axis="sp", size=sp_size, bit=0)
    slots = sp_size // 2
    size = width // sp_size
    down_size = hidden // sp_size
    order_a = list(range(sp_bits))
    order_b = [0, 2, 1] + list(range(3, sp_bits))

    def row_out(cols, dtype=BF16):
        return sds((rows, cols), dtype)

    half_out = sds((frames, half, width), BF16)
    small_out = sds((8, TILE), F32)
    fence = lambda *arrays: lax.optimization_barrier(arrays)

    def meet(groups, *arrays):
        recvs = [r for g in groups for r in g.recvs]
        out = fence(*arrays, *recvs)
        recvs = list(out[len(arrays) :])
        for g in groups:
            g.recvs = [recvs.pop(0) for _ in g.recvs]
            g.step()
        return out[: len(arrays)]

    def buffers(height, tail=0):
        return [sds((slots * height + tail, TILE), BF16)] * 2

    cot_recv = core_swap(cotangent)
    weights = (w_qkv, w_out, w_up, w_down)
    out = call(
        space_forward_kernel,
        (tokens, norm_gain, norm_shift, w_qkv, w_out, w_up, b_up, w_down, b_down),
        [
            half_out, half_out, row_out(width), row_out(3 * width), sds((frames, HEADS, patches), F32),
            row_out(width), row_out(width, F32), row_out(width), row_out(hidden), row_out(hidden),
            sds(tokens.shape, BF16),
        ] + [sds(w.shape[1:], BF16) for _ in range(2) for w in weights],
        16,
        scratch=[
            pltpu.VMEM((2, patches, hidden), BF16), pltpu.VMEM((2, patches, hidden), BF16),
            pltpu.VMEM((patches, width), F32), pltpu.SemaphoreType.DMA((9,)),
            pltpu.SemaphoreType.DMA((2 * frames,)),
        ],
        specs=[HBM, VMEM, VMEM, HBM, HBM, HBM, VMEM, HBM, VMEM],
        out_specs=[VMEM] * 8 + [HBM] * 2 + [VMEM] * 9,
    )
    (x_keep, x_send, h0, qkv0, lse0, o0, xa, h1, act0, slope0, tok) = out[:11]
    w_qkv0, w_out0, w_up0, w_down0, w_qkv1, w_out1, w_up1, w_down1 = out[11:]
    x_recv = core_swap(x_send)

    place_scratch = [
        pltpu.SMEM((GROUP_FRAMES,), jnp.int32),
        pltpu.VMEM((GROUP_FRAMES, half, width), BF16),
    ]
    (out_own, out_send, xt, h2, qkv1, o1, h3, act1, du1, gr1, dxb, small3) = call(
        time_forward_kernel,
        (
            frame_slot, x_keep, x_recv, cotangent, cot_recv, norm_gain, norm_shift, w_qkv1, w_out1, w_up1,
            b_up, w_down1, b_down,
        ),
        [
            half_out, half_out, row_out(width), row_out(width), row_out(3 * width), row_out(width),
            row_out(width), row_out(hidden), row_out(hidden), row_out(width), row_out(width, F32),
            small_out,
        ],
        24,
        scratch=place_scratch + [pltpu.VMEM((2, rows // 4, hidden), BF16)],
        specs=[SMEM] + [VMEM] * 12,
    )
    out_recv = core_swap(out_send)

    def mlp_group(h, du, act, gr, *extra):
        height_b = down_size + (size if extra else 0)
        group = Group(sizes, {"up": (4 * size, False), "down": (height_b, False)}, True)
        return group, call(
            functools.partial(mlp_weights_kernel, (order_a, order_b)), (h, du, act, gr) + extra,
            buffers(4 * size + height_b), 4.5,
        )

    mlp1, out = mlp_group(h3, du1, act1, gr1)
    keep, send, dxb = fence(*out, dxb)
    mlp1.begin(keep, send)

    (dx_own, dx_send, ar1, dqkv1, small2) = call(
        time_backward_kernel,
        (frame_slot, xt, qkv1, dxb, norm_gain, norm_shift, w_qkv1, w_out1),
        [half_out, half_out, row_out(width), row_out(3 * width), small_out],
        8,
        scratch=place_scratch,
        specs=[SMEM] + [VMEM] * 7,
    )
    dx_own, dx_send, dqkv1 = meet((mlp1,), dx_own, dx_send, dqkv1)
    dx_recv = core_swap(dx_send)
    attn1 = Group(sizes, {"attn": (4 * size, False)}, False)
    out = call(
        functools.partial(attn_weights_kernel, order_a), (h2, dqkv1, o1, ar1), buffers(4 * size), 2.4
    )
    keep, send, dx_recv = fence(*out, dx_recv)
    attn1.begin(keep, send)

    (gr0, du0, dxa, ar0, small1) = call(
        space_mlp_back_kernel,
        (dx_own, dx_recv, xa, slope0, norm_gain, norm_shift, w_up0, w_down0),
        [row_out(width), row_out(hidden), row_out(width, F32), row_out(width), small_out],
        6,
    )
    gr0, du0, ar0 = meet((attn1,), gr0, du0, ar0)
    mlp0, out = mlp_group(h1, du0, act0, gr0, o0, ar0)
    keep, send, ar0 = meet((mlp1,), *out, ar0)
    mlp0.begin(keep, send)

    half_spec = [sds((rows // 2, 3 * width), BF16)]
    (dqkv0,) = call(space_attn_back_kernel, (ar0, qkv0, lse0, o0, w_out0), half_spec, 5)
    (dqkv0,) = meet((mlp0,), dqkv0)
    qkv = Group(sizes, {"qkv": (3 * size, False), "small": (32, True)}, False)
    grad_tokens, output, keep, send = call(
        functools.partial(finish_kernel, order_a),
        (
            ar0, qkv0, lse0, o0, w_out0, dqkv0, tok, dxa, out_own, out_recv, norm_gain, norm_shift,
            w_qkv0, h0, small1, small2, small3,
        ),
        [sds(tokens.shape, BF16), sds(tokens.shape, BF16)] + buffers(3 * size, 32),
        10,
        scratch=[pltpu.VMEM((rows // 2, 3 * width), BF16)],
    )
    keep, send = meet((mlp1, attn1), keep, send)
    qkv.begin(keep, send)
    meet((qkv,))
    meet((mlp0, mlp1))
    meet((attn1, qkv))
    meet((mlp0,))
    meet((attn1, qkv))
    for group in (mlp0, qkv, mlp1, attn1):
        while group.left():
            meet((group,))
    pairs = [x for g in (mlp1, attn1, mlp0, qkv) for x in g.pair()]
    finals = [
        sds((4, size), F32), sds((4, size), F32), sds((2, size, 3 * width), F32), sds((2, size, width), F32),
        sds((2, size, hidden), F32), sds((2, down_size), F32), sds((2, down_size, width), F32),
        sds((2, size), F32),
    ]
    results = call(
        functools.partial(result_kernel, sp_size), pairs, finals, 2,
        scratch=[pltpu.VMEM(f.shape, F32) for f in finals]
        + [pltpu.VMEM((32, TILE), F32), pltpu.SemaphoreType.DMA((8,))],
        out_specs=[HBM] * 8,
    )
    return (output, grad_tokens, *results)


def solution(mesh):
    rows = P(("grp", "sp"), None, None)
    in_specs = (rows, P("grp", None), P(), P(), P(), P(), P(), P(), P(), P(), rows)
    out_specs = (
        rows, rows, P(None, "sp"), P(None, "sp"), P(None, "sp", None), P(None, "sp", None),
        P(None, "sp", None), P(None, "sp"), P(None, "sp", None), P(None, "sp"),
    )
    body = functools.partial(shards, (mesh.shape["grp"], mesh.shape["sp"]))
    return jax.shard_map(body, mesh=mesh, in_specs=in_specs, out_specs=out_specs, check_vma=False)
```

```python
import functools

import jax
import jax.numpy as jnp
from jax import lax
from jax.experimental import pallas as pl
from jax.experimental.pallas import tpu as pltpu
from jax.sharding import PartitionSpec as P

HEADS = 8
HEAD = 64
VIDEO_STEPS = 6
GROUP_FRAMES = 8
NORM_EPS = 1e-05
TILE = 512
SCALE = HEAD**-0.5
TANH_A = 0.7978845608028654
TANH_B = TANH_A * 0.044715
PAIRS = [(t, s) for t in range(VIDEO_STEPS) for s in range(t + 1)]
F32 = jnp.float32
BF16 = jnp.bfloat16
MIB = 1024 * 1024
LIMIT1 = 52
LIMIT2 = 24


def dot(left, right):
    return jnp.dot(left, right, preferred_element_type=F32)


def dot_nt(left, right):
    return lax.dot_general(left, right, (((1,), (1,)), ((), ())), preferred_element_type=F32)


def dot_tn(left, right):
    return lax.dot_general(left, right, (((0,), (0,)), ((), ())), preferred_element_type=F32)


def norm(rows, gain, shift):
    centred = rows - jnp.mean(rows, axis=-1, keepdims=True)
    inv = lax.rsqrt(jnp.mean(centred * centred, axis=-1, keepdims=True) + NORM_EPS)
    unit = centred * inv
    return unit * gain + shift, unit, inv


def norm_back(grad, unit, inv, gain):
    grad_unit = grad * gain
    mean_grad = jnp.mean(grad_unit, axis=-1, keepdims=True)
    mean_both = jnp.mean(grad_unit * unit, axis=-1, keepdims=True)
    return inv * (grad_unit - mean_grad - unit * mean_both)


def column_sum(rows):
    return jnp.sum(rows, axis=0, keepdims=True)


def gelu_pair(u):
    square = u * u
    sigma = 0.5 + 0.5 * jnp.tanh(u * (TANH_A + TANH_B * square))
    act = u * sigma
    slope = sigma + act * (1.0 - sigma) * (2.0 * TANH_A + 6.0 * TANH_B * square)
    return act.astype(BF16), slope.astype(BF16)


def head_mask(lanes, which):
    lane = lax.broadcasted_iota(jnp.int32, lanes.shape, 1)
    return (lane < HEAD) if which == 0 else (lane >= HEAD)


def qkv_rows(normed, weight):
    out = []
    for part in range(3):
        piece = dot(normed, weight[:, part * TILE : (part + 1) * TILE])
        if part == 0:
            out.append(piece.astype(BF16) * BF16(SCALE))
        else:
            out.append(piece.astype(BF16))
    return out


def mlp_forward(normed, w_up, b_up, w_down, rows, act_ref, slope_ref):
    chunks = w_up.shape[1] // TILE
    up = lambda j: dot(normed, w_up[:, j * TILE : (j + 1) * TILE])
    total = None
    u = up(0)
    for j in range(chunks):
        cols = slice(j * TILE, (j + 1) * TILE)
        later = up(j + 1) if j + 1 < chunks else None
        act, slope = gelu_pair(u + b_up[j : j + 1, :])
        act_ref[rows, cols] = act
        slope_ref[rows, cols] = slope
        piece = dot(act, w_down[cols, :])
        total = piece if total is None else total + piece
        u = later
    return total


def mlp_backward(grad_low, w_up, w_down, rows, slope_ref, du_ref):
    chunks = w_up.shape[1] // TILE
    down = lambda j: dot_nt(grad_low, w_down[j * TILE : (j + 1) * TILE, :])
    total = None
    sums = []
    da = down(0)
    for j in range(chunks):
        cols = slice(j * TILE, (j + 1) * TILE)
        later = down(j + 1) if j + 1 < chunks else None
        du = (da * slope_ref[rows, cols].astype(F32)).astype(BF16)
        du_ref[rows, cols] = du
        sums.append(column_sum(du.astype(F32)))
        piece = dot_nt(du, w_up[:, cols])
        total = piece if total is None else total + piece
        da = later
    return total, sums


def add_small(small_ref, values, first):
    for i, value in enumerate(values):
        row = slice(i, i + 1) if i < 4 else slice(i, i + 1)
        if value is None:
            continue
        if first:
            small_ref[row, :] = value
        else:
            small_ref[row, :] += value


def half_rows(part, half):
    return pl.ds(pl.multiple_of(part * half, half), half)


def space_forward_kernel(
    tok_hbm, params_ref, wqkv_hbm, wout_hbm, wup_hbm, wdown_hbm,
    keep_ref, send_ref, h0_hbm, qkv_hbm, lse_ref, o_hbm, xa_hbm, h1_hbm, act_hbm, slope_hbm,
    tok_ref, wqkv_ref, wout_ref, wup_ref, wdown_ref, h0_scr, qkv_scr, o_scr, xa_scr, h1_scr, act_scr,
    slope_scr, x1_scr, in_sems, out_sems,
):
    pairs = [
        (tok_hbm, tok_ref), (wqkv_hbm.at[0], wqkv_ref), (wout_hbm.at[0], wout_ref),
        (wup_hbm.at[0], wup_ref), (wdown_hbm.at[0], wdown_ref),
    ]
    copies = [pltpu.make_async_copy(src, dst, in_sems.at[i]) for i, (src, dst) in enumerate(pairs)]
    for copy in copies:
        copy.start()
    gain_ref, shift_ref = params_ref, params_ref.at[4:8]
    part = lax.rem(lax.axis_index("sp"), 2)
    frames, rows = tok_ref.shape[0], tok_ref.shape[1]
    half = rows // 2
    lane = lax.broadcasted_iota(jnp.int32, (rows, 128), 1)
    spills = []
    copies[0].wait()
    for f in range(frames):
        span = slice(f * rows, (f + 1) * rows)
        x0 = tok_ref[f].astype(F32)
        h0 = norm(x0, gain_ref[0:1, :], shift_ref[0:1, :])[0].astype(BF16)
        if f == 0:
            copies[1].wait()
        now = f % 2
        places = (
            (h0_scr, h0_hbm), (qkv_scr, qkv_hbm), (o_scr, o_hbm), (xa_scr, xa_hbm), (h1_scr, h1_hbm),
            (act_scr, act_hbm), (slope_scr, slope_hbm),
        )
        spill = [
            pltpu.make_async_copy(scr.at[now], hbm.at[span], out_sems.at[7 * f + i])
            for i, (scr, hbm) in enumerate(places)
        ]
        if f >= 2:
            for copy in spills[f - 2]:
                copy.wait()
        spills.append(spill)
        h0_scr[now] = h0
        spill[0].start()
        q, k, v = qkv_rows(h0, wqkv_ref)
        qkv_scr[now, :, 0:TILE] = q
        qkv_scr[now, :, TILE : 2 * TILE] = k
        qkv_scr[now, :, 2 * TILE :] = v
        spill[1].start()
        lse_all = jnp.zeros((rows, 128), F32)
        mixed = []
        for pair in range(HEADS // 2):
            cols = slice(pair * 128, (pair + 1) * 128)
            qp, kp, vp = q[:, cols], k[:, cols], v[:, cols]
            zero = jnp.zeros_like(qp)
            mask = head_mask(qp, 0)
            s = dot_nt(jnp.concatenate([jnp.where(mask, qp, zero), jnp.where(mask, zero, qp)], axis=0), kp)
            top = jnp.max(s, axis=-1, keepdims=True)
            p = jnp.exp(s - top)
            total = jnp.sum(p, axis=-1, keepdims=True)
            both = dot(p.astype(BF16), vp) * (1.0 / total)
            lse = top + jnp.log(total)
            lse_all = jnp.where(lane == 2 * pair, lse[:rows], lse_all)
            lse_all = jnp.where(lane == 2 * pair + 1, lse[rows:], lse_all)
            mixed.append(jnp.where(mask, both[:rows], both[rows:]).astype(BF16))
        lse_ref[f] = jnp.transpose(lse_all)[0:HEADS, :]
        o = jnp.concatenate(mixed, axis=1)
        o_scr[now] = o
        spill[2].start()
        if f == 0:
            copies[2].wait()
        xa = x0 + dot(o, wout_ref[...])
        xa_scr[now] = xa
        spill[3].start()
        h1 = norm(xa, gain_ref[1:2, :], shift_ref[1:2, :])[0].astype(BF16)
        h1_scr[now] = h1
        spill[4].start()
        if f == 0:
            copies[3].wait()
            copies[4].wait()
        branch = mlp_forward(
            h1, wup_ref, params_ref.at[8:12], wdown_ref, slice(None), act_scr.at[now], slope_scr.at[now]
        )
        spill[5].start()
        spill[6].start()
        x1_scr[...] = xa + branch + params_ref[16:17, :]
        keep_ref[f] = x1_scr[half_rows(part, half), :].astype(BF16)
        send_ref[f] = x1_scr[half_rows(1 - part, half), :].astype(BF16)
    for copies_of in spills[-2:]:
        for copy in copies_of:
            copy.wait()


def lane_heads(dtype):
    c = lax.broadcasted_iota(jnp.int32, (TILE, 128), 0)
    h = lax.broadcasted_iota(jnp.int32, (TILE, 128), 1)
    return (c // HEAD == h).astype(dtype)


def slot_places(slots_ref, where_scr, frames):
    sp = lax.axis_index("sp")
    group = (sp * frames) // GROUP_FRAMES
    part = lax.rem(sp, GROUP_FRAMES // frames)
    for t in range(GROUP_FRAMES):
        where_scr[slots_ref[group, t]] = lax.rem(t + GROUP_FRAMES - part * frames, GROUP_FRAMES)


def time_scores(q, k, spread):
    parts = []
    for t, s in PAIRS:
        parts.append((q[t] * k[s]).astype(BF16))
    return dot(jnp.concatenate(parts, axis=0), spread)


def time_probs(scores, count):
    blocks = [scores[i * count : (i + 1) * count] for i in range(len(PAIRS))]
    probs = []
    at = 0
    for t in range(VIDEO_STEPS):
        mine = blocks[at : at + t + 1]
        at += t + 1
        top = functools.reduce(jnp.maximum, mine)
        raw = [jnp.exp(b - top) for b in mine]
        inv = 1.0 / functools.reduce(lambda a, b: a + b, raw)
        probs.extend([r * inv for r in raw])
    return probs


def split_slots(rows):
    count = rows.shape[0] // GROUP_FRAMES
    return [rows[s * count : (s + 1) * count].astype(F32) for s in range(GROUP_FRAMES)]


def time_forward_kernel(
    slots_ref, keep_ref, recv_ref, cot_ref, cotr_ref, params_ref,
    wqkv_hbm, wout_hbm, wup_hbm, wdown_hbm,
    own_ref, send_ref, x_ref, h2_ref, qkv_ref, o_ref, h3_ref, act_ref, du_ref, gr_ref, dxb_ref,
    small_ref, wqkv_ref, wout_ref,
    where_scr, both_scr, slope_scr, wup_ref, wdown_ref, in_sems,
):
    pairs = [(wqkv_hbm, wqkv_ref), (wout_hbm, wout_ref), (wup_hbm, wup_ref), (wdown_hbm, wdown_ref)]
    copies = [pltpu.make_async_copy(src.at[1], dst, in_sems.at[i]) for i, (src, dst) in enumerate(pairs)]
    for copy in copies:
        copy.start()
    gain_ref, shift_ref = params_ref, params_ref.at[4:8]
    frames, half = keep_ref.shape[0], keep_ref.shape[1]
    part = lax.rem(lax.axis_index("sp"), GROUP_FRAMES // frames)
    slot_places(slots_ref, where_scr, frames)
    small_ref[...] = jnp.zeros_like(small_ref)
    both_scr[0:frames] = keep_ref[...]
    both_scr[frames:] = recv_ref[...]
    spread = lane_heads(BF16)
    steps = 4
    count = half // steps
    step_rows = count * GROUP_FRAMES
    for i in range(steps):
        span = slice(i * step_rows, (i + 1) * step_rows)
        place = slice(i * count, (i + 1) * count)
        x_low = jnp.concatenate([both_scr[where_scr[s], place] for s in range(GROUP_FRAMES)], axis=0)
        x_ref[span, :] = x_low
        x = x_low.astype(F32)
        h2 = norm(x, gain_ref[2:3, :], shift_ref[2:3, :])[0].astype(BF16)
        h2_ref[span, :] = h2
        if i == 0:
            copies[0].wait()
        q, k, v = qkv_rows(h2, wqkv_ref)
        qkv_ref[span, 0:TILE] = q
        qkv_ref[span, TILE : 2 * TILE] = k
        qkv_ref[span, 2 * TILE :] = v
        qs, ks, vs = split_slots(q), split_slots(k), split_slots(v)
        probs = time_probs(time_scores(qs, ks, spread), count)
        wide = dot_nt(jnp.concatenate([p.astype(BF16) for p in probs], axis=0), spread)
        mixed = []
        at = 0
        for t in range(VIDEO_STEPS):
            total = None
            for s in range(t + 1):
                piece = wide[at * count : (at + 1) * count] * vs[s]
                total = piece if total is None else total + piece
                at += 1
            mixed.append(total)
        mixed.extend(vs[VIDEO_STEPS:])
        o = jnp.concatenate([m.astype(BF16) for m in mixed], axis=0)
        o_ref[span, :] = o
        if i == 0:
            copies[1].wait()
        xb = x + dot(o, wout_ref[...]).astype(BF16).astype(F32)
        h3, unit, inv = norm(xb, gain_ref[3:4, :], shift_ref[3:4, :])
        h3 = h3.astype(BF16)
        h3_ref[span, :] = h3
        slope = slope_scr.at[i % 2]
        if i == 0:
            copies[2].wait()
            copies[3].wait()
        branch = mlp_forward(h3, wup_ref, params_ref.at[12:16], wdown_ref, span, act_ref, SpanView(slope))
        out = (xb + branch + params_ref[17:18, :]).astype(BF16)
        for s in range(GROUP_FRAMES):
            both_scr[where_scr[s], place] = out[s * count : (s + 1) * count]
        grad_low = jnp.concatenate(
            [cot_slot(cot_ref, cotr_ref, where_scr[s], part * half + i * count, count) for s in range(GROUP_FRAMES)],
            axis=0,
        )
        gr_ref[span, :] = grad_low
        grad = grad_low.astype(F32)
        dh, sums = mlp_backward(grad_low, wup_ref, wdown_ref, span, SpanView(slope), du_ref)
        add_small(small_ref, [column_sum(dh * unit), column_sum(dh), column_sum(grad), None] + sums, False)
        dxb_ref[span, :] = grad + norm_back(dh, unit, inv, gain_ref[3:4, :])
    own_ref[...] = both_scr[0:frames]
    send_ref[...] = both_scr[frames:]


class SpanView:
    def __init__(self, ref):
        self.ref = ref

    def __getitem__(self, index):
        return self.ref[:, index[1]]

    def __setitem__(self, index, value):
        self.ref[:, index[1]] = value


def cot_slot(cot_ref, cotr_ref, frame, start, count):
    frames = cot_ref.shape[0]
    places = pl.ds(pl.multiple_of(start, count), count)
    mine = cot_ref[lax.rem(frame, frames), places, :]
    other = cotr_ref[lax.rem(frame, frames), places, :]
    return jnp.where(frame < frames, mine, other)


def time_backward_kernel(
    slots_ref, x_ref, qkv_ref, dxb_ref, params_ref, wqkv_ref, wout_ref,
    own_ref, send_ref, ar_ref, dqkv_ref, small_ref,
    where_scr, both_scr,
):
    frames, half = own_ref.shape[0], own_ref.shape[1]
    slot_places(slots_ref, where_scr, frames)
    small_ref[...] = jnp.zeros_like(small_ref)
    spread = lane_heads(BF16)
    steps = 4
    count = half // steps
    step_rows = count * GROUP_FRAMES
    gain = params_ref[2:3, :]
    for i in range(steps):
        span = slice(i * step_rows, (i + 1) * step_rows)
        place = slice(i * count, (i + 1) * count)
        dxb = dxb_ref[span, :]
        ar = dxb.astype(BF16)
        ar_ref[span, :] = ar
        do = split_slots(dot_nt(ar, wout_ref[...]).astype(BF16))
        qs = split_slots(qkv_ref[span, 0:TILE])
        ks = split_slots(qkv_ref[span, TILE : 2 * TILE])
        vs = split_slots(qkv_ref[span, 2 * TILE :])
        probs = time_probs(time_scores(qs, ks, spread), count)
        dps = time_scores(do, vs, spread)
        dps = [dps[j * count : (j + 1) * count] for j in range(len(PAIRS))]
        dss = []
        at = 0
        for t in range(VIDEO_STEPS):
            centre = functools.reduce(
                lambda a, b: a + b, [probs[at + s] * dps[at + s] for s in range(t + 1)]
            )
            dss.extend([probs[at + s] * (dps[at + s] - centre) for s in range(t + 1)])
            at += t + 1
        wide_p = dot_nt(jnp.concatenate([p.astype(BF16) for p in probs], axis=0), spread)
        wide_ds = dot_nt(jnp.concatenate([d.astype(BF16) for d in dss], axis=0), spread)
        dq = [None] * GROUP_FRAMES
        dk = [None] * GROUP_FRAMES
        dv = [None] * GROUP_FRAMES

        def add(table, index, piece):
            table[index] = piece if table[index] is None else table[index] + piece

        for j, (t, s) in enumerate(PAIRS):
            rows = slice(j * count, (j + 1) * count)
            add(dq, t, wide_ds[rows] * ks[s])
            add(dk, s, wide_ds[rows] * qs[t])
            add(dv, s, wide_p[rows] * do[t])
        for t in range(VIDEO_STEPS, GROUP_FRAMES):
            dq[t] = jnp.zeros_like(do[t])
            dk[t] = jnp.zeros_like(do[t])
            dv[t] = do[t]
        dq = jnp.concatenate([(d * SCALE).astype(BF16) for d in dq], axis=0)
        dk = jnp.concatenate([d.astype(BF16) for d in dk], axis=0)
        dv = jnp.concatenate([d.astype(BF16) for d in dv], axis=0)
        dqkv_ref[span, 0:TILE] = dq
        dqkv_ref[span, TILE : 2 * TILE] = dk
        dqkv_ref[span, 2 * TILE :] = dv
        dh = dot_nt(dqkv_ref[span, :], wqkv_ref[...])
        unit, inv = norm(x_ref[span, :].astype(F32), gain, params_ref[6:7, :])[1:]
        add_small(small_ref, [column_sum(dh * unit), column_sum(dh)], False)
        dxp = norm_back(dh, unit, inv, gain).astype(BF16).astype(F32)
        dx1 = (dxb + dxp).astype(BF16)
        for s in range(GROUP_FRAMES):
            both_scr[where_scr[s], place] = dx1[s * count : (s + 1) * count]
    own_ref[...] = both_scr[0:frames]
    send_ref[...] = both_scr[frames:]


def space_mlp_back_kernel(
    own_ref, recv_ref, xa_ref, slope_ref, params_ref, wup_ref, wdown_ref,
    gr_ref, du_ref, dxa_ref, ar_ref, small_ref,
):
    part = lax.rem(lax.axis_index("sp"), 2)
    small_ref[...] = jnp.zeros_like(small_ref)
    frames, half = own_ref.shape[0], own_ref.shape[1]
    rows = 2 * half
    gain = params_ref[1:2, :]
    for f in range(frames):
        span = slice(f * rows, (f + 1) * rows)
        base = f * rows
        gr_ref[pl.ds(pl.multiple_of(base + part * half, half), half), :] = own_ref[f]
        gr_ref[pl.ds(pl.multiple_of(base + (1 - part) * half, half), half), :] = recv_ref[f]
        grad_low = gr_ref[span, :]
        grad = grad_low.astype(F32)
        dh, sums = mlp_backward(grad_low, wup_ref.at[0], wdown_ref.at[0], span, slope_ref, du_ref)
        unit, inv = norm(xa_ref[span, :], gain, params_ref[5:6, :])[1:]
        add_small(small_ref, [column_sum(dh * unit), column_sum(dh), column_sum(grad), None] + sums, False)
        dxa = grad + norm_back(dh, unit, inv, gain)
        dxa_ref[span, :] = dxa
        ar_ref[span, :] = dxa.astype(BF16)


def head_picker():
    h = lax.broadcasted_iota(jnp.int32, (HEADS, TILE), 0)
    c = lax.broadcasted_iota(jnp.int32, (HEADS, TILE), 1)
    return (c // HEAD == h).astype(BF16)


def attn_back_frame(f, to, ar_ref, qkv_ref, lse_ref, o_ref, wout_ref, pick, dqkv_ref):
    rows = lse_ref.shape[2]
    span = slice(f * rows, (f + 1) * rows)
    dest = slice(to * rows, (to + 1) * rows)
    do = dot_nt(ar_ref[span, :], wout_ref[0]).astype(BF16)
    both = do.astype(F32) * o_ref[span, :].astype(F32)
    high = both.astype(BF16)
    rest = (both - high.astype(F32)).astype(BF16)
    centre = dot_nt(pick, high) + dot_nt(pick, rest)
    for pair in range(HEADS // 2):
        qp = qkv_ref[span, pair * 128 : (pair + 1) * 128]
        kp = qkv_ref[span, TILE + pair * 128 : TILE + (pair + 1) * 128]
        vp = qkv_ref[span, 2 * TILE + pair * 128 : 2 * TILE + (pair + 1) * 128]
        dop = do[:, pair * 128 : (pair + 1) * 128]
        zero = jnp.zeros_like(kp)
        mask = head_mask(kp, 0)
        st = dot_nt(jnp.concatenate([jnp.where(mask, kp, zero), jnp.where(mask, zero, kp)], axis=0), qp)
        dpt = dot_nt(jnp.concatenate([jnp.where(mask, vp, zero), jnp.where(mask, zero, vp)], axis=0), dop)
        pts, dsts, dqs = [], [], []
        for e in range(2):
            row = slice(2 * pair + e, 2 * pair + e + 1)
            keys = slice(e * rows, (e + 1) * rows)
            pt = jnp.exp(st[keys] - lse_ref[f, row, :])
            dst = (pt * (dpt[keys] - centre[row, :])).astype(BF16)
            pts.append(pt.astype(BF16))
            dsts.append(dst)
            dqs.append(dot_tn(dst, kp) * SCALE)
        dk = dot(jnp.concatenate(dsts, axis=0), qp)
        dv = dot(jnp.concatenate(pts, axis=0), dop)
        values = (
            jnp.where(mask, dqs[0], dqs[1]),
            jnp.where(mask, dk[:rows], dk[rows:]),
            jnp.where(mask, dv[:rows], dv[rows:]),
        )
        for index, value in enumerate(values):
            at = index * TILE + pair * 128
            dqkv_ref[dest, at : at + 128] = value.astype(BF16)


def space_attn_back_kernel(ar_ref, qkv_ref, lse_ref, o_ref, wout_ref, dqkv_ref):
    pick = head_picker()
    for f in range(lse_ref.shape[0] // 2):
        attn_back_frame(f, f, ar_ref, qkv_ref, lse_ref, o_ref, wout_ref, pick, dqkv_ref)


def finish_kernel(
    order, ar_ref, qkv_ref, lse_ref, o_ref, wout_ref, first_ref, tok_ref, dxa_ref, own_ref, recv_ref,
    params_ref, wqkv_ref, h_ref, small1_ref, small2_ref, small3_ref,
    gtok_ref, out_ref, keep_ref, send_ref, dqkv_scr,
):
    sp = lax.axis_index("sp")
    part = lax.rem(sp, 2)
    frames, half = own_ref.shape[0], own_ref.shape[1]
    rows = 2 * half
    pick = head_picker()
    for f in range(frames // 2, frames):
        attn_back_frame(f, f - frames // 2, ar_ref, qkv_ref, lse_ref, o_ref, wout_ref, pick, dqkv_scr)
    gain = params_ref[0:1, :]
    sums = []
    for f in range(frames):
        span = slice(f * rows, (f + 1) * rows)
        out_ref[f, half_rows(part, half), :] = own_ref[f]
        out_ref[f, half_rows(1 - part, half), :] = recv_ref[f]
        source = first_ref if f < frames // 2 else dqkv_scr
        at = (f % (frames // 2)) * rows
        dh = dot_nt(source[at : at + rows, :], wqkv_ref[0])
        unit, inv = norm(tok_ref[f].astype(F32), gain, params_ref[4:5, :])[1:]
        sums.append((column_sum(dh * unit), column_sum(dh)))
        gtok_ref[f] = (dxa_ref[span, :] + norm_back(dh, unit, inv, gain)).astype(BF16)
    size = h_ref.shape[1] // lax.axis_size("sp")
    slots = lax.axis_size("sp") // 2
    turned = jnp.transpose(h_ref[...])
    middle = first_ref.shape[0]
    zero = jnp.int32(0)
    for j in range(3):
        cols = slice(j * TILE, (j + 1) * TILE)
        result = dot(turned[:, :middle], first_ref[:, cols]) + dot(turned[:, middle:], dqkv_scr[:, cols])
        put_blocks(result, zero, size, Place(0, 3 * size, j * size), order, keep_ref, send_ref)
    row = lax.broadcasted_iota(jnp.int32, (8, TILE), 0)
    total = [functools.reduce(lambda a, b: a + b, [x[i] for x in sums]) for i in range(2)]
    small0 = jnp.where(row == 0, total[0], jnp.where(row == 1, total[1], 0.0))
    small = jnp.concatenate([small0, small1_ref[...], small2_ref[...], small3_ref[...]], axis=0).astype(BF16)
    base = slots * 3 * size
    keep_ref[base:, :] = small
    send_ref[base:, :] = small


def place_of(block, order, sp):
    bits = len(order)
    mixed = jnp.bitwise_xor(block, sp)
    slot = jnp.int32(0)
    for i, b in enumerate(order):
        bit = jnp.bitwise_and(lax.shift_right_logical(mixed, jnp.int32(b)), 1)
        slot = slot + lax.shift_left(bit, jnp.int32(bits - 1 - i))
    return slot


class Place:
    def __init__(self, base, rows, at):
        self.base, self.rows, self.at = base, rows, at


def put_blocks(result, first, size, place, order, keep_ref, send_ref):
    sp = lax.axis_index("sp")
    part = lax.rem(sp, 2)
    low = result.astype(BF16)
    for j in range(result.shape[0] // (2 * size)):
        even = low[2 * j * size : (2 * j + 1) * size]
        odd = low[(2 * j + 1) * size : (2 * j + 2) * size]
        slot = place_of(first + 2 * j, order[1:], sp)
        rows = pl.ds(pl.multiple_of(place.base + slot * place.rows + place.at, 16), size)
        keep_ref[rows, :] = jnp.where(part == 0, even, odd)
        send_ref[rows, :] = jnp.where(part == 0, odd, even)


def mlp_weights_kernel(orders, *refs):
    h_ref, du_ref, act_ref, gr_ref = refs[:4]
    extra = refs[4:-2]
    keep_ref, send_ref = refs[-2:]
    sp_size = lax.axis_size("sp")
    slots = sp_size // 2
    up_size = h_ref.shape[1] // sp_size
    chunks = du_ref.shape[1] // TILE
    down_size = chunks * TILE // sp_size
    rows_a = chunks * up_size
    rows_b = down_size + (up_size if extra else 0)
    base = slots * rows_a
    zero = jnp.int32(0)
    turned = jnp.transpose(h_ref[...])
    for j in range(chunks):
        cols = slice(j * TILE, (j + 1) * TILE)
        up = dot(turned, du_ref[:, cols])
        put_blocks(up, zero, up_size, Place(0, rows_a, j * up_size), orders[0], keep_ref, send_ref)
        down = dot_tn(act_ref[:, cols], gr_ref[...])
        first = jnp.int32(j * (TILE // down_size))
        put_blocks(down, first, down_size, Place(base, rows_b, 0), orders[1], keep_ref, send_ref)
    if extra:
        out = dot_tn(extra[0][...], extra[1][...])
        put_blocks(out, zero, up_size, Place(base, rows_b, down_size), orders[1], keep_ref, send_ref)


def attn_weights_kernel(order, h_ref, dqkv_ref, o_ref, ar_ref, keep_ref, send_ref):
    size = h_ref.shape[1] // lax.axis_size("sp")
    zero = jnp.int32(0)
    turned = jnp.transpose(h_ref[...])
    for j in range(3):
        cols = slice(j * TILE, (j + 1) * TILE)
        result = dot(turned, dqkv_ref[:, cols])
        put_blocks(result, zero, size, Place(0, 4 * size, j * size), order, keep_ref, send_ref)
    result = dot_tn(o_ref[...], ar_ref[...])
    put_blocks(result, zero, size, Place(0, 4 * size, 3 * size), order, keep_ref, send_ref)


def fold_kernel(moves, count, summed, *refs):
    outs = refs[2 * count :]
    for source, at, rows, out, to, whole in moves:
        keep, recv = refs[2 * source], refs[2 * source + 1]
        if summed:
            outs[out][to : to + rows, :] = keep[at : at + rows, :] + recv[at : at + rows, :]
        elif whole:
            total = keep[at : at + rows, :] + recv[at : at + rows, :]
            outs[2 * out][to : to + rows, :] = total
            outs[2 * out + 1][to : to + rows, :] = total
        else:
            half = rows // 2
            for part in range(2):
                span = slice(at + part * half, at + (part + 1) * half)
                outs[2 * out + part][to : to + half, :] = keep[span, :] + recv[span, :]


class Group:
    def __init__(self, sizes, segments, split):
        grp_size, sp_size = sizes
        self.segments = segments
        names = tuple(segments)
        bits = sp_size.bit_length() - 1
        self.stages = [[("sp", sp_size, 0, names)]]
        for b in range(1, bits):
            if split and b < 3:
                self.stages.append([("sp", sp_size, b, names[:1]), ("sp", sp_size, 3 - b, names[1:])])
            else:
                self.stages.append([("sp", sp_size, b, names)])
        for b in range(grp_size.bit_length() - 1):
            self.stages.append([("grp", grp_size, b, names)])
        self.scatters = bits
        self.slots = sp_size // 2
        self.stage = 0

    def rows(self, name, slots):
        height, whole = self.segments[name]
        return height if whole else height * slots

    def start(self, sends):
        self.sends = sends
        self.recvs = [
            swap(send, axis, size, bit) for send, (axis, size, bit, names) in zip(sends, self.stages[self.stage])
        ]

    def begin(self, keep, send):
        self.keeps = [keep]
        self.start([send])

    def fold(self):
        now, later = self.stages[self.stage], self.stages[self.stage + 1]
        summed = self.slots == 1
        after = self.slots if summed else self.slots // 2
        where = {}
        shapes = []
        for out, entry in enumerate(later):
            at = 0
            for name in entry[3]:
                where[name] = (out, at)
                at += self.rows(name, after)
            shapes += [sds((at, TILE), BF16)] * (1 if summed else 2)
        moves = []
        for source, entry in enumerate(now):
            at = 0
            for name in entry[3]:
                rows = self.rows(name, self.slots)
                moves.append((source, at, rows) + where[name] + (self.segments[name][1],))
                at += rows
        args = [x for pair in zip(self.keeps, self.recvs) for x in pair]
        out = call(functools.partial(fold_kernel, moves, len(now), summed), args, shapes, 0.5, limit=4)
        self.keeps = out if summed else out[0::2]
        self.sends = out if summed else out[1::2]
        self.slots = after
        self.stage += 1

    def left(self):
        return len(self.stages) - 1 - self.stage

    def pair(self):
        return self.keeps[0], self.recvs[0]


def result_kernel(sp_size, *refs):
    mlp1, attn1, mlp0, qkv0 = [(refs[2 * i], refs[2 * i + 1]) for i in range(4)]
    outs = refs[8:16]
    gain_scr, shift_scr, qkv_scr, out_scr, up_scr, bup_scr, down_scr, bdown_scr, small_scr, sems = refs[16:]
    size = TILE // sp_size
    chunks = up_scr.shape[2] // TILE
    down_size = chunks * size

    def total(pair, at, rows):
        return pair[0][at : at + rows, :].astype(F32) + pair[1][at : at + rows, :].astype(F32)

    for layer, (qkv, mlp) in enumerate(((qkv0, mlp0), (attn1, mlp1))):
        for j in range(3):
            qkv_scr[layer, :, j * TILE : (j + 1) * TILE] = total(qkv, j * size, size)
        for j in range(chunks):
            up_scr[layer, :, j * TILE : (j + 1) * TILE] = total(mlp, j * size, size)
        down_scr[layer] = total(mlp, chunks * size, down_size)
    out_scr[0] = total(mlp0, chunks * size + down_size, size)
    out_scr[1] = total(attn1, 3 * size, size)
    small_scr[...] = total(qkv0, 3 * size, 32)
    sp = lax.axis_index("sp")
    back = lax.rem(TILE - sp * size, TILE)
    turned = pltpu.roll(small_scr[...], back, 1)
    for i in range(4):
        gain_scr[i : i + 1, :] = turned[8 * i : 8 * i + 1, :size]
        shift_scr[i : i + 1, :] = turned[8 * i + 1 : 8 * i + 2, :size]
    start = sp * down_size
    line = start // TILE
    back = lax.rem(TILE - lax.rem(start, TILE), TILE)
    for layer in range(2):
        first = 8 + 16 * layer
        bdown_scr[layer : layer + 1, :] = turned[first + 2 : first + 3, :size]
        rows = small_scr[first : first + 8, :]
        lines = lax.broadcasted_iota(jnp.int32, rows.shape, 0)
        picked = jnp.sum(jnp.where(lines == 4 + line, rows, 0.0), axis=0, keepdims=True)
        picked = pltpu.roll(jnp.broadcast_to(picked, rows.shape), back, 1)
        bup_scr[layer : layer + 1, :] = picked[0:1, :down_size]
    scrs = (gain_scr, shift_scr, qkv_scr, out_scr, up_scr, bup_scr, down_scr, bdown_scr)
    copies = [pltpu.make_async_copy(scr, out, sems.at[i]) for i, (scr, out) in enumerate(zip(scrs, outs))]
    for copy in copies:
        copy.start()
    for copy in copies:
        copy.wait()


VMEM = pl.BlockSpec(memory_space=pltpu.VMEM)
SMEM = pl.BlockSpec(memory_space=pltpu.SMEM)
HBM = pl.BlockSpec(memory_space=pltpu.HBM)


def sds(shape, dtype):
    return jax.ShapeDtypeStruct(shape, dtype)


def call(kernel, args, outs, micros, scratch=(), specs=None, out_specs=None, limit=12):
    return pl.pallas_call(
        kernel,
        in_specs=[VMEM] * len(args) if specs is None else specs,
        out_specs=[VMEM] * len(outs) if out_specs is None else out_specs,
        out_shape=outs,
        scratch_shapes=list(scratch),
        compiler_params=pltpu.CompilerParams(vmem_limit_bytes=limit * MIB),
        cost_estimate=pl.CostEstimate(flops=int(micros * 1.15e9), bytes_accessed=0, transcendentals=0),
    )(*args)


def swap(array, axis, size, bit):
    return lax.ppermute(array, axis, [(i, i ^ (1 << bit)) for i in range(size)])


def shards(sizes, tokens, frame_slot, norm_gain, norm_shift, w_qkv, w_out, w_up, b_up, w_down, b_down, cotangent):
    grp_size, sp_size = sizes
    frames, patches, width = tokens.shape
    hidden = w_up.shape[2]
    assert GROUP_FRAMES == 2 * frames and sp_size >= 8
    half = patches // 2
    rows = frames * patches
    sp_bits = sp_size.bit_length() - 1
    core_swap = functools.partial(swap, axis="sp", size=sp_size, bit=0)
    slots = sp_size // 2
    size = width // sp_size
    down_size = hidden // sp_size
    order_a = list(range(sp_bits))
    order_b = [0, 2, 1] + list(range(3, sp_bits))

    def row_out(cols, dtype=BF16):
        return sds((rows, cols), dtype)

    half_out = sds((frames, half, width), BF16)
    small_out = sds((8, TILE), F32)
    fence = lambda *arrays: lax.optimization_barrier(arrays)

    token = []

    def meet(groups, *arrays):
        recvs = [r for g in groups for r in g.recvs]
        out = list(fence(*arrays, *recvs, *token))
        count = len(arrays)
        arrays, recvs = out[:count], out[count:]
        for g in groups:
            g.recvs = [recvs.pop(0) for _ in g.recvs]
            g.fold()
        sends = [x for g in groups for x in g.sends]
        out = list(fence(*arrays, *sends))
        arrays, sends = out[:count], out[count:]
        for g in groups:
            g.start([sends.pop(0) for _ in g.sends])
        token[:] = [groups[-1].sends[-1]] if groups else []
        return arrays

    def buffers(height, tail=0):
        return [sds((slots * height + tail, TILE), BF16)] * 2

    cot_recv = core_swap(cotangent)
    packed = jnp.concatenate(
        [norm_gain, norm_shift, b_up.reshape(2 * hidden // width, width), b_down], axis=0
    )
    weights = (w_qkv, w_out, w_up, w_down)
    shapes = [sds(w.shape[1:], BF16) for w in weights]
    out = call(
        space_forward_kernel,
        (tokens, packed) + weights,
        [
            half_out, half_out, row_out(width), row_out(3 * width), sds((frames, HEADS, patches), F32),
            row_out(width), row_out(width, F32), row_out(width), row_out(hidden), row_out(hidden),
        ],
        16,
        scratch=[pltpu.VMEM(tokens.shape, BF16)]
        + [pltpu.VMEM(x.shape, BF16) for x in shapes]
        + [
            pltpu.VMEM((2, patches, width), BF16), pltpu.VMEM((2, patches, 3 * width), BF16),
            pltpu.VMEM((2, patches, width), BF16), pltpu.VMEM((2, patches, width), F32),
            pltpu.VMEM((2, patches, width), BF16),
            pltpu.VMEM((2, patches, hidden), BF16), pltpu.VMEM((2, patches, hidden), BF16),
            pltpu.VMEM((patches, width), F32), pltpu.SemaphoreType.DMA((5,)),
            pltpu.SemaphoreType.DMA((7 * frames,)),
        ],
        specs=[HBM, VMEM] + [HBM] * 4,
        out_specs=[VMEM, VMEM, HBM, HBM, VMEM] + [HBM] * 5,
        limit=LIMIT1,
    )
    (x_keep, x_send, h0, qkv0, lse0, o0, xa, h1, act0, slope0) = out
    x_recv = core_swap(x_send)

    place_scratch = [
        pltpu.SMEM((GROUP_FRAMES,), jnp.int32),
        pltpu.VMEM((GROUP_FRAMES, half, width), BF16),
    ]
    (out_own, out_send, xt, h2, qkv1, o1, h3, act1, du1, gr1, dxb, small3, w_qkv1, w_out1) = call(
        time_forward_kernel,
        (frame_slot, x_keep, x_recv, cotangent, cot_recv, packed) + weights,
        [
            half_out, half_out, row_out(width), row_out(width), row_out(3 * width), row_out(width),
            row_out(width), row_out(hidden), row_out(hidden), row_out(width), row_out(width, F32),
            small_out,
        ] + shapes[:2],
        24,
        scratch=place_scratch
        + [pltpu.VMEM((2, rows // 4, hidden), BF16)]
        + [pltpu.VMEM(x.shape, BF16) for x in shapes[2:]]
        + [pltpu.SemaphoreType.DMA((4,))],
        specs=[SMEM] + [VMEM] * 5 + [HBM] * 4,
        limit=LIMIT2,
    )
    out_recv = core_swap(out_send)

    def mlp_group(h, du, act, gr, *extra):
        height_b = down_size + (size if extra else 0)
        group = Group(sizes, {"up": (4 * size, False), "down": (height_b, False)}, True)
        return group, call(
            functools.partial(mlp_weights_kernel, (order_a, order_b)), (h, du, act, gr) + extra,
            buffers(4 * size + height_b), 4.5,
        )

    mlp1, out = mlp_group(h3, du1, act1, gr1)
    keep, send, dxb = fence(*out, dxb)
    mlp1.begin(keep, send)

    (dx_own, dx_send, ar1, dqkv1, small2) = call(
        time_backward_kernel,
        (frame_slot, xt, qkv1, dxb, packed, w_qkv1, w_out1),
        [half_out, half_out, row_out(width), row_out(3 * width), small_out],
        8,
        scratch=place_scratch,
        specs=[SMEM] + [VMEM] * 6,
    )
    dx_own, dx_send, dqkv1 = meet((mlp1,), dx_own, dx_send, dqkv1)
    dx_recv = core_swap(dx_send)
    attn1 = Group(sizes, {"attn": (4 * size, False)}, False)
    out = call(
        functools.partial(attn_weights_kernel, order_a), (h2, dqkv1, o1, ar1), buffers(4 * size), 2.4
    )
    keep, send, dx_recv = fence(*out, dx_recv)
    attn1.begin(keep, send)

    (gr0, du0, dxa, ar0, small1) = call(
        space_mlp_back_kernel,
        (dx_own, dx_recv, xa, slope0, packed, w_up, w_down),
        [row_out(width), row_out(hidden), row_out(width, F32), row_out(width), small_out],
        6,
    )
    gr0, du0, ar0 = meet((attn1,), gr0, du0, ar0)
    mlp0, out = mlp_group(h1, du0, act0, gr0, o0, ar0)
    keep, send, ar0 = meet((mlp1,), *out, ar0)
    mlp0.begin(keep, send)

    half_spec = [sds((rows // 2, 3 * width), BF16)]
    (dqkv0,) = call(space_attn_back_kernel, (ar0, qkv0, lse0, o0, w_out), half_spec, 5)
    (dqkv0,) = meet((mlp0, attn1), dqkv0)
    qkv = Group(sizes, {"qkv": (3 * size, False), "small": (32, True)}, False)
    grad_tokens, output, keep, send = call(
        functools.partial(finish_kernel, order_a),
        (
            ar0, qkv0, lse0, o0, w_out, dqkv0, tokens, dxa, out_own, out_recv, packed,
            w_qkv, h0, small1, small2, small3,
        ),
        [sds(tokens.shape, BF16), sds(tokens.shape, BF16)] + buffers(3 * size, 32),
        10,
        scratch=[pltpu.VMEM((rows // 2, 3 * width), BF16)],
    )
    keep, send = fence(keep, send)
    qkv.begin(keep, send)
    token[:] = [send]
    for groups in ((mlp1,), (qkv,), (mlp0,), (attn1,), (qkv,), (mlp0,), (mlp1,), (attn1,), (qkv,), (mlp0,)):
        groups = [g for g in groups if g.left()]
        if groups:
            meet(groups)
    for group in (mlp1, attn1, qkv, mlp0):
        while group.left():
            meet((group,))
    pairs = [x for g in (mlp1, attn1, mlp0, qkv) for x in g.pair()]
    finals = [
        sds((4, size), F32), sds((4, size), F32), sds((2, size, 3 * width), F32), sds((2, size, width), F32),
        sds((2, size, hidden), F32), sds((2, down_size), F32), sds((2, down_size, width), F32),
        sds((2, size), F32),
    ]
    results = call(
        functools.partial(result_kernel, sp_size), pairs, finals, 2,
        scratch=[pltpu.VMEM(f.shape, F32) for f in finals]
        + [pltpu.VMEM((32, TILE), F32), pltpu.SemaphoreType.DMA((8,))],
        out_specs=[HBM] * 8,
    )
    return (output, grad_tokens, *results)


def solution(mesh):
    rows = P(("grp", "sp"), None, None)
    in_specs = (rows, P("grp", None), P(), P(), P(), P(), P(), P(), P(), P(), rows)
    out_specs = (
        rows, rows, P(None, "sp"), P(None, "sp"), P(None, "sp", None), P(None, "sp", None),
        P(None, "sp", None), P(None, "sp"), P(None, "sp", None), P(None, "sp"),
    )
    body = functools.partial(shards, (mesh.shape["grp"], mesh.shape["sp"]))
    return jax.shard_map(body, mesh=mesh, in_specs=in_specs, out_specs=out_specs, check_vma=False)
```

```python
import functools

import jax
import jax.numpy as jnp
from jax import lax
from jax.experimental import pallas as pl
from jax.experimental.pallas import tpu as pltpu
from jax.sharding import PartitionSpec as P

HEADS = 8
HEAD = 64
VIDEO_STEPS = 6
GROUP_FRAMES = 8
NORM_EPS = 1e-05
TILE = 512
SCALE = HEAD**-0.5
TANH_A = 0.7978845608028654
TANH_B = TANH_A * 0.044715
PAIRS = [(t, s) for t in range(VIDEO_STEPS) for s in range(t + 1)]
F32 = jnp.float32
BF16 = jnp.bfloat16
MIB = 1024 * 1024
ROWS = -1
COST = 1.15e9 * 0.02
TAIL = ("qm", "bu", "qm", "bu", "q", "bu", "q", "bu", "q")
LIMIT1 = 52
LIMIT2 = 24


def dot(left, right):
    return jnp.dot(left, right, preferred_element_type=F32)


def dot_nt(left, right):
    return lax.dot_general(left, right, (((1,), (1,)), ((), ())), preferred_element_type=F32)


def dot_tn(left, right):
    return lax.dot_general(left, right, (((0,), (0,)), ((), ())), preferred_element_type=F32)


def norm(rows, gain, shift):
    centred = rows - jnp.mean(rows, axis=-1, keepdims=True)
    inv = lax.rsqrt(jnp.mean(centred * centred, axis=-1, keepdims=True) + NORM_EPS)
    unit = centred * inv
    return unit * gain + shift, unit, inv


def norm_back(grad, unit, inv, gain):
    grad_unit = grad * gain
    mean_grad = jnp.mean(grad_unit, axis=-1, keepdims=True)
    mean_both = jnp.mean(grad_unit * unit, axis=-1, keepdims=True)
    return inv * (grad_unit - mean_grad - unit * mean_both)


def column_sum(rows):
    return jnp.sum(rows, axis=0, keepdims=True)


def gelu_pair(u):
    square = u * u
    sigma = 0.5 + 0.5 * jnp.tanh(u * (TANH_A + TANH_B * square))
    act = u * sigma
    slope = sigma + act * (1.0 - sigma) * (2.0 * TANH_A + 6.0 * TANH_B * square)
    return act.astype(BF16), slope.astype(BF16)


def head_mask(lanes, which):
    lane = lax.broadcasted_iota(jnp.int32, lanes.shape, 1)
    return (lane < HEAD) if which == 0 else (lane >= HEAD)


def qkv_rows(normed, weight):
    out = []
    for part in range(3):
        piece = dot(normed, weight[:, part * TILE : (part + 1) * TILE])
        if part == 0:
            out.append(piece.astype(BF16) * BF16(SCALE))
        else:
            out.append(piece.astype(BF16))
    return out


def mlp_forward(normed, w_up, b_up, w_down, rows, act_ref, slope_ref):
    chunks = w_up.shape[1] // TILE
    up = lambda j: dot(normed, w_up[:, j * TILE : (j + 1) * TILE])
    total = None
    u = up(0)
    for j in range(chunks):
        cols = slice(j * TILE, (j + 1) * TILE)
        later = up(j + 1) if j + 1 < chunks else None
        act, slope = gelu_pair(u + b_up[j : j + 1, :])
        act_ref[rows, cols] = act
        slope_ref[rows, cols] = slope
        piece = dot(act, w_down[cols, :])
        total = piece if total is None else total + piece
        u = later
    return total


def mlp_backward(grad_low, w_up, w_down, rows, slope_ref, du_ref):
    chunks = w_up.shape[1] // TILE
    down = lambda j: dot_nt(grad_low, w_down[j * TILE : (j + 1) * TILE, :])
    total = None
    sums = []
    da = down(0)
    for j in range(chunks):
        cols = slice(j * TILE, (j + 1) * TILE)
        later = down(j + 1) if j + 1 < chunks else None
        du = (da * slope_ref[rows, cols].astype(F32)).astype(BF16)
        du_ref[rows, cols] = du
        sums.append(column_sum(du.astype(F32)))
        piece = dot_nt(du, w_up[:, cols])
        total = piece if total is None else total + piece
        da = later
    return total, sums


def add_small(small_ref, values, first):
    for i, value in enumerate(values):
        row = slice(i, i + 1) if i < 4 else slice(i, i + 1)
        if value is None:
            continue
        if first:
            small_ref[row, :] = value
        else:
            small_ref[row, :] += value


def half_rows(part, half):
    return pl.ds(pl.multiple_of(part * half, half), half)


def space_forward_kernel(
    tok_hbm, params_ref, wqkv_hbm, wout_hbm, wup_hbm, wdown_hbm,
    keep_ref, send_ref, h0_hbm, qkv_hbm, lse_ref, o_hbm, xa_hbm, h1_hbm, act_hbm, slope_hbm,
    tok_ref, wqkv_ref, wout_ref, wup_ref, wdown_ref, h0_scr, qkv_scr, o_scr, xa_scr, h1_scr, act_scr,
    slope_scr, x1_scr, in_sems, out_sems,
):
    pairs = [
        (tok_hbm, tok_ref), (wqkv_hbm.at[0], wqkv_ref), (wout_hbm.at[0], wout_ref),
        (wup_hbm.at[0], wup_ref), (wdown_hbm.at[0], wdown_ref),
    ]
    copies = [pltpu.make_async_copy(src, dst, in_sems.at[i]) for i, (src, dst) in enumerate(pairs)]
    for copy in copies:
        copy.start()
    gain_ref, shift_ref = params_ref, params_ref.at[4:8]
    part = lax.rem(lax.axis_index("sp"), 2)
    frames, rows = tok_ref.shape[0], tok_ref.shape[1]
    half = rows // 2
    lane = lax.broadcasted_iota(jnp.int32, (rows, 128), 1)
    spills = []
    copies[0].wait()
    for f in range(frames):
        span = slice(f * rows, (f + 1) * rows)
        x0 = tok_ref[f].astype(F32)
        h0 = norm(x0, gain_ref[0:1, :], shift_ref[0:1, :])[0].astype(BF16)
        if f == 0:
            copies[1].wait()
        now = f % 2
        places = (
            (h0_scr, h0_hbm), (qkv_scr, qkv_hbm), (o_scr, o_hbm), (xa_scr, xa_hbm), (h1_scr, h1_hbm),
            (act_scr, act_hbm), (slope_scr, slope_hbm),
        )
        spill = [
            pltpu.make_async_copy(scr.at[now], hbm.at[span], out_sems.at[7 * f + i])
            for i, (scr, hbm) in enumerate(places)
        ]
        if f >= 2:
            for copy in spills[f - 2]:
                copy.wait()
        spills.append(spill)
        h0_scr[now] = h0
        spill[0].start()
        q, k, v = qkv_rows(h0, wqkv_ref)
        qkv_scr[now, :, 0:TILE] = q
        qkv_scr[now, :, TILE : 2 * TILE] = k
        qkv_scr[now, :, 2 * TILE :] = v
        spill[1].start()
        lse_all = jnp.zeros((rows, 128), F32)
        mixed = []
        for pair in range(HEADS // 2):
            cols = slice(pair * 128, (pair + 1) * 128)
            qp, kp, vp = q[:, cols], k[:, cols], v[:, cols]
            zero = jnp.zeros_like(qp)
            mask = head_mask(qp, 0)
            s = dot_nt(jnp.concatenate([jnp.where(mask, qp, zero), jnp.where(mask, zero, qp)], axis=0), kp)
            top = jnp.max(s, axis=-1, keepdims=True)
            p = jnp.exp(s - top)
            total = jnp.sum(p, axis=-1, keepdims=True)
            both = dot(p.astype(BF16), vp) * (1.0 / total)
            lse = top + jnp.log(total)
            lse_all = jnp.where(lane == 2 * pair, lse[:rows], lse_all)
            lse_all = jnp.where(lane == 2 * pair + 1, lse[rows:], lse_all)
            mixed.append(jnp.where(mask, both[:rows], both[rows:]).astype(BF16))
        lse_ref[f] = jnp.transpose(lse_all)[0:HEADS, :]
        o = jnp.concatenate(mixed, axis=1)
        o_scr[now] = o
        spill[2].start()
        if f == 0:
            copies[2].wait()
        xa = x0 + dot(o, wout_ref[...])
        xa_scr[now] = xa
        spill[3].start()
        h1 = norm(xa, gain_ref[1:2, :], shift_ref[1:2, :])[0].astype(BF16)
        h1_scr[now] = h1
        spill[4].start()
        if f == 0:
            copies[3].wait()
            copies[4].wait()
        branch = mlp_forward(
            h1, wup_ref, params_ref.at[8:12], wdown_ref, slice(None), act_scr.at[now], slope_scr.at[now]
        )
        spill[5].start()
        spill[6].start()
        x1_scr[...] = xa + branch + params_ref[16:17, :]
        keep_ref[f] = x1_scr[half_rows(part, half), :].astype(BF16)
        send_ref[f] = x1_scr[half_rows(1 - part, half), :].astype(BF16)
    for copies_of in spills[-2:]:
        for copy in copies_of:
            copy.wait()


def lane_heads(dtype):
    c = lax.broadcasted_iota(jnp.int32, (TILE, 128), 0)
    h = lax.broadcasted_iota(jnp.int32, (TILE, 128), 1)
    return (c // HEAD == h).astype(dtype)


def slot_places(slots_ref, where_scr, frames):
    sp = lax.axis_index("sp")
    group = (sp * frames) // GROUP_FRAMES
    part = lax.rem(sp, GROUP_FRAMES // frames)
    for t in range(GROUP_FRAMES):
        where_scr[slots_ref[group, t]] = lax.rem(t + GROUP_FRAMES - part * frames, GROUP_FRAMES)


def time_scores(q, k, spread):
    parts = []
    for t, s in PAIRS:
        parts.append((q[t] * k[s]).astype(BF16))
    return dot(jnp.concatenate(parts, axis=0), spread)


def time_probs(scores, count):
    blocks = [scores[i * count : (i + 1) * count] for i in range(len(PAIRS))]
    probs = []
    at = 0
    for t in range(VIDEO_STEPS):
        mine = blocks[at : at + t + 1]
        at += t + 1
        top = functools.reduce(jnp.maximum, mine)
        raw = [jnp.exp(b - top) for b in mine]
        inv = 1.0 / functools.reduce(lambda a, b: a + b, raw)
        probs.extend([r * inv for r in raw])
    return probs


def split_slots(rows):
    count = rows.shape[0] // GROUP_FRAMES
    return [rows[s * count : (s + 1) * count].astype(F32) for s in range(GROUP_FRAMES)]


def time_forward_kernel(
    slots_ref, keep_ref, recv_ref, cot_ref, cotr_ref, params_ref,
    wqkv_hbm, wout_hbm, wup_hbm, wdown_hbm,
    own_ref, send_ref, x_ref, h2_ref, qkv_ref, o_ref, h3_ref, act_ref, du_ref, gr_ref, dxb_ref,
    small_ref, wqkv_ref, wout_ref,
    where_scr, both_scr, slope_scr, wup_ref, wdown_ref, in_sems,
):
    pairs = [(wqkv_hbm, wqkv_ref), (wout_hbm, wout_ref), (wup_hbm, wup_ref), (wdown_hbm, wdown_ref)]
    copies = [pltpu.make_async_copy(src.at[1], dst, in_sems.at[i]) for i, (src, dst) in enumerate(pairs)]
    for copy in copies:
        copy.start()
    gain_ref, shift_ref = params_ref, params_ref.at[4:8]
    frames, half = keep_ref.shape[0], keep_ref.shape[1]
    part = lax.rem(lax.axis_index("sp"), GROUP_FRAMES // frames)
    slot_places(slots_ref, where_scr, frames)
    small_ref[...] = jnp.zeros_like(small_ref)
    both_scr[0:frames] = keep_ref[...]
    both_scr[frames:] = recv_ref[...]
    spread = lane_heads(BF16)
    steps = 4
    count = half // steps
    step_rows = count * GROUP_FRAMES
    for i in range(steps):
        span = slice(i * step_rows, (i + 1) * step_rows)
        place = slice(i * count, (i + 1) * count)
        x_low = jnp.concatenate([both_scr[where_scr[s], place] for s in range(GROUP_FRAMES)], axis=0)
        x_ref[span, :] = x_low
        x = x_low.astype(F32)
        h2 = norm(x, gain_ref[2:3, :], shift_ref[2:3, :])[0].astype(BF16)
        h2_ref[span, :] = h2
        if i == 0:
            copies[0].wait()
        q, k, v = qkv_rows(h2, wqkv_ref)
        qkv_ref[span, 0:TILE] = q
        qkv_ref[span, TILE : 2 * TILE] = k
        qkv_ref[span, 2 * TILE :] = v
        qs, ks, vs = split_slots(q), split_slots(k), split_slots(v)
        probs = time_probs(time_scores(qs, ks, spread), count)
        wide = dot_nt(jnp.concatenate([p.astype(BF16) for p in probs], axis=0), spread)
        mixed = []
        at = 0
        for t in range(VIDEO_STEPS):
            total = None
            for s in range(t + 1):
                piece = wide[at * count : (at + 1) * count] * vs[s]
                total = piece if total is None else total + piece
                at += 1
            mixed.append(total)
        mixed.extend(vs[VIDEO_STEPS:])
        o = jnp.concatenate([m.astype(BF16) for m in mixed], axis=0)
        o_ref[span, :] = o
        if i == 0:
            copies[1].wait()
        xb = x + dot(o, wout_ref[...]).astype(BF16).astype(F32)
        h3, unit, inv = norm(xb, gain_ref[3:4, :], shift_ref[3:4, :])
        h3 = h3.astype(BF16)
        h3_ref[span, :] = h3
        slope = slope_scr.at[i % 2]
        if i == 0:
            copies[2].wait()
            copies[3].wait()
        branch = mlp_forward(h3, wup_ref, params_ref.at[12:16], wdown_ref, span, act_ref, SpanView(slope))
        out = (xb + branch + params_ref[17:18, :]).astype(BF16)
        for s in range(GROUP_FRAMES):
            both_scr[where_scr[s], place] = out[s * count : (s + 1) * count]
        grad_low = jnp.concatenate(
            [cot_slot(cot_ref, cotr_ref, where_scr[s], part * half + i * count, count) for s in range(GROUP_FRAMES)],
            axis=0,
        )
        gr_ref[span, :] = grad_low
        grad = grad_low.astype(F32)
        dh, sums = mlp_backward(grad_low, wup_ref, wdown_ref, span, SpanView(slope), du_ref)
        add_small(small_ref, [column_sum(dh * unit), column_sum(dh), column_sum(grad), None] + sums, False)
        dxb_ref[span, :] = grad + norm_back(dh, unit, inv, gain_ref[3:4, :])
    own_ref[...] = both_scr[0:frames]
    send_ref[...] = both_scr[frames:]


class SpanView:
    def __init__(self, ref):
        self.ref = ref

    def __getitem__(self, index):
        return self.ref[:, index[1]]

    def __setitem__(self, index, value):
        self.ref[:, index[1]] = value


def cot_slot(cot_ref, cotr_ref, frame, start, count):
    frames = cot_ref.shape[0]
    places = pl.ds(pl.multiple_of(start, count), count)
    mine = cot_ref[lax.rem(frame, frames), places, :]
    other = cotr_ref[lax.rem(frame, frames), places, :]
    return jnp.where(frame < frames, mine, other)


def time_backward_kernel(
    slots_ref, x_ref, qkv_ref, dxb_ref, params_ref, wqkv_ref, wout_ref,
    own_ref, send_ref, ar_ref, dqkv_ref, small_ref,
    where_scr, both_scr,
):
    frames, half = own_ref.shape[0], own_ref.shape[1]
    slot_places(slots_ref, where_scr, frames)
    small_ref[...] = jnp.zeros_like(small_ref)
    spread = lane_heads(BF16)
    steps = 4
    count = half // steps
    step_rows = count * GROUP_FRAMES
    gain = params_ref[2:3, :]
    for i in range(steps):
        span = slice(i * step_rows, (i + 1) * step_rows)
        place = slice(i * count, (i + 1) * count)
        dxb = dxb_ref[span, :]
        ar = dxb.astype(BF16)
        ar_ref[span, :] = ar
        do = split_slots(dot_nt(ar, wout_ref[...]).astype(BF16))
        qs = split_slots(qkv_ref[span, 0:TILE])
        ks = split_slots(qkv_ref[span, TILE : 2 * TILE])
        vs = split_slots(qkv_ref[span, 2 * TILE :])
        probs = time_probs(time_scores(qs, ks, spread), count)
        dps = time_scores(do, vs, spread)
        dps = [dps[j * count : (j + 1) * count] for j in range(len(PAIRS))]
        dss = []
        at = 0
        for t in range(VIDEO_STEPS):
            centre = functools.reduce(
                lambda a, b: a + b, [probs[at + s] * dps[at + s] for s in range(t + 1)]
            )
            dss.extend([probs[at + s] * (dps[at + s] - centre) for s in range(t + 1)])
            at += t + 1
        wide_p = dot_nt(jnp.concatenate([p.astype(BF16) for p in probs], axis=0), spread)
        wide_ds = dot_nt(jnp.concatenate([d.astype(BF16) for d in dss], axis=0), spread)
        dq = [None] * GROUP_FRAMES
        dk = [None] * GROUP_FRAMES
        dv = [None] * GROUP_FRAMES

        def add(table, index, piece):
            table[index] = piece if table[index] is None else table[index] + piece

        for j, (t, s) in enumerate(PAIRS):
            rows = slice(j * count, (j + 1) * count)
            add(dq, t, wide_ds[rows] * ks[s])
            add(dk, s, wide_ds[rows] * qs[t])
            add(dv, s, wide_p[rows] * do[t])
        for t in range(VIDEO_STEPS, GROUP_FRAMES):
            dq[t] = jnp.zeros_like(do[t])
            dk[t] = jnp.zeros_like(do[t])
            dv[t] = do[t]
        dq = jnp.concatenate([(d * SCALE).astype(BF16) for d in dq], axis=0)
        dk = jnp.concatenate([d.astype(BF16) for d in dk], axis=0)
        dv = jnp.concatenate([d.astype(BF16) for d in dv], axis=0)
        dqkv_ref[span, 0:TILE] = dq
        dqkv_ref[span, TILE : 2 * TILE] = dk
        dqkv_ref[span, 2 * TILE :] = dv
        dh = dot_nt(dqkv_ref[span, :], wqkv_ref[...])
        unit, inv = norm(x_ref[span, :].astype(F32), gain, params_ref[6:7, :])[1:]
        add_small(small_ref, [column_sum(dh * unit), column_sum(dh)], False)
        dxp = norm_back(dh, unit, inv, gain).astype(BF16).astype(F32)
        dx1 = (dxb + dxp).astype(BF16)
        for s in range(GROUP_FRAMES):
            both_scr[where_scr[s], place] = dx1[s * count : (s + 1) * count]
    own_ref[...] = both_scr[0:frames]
    send_ref[...] = both_scr[frames:]


def space_mlp_back_kernel(
    gr_ref, xa_ref, slope_ref, params_ref, wup_ref, wdown_ref,
    du_ref, dxa_ref, ar_ref, small_ref,
):
    small_ref[...] = jnp.zeros_like(small_ref)
    rows = 256
    gain = params_ref[1:2, :]
    for f in range(gr_ref.shape[0] // rows):
        span = slice(f * rows, (f + 1) * rows)
        grad_low = gr_ref[span, :]
        grad = grad_low.astype(F32)
        dh, sums = mlp_backward(grad_low, wup_ref.at[0], wdown_ref.at[0], span, slope_ref, du_ref)
        unit, inv = norm(xa_ref[span, :], gain, params_ref[5:6, :])[1:]
        add_small(small_ref, [column_sum(dh * unit), column_sum(dh), column_sum(grad), None] + sums, False)
        dxa = grad + norm_back(dh, unit, inv, gain)
        dxa_ref[span, :] = dxa
        ar_ref[span, :] = dxa.astype(BF16)


def head_picker():
    h = lax.broadcasted_iota(jnp.int32, (HEADS, TILE), 0)
    c = lax.broadcasted_iota(jnp.int32, (HEADS, TILE), 1)
    return (c // HEAD == h).astype(BF16)


def attn_back_frame(f, to, ar_ref, qkv_ref, lse_ref, o_ref, wout_ref, pick, dqkv_ref):
    rows = lse_ref.shape[2]
    span = slice(f * rows, (f + 1) * rows)
    dest = slice(to * rows, (to + 1) * rows)
    do = dot_nt(ar_ref[span, :], wout_ref[0]).astype(BF16)
    both = do.astype(F32) * o_ref[span, :].astype(F32)
    high = both.astype(BF16)
    rest = (both - high.astype(F32)).astype(BF16)
    centre = dot_nt(pick, high) + dot_nt(pick, rest)
    for pair in range(HEADS // 2):
        qp = qkv_ref[span, pair * 128 : (pair + 1) * 128]
        kp = qkv_ref[span, TILE + pair * 128 : TILE + (pair + 1) * 128]
        vp = qkv_ref[span, 2 * TILE + pair * 128 : 2 * TILE + (pair + 1) * 128]
        dop = do[:, pair * 128 : (pair + 1) * 128]
        zero = jnp.zeros_like(kp)
        mask = head_mask(kp, 0)
        st = dot_nt(jnp.concatenate([jnp.where(mask, kp, zero), jnp.where(mask, zero, kp)], axis=0), qp)
        dpt = dot_nt(jnp.concatenate([jnp.where(mask, vp, zero), jnp.where(mask, zero, vp)], axis=0), dop)
        pts, dsts, dqs = [], [], []
        for e in range(2):
            row = slice(2 * pair + e, 2 * pair + e + 1)
            keys = slice(e * rows, (e + 1) * rows)
            pt = jnp.exp(st[keys] - lse_ref[f, row, :])
            dst = (pt * (dpt[keys] - centre[row, :])).astype(BF16)
            pts.append(pt.astype(BF16))
            dsts.append(dst)
            dqs.append(dot_tn(dst, kp) * SCALE)
        dk = dot(jnp.concatenate(dsts, axis=0), qp)
        dv = dot(jnp.concatenate(pts, axis=0), dop)
        values = (
            jnp.where(mask, dqs[0], dqs[1]),
            jnp.where(mask, dk[:rows], dk[rows:]),
            jnp.where(mask, dv[:rows], dv[rows:]),
        )
        for index, value in enumerate(values):
            at = index * TILE + pair * 128
            dqkv_ref[dest, at : at + 128] = value.astype(BF16)


def space_attn_back_kernel(first, ar_ref, qkv_ref, lse_ref, o_ref, wout_ref, dqkv_ref):
    pick = head_picker()
    for f in range(lse_ref.shape[0] // 2):
        attn_back_frame(first + f, f, ar_ref, qkv_ref, lse_ref, o_ref, wout_ref, pick, dqkv_ref)


def qkv_weights_kernel(order, first_ref, last_ref, h_ref, keep_ref, send_ref):
    size = h_ref.shape[1] // lax.axis_size("sp")
    turned = jnp.transpose(h_ref[...])
    middle = first_ref.shape[0]
    for j in range(3):
        cols = slice(j * TILE, (j + 1) * TILE)
        result = dot(turned[:, :middle], first_ref[:, cols]) + dot(turned[:, middle:], last_ref[:, cols])
        put_blocks(result, jnp.int32(0), size, Place(0, 3 * size, j * size), order, keep_ref, send_ref)


def finish_kernel(
    first_ref, last_ref, tok_ref, dxa_ref, own_ref, recv_ref, params_ref, wqkv_ref, small1_ref,
    small2_ref, small3_ref, gtok_ref, out_ref, small_ref,
):
    part = lax.rem(lax.axis_index("sp"), 2)
    frames, half = own_ref.shape[0], own_ref.shape[1]
    rows = 2 * half
    gain = params_ref[0:1, :]
    sums = []
    for f in range(frames):
        span = slice(f * rows, (f + 1) * rows)
        out_ref[f, half_rows(part, half), :] = own_ref[f]
        out_ref[f, half_rows(1 - part, half), :] = recv_ref[f]
        source = first_ref if f < frames // 2 else last_ref
        at = (f % (frames // 2)) * rows
        dh = dot_nt(source[at : at + rows, :], wqkv_ref[0])
        unit, inv = norm(tok_ref[f].astype(F32), gain, params_ref[4:5, :])[1:]
        sums.append((column_sum(dh * unit), column_sum(dh)))
        gtok_ref[f] = (dxa_ref[span, :] + norm_back(dh, unit, inv, gain)).astype(BF16)
    row = lax.broadcasted_iota(jnp.int32, (8, TILE), 0)
    total = [functools.reduce(lambda a, b: a + b, [x[i] for x in sums]) for i in range(2)]
    small0 = jnp.where(row == 0, total[0], jnp.where(row == 1, total[1], 0.0))
    small = jnp.concatenate([small0, small1_ref[...], small2_ref[...], small3_ref[...]], axis=0)
    small_ref[...] = small.astype(BF16)


def place_of(block, order, sp):
    bits = len(order)
    mixed = jnp.bitwise_xor(block, sp)
    slot = jnp.int32(0)
    for i, b in enumerate(order):
        bit = jnp.bitwise_and(lax.shift_right_logical(mixed, jnp.int32(b)), 1)
        slot = slot + lax.shift_left(bit, jnp.int32(bits - 1 - i))
    return slot


class Place:
    def __init__(self, base, rows, at):
        self.base, self.rows, self.at = base, rows, at


def put_blocks(result, first, size, place, order, keep_ref, send_ref):
    sp = lax.axis_index("sp")
    part = lax.rem(sp, 2)
    low = result.astype(BF16)
    for j in range(result.shape[0] // (2 * size)):
        even = low[2 * j * size : (2 * j + 1) * size]
        odd = low[(2 * j + 1) * size : (2 * j + 2) * size]
        slot = place_of(first + 2 * j, order[1:], sp)
        rows = pl.ds(pl.multiple_of(place.base + slot * place.rows + place.at, 16), size)
        keep_ref[rows, :] = jnp.where(part == 0, even, odd)
        send_ref[rows, :] = jnp.where(part == 0, odd, even)


def sp_blocks():
    sp_size = lax.axis_size("sp")
    return sp_size, sp_size // 2


def put_up(h_ref, du_ref, base, rows, order, keep_ref, send_ref):
    sp_size, slots = sp_blocks()
    size = h_ref.shape[1] // sp_size
    turned = jnp.transpose(h_ref[...])
    for j in range(du_ref.shape[1] // TILE):
        up = dot(turned, du_ref[:, j * TILE : (j + 1) * TILE])
        put_blocks(up, jnp.int32(0), size, Place(base, rows, j * size), order, keep_ref, send_ref)


def put_down(act_ref, gr_ref, base, order, keep_ref, send_ref):
    sp_size, slots = sp_blocks()
    size = act_ref.shape[1] // sp_size
    for j in range(act_ref.shape[1] // TILE):
        down = dot_tn(act_ref[:, j * TILE : (j + 1) * TILE], gr_ref[...])
        first = jnp.int32(j * (TILE // size))
        put_blocks(down, first, size, Place(base, size, 0), order, keep_ref, send_ref)


def mlp_weights_kernel(orders, h_ref, du_ref, act_ref, gr_ref, keep_ref, send_ref):
    sp_size, slots = sp_blocks()
    rows = du_ref.shape[1] // TILE * (h_ref.shape[1] // sp_size)
    put_up(h_ref, du_ref, 0, rows, orders[0], keep_ref, send_ref)
    put_down(act_ref, gr_ref, slots * rows, orders[1], keep_ref, send_ref)


def down_weights_kernel(order, act_ref, own_ref, recv_ref, gr_ref, keep_ref, send_ref):
    part = lax.rem(lax.axis_index("sp"), 2)
    frames, half = own_ref.shape[0], own_ref.shape[1]
    for f in range(frames):
        base = f * 2 * half
        gr_ref[pl.ds(pl.multiple_of(base + part * half, half), half), :] = own_ref[f]
        gr_ref[pl.ds(pl.multiple_of(base + (1 - part) * half, half), half), :] = recv_ref[f]
    put_down(act_ref, gr_ref, 0, order, keep_ref, send_ref)


def up_weights_kernel(order, h_ref, du_ref, o_ref, ar_ref, keep_ref, send_ref):
    sp_size, slots = sp_blocks()
    size = h_ref.shape[1] // sp_size
    at = du_ref.shape[1] // TILE * size
    put_up(h_ref, du_ref, 0, at + size, order, keep_ref, send_ref)
    out = dot_tn(o_ref[...], ar_ref[...])
    put_blocks(out, jnp.int32(0), size, Place(0, at + size, at), order, keep_ref, send_ref)


def attn_weights_kernel(order, h_ref, dqkv_ref, o_ref, ar_ref, keep_ref, send_ref):
    size = h_ref.shape[1] // lax.axis_size("sp")
    zero = jnp.int32(0)
    turned = jnp.transpose(h_ref[...])
    for j in range(3):
        cols = slice(j * TILE, (j + 1) * TILE)
        result = dot(turned, dqkv_ref[:, cols])
        put_blocks(result, zero, size, Place(0, 4 * size, j * size), order, keep_ref, send_ref)
    result = dot_tn(o_ref[...], ar_ref[...])
    put_blocks(result, zero, size, Place(0, 4 * size, 3 * size), order, keep_ref, send_ref)


def fold_kernel(moves, count, *refs):
    outs = refs[2 * count :]
    row_half = lax.rem(lax.axis_index("grp"), 2)
    for source, at, rows, slots, targets, to, split in moves:
        keep, recv = refs[2 * source], refs[2 * source + 1]
        if split == "none":
            span = slice(at, at + rows)
            total = keep[span, :] + recv[span, :]
            for target in targets:
                outs[target][to : to + rows, :] = total
        elif split == "slots":
            half = rows // 2
            for part, target in enumerate(targets):
                span = slice(at + part * half, at + (part + 1) * half)
                outs[target][to : to + half, :] = keep[span, :] + recv[span, :]
        else:
            half = rows // (2 * slots)
            for slot in range(slots):
                for part, target in enumerate(targets):
                    side = row_half if part == 0 else 1 - row_half
                    span = pl.ds(pl.multiple_of(at + 2 * slot * half + side * half, 16), half)
                    place = to + slot * half
                    outs[target][place : place + half, :] = keep[span, :] + recv[span, :]


class Group:
    def __init__(self, sizes, segments, apart=False):
        grp_size, sp_size = sizes
        bits = sp_size.bit_length() - 1
        grp_bits = grp_size.bit_length() - 1
        names = tuple(segments)
        self.halved = grp_bits > 0 and all(
            whole or (height // 2) % 16 == 0 for height, whole, path in segments.values()
        )
        self.segments = {}
        self.state = {}
        for name, (height, whole, path) in segments.items():
            path = [step for step in path if step != ROWS or self.halved] + list(range(4, bits))
            self.segments[name] = (height, whole, path)
            self.state[name] = [sp_size // 2, 1]
        self.stages = []
        for i in range(bits + (1 if self.halved else 0)):
            entries = {}
            for name in names:
                key = (self.segments[name][2][i], name if apart and i == 0 else None)
                entries.setdefault(key, []).append(name)
            stage = []
            for (step, _), who in entries.items():
                stage.append(("grp", grp_size, 0, who, "rows") if step == ROWS else ("sp", sp_size, step, who, "slots"))
            self.stages.append(stage)
        for b in range(1 if self.halved else 0, grp_bits):
            self.stages.append([("grp", grp_size, b, names, "none")])
        if self.halved:
            self.stages.append([("grp", grp_size, 0, names, "none")])
        self.stage = 0
        self.keeps, self.recvs = [], []

    def height(self, name):
        height, whole, _ = self.segments[name]
        slots, cut = self.state[name]
        return height if whole else height // cut * slots

    def start(self, sends):
        self.sends = sends
        self.recvs = [swap(send, *entry[:3]) for send, entry in zip(sends, self.stages[self.stage])]

    def begin(self, keep, send):
        entry = self.stages[0][len(self.keeps)]
        self.keeps.append(keep)
        self.recvs.append(swap(send, *entry[:3]))

    def fold(self):
        places = {}
        for source, entry in enumerate(self.stages[self.stage]):
            at = 0
            for name in entry[3]:
                places[name] = (source, at, self.height(name), self.state[name][0])
                at += self.height(name)
        shapes, moves, keeps, sends = [], [], [], []
        for entry in self.stages[self.stage + 1]:
            split = entry[4]
            keeps.append(len(shapes))
            sends.append(len(shapes) + (0 if split == "none" else 1))
            targets = (keeps[-1],) if split == "none" else (keeps[-1], sends[-1])
            to = 0
            for name in entry[3]:
                whole = self.segments[name][1]
                if split == "slots":
                    self.state[name][0] //= 2
                elif split == "rows":
                    self.state[name][1] = 2
                moves.append(places[name] + (targets, to, "none" if whole else split))
                to += self.height(name)
            shapes += [sds((to, TILE), BF16)] * len(targets)
        args = [x for pair in zip(self.keeps, self.recvs) for x in pair]
        out = call(functools.partial(fold_kernel, moves, len(args) // 2), args, shapes, 0.5, limit=4)
        self.keeps = [out[i] for i in keeps]
        self.sends = [out[i] for i in sends]
        self.stage += 1

    def left(self):
        return len(self.stages) - 1 - self.stage

    def pair(self):
        return self.keeps[0], self.recvs[0]


def result_kernel(sp_size, halved, *refs):
    outs = refs[8:16]
    gain_scr, shift_scr, qkv_scr, out_scr, up_scr, bup_scr, down_scr, bdown_scr = refs[16:24]
    mlp1, both, up0, qkv0 = refs[24:28]
    small_scr, sems = refs[28:]
    size = TILE // sp_size
    chunks = up_scr.shape[2] // TILE
    down_size = chunks * size
    row_half = lax.rem(lax.axis_index("grp"), 2)
    segments = (
        (mlp1, (chunks * size, down_size)), (both, (4 * size, down_size)),
        (up0, (chunks * size + size,)), (qkv0, (3 * size,)),
    )
    for i, (scr, heights) in enumerate(segments):
        mine, other = refs[2 * i], refs[2 * i + 1]
        at = 0
        base = 0
        for height in heights:
            if halved[i]:
                half = height // 2
                for ref, side in ((mine, row_half), (other, 1 - row_half)):
                    place = pl.ds(pl.multiple_of(base + side * half, 16), half)
                    scr[place, :] = ref[at : at + half, :].astype(F32)
                at += half
            else:
                span = slice(at, at + height)
                scr[base : base + height, :] = mine[span, :].astype(F32) + other[span, :].astype(F32)
                at += height
            base += height
    mine, other = refs[6], refs[7]
    at = 3 * size // (2 if halved[3] else 1)
    small = mine[at : at + 32, :].astype(F32)
    small_scr[...] = small if halved[3] else small + other[at : at + 32, :].astype(F32)
    for layer, (qkv, up, down, out, first, last) in enumerate((
        (qkv0, up0, both, up0, 4 * size, chunks * size),
        (both, mlp1, mlp1, both, chunks * size, 3 * size),
    )):
        for j in range(3):
            qkv_scr[layer, :, j * TILE : (j + 1) * TILE] = qkv[j * size : (j + 1) * size, :]
        for j in range(chunks):
            up_scr[layer, :, j * TILE : (j + 1) * TILE] = up[j * size : (j + 1) * size, :]
        down_scr[layer] = down[first : first + down_size, :]
        out_scr[layer] = out[last : last + size, :]
    sp = lax.axis_index("sp")
    back = lax.rem(TILE - sp * size, TILE)
    turned = pltpu.roll(small_scr[...], back, 1)
    for i in range(4):
        gain_scr[i : i + 1, :] = turned[8 * i : 8 * i + 1, :size]
        shift_scr[i : i + 1, :] = turned[8 * i + 1 : 8 * i + 2, :size]
    start = sp * down_size
    line = start // TILE
    back = lax.rem(TILE - lax.rem(start, TILE), TILE)
    for layer in range(2):
        first = 8 + 16 * layer
        bdown_scr[layer : layer + 1, :] = turned[first + 2 : first + 3, :size]
        rows = small_scr[first : first + 8, :]
        lines = lax.broadcasted_iota(jnp.int32, rows.shape, 0)
        picked = jnp.sum(jnp.where(lines == 4 + line, rows, 0.0), axis=0, keepdims=True)
        picked = pltpu.roll(jnp.broadcast_to(picked, rows.shape), back, 1)
        bup_scr[layer : layer + 1, :] = picked[0:1, :down_size]
    scrs = (gain_scr, shift_scr, qkv_scr, out_scr, up_scr, bup_scr, down_scr, bdown_scr)
    copies = [pltpu.make_async_copy(scr, out, sems.at[i]) for i, (scr, out) in enumerate(zip(scrs, outs))]
    for copy in copies:
        copy.start()
    for copy in copies:
        copy.wait()


VMEM = pl.BlockSpec(memory_space=pltpu.VMEM)
SMEM = pl.BlockSpec(memory_space=pltpu.SMEM)
HBM = pl.BlockSpec(memory_space=pltpu.HBM)


def sds(shape, dtype):
    return jax.ShapeDtypeStruct(shape, dtype)


def call(kernel, args, outs, micros, scratch=(), specs=None, out_specs=None, limit=12):
    return pl.pallas_call(
        kernel,
        in_specs=[VMEM] * len(args) if specs is None else specs,
        out_specs=[VMEM] * len(outs) if out_specs is None else out_specs,
        out_shape=outs,
        scratch_shapes=list(scratch),
        compiler_params=pltpu.CompilerParams(vmem_limit_bytes=limit * MIB),
        cost_estimate=pl.CostEstimate(flops=int(micros * COST), bytes_accessed=0, transcendentals=0),
    )(*args)


def swap(array, axis, size, bit):
    return lax.ppermute(array, axis, [(i, i ^ (1 << bit)) for i in range(size)])


def shards(sizes, tokens, frame_slot, norm_gain, norm_shift, w_qkv, w_out, w_up, b_up, w_down, b_down, cotangent):
    grp_size, sp_size = sizes
    frames, patches, width = tokens.shape
    hidden = w_up.shape[2]
    assert GROUP_FRAMES == 2 * frames and sp_size >= 8
    half = patches // 2
    rows = frames * patches
    sp_bits = sp_size.bit_length() - 1
    core_swap = functools.partial(swap, axis="sp", size=sp_size, bit=0)
    slots = sp_size // 2
    size = width // sp_size
    down_size = hidden // sp_size
    def slots_of(path):
        return [step for step in path if step != ROWS] + list(range(4, sp_bits))

    path_up1, path_down1 = (0, 1, 2, ROWS, 3), (0, 2, 1, ROWS, 3)
    path_attn1, path_down0 = (0, ROWS, 2, 1, 3), (0, 2, 1, ROWS, 3)
    path_up0, path_qkv0 = (0, 1, ROWS, 2, 3), (0, 2, 1, ROWS, 3)

    def row_out(cols, dtype=BF16):
        return sds((rows, cols), dtype)

    half_out = sds((frames, half, width), BF16)
    small_out = sds((8, TILE), F32)
    fence = lambda *arrays: lax.optimization_barrier(arrays)

    token = []

    def meet(groups, *arrays):
        recvs = [r for g in groups for r in g.recvs]
        out = list(fence(*arrays, *recvs, *token))
        count = len(arrays)
        arrays, recvs = out[:count], out[count:]
        for g in groups:
            g.recvs = [recvs.pop(0) for _ in g.recvs]
            g.fold()
        sends = [x for g in groups for x in g.sends]
        out = list(fence(*arrays, *sends))
        arrays, sends = out[:count], out[count:]
        for g in groups:
            g.start([sends.pop(0) for _ in g.sends])
        token[:] = [groups[-1].sends[-1]] if groups else []
        return arrays

    def buffers(height):
        return [sds((slots * height, TILE), BF16)] * 2

    cot_recv = core_swap(cotangent)
    packed = jnp.concatenate(
        [norm_gain, norm_shift, b_up.reshape(2 * hidden // width, width), b_down], axis=0
    )
    weights = (w_qkv, w_out, w_up, w_down)
    shapes = [sds(w.shape[1:], BF16) for w in weights]
    out = call(
        space_forward_kernel,
        (tokens, packed) + weights,
        [
            half_out, half_out, row_out(width), row_out(3 * width), sds((frames, HEADS, patches), F32),
            row_out(width), row_out(width, F32), row_out(width), row_out(hidden), row_out(hidden),
        ],
        16,
        scratch=[pltpu.VMEM(tokens.shape, BF16)]
        + [pltpu.VMEM(x.shape, BF16) for x in shapes]
        + [
            pltpu.VMEM((2, patches, width), BF16), pltpu.VMEM((2, patches, 3 * width), BF16),
            pltpu.VMEM((2, patches, width), BF16), pltpu.VMEM((2, patches, width), F32),
            pltpu.VMEM((2, patches, width), BF16),
            pltpu.VMEM((2, patches, hidden), BF16), pltpu.VMEM((2, patches, hidden), BF16),
            pltpu.VMEM((patches, width), F32), pltpu.SemaphoreType.DMA((5,)),
            pltpu.SemaphoreType.DMA((7 * frames,)),
        ],
        specs=[HBM, VMEM] + [HBM] * 4,
        out_specs=[VMEM, VMEM, HBM, HBM, VMEM] + [HBM] * 5,
        limit=LIMIT1,
    )
    (x_keep, x_send, h0, qkv0, lse0, o0, xa, h1, act0, slope0) = out
    x_recv = core_swap(x_send)

    place_scratch = [
        pltpu.SMEM((GROUP_FRAMES,), jnp.int32),
        pltpu.VMEM((GROUP_FRAMES, half, width), BF16),
    ]
    (out_own, out_send, xt, h2, qkv1, o1, h3, act1, du1, gr1, dxb, small3, w_qkv1, w_out1) = call(
        time_forward_kernel,
        (frame_slot, x_keep, x_recv, cotangent, cot_recv, packed) + weights,
        [
            half_out, half_out, row_out(width), row_out(width), row_out(3 * width), row_out(width),
            row_out(width), row_out(hidden), row_out(hidden), row_out(width), row_out(width, F32),
            small_out,
        ] + shapes[:2],
        24,
        scratch=place_scratch
        + [pltpu.VMEM((2, rows // 4, hidden), BF16)]
        + [pltpu.VMEM(x.shape, BF16) for x in shapes[2:]]
        + [pltpu.SemaphoreType.DMA((4,))],
        specs=[SMEM] + [VMEM] * 5 + [HBM] * 4,
        limit=LIMIT2,
    )
    out_recv = core_swap(out_send)

    out = call(
        functools.partial(mlp_weights_kernel, (slots_of(path_up1), slots_of(path_down1))), (h3, du1, act1, gr1),
        buffers(4 * size + down_size), 4.5,
    )
    keep, send, dxb = fence(*out, dxb)
    mlp1 = Group(sizes, {"up": (4 * size, False, path_up1), "down": (down_size, False, path_down1)})
    mlp1.begin(keep, send)

    (dx_own, dx_send, ar1, dqkv1, small2) = call(
        time_backward_kernel,
        (frame_slot, xt, qkv1, dxb, packed, w_qkv1, w_out1),
        [half_out, half_out, row_out(width), row_out(3 * width), small_out],
        8,
        scratch=place_scratch,
        specs=[SMEM] + [VMEM] * 6,
    )
    dx_recv = core_swap(dx_send)
    dx_own, dx_recv, dqkv1, out_recv = meet((mlp1,), dx_own, dx_recv, dqkv1, out_recv)
    keep_attn, send_attn = call(
        functools.partial(attn_weights_kernel, slots_of(path_attn1)), (h2, dqkv1, o1, ar1),
        buffers(4 * size), 2.4,
    )
    gr0, keep_down, send_down = call(
        functools.partial(down_weights_kernel, slots_of(path_down0)), (act0, dx_own, dx_recv),
        [row_out(width)] + buffers(down_size), 2.4,
    )
    (du0, dxa, ar0, small1) = call(
        space_mlp_back_kernel,
        (gr0, xa, slope0, packed, w_up, w_down),
        [row_out(hidden), row_out(width, F32), row_out(width), small_out],
        6,
    )
    keep_up, send_up = call(
        functools.partial(up_weights_kernel, slots_of(path_up0)), (h1, du0, o0, ar0), buffers(5 * size), 3
    )
    keep_attn, send_attn, keep_down, send_down, keep_up, send_up, ar0 = meet(
        (mlp1,), keep_attn, send_attn, keep_down, send_down, keep_up, send_up, ar0
    )
    both = Group(
        sizes,
        {"attn": (4 * size, False, path_attn1), "down": (down_size, False, path_down0)},
        apart=True,
    )
    both.begin(keep_attn, send_attn)
    both.begin(keep_down, send_down)
    up0 = Group(sizes, {"up": (5 * size, False, path_up0)})
    up0.begin(keep_up, send_up)

    def attn_back(first):
        return call(
            functools.partial(space_attn_back_kernel, first), (ar0, qkv0, lse0, o0, w_out),
            [sds((rows // 2, 3 * width), BF16)], 5,
        )[0]

    dqkv_a = attn_back(0)
    dqkv_b = attn_back(frames // 2)
    dqkv_a, dqkv_b = meet((up0, both, mlp1), dqkv_a, dqkv_b)
    out = call(
        functools.partial(qkv_weights_kernel, slots_of(path_qkv0)), (dqkv_a, dqkv_b, h0), buffers(3 * size), 2
    )
    keep, send, dqkv_b = fence(*out, dqkv_b)
    qkv = Group(
        sizes, {"qkv": (3 * size, False, path_qkv0), "small": (32, True, path_qkv0)}, apart=True
    )
    qkv.begin(keep, send)
    grad_tokens, output, small = call(
        finish_kernel,
        (
            dqkv_a, dqkv_b, tokens, dxa, out_own, out_recv, packed, w_qkv, small1, small2, small3,
        ),
        [sds(tokens.shape, BF16), sds(tokens.shape, BF16), sds((32, TILE), BF16)],
        4,
    )
    (small,) = fence(small)
    qkv.begin(small, small)
    everyone = (mlp1, both, up0, qkv)
    for names in TAIL:
        groups = [g for g in (dict(zip("mbuq", everyone))[c] for c in names) if g.left()]
        if groups:
            meet(groups)
    while any(g.left() for g in everyone):
        meet([g for g in everyone if g.left()])
    finals = [
        sds((4, size), F32), sds((4, size), F32), sds((2, size, 3 * width), F32), sds((2, size, width), F32),
        sds((2, size, hidden), F32), sds((2, down_size), F32), sds((2, down_size, width), F32),
        sds((2, size), F32),
    ]
    heights = (4 * size + down_size, 4 * size + down_size, 5 * size, 3 * size)
    results = call(
        functools.partial(result_kernel, sp_size, tuple(g.halved for g in everyone)),
        [x for g in everyone for x in g.pair()], finals, 2,
        scratch=[pltpu.VMEM(f.shape, F32) for f in finals]
        + [pltpu.VMEM((h, TILE), F32) for h in heights]
        + [pltpu.VMEM((32, TILE), F32), pltpu.SemaphoreType.DMA((8,))],
        out_specs=[HBM] * 8,
    )
    return (output, grad_tokens, *results)


def solution(mesh):
    rows = P(("grp", "sp"), None, None)
    in_specs = (rows, P("grp", None), P(), P(), P(), P(), P(), P(), P(), P(), rows)
    out_specs = (
        rows, rows, P(None, "sp"), P(None, "sp"), P(None, "sp", None), P(None, "sp", None),
        P(None, "sp", None), P(None, "sp"), P(None, "sp", None), P(None, "sp"),
    )
    body = functools.partial(shards, (mesh.shape["grp"], mesh.shape["sp"]))
    return jax.shard_map(body, mesh=mesh, in_specs=in_specs, out_specs=out_specs, check_vma=False)
```

```python
import functools

import jax
import jax.numpy as jnp
from jax import lax
from jax.experimental import pallas as pl
from jax.experimental.pallas import tpu as pltpu
from jax.sharding import PartitionSpec as P

HEADS = 8
HEAD = 64
VIDEO_STEPS = 6
GROUP_FRAMES = 8
NORM_EPS = 1e-05
TILE = 512
SCALE = HEAD**-0.5
TANH_A = 0.7978845608028654
TANH_B = TANH_A * 0.044715
PAIRS = [(t, s) for t in range(VIDEO_STEPS) for s in range(t + 1)]
F32 = jnp.float32
BF16 = jnp.bfloat16
MIB = 1024 * 1024
ROWS = -1
COST = 1.15e9 * 0.02
TAIL = ("qm", "bu", "qm", "bu", "q", "bu", "q", "bu", "q")
LIMIT1 = 52
LIMIT2 = 24


def dot(left, right):
    return jnp.dot(left, right, preferred_element_type=F32)


def dot_nt(left, right):
    return lax.dot_general(left, right, (((1,), (1,)), ((), ())), preferred_element_type=F32)


def dot_tn(left, right):
    return lax.dot_general(left, right, (((0,), (0,)), ((), ())), preferred_element_type=F32)


def norm(rows, gain, shift):
    centred = rows - jnp.mean(rows, axis=-1, keepdims=True)
    inv = lax.rsqrt(jnp.mean(centred * centred, axis=-1, keepdims=True) + NORM_EPS)
    unit = centred * inv
    return unit * gain + shift, unit, inv


def norm_back(grad, unit, inv, gain):
    grad_unit = grad * gain
    mean_grad = jnp.mean(grad_unit, axis=-1, keepdims=True)
    mean_both = jnp.mean(grad_unit * unit, axis=-1, keepdims=True)
    return inv * (grad_unit - mean_grad - unit * mean_both)


def column_sum(rows):
    return jnp.sum(rows, axis=0, keepdims=True)


def gelu_pair(u):
    square = u * u
    sigma = 0.5 + 0.5 * jnp.tanh(u * (TANH_A + TANH_B * square))
    act = u * sigma
    slope = sigma + act * (1.0 - sigma) * (2.0 * TANH_A + 6.0 * TANH_B * square)
    return act.astype(BF16), slope.astype(BF16)


def head_mask(lanes, which):
    lane = lax.broadcasted_iota(jnp.int32, lanes.shape, 1)
    return (lane < HEAD) if which == 0 else (lane >= HEAD)


def qkv_rows(normed, weight):
    out = []
    for part in range(3):
        piece = dot(normed, weight[:, part * TILE : (part + 1) * TILE])
        if part == 0:
            out.append(piece.astype(BF16) * BF16(SCALE))
        else:
            out.append(piece.astype(BF16))
    return out


def mlp_forward(normed, w_up, b_up, w_down, rows, act_ref, slope_ref):
    chunks = w_up.shape[1] // TILE
    up = lambda j: dot(normed, w_up[:, j * TILE : (j + 1) * TILE])
    total = None
    u = up(0)
    for j in range(chunks):
        cols = slice(j * TILE, (j + 1) * TILE)
        later = up(j + 1) if j + 1 < chunks else None
        act, slope = gelu_pair(u + b_up[j : j + 1, :])
        act_ref[rows, cols] = act
        slope_ref[rows, cols] = slope
        piece = dot(act, w_down[cols, :])
        total = piece if total is None else total + piece
        u = later
    return total


def mlp_backward(grad_low, w_up, w_down, rows, slope_ref, du_ref):
    chunks = w_up.shape[1] // TILE
    down = lambda j: dot_nt(grad_low, w_down[j * TILE : (j + 1) * TILE, :])
    total = None
    sums = []
    da = down(0)
    for j in range(chunks):
        cols = slice(j * TILE, (j + 1) * TILE)
        later = down(j + 1) if j + 1 < chunks else None
        du = (da * slope_ref[rows, cols].astype(F32)).astype(BF16)
        du_ref[rows, cols] = du
        sums.append(column_sum(du.astype(F32)))
        piece = dot_nt(du, w_up[:, cols])
        total = piece if total is None else total + piece
        da = later
    return total, sums


def add_small(small_ref, values, first):
    for i, value in enumerate(values):
        row = slice(i, i + 1) if i < 4 else slice(i, i + 1)
        if value is None:
            continue
        if first:
            small_ref[row, :] = value
        else:
            small_ref[row, :] += value


def rows_at(index, count):
    return pl.ds(pl.multiple_of(index * count, count), count)


def half_rows(part, half):
    return pl.ds(pl.multiple_of(part * half, half), half)


def space_forward_kernel(
    tok_hbm, params_ref, wqkv_hbm, wout_hbm, wup_hbm, wdown_hbm,
    keep_ref, send_ref, h0_hbm, qkv_hbm, lse_ref, o_hbm, xa_hbm, h1_hbm, act_hbm, slope_hbm,
    tok_ref, wqkv_ref, wout_ref, wup_ref, wdown_ref, h0_scr, qkv_scr, o_scr, xa_scr, h1_scr, act_scr,
    slope_scr, x1_scr, in_sems, out_sems,
):
    pairs = [
        (tok_hbm, tok_ref), (wqkv_hbm.at[0], wqkv_ref), (wout_hbm.at[0], wout_ref),
        (wup_hbm.at[0], wup_ref), (wdown_hbm.at[0], wdown_ref),
    ]
    copies = [pltpu.make_async_copy(src, dst, in_sems.at[i]) for i, (src, dst) in enumerate(pairs)]
    for copy in copies:
        copy.start()
    gain_ref, shift_ref = params_ref, params_ref.at[4:8]
    part = lax.rem(lax.axis_index("sp"), 2)
    frames, rows = tok_ref.shape[0], tok_ref.shape[1]
    half = rows // 2
    lane = lax.broadcasted_iota(jnp.int32, (rows, 128), 1)
    places = (
        (h0_scr, h0_hbm), (qkv_scr, qkv_hbm), (o_scr, o_hbm), (xa_scr, xa_hbm), (h1_scr, h1_hbm),
        (act_scr, act_hbm), (slope_scr, slope_hbm),
    )

    def spills(f):
        now = lax.rem(f, 2)
        return [
            pltpu.make_async_copy(scr.at[now], hbm.at[rows_at(f, rows)], out_sems.at[7 * now + i])
            for i, (scr, hbm) in enumerate(places)
        ]

    def await_first(f, *which):
        @pl.when(f == 0)
        def _():
            for i in which:
                copies[i].wait()

    copies[0].wait()

    @pl.loop(0, frames)
    def _(f):
        now = lax.rem(f, 2)
        spill = spills(f)

        @pl.when(f >= 2)
        def _():
            for copy in spills(f - 2):
                copy.wait()

        x0 = tok_ref[f].astype(F32)
        h0 = norm(x0, gain_ref[0:1, :], shift_ref[0:1, :])[0].astype(BF16)
        h0_scr[now] = h0
        spill[0].start()
        await_first(f, 1)
        q, k, v = qkv_rows(h0, wqkv_ref)
        qkv_scr[now, :, 0:TILE] = q
        qkv_scr[now, :, TILE : 2 * TILE] = k
        qkv_scr[now, :, 2 * TILE :] = v
        spill[1].start()
        lse_all = jnp.zeros((rows, 128), F32)
        mixed = []
        for pair in range(HEADS // 2):
            cols = slice(pair * 128, (pair + 1) * 128)
            qp, kp, vp = q[:, cols], k[:, cols], v[:, cols]
            zero = jnp.zeros_like(qp)
            mask = head_mask(qp, 0)
            s = dot_nt(jnp.concatenate([jnp.where(mask, qp, zero), jnp.where(mask, zero, qp)], axis=0), kp)
            top = jnp.max(s, axis=-1, keepdims=True)
            p = jnp.exp(s - top)
            total = jnp.sum(p, axis=-1, keepdims=True)
            both = dot(p.astype(BF16), vp) * (1.0 / total)
            lse = top + jnp.log(total)
            lse_all = jnp.where(lane == 2 * pair, lse[:rows], lse_all)
            lse_all = jnp.where(lane == 2 * pair + 1, lse[rows:], lse_all)
            mixed.append(jnp.where(mask, both[:rows], both[rows:]).astype(BF16))
        lse_ref[f] = jnp.transpose(lse_all)[0:HEADS, :]
        o = jnp.concatenate(mixed, axis=1)
        o_scr[now] = o
        spill[2].start()
        await_first(f, 2)
        xa = x0 + dot(o, wout_ref[...])
        xa_scr[now] = xa
        spill[3].start()
        h1 = norm(xa, gain_ref[1:2, :], shift_ref[1:2, :])[0].astype(BF16)
        h1_scr[now] = h1
        spill[4].start()
        await_first(f, 3, 4)
        branch = mlp_forward(
            h1, wup_ref, params_ref.at[8:12], wdown_ref, slice(None), act_scr.at[now], slope_scr.at[now]
        )
        spill[5].start()
        spill[6].start()
        x1_scr[...] = xa + branch + params_ref[16:17, :]
        keep_ref[f] = x1_scr[half_rows(part, half), :].astype(BF16)
        send_ref[f] = x1_scr[half_rows(1 - part, half), :].astype(BF16)

    for f in (frames - 2, frames - 1):
        for copy in spills(jnp.int32(f)):
            copy.wait()


def lane_heads(dtype):
    c = lax.broadcasted_iota(jnp.int32, (TILE, 128), 0)
    h = lax.broadcasted_iota(jnp.int32, (TILE, 128), 1)
    return (c // HEAD == h).astype(dtype)


def slot_places(slots_ref, where_scr, frames):
    sp = lax.axis_index("sp")
    group = (sp * frames) // GROUP_FRAMES
    part = lax.rem(sp, GROUP_FRAMES // frames)
    for t in range(GROUP_FRAMES):
        where_scr[slots_ref[group, t]] = lax.rem(t + GROUP_FRAMES - part * frames, GROUP_FRAMES)


def time_scores(q, k, spread):
    parts = []
    for t, s in PAIRS:
        parts.append((q[t] * k[s]).astype(BF16))
    return dot(jnp.concatenate(parts, axis=0), spread)


def time_probs(scores, count):
    blocks = [scores[i * count : (i + 1) * count] for i in range(len(PAIRS))]
    probs = []
    at = 0
    for t in range(VIDEO_STEPS):
        mine = blocks[at : at + t + 1]
        at += t + 1
        top = functools.reduce(jnp.maximum, mine)
        raw = [jnp.exp(b - top) for b in mine]
        inv = 1.0 / functools.reduce(lambda a, b: a + b, raw)
        probs.extend([r * inv for r in raw])
    return probs


def split_slots(rows):
    count = rows.shape[0] // GROUP_FRAMES
    return [rows[s * count : (s + 1) * count].astype(F32) for s in range(GROUP_FRAMES)]


def time_forward_kernel(
    slots_ref, keep_ref, recv_ref, cot_ref, cotr_ref, params_ref,
    wqkv_hbm, wout_hbm, wup_hbm, wdown_hbm,
    own_ref, send_ref, x_ref, h2_ref, qkv_ref, o_ref, h3_ref, act_ref, du_ref, gr_ref, dxb_ref,
    small_ref, wqkv_ref, wout_ref,
    where_scr, both_scr, slope_scr, wup_ref, wdown_ref, in_sems,
):
    pairs = [(wqkv_hbm, wqkv_ref), (wout_hbm, wout_ref), (wup_hbm, wup_ref), (wdown_hbm, wdown_ref)]
    copies = [pltpu.make_async_copy(src.at[1], dst, in_sems.at[i]) for i, (src, dst) in enumerate(pairs)]
    for copy in copies:
        copy.start()
    gain_ref, shift_ref = params_ref, params_ref.at[4:8]
    frames, half = keep_ref.shape[0], keep_ref.shape[1]
    part = lax.rem(lax.axis_index("sp"), GROUP_FRAMES // frames)
    slot_places(slots_ref, where_scr, frames)
    small_ref[...] = jnp.zeros_like(small_ref)
    both_scr[0:frames] = keep_ref[...]
    both_scr[frames:] = recv_ref[...]
    spread = lane_heads(BF16)
    steps = 4
    count = half // steps
    step_rows = count * GROUP_FRAMES

    def await_first(i, *which):
        @pl.when(i == 0)
        def _():
            for w in which:
                copies[w].wait()

    @pl.loop(0, steps)
    def _(i):
        span = rows_at(i, step_rows)
        place = rows_at(i, count)
        x_low = jnp.concatenate([both_scr[where_scr[s], place] for s in range(GROUP_FRAMES)], axis=0)
        x_ref[span, :] = x_low
        x = x_low.astype(F32)
        h2 = norm(x, gain_ref[2:3, :], shift_ref[2:3, :])[0].astype(BF16)
        h2_ref[span, :] = h2
        await_first(i, 0)
        q, k, v = qkv_rows(h2, wqkv_ref)
        qkv_ref[span, 0:TILE] = q
        qkv_ref[span, TILE : 2 * TILE] = k
        qkv_ref[span, 2 * TILE :] = v
        qs, ks, vs = split_slots(q), split_slots(k), split_slots(v)
        probs = time_probs(time_scores(qs, ks, spread), count)
        wide = dot_nt(jnp.concatenate([p.astype(BF16) for p in probs], axis=0), spread)
        mixed = []
        at = 0
        for t in range(VIDEO_STEPS):
            total = None
            for s in range(t + 1):
                piece = wide[at * count : (at + 1) * count] * vs[s]
                total = piece if total is None else total + piece
                at += 1
            mixed.append(total)
        mixed.extend(vs[VIDEO_STEPS:])
        o = jnp.concatenate([m.astype(BF16) for m in mixed], axis=0)
        o_ref[span, :] = o
        await_first(i, 1)
        xb = x + dot(o, wout_ref[...]).astype(BF16).astype(F32)
        h3, unit, inv = norm(xb, gain_ref[3:4, :], shift_ref[3:4, :])
        h3 = h3.astype(BF16)
        h3_ref[span, :] = h3
        slope = slope_scr
        await_first(i, 2, 3)
        branch = mlp_forward(h3, wup_ref, params_ref.at[12:16], wdown_ref, span, act_ref, SpanView(slope))
        out = (xb + branch + params_ref[17:18, :]).astype(BF16)
        for s in range(GROUP_FRAMES):
            both_scr[where_scr[s], place] = out[s * count : (s + 1) * count]
        grad_low = jnp.concatenate(
            [cot_slot(cot_ref, cotr_ref, where_scr[s], part * half + i * count, count) for s in range(GROUP_FRAMES)],
            axis=0,
        )
        gr_ref[span, :] = grad_low
        grad = grad_low.astype(F32)
        dh, sums = mlp_backward(grad_low, wup_ref, wdown_ref, span, SpanView(slope), du_ref)
        add_small(small_ref, [column_sum(dh * unit), column_sum(dh), column_sum(grad), None] + sums, False)
        dxb_ref[span, :] = grad + norm_back(dh, unit, inv, gain_ref[3:4, :])

    own_ref[...] = both_scr[0:frames]
    send_ref[...] = both_scr[frames:]


class SpanView:
    def __init__(self, ref):
        self.ref = ref

    def __getitem__(self, index):
        return self.ref[:, index[1]]

    def __setitem__(self, index, value):
        self.ref[:, index[1]] = value


def cot_slot(cot_ref, cotr_ref, frame, start, count):
    frames = cot_ref.shape[0]
    places = pl.ds(pl.multiple_of(start, count), count)
    mine = cot_ref[lax.rem(frame, frames), places, :]
    other = cotr_ref[lax.rem(frame, frames), places, :]
    return jnp.where(frame < frames, mine, other)


def time_backward_kernel(
    slots_ref, x_ref, qkv_ref, dxb_ref, params_ref, wqkv_ref, wout_ref,
    own_ref, send_ref, ar_ref, dqkv_ref, small_ref,
    where_scr, both_scr,
):
    frames, half = own_ref.shape[0], own_ref.shape[1]
    slot_places(slots_ref, where_scr, frames)
    small_ref[...] = jnp.zeros_like(small_ref)
    spread = lane_heads(BF16)
    steps = 4
    count = half // steps
    step_rows = count * GROUP_FRAMES
    gain = params_ref[2:3, :]

    @pl.loop(0, steps)
    def _(i):
        span = rows_at(i, step_rows)
        place = rows_at(i, count)
        dxb = dxb_ref[span, :]
        ar = dxb.astype(BF16)
        ar_ref[span, :] = ar
        do = split_slots(dot_nt(ar, wout_ref[...]).astype(BF16))
        qs = split_slots(qkv_ref[span, 0:TILE])
        ks = split_slots(qkv_ref[span, TILE : 2 * TILE])
        vs = split_slots(qkv_ref[span, 2 * TILE :])
        probs = time_probs(time_scores(qs, ks, spread), count)
        dps = time_scores(do, vs, spread)
        dps = [dps[j * count : (j + 1) * count] for j in range(len(PAIRS))]
        dss = []
        at = 0
        for t in range(VIDEO_STEPS):
            centre = functools.reduce(
                lambda a, b: a + b, [probs[at + s] * dps[at + s] for s in range(t + 1)]
            )
            dss.extend([probs[at + s] * (dps[at + s] - centre) for s in range(t + 1)])
            at += t + 1
        wide_p = dot_nt(jnp.concatenate([p.astype(BF16) for p in probs], axis=0), spread)
        wide_ds = dot_nt(jnp.concatenate([d.astype(BF16) for d in dss], axis=0), spread)
        dq = [None] * GROUP_FRAMES
        dk = [None] * GROUP_FRAMES
        dv = [None] * GROUP_FRAMES

        def add(table, index, piece):
            table[index] = piece if table[index] is None else table[index] + piece

        for j, (t, s) in enumerate(PAIRS):
            rows = slice(j * count, (j + 1) * count)
            add(dq, t, wide_ds[rows] * ks[s])
            add(dk, s, wide_ds[rows] * qs[t])
            add(dv, s, wide_p[rows] * do[t])
        for t in range(VIDEO_STEPS, GROUP_FRAMES):
            dq[t] = jnp.zeros_like(do[t])
            dk[t] = jnp.zeros_like(do[t])
            dv[t] = do[t]
        dq = jnp.concatenate([(d * SCALE).astype(BF16) for d in dq], axis=0)
        dk = jnp.concatenate([d.astype(BF16) for d in dk], axis=0)
        dv = jnp.concatenate([d.astype(BF16) for d in dv], axis=0)
        dqkv_ref[span, 0:TILE] = dq
        dqkv_ref[span, TILE : 2 * TILE] = dk
        dqkv_ref[span, 2 * TILE :] = dv
        dh = dot_nt(dqkv_ref[span, :], wqkv_ref[...])
        unit, inv = norm(x_ref[span, :].astype(F32), gain, params_ref[6:7, :])[1:]
        add_small(small_ref, [column_sum(dh * unit), column_sum(dh)], False)
        dxp = norm_back(dh, unit, inv, gain).astype(BF16).astype(F32)
        dx1 = (dxb + dxp).astype(BF16)
        for s in range(GROUP_FRAMES):
            both_scr[where_scr[s], place] = dx1[s * count : (s + 1) * count]

    own_ref[...] = both_scr[0:frames]
    send_ref[...] = both_scr[frames:]


def space_mlp_back_kernel(
    gr_ref, xa_ref, slope_ref, params_ref, wup_ref, wdown_ref,
    du_ref, dxa_ref, ar_ref, small_ref,
):
    small_ref[...] = jnp.zeros_like(small_ref)
    rows = 256
    gain = params_ref[1:2, :]

    @pl.loop(0, gr_ref.shape[0] // rows)
    def _(f):
        span = rows_at(f, rows)
        grad_low = gr_ref[span, :]
        grad = grad_low.astype(F32)
        dh, sums = mlp_backward(grad_low, wup_ref.at[0], wdown_ref.at[0], span, slope_ref, du_ref)
        unit, inv = norm(xa_ref[span, :], gain, params_ref[5:6, :])[1:]
        add_small(small_ref, [column_sum(dh * unit), column_sum(dh), column_sum(grad), None] + sums, False)
        dxa = grad + norm_back(dh, unit, inv, gain)
        dxa_ref[span, :] = dxa
        ar_ref[span, :] = dxa.astype(BF16)


def head_picker():
    h = lax.broadcasted_iota(jnp.int32, (HEADS, TILE), 0)
    c = lax.broadcasted_iota(jnp.int32, (HEADS, TILE), 1)
    return (c // HEAD == h).astype(BF16)


def attn_back_frame(f, ar_ref, qkv_ref, lse_ref, o_ref, wout_ref, pick, dqkv_ref):
    rows = lse_ref.shape[2]
    span = rows_at(f, rows)
    do = dot_nt(ar_ref[span, :], wout_ref[0]).astype(BF16)
    both = do.astype(F32) * o_ref[span, :].astype(F32)
    high = both.astype(BF16)
    rest = (both - high.astype(F32)).astype(BF16)
    centre = dot_nt(pick, high) + dot_nt(pick, rest)
    for pair in range(HEADS // 2):
        qp = qkv_ref[span, pair * 128 : (pair + 1) * 128]
        kp = qkv_ref[span, TILE + pair * 128 : TILE + (pair + 1) * 128]
        vp = qkv_ref[span, 2 * TILE + pair * 128 : 2 * TILE + (pair + 1) * 128]
        dop = do[:, pair * 128 : (pair + 1) * 128]
        zero = jnp.zeros_like(kp)
        mask = head_mask(kp, 0)
        st = dot_nt(jnp.concatenate([jnp.where(mask, kp, zero), jnp.where(mask, zero, kp)], axis=0), qp)
        dpt = dot_nt(jnp.concatenate([jnp.where(mask, vp, zero), jnp.where(mask, zero, vp)], axis=0), dop)
        pts, dsts, dqs = [], [], []
        for e in range(2):
            row = slice(2 * pair + e, 2 * pair + e + 1)
            keys = slice(e * rows, (e + 1) * rows)
            pt = jnp.exp(st[keys] - lse_ref[f, row, :])
            dst = (pt * (dpt[keys] - centre[row, :])).astype(BF16)
            pts.append(pt.astype(BF16))
            dsts.append(dst)
            dqs.append(dot_tn(dst, kp) * SCALE)
        dk = dot(jnp.concatenate(dsts, axis=0), qp)
        dv = dot(jnp.concatenate(pts, axis=0), dop)
        values = (
            jnp.where(mask, dqs[0], dqs[1]),
            jnp.where(mask, dk[:rows], dk[rows:]),
            jnp.where(mask, dv[:rows], dv[rows:]),
        )
        for index, value in enumerate(values):
            at = index * TILE + pair * 128
            dqkv_ref[span, at : at + 128] = value.astype(BF16)


def space_attn_back_kernel(ar_ref, qkv_ref, lse_ref, o_ref, wout_ref, dqkv_ref):
    pick = head_picker()

    @pl.loop(0, lse_ref.shape[0])
    def _(f):
        attn_back_frame(f, ar_ref, qkv_ref, lse_ref, o_ref, wout_ref, pick, dqkv_ref)


def qkv_weights_kernel(order, dqkv_ref, h_ref, keep_ref, send_ref):
    size = h_ref.shape[1] // lax.axis_size("sp")
    turned_columns(h_ref, dqkv_ref, 3, 0, 3 * size, size, order, keep_ref, send_ref)


def finish_kernel(
    dqkv_ref, tok_ref, dxa_ref, own_ref, recv_ref, params_ref, wqkv_ref, small1_ref,
    small2_ref, small3_ref, gtok_ref, out_ref, small_ref, sums_scr,
):
    part = lax.rem(lax.axis_index("sp"), 2)
    frames, half = own_ref.shape[0], own_ref.shape[1]
    rows = 2 * half
    gain = params_ref[0:1, :]
    sums_scr[...] = jnp.zeros_like(sums_scr)

    @pl.loop(0, frames)
    def _(f):
        span = rows_at(f, rows)
        out_ref[f, half_rows(part, half), :] = own_ref[f]
        out_ref[f, half_rows(1 - part, half), :] = recv_ref[f]
        dh = dot_nt(dqkv_ref[span, :], wqkv_ref[0])
        unit, inv = norm(tok_ref[f].astype(F32), gain, params_ref[4:5, :])[1:]
        add_small(sums_scr, [column_sum(dh * unit), column_sum(dh)], False)
        gtok_ref[f] = (dxa_ref[span, :] + norm_back(dh, unit, inv, gain)).astype(BF16)

    small = jnp.concatenate([sums_scr[...], small1_ref[...], small2_ref[...], small3_ref[...]], axis=0)
    small_ref[...] = small.astype(BF16)


def place_of(block, order, sp):
    bits = len(order)
    mixed = jnp.bitwise_xor(block, sp)
    slot = jnp.int32(0)
    for i, b in enumerate(order):
        bit = jnp.bitwise_and(lax.shift_right_logical(mixed, jnp.int32(b)), 1)
        slot = slot + lax.shift_left(bit, jnp.int32(bits - 1 - i))
    return slot


class Place:
    def __init__(self, base, rows, at):
        self.base, self.rows, self.at = base, rows, at


def put_blocks(result, first, size, place, order, keep_ref, send_ref):
    sp = lax.axis_index("sp")
    part = lax.rem(sp, 2)
    low = result.astype(BF16)
    for j in range(result.shape[0] // (2 * size)):
        even = low[2 * j * size : (2 * j + 1) * size]
        odd = low[(2 * j + 1) * size : (2 * j + 2) * size]
        slot = place_of(first + 2 * j, order[1:], sp)
        rows = pl.ds(pl.multiple_of(place.base + slot * place.rows + place.at, 16), size)
        keep_ref[rows, :] = jnp.where(part == 0, even, odd)
        send_ref[rows, :] = jnp.where(part == 0, odd, even)


def turned_columns(h_ref, wide_ref, chunks, base, rows, size, order, keep_ref, send_ref):
    turned = jnp.transpose(h_ref[...])

    @pl.loop(0, chunks)
    def _(j):
        result = dot(turned, wide_ref[:, rows_at(j, TILE)])
        put_blocks(result, jnp.int32(0), size, Place(base, rows, j * size), order, keep_ref, send_ref)


def put_up(h_ref, du_ref, base, rows, order, keep_ref, send_ref):
    size = h_ref.shape[1] // lax.axis_size("sp")
    turned_columns(h_ref, du_ref, du_ref.shape[1] // TILE, base, rows, size, order, keep_ref, send_ref)


def put_down(act_ref, gr_ref, base, order, keep_ref, send_ref):
    size = act_ref.shape[1] // lax.axis_size("sp")

    @pl.loop(0, act_ref.shape[1] // TILE)
    def _(j):
        down = dot_tn(act_ref[:, rows_at(j, TILE)], gr_ref[...])
        put_blocks(down, j * (TILE // size), size, Place(base, size, 0), order, keep_ref, send_ref)


def mlp_weights_kernel(orders, h_ref, du_ref, act_ref, gr_ref, keep_ref, send_ref):
    sp_size = lax.axis_size("sp")
    rows = du_ref.shape[1] // TILE * (h_ref.shape[1] // sp_size)
    put_up(h_ref, du_ref, 0, rows, orders[0], keep_ref, send_ref)
    put_down(act_ref, gr_ref, sp_size // 2 * rows, orders[1], keep_ref, send_ref)


def down_weights_kernel(order, act_ref, own_ref, recv_ref, gr_ref, keep_ref, send_ref):
    part = lax.rem(lax.axis_index("sp"), 2)
    frames, half = own_ref.shape[0], own_ref.shape[1]
    for f in range(frames):
        base = f * 2 * half
        gr_ref[pl.ds(pl.multiple_of(base + part * half, half), half), :] = own_ref[f]
        gr_ref[pl.ds(pl.multiple_of(base + (1 - part) * half, half), half), :] = recv_ref[f]
    put_down(act_ref, gr_ref, 0, order, keep_ref, send_ref)


def up_weights_kernel(order, h_ref, du_ref, o_ref, ar_ref, keep_ref, send_ref):
    size = h_ref.shape[1] // lax.axis_size("sp")
    at = du_ref.shape[1] // TILE * size
    put_up(h_ref, du_ref, 0, at + size, order, keep_ref, send_ref)
    out = dot_tn(o_ref[...], ar_ref[...])
    put_blocks(out, jnp.int32(0), size, Place(0, at + size, at), order, keep_ref, send_ref)


def attn_weights_kernel(order, h_ref, dqkv_ref, o_ref, ar_ref, keep_ref, send_ref):
    size = h_ref.shape[1] // lax.axis_size("sp")
    turned_columns(h_ref, dqkv_ref, 3, 0, 4 * size, size, order, keep_ref, send_ref)
    out = dot_tn(o_ref[...], ar_ref[...])
    put_blocks(out, jnp.int32(0), size, Place(0, 4 * size, 3 * size), order, keep_ref, send_ref)


def fold_kernel(moves, count, *refs):
    outs = refs[2 * count :]
    row_half = lax.rem(lax.axis_index("grp"), 2)
    for source, at, rows, slots, targets, to, split in moves:
        keep, recv = refs[2 * source], refs[2 * source + 1]
        if split == "none":
            span = slice(at, at + rows)
            total = keep[span, :] + recv[span, :]
            for target in targets:
                outs[target][to : to + rows, :] = total
        elif split == "slots":
            half = rows // 2
            for part, target in enumerate(targets):
                span = slice(at + part * half, at + (part + 1) * half)
                outs[target][to : to + half, :] = keep[span, :] + recv[span, :]
        else:
            half = rows // (2 * slots)
            for slot in range(slots):
                for part, target in enumerate(targets):
                    side = row_half if part == 0 else 1 - row_half
                    span = pl.ds(pl.multiple_of(at + 2 * slot * half + side * half, 16), half)
                    place = to + slot * half
                    outs[target][place : place + half, :] = keep[span, :] + recv[span, :]


class Group:
    def __init__(self, sizes, segments, apart=False):
        grp_size, sp_size = sizes
        bits = sp_size.bit_length() - 1
        grp_bits = grp_size.bit_length() - 1
        names = tuple(segments)
        self.halved = grp_bits > 0 and all(
            whole or (height // 2) % 16 == 0 for height, whole, path in segments.values()
        )
        self.segments = {}
        self.state = {}
        for name, (height, whole, path) in segments.items():
            path = [step for step in path if step != ROWS or self.halved] + list(range(4, bits))
            self.segments[name] = (height, whole, path)
            self.state[name] = [sp_size // 2, 1]
        self.stages = []
        for i in range(bits + (1 if self.halved else 0)):
            entries = {}
            for name in names:
                key = (self.segments[name][2][i], name if apart and i == 0 else None)
                entries.setdefault(key, []).append(name)
            stage = []
            for (step, _), who in entries.items():
                stage.append(("grp", grp_size, 0, who, "rows") if step == ROWS else ("sp", sp_size, step, who, "slots"))
            self.stages.append(stage)
        for b in range(1 if self.halved else 0, grp_bits):
            self.stages.append([("grp", grp_size, b, names, "none")])
        if self.halved:
            self.stages.append([("grp", grp_size, 0, names, "none")])
        self.stage = 0
        self.keeps, self.recvs = [], []

    def height(self, name):
        height, whole, _ = self.segments[name]
        slots, cut = self.state[name]
        return height if whole else height // cut * slots

    def start(self, sends):
        self.sends = sends
        self.recvs = [swap(send, *entry[:3]) for send, entry in zip(sends, self.stages[self.stage])]

    def begin(self, keep, send):
        entry = self.stages[0][len(self.keeps)]
        self.keeps.append(keep)
        self.recvs.append(swap(send, *entry[:3]))

    def fold(self):
        places = {}
        for source, entry in enumerate(self.stages[self.stage]):
            at = 0
            for name in entry[3]:
                places[name] = (source, at, self.height(name), self.state[name][0])
                at += self.height(name)
        shapes, moves, keeps, sends = [], [], [], []
        for entry in self.stages[self.stage + 1]:
            split = entry[4]
            keeps.append(len(shapes))
            sends.append(len(shapes) + (0 if split == "none" else 1))
            targets = (keeps[-1],) if split == "none" else (keeps[-1], sends[-1])
            to = 0
            for name in entry[3]:
                whole = self.segments[name][1]
                if split == "slots":
                    self.state[name][0] //= 2
                elif split == "rows":
                    self.state[name][1] = 2
                moves.append(places[name] + (targets, to, "none" if whole else split))
                to += self.height(name)
            shapes += [sds((to, TILE), BF16)] * len(targets)
        args = [x for pair in zip(self.keeps, self.recvs) for x in pair]
        out = call(functools.partial(fold_kernel, moves, len(args) // 2), args, shapes, 0.5, limit=4)
        self.keeps = [out[i] for i in keeps]
        self.sends = [out[i] for i in sends]
        self.stage += 1

    def left(self):
        return len(self.stages) - 1 - self.stage

    def pair(self):
        return self.keeps[0], self.recvs[0]


def result_kernel(sp_size, halved, *refs):
    outs = refs[8:16]
    gain_scr, shift_scr, qkv_scr, out_scr, up_scr, bup_scr, down_scr, bdown_scr = refs[16:24]
    mlp1, both, up0, qkv0 = refs[24:28]
    small_scr, sems = refs[28:]
    size = TILE // sp_size
    chunks = up_scr.shape[2] // TILE
    down_size = chunks * size
    row_half = lax.rem(lax.axis_index("grp"), 2)
    segments = (
        (mlp1, (chunks * size, down_size)), (both, (4 * size, down_size)),
        (up0, (chunks * size + size,)), (qkv0, (3 * size,)),
    )
    for i, (scr, heights) in enumerate(segments):
        mine, other = refs[2 * i], refs[2 * i + 1]
        at = 0
        base = 0
        for height in heights:
            if halved[i]:
                half = height // 2
                for ref, side in ((mine, row_half), (other, 1 - row_half)):
                    place = pl.ds(pl.multiple_of(base + side * half, 16), half)
                    scr[place, :] = ref[at : at + half, :].astype(F32)
                at += half
            else:
                span = slice(at, at + height)
                scr[base : base + height, :] = mine[span, :].astype(F32) + other[span, :].astype(F32)
                at += height
            base += height
    mine, other = refs[6], refs[7]
    at = 3 * size // (2 if halved[3] else 1)
    small = mine[at : at + 32, :].astype(F32)
    small_scr[...] = small if halved[3] else small + other[at : at + 32, :].astype(F32)
    for layer, (qkv, up, down, out, first, last) in enumerate((
        (qkv0, up0, both, up0, 4 * size, chunks * size),
        (both, mlp1, mlp1, both, chunks * size, 3 * size),
    )):
        for j in range(3):
            qkv_scr[layer, :, j * TILE : (j + 1) * TILE] = qkv[j * size : (j + 1) * size, :]
        for j in range(chunks):
            up_scr[layer, :, j * TILE : (j + 1) * TILE] = up[j * size : (j + 1) * size, :]
        down_scr[layer] = down[first : first + down_size, :]
        out_scr[layer] = out[last : last + size, :]
    sp = lax.axis_index("sp")
    back = lax.rem(TILE - sp * size, TILE)
    turned = pltpu.roll(small_scr[...], back, 1)
    for i in range(4):
        gain_scr[i : i + 1, :] = turned[8 * i : 8 * i + 1, :size]
        shift_scr[i : i + 1, :] = turned[8 * i + 1 : 8 * i + 2, :size]
    start = sp * down_size
    line = start // TILE
    back = lax.rem(TILE - lax.rem(start, TILE), TILE)
    for layer in range(2):
        first = 8 + 16 * layer
        bdown_scr[layer : layer + 1, :] = turned[first + 2 : first + 3, :size]
        rows = small_scr[first : first + 8, :]
        lines = lax.broadcasted_iota(jnp.int32, rows.shape, 0)
        picked = jnp.sum(jnp.where(lines == 4 + line, rows, 0.0), axis=0, keepdims=True)
        picked = pltpu.roll(jnp.broadcast_to(picked, rows.shape), back, 1)
        bup_scr[layer : layer + 1, :] = picked[0:1, :down_size]
    scrs = (gain_scr, shift_scr, qkv_scr, out_scr, up_scr, bup_scr, down_scr, bdown_scr)
    copies = [pltpu.make_async_copy(scr, out, sems.at[i]) for i, (scr, out) in enumerate(zip(scrs, outs))]
    for copy in copies:
        copy.start()
    for copy in copies:
        copy.wait()


VMEM = pl.BlockSpec(memory_space=pltpu.VMEM)
SMEM = pl.BlockSpec(memory_space=pltpu.SMEM)
HBM = pl.BlockSpec(memory_space=pltpu.HBM)


def sds(shape, dtype):
    return jax.ShapeDtypeStruct(shape, dtype)


def call(kernel, args, outs, micros, scratch=(), specs=None, out_specs=None, limit=12):
    return pl.pallas_call(
        kernel,
        in_specs=[VMEM] * len(args) if specs is None else specs,
        out_specs=[VMEM] * len(outs) if out_specs is None else out_specs,
        out_shape=outs,
        scratch_shapes=list(scratch),
        compiler_params=pltpu.CompilerParams(vmem_limit_bytes=limit * MIB),
        cost_estimate=pl.CostEstimate(flops=int(micros * COST), bytes_accessed=0, transcendentals=0),
    )(*args)


def swap(array, axis, size, bit):
    return lax.ppermute(array, axis, [(i, i ^ (1 << bit)) for i in range(size)])


def shards(sizes, tokens, frame_slot, norm_gain, norm_shift, w_qkv, w_out, w_up, b_up, w_down, b_down, cotangent):
    grp_size, sp_size = sizes
    frames, patches, width = tokens.shape
    hidden = w_up.shape[2]
    assert GROUP_FRAMES == 2 * frames and sp_size >= 8
    half = patches // 2
    rows = frames * patches
    sp_bits = sp_size.bit_length() - 1
    core_swap = functools.partial(swap, axis="sp", size=sp_size, bit=0)
    slots = sp_size // 2
    size = width // sp_size
    down_size = hidden // sp_size
    def slots_of(path):
        return [step for step in path if step != ROWS] + list(range(4, sp_bits))

    path_up1, path_down1 = (0, 1, 2, ROWS, 3), (0, 2, 1, ROWS, 3)
    path_attn1, path_down0 = (0, ROWS, 2, 1, 3), (0, 2, 1, ROWS, 3)
    path_up0, path_qkv0 = (0, 1, ROWS, 2, 3), (0, 2, 1, ROWS, 3)

    def row_out(cols, dtype=BF16):
        return sds((rows, cols), dtype)

    half_out = sds((frames, half, width), BF16)
    small_out = sds((8, TILE), F32)
    fence = lambda *arrays: lax.optimization_barrier(arrays)

    token = []

    def meet(groups, *arrays):
        recvs = [r for g in groups for r in g.recvs]
        out = list(fence(*arrays, *recvs, *token))
        count = len(arrays)
        arrays, recvs = out[:count], out[count:]
        for g in groups:
            g.recvs = [recvs.pop(0) for _ in g.recvs]
            g.fold()
        sends = [x for g in groups for x in g.sends]
        out = list(fence(*arrays, *sends))
        arrays, sends = out[:count], out[count:]
        for g in groups:
            g.start([sends.pop(0) for _ in g.sends])
        token[:] = [groups[-1].sends[-1]] if groups else []
        return arrays

    def buffers(height):
        return [sds((slots * height, TILE), BF16)] * 2

    cot_recv = core_swap(cotangent)
    packed = jnp.concatenate(
        [norm_gain, norm_shift, b_up.reshape(2 * hidden // width, width), b_down], axis=0
    )
    weights = (w_qkv, w_out, w_up, w_down)
    shapes = [sds(w.shape[1:], BF16) for w in weights]
    out = call(
        space_forward_kernel,
        (tokens, packed) + weights,
        [
            half_out, half_out, row_out(width), row_out(3 * width), sds((frames, HEADS, patches), F32),
            row_out(width), row_out(width, F32), row_out(width), row_out(hidden), row_out(hidden),
        ],
        16,
        scratch=[pltpu.VMEM(tokens.shape, BF16)]
        + [pltpu.VMEM(x.shape, BF16) for x in shapes]
        + [
            pltpu.VMEM((2, patches, width), BF16), pltpu.VMEM((2, patches, 3 * width), BF16),
            pltpu.VMEM((2, patches, width), BF16), pltpu.VMEM((2, patches, width), F32),
            pltpu.VMEM((2, patches, width), BF16),
            pltpu.VMEM((2, patches, hidden), BF16), pltpu.VMEM((2, patches, hidden), BF16),
            pltpu.VMEM((patches, width), F32), pltpu.SemaphoreType.DMA((5,)),
            pltpu.SemaphoreType.DMA((14,)),
        ],
        specs=[HBM, VMEM] + [HBM] * 4,
        out_specs=[VMEM, VMEM, HBM, HBM, VMEM] + [HBM] * 5,
        limit=LIMIT1,
    )
    (x_keep, x_send, h0, qkv0, lse0, o0, xa, h1, act0, slope0) = out
    x_recv = core_swap(x_send)

    place_scratch = [
        pltpu.SMEM((GROUP_FRAMES,), jnp.int32),
        pltpu.VMEM((GROUP_FRAMES, half, width), BF16),
    ]
    (out_own, out_send, xt, h2, qkv1, o1, h3, act1, du1, gr1, dxb, small3, w_qkv1, w_out1) = call(
        time_forward_kernel,
        (frame_slot, x_keep, x_recv, cotangent, cot_recv, packed) + weights,
        [
            half_out, half_out, row_out(width), row_out(width), row_out(3 * width), row_out(width),
            row_out(width), row_out(hidden), row_out(hidden), row_out(width), row_out(width, F32),
            small_out,
        ] + shapes[:2],
        24,
        scratch=place_scratch
        + [pltpu.VMEM((rows // 4, hidden), BF16)]
        + [pltpu.VMEM(x.shape, BF16) for x in shapes[2:]]
        + [pltpu.SemaphoreType.DMA((4,))],
        specs=[SMEM] + [VMEM] * 5 + [HBM] * 4,
        limit=LIMIT2,
    )
    out_recv = core_swap(out_send)

    out = call(
        functools.partial(mlp_weights_kernel, (slots_of(path_up1), slots_of(path_down1))), (h3, du1, act1, gr1),
        buffers(4 * size + down_size), 4.5,
    )
    keep, send, dxb = fence(*out, dxb)
    mlp1 = Group(sizes, {"up": (4 * size, False, path_up1), "down": (down_size, False, path_down1)})
    mlp1.begin(keep, send)

    (dx_own, dx_send, ar1, dqkv1, small2) = call(
        time_backward_kernel,
        (frame_slot, xt, qkv1, dxb, packed, w_qkv1, w_out1),
        [half_out, half_out, row_out(width), row_out(3 * width), small_out],
        8,
        scratch=place_scratch,
        specs=[SMEM] + [VMEM] * 6,
    )
    dx_recv = core_swap(dx_send)
    dx_own, dx_recv, dqkv1, out_recv = meet((mlp1,), dx_own, dx_recv, dqkv1, out_recv)
    keep_attn, send_attn = call(
        functools.partial(attn_weights_kernel, slots_of(path_attn1)), (h2, dqkv1, o1, ar1),
        buffers(4 * size), 2.4,
    )
    gr0, keep_down, send_down = call(
        functools.partial(down_weights_kernel, slots_of(path_down0)), (act0, dx_own, dx_recv),
        [row_out(width)] + buffers(down_size), 2.4,
    )
    (du0, dxa, ar0, small1) = call(
        space_mlp_back_kernel,
        (gr0, xa, slope0, packed, w_up, w_down),
        [row_out(hidden), row_out(width, F32), row_out(width), small_out],
        6,
    )
    keep_up, send_up = call(
        functools.partial(up_weights_kernel, slots_of(path_up0)), (h1, du0, o0, ar0), buffers(5 * size), 3
    )
    keep_attn, send_attn, keep_down, send_down, keep_up, send_up, ar0 = meet(
        (mlp1,), keep_attn, send_attn, keep_down, send_down, keep_up, send_up, ar0
    )
    both = Group(
        sizes,
        {"attn": (4 * size, False, path_attn1), "down": (down_size, False, path_down0)},
        apart=True,
    )
    both.begin(keep_attn, send_attn)
    both.begin(keep_down, send_down)
    up0 = Group(sizes, {"up": (5 * size, False, path_up0)})
    up0.begin(keep_up, send_up)

    (dqkv0,) = call(
        space_attn_back_kernel, (ar0, qkv0, lse0, o0, w_out), [row_out(3 * width)], 10
    )
    (dqkv0,) = meet((up0, both, mlp1), dqkv0)
    out = call(
        functools.partial(qkv_weights_kernel, slots_of(path_qkv0)), (dqkv0, h0), buffers(3 * size), 2
    )
    keep, send, dqkv0 = fence(*out, dqkv0)
    qkv = Group(
        sizes, {"qkv": (3 * size, False, path_qkv0), "small": (32, True, path_qkv0)}, apart=True
    )
    qkv.begin(keep, send)
    grad_tokens, output, small = call(
        finish_kernel,
        (
            dqkv0, tokens, dxa, out_own, out_recv, packed, w_qkv, small1, small2, small3,
        ),
        [sds(tokens.shape, BF16), sds(tokens.shape, BF16), sds((32, TILE), BF16)],
        4,
        scratch=[pltpu.VMEM((8, TILE), F32)],
    )
    (small,) = fence(small)
    qkv.begin(small, small)
    everyone = (mlp1, both, up0, qkv)
    for names in TAIL:
        groups = [g for g in (dict(zip("mbuq", everyone))[c] for c in names) if g.left()]
        if groups:
            meet(groups)
    while any(g.left() for g in everyone):
        meet([g for g in everyone if g.left()])
    finals = [
        sds((4, size), F32), sds((4, size), F32), sds((2, size, 3 * width), F32), sds((2, size, width), F32),
        sds((2, size, hidden), F32), sds((2, down_size), F32), sds((2, down_size, width), F32),
        sds((2, size), F32),
    ]
    heights = (4 * size + down_size, 4 * size + down_size, 5 * size, 3 * size)
    results = call(
        functools.partial(result_kernel, sp_size, tuple(g.halved for g in everyone)),
        [x for g in everyone for x in g.pair()], finals, 2,
        scratch=[pltpu.VMEM(f.shape, F32) for f in finals]
        + [pltpu.VMEM((h, TILE), F32) for h in heights]
        + [pltpu.VMEM((32, TILE), F32), pltpu.SemaphoreType.DMA((8,))],
        out_specs=[HBM] * 8,
    )
    return (output, grad_tokens, *results)


def solution(mesh):
    rows = P(("grp", "sp"), None, None)
    in_specs = (rows, P("grp", None), P(), P(), P(), P(), P(), P(), P(), P(), rows)
    out_specs = (
        rows, rows, P(None, "sp"), P(None, "sp"), P(None, "sp", None), P(None, "sp", None),
        P(None, "sp", None), P(None, "sp"), P(None, "sp", None), P(None, "sp"),
    )
    body = functools.partial(shards, (mesh.shape["grp"], mesh.shape["sp"]))
    return jax.shard_map(body, mesh=mesh, in_specs=in_specs, out_specs=out_specs, check_vma=False)
```

```python
import functools

import jax
import jax.numpy as jnp
from jax import lax
from jax.experimental import pallas as pl
from jax.experimental.pallas import tpu as pltpu
from jax.sharding import PartitionSpec as P

HEADS = 8
HEAD = 64
VIDEO_STEPS = 6
GROUP_FRAMES = 8
NORM_EPS = 1e-05
TILE = 512
STEP = 1024
SCALE = HEAD**-0.5
TANH_A = 0.7978845608028654
TANH_B = TANH_A * 0.044715
PAIRS = [(t, s) for t in range(VIDEO_STEPS) for s in range(t + 1)]
F32 = jnp.float32
BF16 = jnp.bfloat16
MIB = 1024 * 1024
ROWS = -1
COST = 1.15e9 * 0.02
TAIL = ("q", "bu", "qm", "bu", "qm", "bu", "qm", "bu", "q")
LIMIT1 = 52
LIMIT2 = 24


def dot(left, right):
    return jnp.dot(left, right, preferred_element_type=F32)


def dot_nt(left, right):
    return lax.dot_general(left, right, (((1,), (1,)), ((), ())), preferred_element_type=F32)


def dot_tn(left, right):
    return lax.dot_general(left, right, (((0,), (0,)), ((), ())), preferred_element_type=F32)


def norm(rows, gain, shift):
    centred = rows - jnp.mean(rows, axis=-1, keepdims=True)
    inv = lax.rsqrt(jnp.mean(centred * centred, axis=-1, keepdims=True) + NORM_EPS)
    unit = centred * inv
    return unit * gain + shift, unit, inv


def norm_back(grad, unit, inv, gain):
    grad_unit = grad * gain
    mean_grad = jnp.mean(grad_unit, axis=-1, keepdims=True)
    mean_both = jnp.mean(grad_unit * unit, axis=-1, keepdims=True)
    return inv * (grad_unit - mean_grad - unit * mean_both)


def column_sum(rows):
    return jnp.sum(rows, axis=0, keepdims=True)


def gelu_pair(u):
    square = u * u
    sigma = 0.5 + 0.5 * jnp.tanh(u * (TANH_A + TANH_B * square))
    act = u * sigma
    slope = sigma + act * (1.0 - sigma) * (2.0 * TANH_A + 6.0 * TANH_B * square)
    return act.astype(BF16), slope.astype(BF16)


def head_mask(lanes, which):
    lane = lax.broadcasted_iota(jnp.int32, lanes.shape, 1)
    return (lane < HEAD) if which == 0 else (lane >= HEAD)


def qkv_rows(normed, weight):
    out = []
    for part in range(3):
        piece = dot(normed, weight[:, part * TILE : (part + 1) * TILE])
        if part == 0:
            out.append(piece.astype(BF16) * BF16(SCALE))
        else:
            out.append(piece.astype(BF16))
    return out


def mlp_forward(normed, w_up, b_up, w_down, rows, act_ref, slope_ref):
    chunks = w_up.shape[1] // STEP
    up = lambda j: dot(normed, w_up[:, j * STEP : (j + 1) * STEP])
    total = None
    u = up(0)
    for j in range(chunks):
        cols = slice(j * STEP, (j + 1) * STEP)
        later = up(j + 1) if j + 1 < chunks else None
        act, slope = gelu_pair(u + b_up[0:1, cols])
        act_ref[rows, cols] = act
        slope_ref[rows, cols] = slope
        piece = dot(act, w_down[cols, :])
        total = piece if total is None else total + piece
        u = later
    return total


def mlp_backward(grad_low, w_up, w_down, rows, slope_ref, du_ref):
    chunks = w_up.shape[1] // STEP
    down = lambda j: dot_nt(grad_low, w_down[j * STEP : (j + 1) * STEP, :])
    total = None
    sums = []
    da = down(0)
    for j in range(chunks):
        cols = slice(j * STEP, (j + 1) * STEP)
        later = down(j + 1) if j + 1 < chunks else None
        du = (da * slope_ref[rows, cols].astype(F32)).astype(BF16)
        du_ref[rows, cols] = du
        sums.append(column_sum(du.astype(F32)))
        piece = dot_nt(du, w_up[:, cols])
        total = piece if total is None else total + piece
        da = later
    return total, [x[:, k : k + TILE] for x in sums for k in range(0, STEP, TILE)]


def add_small(small_ref, values, first):
    for i, value in enumerate(values):
        row = slice(i, i + 1) if i < 4 else slice(i, i + 1)
        if value is None:
            continue
        if first:
            small_ref[row, :] = value
        else:
            small_ref[row, :] += value


def rows_at(index, count):
    return pl.ds(pl.multiple_of(index * count, count), count)


def half_rows(part, half):
    return pl.ds(pl.multiple_of(part * half, half), half)


def space_forward_kernel(
    tok_hbm, params_ref, wqkv_hbm, wout_hbm, wup_hbm, wdown_hbm,
    keep_ref, send_ref, h0_hbm, qkv_hbm, lse_ref, o_hbm, xa_hbm, h1_hbm, act_hbm, slope_hbm,
    tok_ref, wqkv_ref, wout_ref, wup_ref, wdown_ref, h0_scr, qkv_scr, o_scr, xa_scr, h1_scr, act_scr,
    slope_scr, x1_scr, in_sems, out_sems,
):
    pairs = [
        (tok_hbm, tok_ref), (wqkv_hbm.at[0], wqkv_ref), (wout_hbm.at[0], wout_ref),
        (wup_hbm.at[0], wup_ref), (wdown_hbm.at[0], wdown_ref),
    ]
    copies = [pltpu.make_async_copy(src, dst, in_sems.at[i]) for i, (src, dst) in enumerate(pairs)]
    for copy in copies[:2]:
        copy.start()
    gain_ref, shift_ref = params_ref.at[0:4, 0:TILE], params_ref.at[4:8, 0:TILE]
    part = lax.rem(lax.axis_index("sp"), 2)
    frames, rows = tok_ref.shape[0], tok_ref.shape[1]
    half = rows // 2
    lane = lax.broadcasted_iota(jnp.int32, (rows, 128), 1)
    places = (
        (h0_scr, h0_hbm), (qkv_scr, qkv_hbm), (o_scr, o_hbm), (xa_scr, xa_hbm), (h1_scr, h1_hbm),
        (act_scr, act_hbm), (slope_scr, slope_hbm),
    )

    def spills(f):
        now = lax.rem(f, 2)
        return [
            pltpu.make_async_copy(scr.at[now], hbm.at[rows_at(f, rows)], out_sems.at[7 * now + i])
            for i, (scr, hbm) in enumerate(places)
        ]

    def await_first(f, *which):
        @pl.when(f == 0)
        def _():
            for i in which:
                copies[i].wait()

    copies[0].wait()
    for copy in copies[2:]:
        copy.start()

    @pl.loop(0, frames)
    def _(f):
        now = lax.rem(f, 2)
        spill = spills(f)

        @pl.when(f >= 2)
        def _():
            for copy in spills(f - 2):
                copy.wait()

        x0 = tok_ref[f].astype(F32)
        h0 = norm(x0, gain_ref[0:1, :], shift_ref[0:1, :])[0].astype(BF16)
        h0_scr[now] = h0
        spill[0].start()
        await_first(f, 1)
        q, k, v = qkv_rows(h0, wqkv_ref)
        qkv_scr[now, :, 0:TILE] = q
        qkv_scr[now, :, TILE : 2 * TILE] = k
        qkv_scr[now, :, 2 * TILE :] = v
        spill[1].start()
        lse_all = jnp.zeros((rows, 128), F32)
        mixed = []
        for pair in range(HEADS // 2):
            cols = slice(pair * 128, (pair + 1) * 128)
            qp, kp, vp = q[:, cols], k[:, cols], v[:, cols]
            zero = jnp.zeros_like(qp)
            mask = head_mask(qp, 0)
            s = dot_nt(jnp.concatenate([jnp.where(mask, qp, zero), jnp.where(mask, zero, qp)], axis=0), kp)
            top = jnp.max(s, axis=-1, keepdims=True)
            p = jnp.exp(s - top)
            total = jnp.sum(p, axis=-1, keepdims=True)
            both = dot(p.astype(BF16), vp) * (1.0 / total)
            lse = top + jnp.log(total)
            lse_all = jnp.where(lane == 2 * pair, lse[:rows], lse_all)
            lse_all = jnp.where(lane == 2 * pair + 1, lse[rows:], lse_all)
            mixed.append(jnp.where(mask, both[:rows], both[rows:]).astype(BF16))
        lse_ref[f] = jnp.transpose(lse_all)[0:HEADS, :]
        o = jnp.concatenate(mixed, axis=1)
        o_scr[now] = o
        spill[2].start()
        await_first(f, 2)
        xa = x0 + dot(o, wout_ref[...])
        xa_scr[now] = xa
        spill[3].start()
        h1 = norm(xa, gain_ref[1:2, :], shift_ref[1:2, :])[0].astype(BF16)
        h1_scr[now] = h1
        spill[4].start()
        await_first(f, 3, 4)
        branch = mlp_forward(
            h1, wup_ref, params_ref.at[8:9], wdown_ref, slice(None), act_scr.at[now], slope_scr.at[now]
        )
        spill[5].start()
        spill[6].start()
        x1_scr[...] = xa + branch + params_ref[10:11, 0:TILE]
        keep_ref[f] = x1_scr[half_rows(part, half), :].astype(BF16)
        send_ref[f] = x1_scr[half_rows(1 - part, half), :].astype(BF16)

    for f in (frames - 2, frames - 1):
        for copy in spills(jnp.int32(f)):
            copy.wait()


def lane_heads(dtype):
    c = lax.broadcasted_iota(jnp.int32, (TILE, 128), 0)
    h = lax.broadcasted_iota(jnp.int32, (TILE, 128), 1)
    return (c // HEAD == h).astype(dtype)


def slot_places(slots_ref, where_scr, frames):
    sp = lax.axis_index("sp")
    group = (sp * frames) // GROUP_FRAMES
    part = lax.rem(sp, GROUP_FRAMES // frames)
    for t in range(GROUP_FRAMES):
        where_scr[slots_ref[group, t]] = lax.rem(t + GROUP_FRAMES - part * frames, GROUP_FRAMES)


def time_scores(q, k, spread):
    parts = []
    for t, s in PAIRS:
        parts.append((q[t] * k[s]).astype(BF16))
    return dot(jnp.concatenate(parts, axis=0), spread)


def time_probs(scores, count):
    blocks = [scores[i * count : (i + 1) * count] for i in range(len(PAIRS))]
    probs = []
    at = 0
    for t in range(VIDEO_STEPS):
        mine = blocks[at : at + t + 1]
        at += t + 1
        top = functools.reduce(jnp.maximum, mine)
        raw = [jnp.exp(b - top) for b in mine]
        inv = 1.0 / functools.reduce(lambda a, b: a + b, raw)
        probs.extend([r * inv for r in raw])
    return probs


def split_slots(rows):
    count = rows.shape[0] // GROUP_FRAMES
    return [rows[s * count : (s + 1) * count].astype(F32) for s in range(GROUP_FRAMES)]


def time_forward_kernel(
    slots_ref, keep_ref, recv_ref, cot_ref, cotr_ref, params_ref,
    wqkv_hbm, wout_hbm, wup_hbm, wdown_hbm,
    own_ref, send_ref, x_ref, h2_ref, qkv_ref, o_ref, h3_ref, act_ref, du_ref, gr_ref, dxb_ref,
    small_ref, wqkv_ref, wout_ref,
    where_scr, both_scr, slope_scr, wup_ref, wdown_ref, in_sems,
):
    pairs = [(wqkv_hbm, wqkv_ref), (wout_hbm, wout_ref), (wup_hbm, wup_ref), (wdown_hbm, wdown_ref)]
    copies = [pltpu.make_async_copy(src.at[1], dst, in_sems.at[i]) for i, (src, dst) in enumerate(pairs)]
    for copy in copies:
        copy.start()
    gain_ref, shift_ref = params_ref.at[0:4, 0:TILE], params_ref.at[4:8, 0:TILE]
    frames, half = keep_ref.shape[0], keep_ref.shape[1]
    part = lax.rem(lax.axis_index("sp"), GROUP_FRAMES // frames)
    slot_places(slots_ref, where_scr, frames)
    small_ref[...] = jnp.zeros_like(small_ref)
    both_scr[0:frames] = keep_ref[...]
    both_scr[frames:] = recv_ref[...]
    spread = lane_heads(BF16)
    steps = 4
    count = half // steps
    step_rows = count * GROUP_FRAMES

    def await_first(i, *which):
        @pl.when(i == 0)
        def _():
            for w in which:
                copies[w].wait()

    @pl.loop(0, steps)
    def _(i):
        span = rows_at(i, step_rows)
        place = rows_at(i, count)
        x_low = jnp.concatenate([both_scr[where_scr[s], place] for s in range(GROUP_FRAMES)], axis=0)
        x_ref[span, :] = x_low
        x = x_low.astype(F32)
        h2 = norm(x, gain_ref[2:3, :], shift_ref[2:3, :])[0].astype(BF16)
        h2_ref[span, :] = h2
        await_first(i, 0)
        q, k, v = qkv_rows(h2, wqkv_ref)
        qkv_ref[span, 0:TILE] = q
        qkv_ref[span, TILE : 2 * TILE] = k
        qkv_ref[span, 2 * TILE :] = v
        qs, ks, vs = split_slots(q), split_slots(k), split_slots(v)
        probs = time_probs(time_scores(qs, ks, spread), count)
        wide = dot_nt(jnp.concatenate([p.astype(BF16) for p in probs], axis=0), spread)
        mixed = []
        at = 0
        for t in range(VIDEO_STEPS):
            total = None
            for s in range(t + 1):
                piece = wide[at * count : (at + 1) * count] * vs[s]
                total = piece if total is None else total + piece
                at += 1
            mixed.append(total)
        mixed.extend(vs[VIDEO_STEPS:])
        o = jnp.concatenate([m.astype(BF16) for m in mixed], axis=0)
        o_ref[span, :] = o
        await_first(i, 1)
        xb = x + dot(o, wout_ref[...]).astype(BF16).astype(F32)
        h3, unit, inv = norm(xb, gain_ref[3:4, :], shift_ref[3:4, :])
        h3 = h3.astype(BF16)
        h3_ref[span, :] = h3
        slope = slope_scr
        await_first(i, 2, 3)
        branch = mlp_forward(h3, wup_ref, params_ref.at[9:10], wdown_ref, span, act_ref, SpanView(slope))
        out = (xb + branch + params_ref[11:12, 0:TILE]).astype(BF16)
        for s in range(GROUP_FRAMES):
            both_scr[where_scr[s], place] = out[s * count : (s + 1) * count]
        grad_low = jnp.concatenate(
            [cot_slot(cot_ref, cotr_ref, where_scr[s], part * half + i * count, count) for s in range(GROUP_FRAMES)],
            axis=0,
        )
        gr_ref[span, :] = grad_low
        grad = grad_low.astype(F32)
        dh, sums = mlp_backward(grad_low, wup_ref, wdown_ref, span, SpanView(slope), du_ref)
        add_small(small_ref, [column_sum(dh * unit), column_sum(dh), column_sum(grad), None] + sums, False)
        dxb_ref[span, :] = grad + norm_back(dh, unit, inv, gain_ref[3:4, :])

    own_ref[...] = both_scr[0:frames]
    send_ref[...] = both_scr[frames:]


class SpanView:
    def __init__(self, ref):
        self.ref = ref

    def __getitem__(self, index):
        return self.ref[:, index[1]]

    def __setitem__(self, index, value):
        self.ref[:, index[1]] = value


def cot_slot(cot_ref, cotr_ref, frame, start, count):
    frames = cot_ref.shape[0]
    places = pl.ds(pl.multiple_of(start, count), count)
    mine = cot_ref[lax.rem(frame, frames), places, :]
    other = cotr_ref[lax.rem(frame, frames), places, :]
    return jnp.where(frame < frames, mine, other)


def time_backward_kernel(
    slots_ref, x_ref, qkv_ref, dxb_ref, params_ref, wqkv_ref, wout_ref,
    own_ref, send_ref, ar_ref, dqkv_ref, small_ref,
    where_scr, both_scr,
):
    frames, half = own_ref.shape[0], own_ref.shape[1]
    slot_places(slots_ref, where_scr, frames)
    small_ref[...] = jnp.zeros_like(small_ref)
    spread = lane_heads(BF16)
    steps = 4
    count = half // steps
    step_rows = count * GROUP_FRAMES
    gain = params_ref[2:3, 0:TILE]

    @pl.loop(0, steps)
    def _(i):
        span = rows_at(i, step_rows)
        place = rows_at(i, count)
        dxb = dxb_ref[span, :]
        ar = dxb.astype(BF16)
        ar_ref[span, :] = ar
        do = split_slots(dot_nt(ar, wout_ref[...]).astype(BF16))
        qs = split_slots(qkv_ref[span, 0:TILE])
        ks = split_slots(qkv_ref[span, TILE : 2 * TILE])
        vs = split_slots(qkv_ref[span, 2 * TILE :])
        probs = time_probs(time_scores(qs, ks, spread), count)
        dps = time_scores(do, vs, spread)
        dps = [dps[j * count : (j + 1) * count] for j in range(len(PAIRS))]
        dss = []
        at = 0
        for t in range(VIDEO_STEPS):
            centre = functools.reduce(
                lambda a, b: a + b, [probs[at + s] * dps[at + s] for s in range(t + 1)]
            )
            dss.extend([probs[at + s] * (dps[at + s] - centre) for s in range(t + 1)])
            at += t + 1
        wide_p = dot_nt(jnp.concatenate([p.astype(BF16) for p in probs], axis=0), spread)
        wide_ds = dot_nt(jnp.concatenate([d.astype(BF16) for d in dss], axis=0), spread)
        dq = [None] * GROUP_FRAMES
        dk = [None] * GROUP_FRAMES
        dv = [None] * GROUP_FRAMES

        def add(table, index, piece):
            table[index] = piece if table[index] is None else table[index] + piece

        for j, (t, s) in enumerate(PAIRS):
            rows = slice(j * count, (j + 1) * count)
            add(dq, t, wide_ds[rows] * ks[s])
            add(dk, s, wide_ds[rows] * qs[t])
            add(dv, s, wide_p[rows] * do[t])
        for t in range(VIDEO_STEPS, GROUP_FRAMES):
            dq[t] = jnp.zeros_like(do[t])
            dk[t] = jnp.zeros_like(do[t])
            dv[t] = do[t]
        dq = jnp.concatenate([(d * SCALE).astype(BF16) for d in dq], axis=0)
        dk = jnp.concatenate([d.astype(BF16) for d in dk], axis=0)
        dv = jnp.concatenate([d.astype(BF16) for d in dv], axis=0)
        dqkv_ref[span, 0:TILE] = dq
        dqkv_ref[span, TILE : 2 * TILE] = dk
        dqkv_ref[span, 2 * TILE :] = dv
        dh = dot_nt(dqkv_ref[span, :], wqkv_ref[...])
        unit, inv = norm(x_ref[span, :].astype(F32), gain, params_ref[6:7, 0:TILE])[1:]
        add_small(small_ref, [column_sum(dh * unit), column_sum(dh)], False)
        dxp = norm_back(dh, unit, inv, gain).astype(BF16).astype(F32)
        dx1 = (dxb + dxp).astype(BF16)
        for s in range(GROUP_FRAMES):
            both_scr[where_scr[s], place] = dx1[s * count : (s + 1) * count]

    own_ref[...] = both_scr[0:frames]
    send_ref[...] = both_scr[frames:]


def space_mlp_back_kernel(
    gr_ref, xa_ref, slope_ref, params_ref, wup_ref, wdown_ref,
    du_ref, dxa_ref, ar_ref, small_ref,
):
    small_ref[...] = jnp.zeros_like(small_ref)
    rows = 256
    gain = params_ref[1:2, 0:TILE]

    @pl.loop(0, gr_ref.shape[0] // rows)
    def _(f):
        span = rows_at(f, rows)
        grad_low = gr_ref[span, :]
        grad = grad_low.astype(F32)
        dh, sums = mlp_backward(grad_low, wup_ref.at[0], wdown_ref.at[0], span, slope_ref, du_ref)
        unit, inv = norm(xa_ref[span, :], gain, params_ref[5:6, 0:TILE])[1:]
        add_small(small_ref, [column_sum(dh * unit), column_sum(dh), column_sum(grad), None] + sums, False)
        dxa = grad + norm_back(dh, unit, inv, gain)
        dxa_ref[span, :] = dxa
        ar_ref[span, :] = dxa.astype(BF16)


def head_picker():
    h = lax.broadcasted_iota(jnp.int32, (HEADS, TILE), 0)
    c = lax.broadcasted_iota(jnp.int32, (HEADS, TILE), 1)
    return (c // HEAD == h).astype(BF16)


def attn_back_frame(f, ar_ref, qkv_ref, lse_ref, o_ref, wout_ref, pick, dqkv_ref):
    rows = lse_ref.shape[2]
    span = rows_at(f, rows)
    do = dot_nt(ar_ref[span, :], wout_ref[0]).astype(BF16)
    both = do.astype(F32) * o_ref[span, :].astype(F32)
    high = both.astype(BF16)
    rest = (both - high.astype(F32)).astype(BF16)
    centre = dot_nt(pick, high) + dot_nt(pick, rest)
    for pair in range(HEADS // 2):
        qp = qkv_ref[span, pair * 128 : (pair + 1) * 128]
        kp = qkv_ref[span, TILE + pair * 128 : TILE + (pair + 1) * 128]
        vp = qkv_ref[span, 2 * TILE + pair * 128 : 2 * TILE + (pair + 1) * 128]
        dop = do[:, pair * 128 : (pair + 1) * 128]
        zero = jnp.zeros_like(kp)
        mask = head_mask(kp, 0)
        st = dot_nt(jnp.concatenate([jnp.where(mask, kp, zero), jnp.where(mask, zero, kp)], axis=0), qp)
        dpt = dot_nt(jnp.concatenate([jnp.where(mask, vp, zero), jnp.where(mask, zero, vp)], axis=0), dop)
        pts, dsts, dqs = [], [], []
        for e in range(2):
            row = slice(2 * pair + e, 2 * pair + e + 1)
            keys = slice(e * rows, (e + 1) * rows)
            pt = jnp.exp(st[keys] - lse_ref[f, row, :])
            dst = (pt * (dpt[keys] - centre[row, :])).astype(BF16)
            pts.append(pt.astype(BF16))
            dsts.append(dst)
            dqs.append(dot_tn(dst, kp) * SCALE)
        dk = dot(jnp.concatenate(dsts, axis=0), qp)
        dv = dot(jnp.concatenate(pts, axis=0), dop)
        values = (
            jnp.where(mask, dqs[0], dqs[1]),
            jnp.where(mask, dk[:rows], dk[rows:]),
            jnp.where(mask, dv[:rows], dv[rows:]),
        )
        for index, value in enumerate(values):
            at = index * TILE + pair * 128
            dqkv_ref[span, at : at + 128] = value.astype(BF16)


def space_attn_back_kernel(ar_ref, qkv_ref, lse_ref, o_ref, wout_ref, dqkv_ref):
    pick = head_picker()

    @pl.loop(0, lse_ref.shape[0])
    def _(f):
        attn_back_frame(f, ar_ref, qkv_ref, lse_ref, o_ref, wout_ref, pick, dqkv_ref)


def qkv_weights_kernel(order, dqkv_ref, h_ref, keep_ref, send_ref):
    size = h_ref.shape[1] // lax.axis_size("sp")
    turned_columns(h_ref, dqkv_ref, 3, 0, 3 * size, size, order, keep_ref, send_ref)


def finish_kernel(
    dqkv_ref, tok_ref, dxa_ref, own_ref, recv_ref, params_ref, wqkv_ref, small1_ref,
    small2_ref, small3_ref, gtok_ref, out_ref, small_ref, sums_scr,
):
    part = lax.rem(lax.axis_index("sp"), 2)
    frames, half = own_ref.shape[0], own_ref.shape[1]
    rows = 2 * half
    gain = params_ref[0:1, 0:TILE]
    sums_scr[...] = jnp.zeros_like(sums_scr)

    @pl.loop(0, frames)
    def _(f):
        span = rows_at(f, rows)
        out_ref[f, half_rows(part, half), :] = own_ref[f]
        out_ref[f, half_rows(1 - part, half), :] = recv_ref[f]
        dh = dot_nt(dqkv_ref[span, :], wqkv_ref[0])
        unit, inv = norm(tok_ref[f].astype(F32), gain, params_ref[4:5, 0:TILE])[1:]
        add_small(sums_scr, [column_sum(dh * unit), column_sum(dh)], False)
        gtok_ref[f] = (dxa_ref[span, :] + norm_back(dh, unit, inv, gain)).astype(BF16)

    small = jnp.concatenate([sums_scr[...], small1_ref[...], small2_ref[...], small3_ref[...]], axis=0)
    small_ref[...] = small.astype(BF16)


def place_of(block, order, sp):
    bits = len(order)
    mixed = jnp.bitwise_xor(block, sp)
    slot = jnp.int32(0)
    for i, b in enumerate(order):
        bit = jnp.bitwise_and(lax.shift_right_logical(mixed, jnp.int32(b)), 1)
        slot = slot + lax.shift_left(bit, jnp.int32(bits - 1 - i))
    return slot


class Place:
    def __init__(self, base, rows, at):
        self.base, self.rows, self.at = base, rows, at


def put_blocks(result, first, size, place, order, keep_ref, send_ref):
    sp = lax.axis_index("sp")
    part = lax.rem(sp, 2)
    low = result.astype(BF16)
    for j in range(result.shape[0] // (2 * size)):
        even = low[2 * j * size : (2 * j + 1) * size]
        odd = low[(2 * j + 1) * size : (2 * j + 2) * size]
        slot = place_of(first + 2 * j, order[1:], sp)
        rows = pl.ds(pl.multiple_of(place.base + slot * place.rows + place.at, 16), size)
        keep_ref[rows, :] = jnp.where(part == 0, even, odd)
        send_ref[rows, :] = jnp.where(part == 0, odd, even)


def turned_columns(h_ref, wide_ref, chunks, base, rows, size, order, keep_ref, send_ref):
    turned = jnp.transpose(h_ref[...])
    for j in range(chunks):
        result = dot(turned, wide_ref[:, j * TILE : (j + 1) * TILE])
        put_blocks(result, jnp.int32(0), size, Place(base, rows, j * size), order, keep_ref, send_ref)


def put_up(h_ref, du_ref, base, rows, order, keep_ref, send_ref):
    size = h_ref.shape[1] // lax.axis_size("sp")
    turned_columns(h_ref, du_ref, du_ref.shape[1] // TILE, base, rows, size, order, keep_ref, send_ref)


def put_down(act_ref, gr_ref, base, order, keep_ref, send_ref):
    size = act_ref.shape[1] // lax.axis_size("sp")
    for j in range(act_ref.shape[1] // TILE):
        down = dot_tn(act_ref[:, j * TILE : (j + 1) * TILE], gr_ref[...])
        put_blocks(down, jnp.int32(j * (TILE // size)), size, Place(base, size, 0), order, keep_ref, send_ref)


def mlp_weights_kernel(orders, h_ref, du_ref, act_ref, gr_ref, keep_ref, send_ref):
    sp_size = lax.axis_size("sp")
    rows = du_ref.shape[1] // TILE * (h_ref.shape[1] // sp_size)
    put_up(h_ref, du_ref, 0, rows, orders[0], keep_ref, send_ref)
    put_down(act_ref, gr_ref, sp_size // 2 * rows, orders[1], keep_ref, send_ref)


def down_weights_kernel(order, act_ref, own_ref, recv_ref, gr_ref, keep_ref, send_ref):
    part = lax.rem(lax.axis_index("sp"), 2)
    frames, half = own_ref.shape[0], own_ref.shape[1]
    for f in range(frames):
        base = f * 2 * half
        gr_ref[pl.ds(pl.multiple_of(base + part * half, half), half), :] = own_ref[f]
        gr_ref[pl.ds(pl.multiple_of(base + (1 - part) * half, half), half), :] = recv_ref[f]
    put_down(act_ref, gr_ref, 0, order, keep_ref, send_ref)


def up_weights_kernel(order, h_ref, du_ref, o_ref, ar_ref, keep_ref, send_ref):
    size = h_ref.shape[1] // lax.axis_size("sp")
    at = du_ref.shape[1] // TILE * size
    put_up(h_ref, du_ref, 0, at + size, order, keep_ref, send_ref)
    out = dot_tn(o_ref[...], ar_ref[...])
    put_blocks(out, jnp.int32(0), size, Place(0, at + size, at), order, keep_ref, send_ref)


def attn_weights_kernel(order, h_ref, dqkv_ref, o_ref, ar_ref, keep_ref, send_ref):
    size = h_ref.shape[1] // lax.axis_size("sp")
    turned_columns(h_ref, dqkv_ref, 3, 0, 4 * size, size, order, keep_ref, send_ref)
    out = dot_tn(o_ref[...], ar_ref[...])
    put_blocks(out, jnp.int32(0), size, Place(0, 4 * size, 3 * size), order, keep_ref, send_ref)


def fold_kernel(moves, count, *refs):
    outs = refs[2 * count :]
    row_half = lax.rem(lax.axis_index("grp"), 2)
    for source, at, rows, slots, targets, to, split in moves:
        keep, recv = refs[2 * source], refs[2 * source + 1]
        if split == "none":
            span = slice(at, at + rows)
            total = keep[span, :] + recv[span, :]
            for target in targets:
                outs[target][to : to + rows, :] = total
        elif split == "slots":
            half = rows // 2
            for part, target in enumerate(targets):
                span = slice(at + part * half, at + (part + 1) * half)
                outs[target][to : to + half, :] = keep[span, :] + recv[span, :]
        else:
            half = rows // (2 * slots)
            for slot in range(slots):
                for part, target in enumerate(targets):
                    side = row_half if part == 0 else 1 - row_half
                    span = pl.ds(pl.multiple_of(at + 2 * slot * half + side * half, 16), half)
                    place = to + slot * half
                    outs[target][place : place + half, :] = keep[span, :] + recv[span, :]


class Group:
    def __init__(self, sizes, segments, apart=False):
        grp_size, sp_size = sizes
        bits = sp_size.bit_length() - 1
        grp_bits = grp_size.bit_length() - 1
        names = tuple(segments)
        self.halved = grp_bits > 0 and all(
            whole or (height // 2) % 16 == 0 for height, whole, path in segments.values()
        )
        self.segments = {}
        self.state = {}
        for name, (height, whole, path) in segments.items():
            path = [step for step in path if step != ROWS or self.halved] + list(range(4, bits))
            self.segments[name] = (height, whole, path)
            self.state[name] = [sp_size // 2, 1]
        self.stages = []
        for i in range(bits + (1 if self.halved else 0)):
            entries = {}
            for name in names:
                key = (self.segments[name][2][i], name if apart and i == 0 else None)
                entries.setdefault(key, []).append(name)
            stage = []
            for (step, _), who in entries.items():
                stage.append(("grp", grp_size, 0, who, "rows") if step == ROWS else ("sp", sp_size, step, who, "slots"))
            self.stages.append(stage)
        for b in range(1 if self.halved else 0, grp_bits):
            self.stages.append([("grp", grp_size, b, names, "none")])
        if self.halved:
            self.stages.append([("grp", grp_size, 0, names, "none")])
        self.stage = 0
        self.keeps, self.recvs = [], []

    def height(self, name):
        height, whole, _ = self.segments[name]
        slots, cut = self.state[name]
        return height if whole else height // cut * slots

    def start(self, sends):
        self.sends = sends
        self.recvs = [swap(send, *entry[:3]) for send, entry in zip(sends, self.stages[self.stage])]

    def begin(self, keep, send):
        entry = self.stages[0][len(self.keeps)]
        self.keeps.append(keep)
        self.recvs.append(swap(send, *entry[:3]))

    def fold(self):
        places = {}
        for source, entry in enumerate(self.stages[self.stage]):
            at = 0
            for name in entry[3]:
                places[name] = (source, at, self.height(name), self.state[name][0])
                at += self.height(name)
        shapes, moves, keeps, sends = [], [], [], []
        for entry in self.stages[self.stage + 1]:
            split = entry[4]
            keeps.append(len(shapes))
            sends.append(len(shapes) + (0 if split == "none" else 1))
            targets = (keeps[-1],) if split == "none" else (keeps[-1], sends[-1])
            to = 0
            for name in entry[3]:
                whole = self.segments[name][1]
                if split == "slots":
                    self.state[name][0] //= 2
                elif split == "rows":
                    self.state[name][1] = 2
                moves.append(places[name] + (targets, to, "none" if whole else split))
                to += self.height(name)
            shapes += [sds((to, TILE), BF16)] * len(targets)
        args = [x for pair in zip(self.keeps, self.recvs) for x in pair]
        out = call(functools.partial(fold_kernel, moves, len(args) // 2), args, shapes, 0.5, limit=4)
        self.keeps = [out[i] for i in keeps]
        self.sends = [out[i] for i in sends]
        self.stage += 1

    def left(self):
        return len(self.stages) - 1 - self.stage

    def pair(self):
        return self.keeps[0], self.recvs[0]


def result_kernel(sp_size, halved, *refs):
    outs = refs[8:16]
    gain_scr, shift_scr, qkv_scr, out_scr, up_scr, bup_scr, down_scr, bdown_scr = refs[16:24]
    mlp1, both, up0, qkv0 = refs[24:28]
    small_scr, sems = refs[28:]
    size = TILE // sp_size
    chunks = up_scr.shape[2] // TILE
    down_size = chunks * size
    row_half = lax.rem(lax.axis_index("grp"), 2)
    segments = (
        (mlp1, (chunks * size, down_size)), (both, (4 * size, down_size)),
        (up0, (chunks * size + size,)), (qkv0, (3 * size,)),
    )
    for i, (scr, heights) in enumerate(segments):
        mine, other = refs[2 * i], refs[2 * i + 1]
        at = 0
        base = 0
        for height in heights:
            if halved[i]:
                half = height // 2
                for ref, side in ((mine, row_half), (other, 1 - row_half)):
                    place = pl.ds(pl.multiple_of(base + side * half, 16), half)
                    scr[place, :] = ref[at : at + half, :].astype(F32)
                at += half
            else:
                span = slice(at, at + height)
                scr[base : base + height, :] = mine[span, :].astype(F32) + other[span, :].astype(F32)
                at += height
            base += height
    mine, other = refs[6], refs[7]
    at = 3 * size // (2 if halved[3] else 1)
    small = mine[at : at + 32, :].astype(F32)
    small_scr[...] = small if halved[3] else small + other[at : at + 32, :].astype(F32)
    for layer, (qkv, up, down, out, first, last) in enumerate((
        (qkv0, up0, both, up0, 4 * size, chunks * size),
        (both, mlp1, mlp1, both, chunks * size, 3 * size),
    )):
        for j in range(3):
            qkv_scr[layer, :, j * TILE : (j + 1) * TILE] = qkv[j * size : (j + 1) * size, :]
        for j in range(chunks):
            up_scr[layer, :, j * TILE : (j + 1) * TILE] = up[j * size : (j + 1) * size, :]
        down_scr[layer] = down[first : first + down_size, :]
        out_scr[layer] = out[last : last + size, :]
    sp = lax.axis_index("sp")
    back = lax.rem(TILE - sp * size, TILE)
    turned = pltpu.roll(small_scr[...], back, 1)
    for i in range(4):
        gain_scr[i : i + 1, :] = turned[8 * i : 8 * i + 1, :size]
        shift_scr[i : i + 1, :] = turned[8 * i + 1 : 8 * i + 2, :size]
    start = sp * down_size
    line = start // TILE
    back = lax.rem(TILE - lax.rem(start, TILE), TILE)
    for layer in range(2):
        first = 8 + 16 * layer
        bdown_scr[layer : layer + 1, :] = turned[first + 2 : first + 3, :size]
        rows = small_scr[first : first + 8, :]
        lines = lax.broadcasted_iota(jnp.int32, rows.shape, 0)
        picked = jnp.sum(jnp.where(lines == 4 + line, rows, 0.0), axis=0, keepdims=True)
        picked = pltpu.roll(jnp.broadcast_to(picked, rows.shape), back, 1)
        bup_scr[layer : layer + 1, :] = picked[0:1, :down_size]
    scrs = (gain_scr, shift_scr, qkv_scr, out_scr, up_scr, bup_scr, down_scr, bdown_scr)
    copies = [pltpu.make_async_copy(scr, out, sems.at[i]) for i, (scr, out) in enumerate(zip(scrs, outs))]
    for copy in copies:
        copy.start()
    for copy in copies:
        copy.wait()


VMEM = pl.BlockSpec(memory_space=pltpu.VMEM)
SMEM = pl.BlockSpec(memory_space=pltpu.SMEM)
HBM = pl.BlockSpec(memory_space=pltpu.HBM)


def sds(shape, dtype):
    return jax.ShapeDtypeStruct(shape, dtype)


def call(kernel, args, outs, micros, scratch=(), specs=None, out_specs=None, limit=12):
    return pl.pallas_call(
        kernel,
        in_specs=[VMEM] * len(args) if specs is None else specs,
        out_specs=[VMEM] * len(outs) if out_specs is None else out_specs,
        out_shape=outs,
        scratch_shapes=list(scratch),
        compiler_params=pltpu.CompilerParams(vmem_limit_bytes=limit * MIB),
        cost_estimate=pl.CostEstimate(flops=int(micros * COST), bytes_accessed=0, transcendentals=0),
    )(*args)


def swap(array, axis, size, bit):
    return lax.ppermute(array, axis, [(i, i ^ (1 << bit)) for i in range(size)])


def shards(sizes, tokens, frame_slot, norm_gain, norm_shift, w_qkv, w_out, w_up, b_up, w_down, b_down, cotangent):
    grp_size, sp_size = sizes
    frames, patches, width = tokens.shape
    hidden = w_up.shape[2]
    assert GROUP_FRAMES == 2 * frames and sp_size >= 8
    half = patches // 2
    rows = frames * patches
    sp_bits = sp_size.bit_length() - 1
    core_swap = functools.partial(swap, axis="sp", size=sp_size, bit=0)
    slots = sp_size // 2
    size = width // sp_size
    down_size = hidden // sp_size
    def slots_of(path):
        return [step for step in path if step != ROWS] + list(range(4, sp_bits))

    path_up1, path_down1 = (0, 1, 2, ROWS, 3), (0, 2, 1, ROWS, 3)
    path_attn1, path_down0 = (0, ROWS, 2, 1, 3), (0, 2, 1, ROWS, 3)
    path_up0, path_qkv0 = (0, 1, ROWS, 2, 3), (0, 2, 1, ROWS, 3)

    def row_out(cols, dtype=BF16):
        return sds((rows, cols), dtype)

    half_out = sds((frames, half, width), BF16)
    small_out = sds((8, TILE), F32)
    fence = lambda *arrays: lax.optimization_barrier(arrays)

    token = []

    def meet(groups, *arrays):
        recvs = [r for g in groups for r in g.recvs]
        out = list(fence(*arrays, *recvs, *token))
        count = len(arrays)
        arrays, recvs = out[:count], out[count:]
        for g in groups:
            g.recvs = [recvs.pop(0) for _ in g.recvs]
            g.fold()
        sends = [x for g in groups for x in g.sends]
        out = list(fence(*arrays, *sends))
        arrays, sends = out[:count], out[count:]
        for g in groups:
            g.start([sends.pop(0) for _ in g.sends])
        token[:] = [groups[-1].sends[-1]] if groups else []
        return arrays

    def buffers(height):
        return [sds((slots * height, TILE), BF16)] * 2

    cot_recv = core_swap(cotangent)
    widen = lambda a: jnp.pad(a, ((0, 0), (0, hidden - width)))
    packed = jnp.concatenate([widen(norm_gain), widen(norm_shift), b_up, widen(b_down)], axis=0)
    weights = (w_qkv, w_out, w_up, w_down)
    shapes = [sds(w.shape[1:], BF16) for w in weights]
    out = call(
        space_forward_kernel,
        (tokens, packed) + weights,
        [
            half_out, half_out, row_out(width), row_out(3 * width), sds((frames, HEADS, patches), F32),
            row_out(width), row_out(width, F32), row_out(width), row_out(hidden), row_out(hidden),
        ],
        16,
        scratch=[pltpu.VMEM(tokens.shape, BF16)]
        + [pltpu.VMEM(x.shape, BF16) for x in shapes]
        + [
            pltpu.VMEM((2, patches, width), BF16), pltpu.VMEM((2, patches, 3 * width), BF16),
            pltpu.VMEM((2, patches, width), BF16), pltpu.VMEM((2, patches, width), F32),
            pltpu.VMEM((2, patches, width), BF16),
            pltpu.VMEM((2, patches, hidden), BF16), pltpu.VMEM((2, patches, hidden), BF16),
            pltpu.VMEM((patches, width), F32), pltpu.SemaphoreType.DMA((5,)),
            pltpu.SemaphoreType.DMA((14,)),
        ],
        specs=[HBM, VMEM] + [HBM] * 4,
        out_specs=[VMEM, VMEM, HBM, HBM, VMEM] + [HBM] * 5,
        limit=LIMIT1,
    )
    (x_keep, x_send, h0, qkv0, lse0, o0, xa, h1, act0, slope0) = out
    x_recv = core_swap(x_send)

    place_scratch = [
        pltpu.SMEM((GROUP_FRAMES,), jnp.int32),
        pltpu.VMEM((GROUP_FRAMES, half, width), BF16),
    ]
    (out_own, out_send, xt, h2, qkv1, o1, h3, act1, du1, gr1, dxb, small3, w_qkv1, w_out1) = call(
        time_forward_kernel,
        (frame_slot, x_keep, x_recv, cotangent, cot_recv, packed) + weights,
        [
            half_out, half_out, row_out(width), row_out(width), row_out(3 * width), row_out(width),
            row_out(width), row_out(hidden), row_out(hidden), row_out(width), row_out(width, F32),
            small_out,
        ] + shapes[:2],
        24,
        scratch=place_scratch
        + [pltpu.VMEM((rows // 4, hidden), BF16)]
        + [pltpu.VMEM(x.shape, BF16) for x in shapes[2:]]
        + [pltpu.SemaphoreType.DMA((4,))],
        specs=[SMEM] + [VMEM] * 5 + [HBM] * 4,
        limit=LIMIT2,
    )
    out_recv = core_swap(out_send)

    out = call(
        functools.partial(mlp_weights_kernel, (slots_of(path_up1), slots_of(path_down1))), (h3, du1, act1, gr1),
        buffers(4 * size + down_size), 4.5,
    )
    keep, send, dxb = fence(*out, dxb)
    mlp1 = Group(sizes, {"up": (4 * size, False, path_up1), "down": (down_size, False, path_down1)})
    mlp1.begin(keep, send)

    (dx_own, dx_send, ar1, dqkv1, small2) = call(
        time_backward_kernel,
        (frame_slot, xt, qkv1, dxb, packed, w_qkv1, w_out1),
        [half_out, half_out, row_out(width), row_out(3 * width), small_out],
        8,
        scratch=place_scratch,
        specs=[SMEM] + [VMEM] * 6,
    )
    dx_recv = core_swap(dx_send)
    dx_own, dx_recv, dqkv1, out_recv = meet((mlp1,), dx_own, dx_recv, dqkv1, out_recv)
    keep_attn, send_attn = call(
        functools.partial(attn_weights_kernel, slots_of(path_attn1)), (h2, dqkv1, o1, ar1),
        buffers(4 * size), 2.4,
    )
    gr0, keep_down, send_down = call(
        functools.partial(down_weights_kernel, slots_of(path_down0)), (act0, dx_own, dx_recv),
        [row_out(width)] + buffers(down_size), 2.4,
    )
    (du0, dxa, ar0, small1) = call(
        space_mlp_back_kernel,
        (gr0, xa, slope0, packed, w_up, w_down),
        [row_out(hidden), row_out(width, F32), row_out(width), small_out],
        6,
    )
    keep_up, send_up = call(
        functools.partial(up_weights_kernel, slots_of(path_up0)), (h1, du0, o0, ar0), buffers(5 * size), 3
    )
    keep_attn, send_attn, keep_down, send_down, keep_up, send_up, ar0 = meet(
        (mlp1,), keep_attn, send_attn, keep_down, send_down, keep_up, send_up, ar0
    )
    both = Group(
        sizes,
        {"attn": (4 * size, False, path_attn1), "down": (down_size, False, path_down0)},
        apart=True,
    )
    both.begin(keep_attn, send_attn)
    both.begin(keep_down, send_down)
    up0 = Group(sizes, {"up": (5 * size, False, path_up0)})
    up0.begin(keep_up, send_up)

    (dqkv0,) = call(
        space_attn_back_kernel, (ar0, qkv0, lse0, o0, w_out), [row_out(3 * width)], 10
    )
    (dqkv0,) = meet((up0, both, mlp1), dqkv0)
    out = call(
        functools.partial(qkv_weights_kernel, slots_of(path_qkv0)), (dqkv0, h0), buffers(3 * size), 2
    )
    keep, send, dqkv0 = fence(*out, dqkv0)
    qkv = Group(
        sizes, {"qkv": (3 * size, False, path_qkv0), "small": (32, True, path_qkv0)}, apart=True
    )
    qkv.begin(keep, send)
    grad_tokens, output, small = call(
        finish_kernel,
        (
            dqkv0, tokens, dxa, out_own, out_recv, packed, w_qkv, small1, small2, small3,
        ),
        [sds(tokens.shape, BF16), sds(tokens.shape, BF16), sds((32, TILE), BF16)],
        4,
        scratch=[pltpu.VMEM((8, TILE), F32)],
    )
    (small,) = fence(small)
    qkv.begin(small, small)
    everyone = (mlp1, both, up0, qkv)
    for names in TAIL:
        groups = [g for g in (dict(zip("mbuq", everyone))[c] for c in names) if g.left()]
        if groups:
            meet(groups)
    while any(g.left() for g in everyone):
        meet([g for g in everyone if g.left()])
    finals = [
        sds((4, size), F32), sds((4, size), F32), sds((2, size, 3 * width), F32), sds((2, size, width), F32),
        sds((2, size, hidden), F32), sds((2, down_size), F32), sds((2, down_size, width), F32),
        sds((2, size), F32),
    ]
    heights = (4 * size + down_size, 4 * size + down_size, 5 * size, 3 * size)
    results = call(
        functools.partial(result_kernel, sp_size, tuple(g.halved for g in everyone)),
        [x for g in everyone for x in g.pair()], finals, 2,
        scratch=[pltpu.VMEM(f.shape, F32) for f in finals]
        + [pltpu.VMEM((h, TILE), F32) for h in heights]
        + [pltpu.VMEM((32, TILE), F32), pltpu.SemaphoreType.DMA((8,))],
        out_specs=[HBM] * 8,
    )
    return (output, grad_tokens, *results)


def solution(mesh):
    rows = P(("grp", "sp"), None, None)
    in_specs = (rows, P("grp", None), P(), P(), P(), P(), P(), P(), P(), P(), rows)
    out_specs = (
        rows, rows, P(None, "sp"), P(None, "sp"), P(None, "sp", None), P(None, "sp", None),
        P(None, "sp", None), P(None, "sp"), P(None, "sp", None), P(None, "sp"),
    )
    body = functools.partial(shards, (mesh.shape["grp"], mesh.shape["sp"]))
    return jax.shard_map(body, mesh=mesh, in_specs=in_specs, out_specs=out_specs, check_vma=False)
```

```python
import functools

import jax
import jax.numpy as jnp
from jax import lax
from jax.experimental import pallas as pl
from jax.experimental.pallas import tpu as pltpu
from jax.sharding import PartitionSpec as P

HEADS = 8
HEAD = 64
VIDEO_STEPS = 6
GROUP_FRAMES = 8
NORM_EPS = 1e-05
TILE = 512
STEP = 1024
SCALE = HEAD**-0.5
TANH_A = 0.7978845608028654
TANH_B = TANH_A * 0.044715
PAIRS = [(t, s) for t in range(VIDEO_STEPS) for s in range(t + 1)]
F32 = jnp.float32
BF16 = jnp.bfloat16
MIB = 1024 * 1024
ROWS = -1
COST = 1.15e9 * 0.02
TAIL = ("q", "m", "bu", "q", "m", "bu", "q", "bu", "q", "bu", "q")
LIMIT1 = 52
LIMIT2 = 24


def dot(left, right):
    return jnp.dot(left, right, preferred_element_type=F32)


def dot_nt(left, right):
    return lax.dot_general(left, right, (((1,), (1,)), ((), ())), preferred_element_type=F32)


def dot_tn(left, right):
    return lax.dot_general(left, right, (((0,), (0,)), ((), ())), preferred_element_type=F32)


def norm(rows, gain, shift):
    centred = rows - jnp.mean(rows, axis=-1, keepdims=True)
    inv = lax.rsqrt(jnp.mean(centred * centred, axis=-1, keepdims=True) + NORM_EPS)
    unit = centred * inv
    return unit * gain + shift, unit, inv


def norm_back(grad, unit, inv, gain):
    grad_unit = grad * gain
    mean_grad = jnp.mean(grad_unit, axis=-1, keepdims=True)
    mean_both = jnp.mean(grad_unit * unit, axis=-1, keepdims=True)
    return inv * (grad_unit - mean_grad - unit * mean_both)


def column_sum(rows):
    return jnp.sum(rows, axis=0, keepdims=True)


def gelu_pair(u):
    square = u * u
    sigma = 0.5 + 0.5 * jnp.tanh(u * (TANH_A + TANH_B * square))
    act = u * sigma
    slope = sigma + act * (1.0 - sigma) * (2.0 * TANH_A + 6.0 * TANH_B * square)
    return act.astype(BF16), slope.astype(BF16)


def head_mask(lanes, which):
    lane = lax.broadcasted_iota(jnp.int32, lanes.shape, 1)
    return (lane < HEAD) if which == 0 else (lane >= HEAD)


def qkv_rows(normed, weight):
    out = []
    for part in range(3):
        piece = dot(normed, weight[:, part * TILE : (part + 1) * TILE])
        if part == 0:
            out.append(piece.astype(BF16) * BF16(SCALE))
        else:
            out.append(piece.astype(BF16))
    return out


def mlp_forward(normed, w_up, b_up, w_down, rows, act_ref, slope_ref):
    chunks = w_up.shape[1] // STEP
    up = lambda j: dot(normed, w_up[:, j * STEP : (j + 1) * STEP])
    total = None
    u = up(0)
    for j in range(chunks):
        cols = slice(j * STEP, (j + 1) * STEP)
        later = up(j + 1) if j + 1 < chunks else None
        act, slope = gelu_pair(u + b_up[0:1, cols])
        act_ref[rows, cols] = act
        slope_ref[rows, cols] = slope
        piece = dot(act, w_down[cols, :])
        total = piece if total is None else total + piece
        u = later
    return total


def mlp_backward(grad_low, w_up, w_down, rows, slope_ref, du_ref):
    chunks = w_up.shape[1] // STEP
    down = lambda j: dot_nt(grad_low, w_down[j * STEP : (j + 1) * STEP, :])
    total = None
    sums = []
    da = down(0)
    for j in range(chunks):
        cols = slice(j * STEP, (j + 1) * STEP)
        later = down(j + 1) if j + 1 < chunks else None
        du = (da * slope_ref[rows, cols].astype(F32)).astype(BF16)
        du_ref[rows, cols] = du
        sums.append(column_sum(du.astype(F32)))
        piece = dot_nt(du, w_up[:, cols])
        total = piece if total is None else total + piece
        da = later
    return total, [x[:, k : k + TILE] for x in sums for k in range(0, STEP, TILE)]


def add_small(small_ref, values, first):
    for i, value in enumerate(values):
        row = slice(i, i + 1) if i < 4 else slice(i, i + 1)
        if value is None:
            continue
        if first:
            small_ref[row, :] = value
        else:
            small_ref[row, :] += value


def rows_at(index, count):
    return pl.ds(pl.multiple_of(index * count, count), count)


def half_rows(part, half):
    return pl.ds(pl.multiple_of(part * half, half), half)


def space_forward_kernel(
    tok_hbm, params_ref, wqkv_hbm, wout_hbm, wup_hbm, wdown_hbm,
    keep_ref, send_ref, h0_hbm, qkv_hbm, lse_ref, o_hbm, xa_hbm, h1_hbm, act_hbm, slope_hbm,
    tok_ref, wqkv_ref, wout_ref, wup_ref, wdown_ref, h0_scr, qkv_scr, o_scr, xa_scr, h1_scr, act_scr,
    slope_scr, x1_scr, in_sems, out_sems,
):
    pairs = [
        (tok_hbm, tok_ref), (wqkv_hbm.at[0], wqkv_ref), (wout_hbm.at[0], wout_ref),
        (wup_hbm.at[0], wup_ref), (wdown_hbm.at[0], wdown_ref),
    ]
    copies = [pltpu.make_async_copy(src, dst, in_sems.at[i]) for i, (src, dst) in enumerate(pairs)]
    for copy in copies[:2]:
        copy.start()
    gain_ref, shift_ref = params_ref.at[0:4, 0:TILE], params_ref.at[4:8, 0:TILE]
    part = lax.rem(lax.axis_index("sp"), 2)
    frames, rows = tok_ref.shape[0], tok_ref.shape[1]
    half = rows // 2
    lane = lax.broadcasted_iota(jnp.int32, (rows, 128), 1)
    places = (
        (h0_scr, h0_hbm), (qkv_scr, qkv_hbm), (o_scr, o_hbm), (xa_scr, xa_hbm), (h1_scr, h1_hbm),
        (act_scr, act_hbm), (slope_scr, slope_hbm),
    )

    def spills(f):
        now = lax.rem(f, 2)
        return [
            pltpu.make_async_copy(scr.at[now], hbm.at[rows_at(f, rows)], out_sems.at[7 * now + i])
            for i, (scr, hbm) in enumerate(places)
        ]

    def await_first(f, *which):
        @pl.when(f == 0)
        def _():
            for i in which:
                copies[i].wait()

    copies[0].wait()
    for copy in copies[2:]:
        copy.start()

    @pl.loop(0, frames, unroll=True)
    def _(f):
        now = lax.rem(f, 2)
        spill = spills(f)

        @pl.when(f >= 2)
        def _():
            for copy in spills(f - 2):
                copy.wait()

        x0 = tok_ref[f].astype(F32)
        h0 = norm(x0, gain_ref[0:1, :], shift_ref[0:1, :])[0].astype(BF16)
        h0_scr[now] = h0
        spill[0].start()
        await_first(f, 1)
        q, k, v = qkv_rows(h0, wqkv_ref)
        qkv_scr[now, :, 0:TILE] = q
        qkv_scr[now, :, TILE : 2 * TILE] = k
        qkv_scr[now, :, 2 * TILE :] = v
        spill[1].start()
        lse_all = jnp.zeros((rows, 128), F32)
        mixed = []
        for pair in range(HEADS // 2):
            cols = slice(pair * 128, (pair + 1) * 128)
            qp, kp, vp = q[:, cols], k[:, cols], v[:, cols]
            zero = jnp.zeros_like(qp)
            mask = head_mask(qp, 0)
            s = dot_nt(jnp.concatenate([jnp.where(mask, qp, zero), jnp.where(mask, zero, qp)], axis=0), kp)
            top = jnp.max(s, axis=-1, keepdims=True)
            p = jnp.exp(s - top)
            total = jnp.sum(p, axis=-1, keepdims=True)
            both = dot(p.astype(BF16), vp) * (1.0 / total)
            lse = top + jnp.log(total)
            lse_all = jnp.where(lane == 2 * pair, lse[:rows], lse_all)
            lse_all = jnp.where(lane == 2 * pair + 1, lse[rows:], lse_all)
            mixed.append(jnp.where(mask, both[:rows], both[rows:]).astype(BF16))
        lse_ref[f] = jnp.transpose(lse_all)[0:HEADS, :]
        o = jnp.concatenate(mixed, axis=1)
        o_scr[now] = o
        spill[2].start()
        await_first(f, 2)
        xa = x0 + dot(o, wout_ref[...])
        xa_scr[now] = xa
        spill[3].start()
        h1 = norm(xa, gain_ref[1:2, :], shift_ref[1:2, :])[0].astype(BF16)
        h1_scr[now] = h1
        spill[4].start()
        await_first(f, 3, 4)
        branch = mlp_forward(
            h1, wup_ref, params_ref.at[8:9], wdown_ref, slice(None), act_scr.at[now], slope_scr.at[now]
        )
        spill[5].start()
        spill[6].start()
        x1_scr[...] = xa + branch + params_ref[10:11, 0:TILE]
        keep_ref[f] = x1_scr[half_rows(part, half), :].astype(BF16)
        send_ref[f] = x1_scr[half_rows(1 - part, half), :].astype(BF16)

    for f in (frames - 2, frames - 1):
        for copy in spills(jnp.int32(f)):
            copy.wait()


def lane_heads(dtype):
    c = lax.broadcasted_iota(jnp.int32, (TILE, 128), 0)
    h = lax.broadcasted_iota(jnp.int32, (TILE, 128), 1)
    return (c // HEAD == h).astype(dtype)


def slot_places(slots_ref, where_scr, frames):
    sp = lax.axis_index("sp")
    group = (sp * frames) // GROUP_FRAMES
    part = lax.rem(sp, GROUP_FRAMES // frames)
    for t in range(GROUP_FRAMES):
        where_scr[slots_ref[group, t]] = lax.rem(t + GROUP_FRAMES - part * frames, GROUP_FRAMES)


def time_scores(q, k, spread):
    parts = []
    for t, s in PAIRS:
        parts.append((q[t] * k[s]).astype(BF16))
    return dot(jnp.concatenate(parts, axis=0), spread)


def time_probs(scores, count):
    blocks = [scores[i * count : (i + 1) * count] for i in range(len(PAIRS))]
    probs = []
    at = 0
    for t in range(VIDEO_STEPS):
        mine = blocks[at : at + t + 1]
        at += t + 1
        top = functools.reduce(jnp.maximum, mine)
        raw = [jnp.exp(b - top) for b in mine]
        inv = 1.0 / functools.reduce(lambda a, b: a + b, raw)
        probs.extend([r * inv for r in raw])
    return probs


def split_slots(rows):
    count = rows.shape[0] // GROUP_FRAMES
    return [rows[s * count : (s + 1) * count].astype(F32) for s in range(GROUP_FRAMES)]


def time_forward_kernel(
    slots_ref, keep_ref, recv_ref, cot_ref, cotr_ref, params_ref,
    wqkv_hbm, wout_hbm, wup_hbm, wdown_hbm,
    own_ref, send_ref, x_ref, h2_ref, qkv_ref, o_ref, h3_ref, act_ref, du_ref, gr_ref, dxb_ref,
    small_ref, wqkv_ref, wout_ref,
    where_scr, both_scr, slope_scr, wup_ref, wdown_ref, in_sems,
):
    pairs = [(wqkv_hbm, wqkv_ref), (wout_hbm, wout_ref), (wup_hbm, wup_ref), (wdown_hbm, wdown_ref)]
    copies = [pltpu.make_async_copy(src.at[1], dst, in_sems.at[i]) for i, (src, dst) in enumerate(pairs)]
    for copy in copies:
        copy.start()
    gain_ref, shift_ref = params_ref.at[0:4, 0:TILE], params_ref.at[4:8, 0:TILE]
    frames, half = keep_ref.shape[0], keep_ref.shape[1]
    part = lax.rem(lax.axis_index("sp"), GROUP_FRAMES // frames)
    slot_places(slots_ref, where_scr, frames)
    small_ref[...] = jnp.zeros_like(small_ref)
    both_scr[0:frames] = keep_ref[...]
    both_scr[frames:] = recv_ref[...]
    spread = lane_heads(BF16)
    steps = 4
    count = half // steps
    step_rows = count * GROUP_FRAMES

    def await_first(i, *which):
        @pl.when(i == 0)
        def _():
            for w in which:
                copies[w].wait()

    @pl.loop(0, steps)
    def _(i):
        span = rows_at(i, step_rows)
        place = rows_at(i, count)
        x_low = jnp.concatenate([both_scr[where_scr[s], place] for s in range(GROUP_FRAMES)], axis=0)
        x_ref[span, :] = x_low
        x = x_low.astype(F32)
        h2 = norm(x, gain_ref[2:3, :], shift_ref[2:3, :])[0].astype(BF16)
        h2_ref[span, :] = h2
        await_first(i, 0)
        q, k, v = qkv_rows(h2, wqkv_ref)
        qkv_ref[span, 0:TILE] = q
        qkv_ref[span, TILE : 2 * TILE] = k
        qkv_ref[span, 2 * TILE :] = v
        qs, ks, vs = split_slots(q), split_slots(k), split_slots(v)
        probs = time_probs(time_scores(qs, ks, spread), count)
        wide = dot_nt(jnp.concatenate([p.astype(BF16) for p in probs], axis=0), spread)
        mixed = []
        at = 0
        for t in range(VIDEO_STEPS):
            total = None
            for s in range(t + 1):
                piece = wide[at * count : (at + 1) * count] * vs[s]
                total = piece if total is None else total + piece
                at += 1
            mixed.append(total)
        mixed.extend(vs[VIDEO_STEPS:])
        o = jnp.concatenate([m.astype(BF16) for m in mixed], axis=0)
        o_ref[span, :] = o
        await_first(i, 1)
        xb = x + dot(o, wout_ref[...]).astype(BF16).astype(F32)
        h3, unit, inv = norm(xb, gain_ref[3:4, :], shift_ref[3:4, :])
        h3 = h3.astype(BF16)
        h3_ref[span, :] = h3
        slope = slope_scr
        await_first(i, 2, 3)
        branch = mlp_forward(h3, wup_ref, params_ref.at[9:10], wdown_ref, span, act_ref, SpanView(slope))
        out = (xb + branch + params_ref[11:12, 0:TILE]).astype(BF16)
        for s in range(GROUP_FRAMES):
            both_scr[where_scr[s], place] = out[s * count : (s + 1) * count]
        grad_low = jnp.concatenate(
            [cot_slot(cot_ref, cotr_ref, where_scr[s], part * half + i * count, count) for s in range(GROUP_FRAMES)],
            axis=0,
        )
        gr_ref[span, :] = grad_low
        grad = grad_low.astype(F32)
        dh, sums = mlp_backward(grad_low, wup_ref, wdown_ref, span, SpanView(slope), du_ref)
        add_small(small_ref, [column_sum(dh * unit), column_sum(dh), column_sum(grad), None] + sums, False)
        dxb_ref[span, :] = grad + norm_back(dh, unit, inv, gain_ref[3:4, :])

    own_ref[...] = both_scr[0:frames]
    send_ref[...] = both_scr[frames:]


class SpanView:
    def __init__(self, ref):
        self.ref = ref

    def __getitem__(self, index):
        return self.ref[:, index[1]]

    def __setitem__(self, index, value):
        self.ref[:, index[1]] = value


def cot_slot(cot_ref, cotr_ref, frame, start, count):
    frames = cot_ref.shape[0]
    places = pl.ds(pl.multiple_of(start, count), count)
    mine = cot_ref[lax.rem(frame, frames), places, :]
    other = cotr_ref[lax.rem(frame, frames), places, :]
    return jnp.where(frame < frames, mine, other)


def time_backward_kernel(
    slots_ref, x_ref, qkv_ref, dxb_ref, params_ref, wqkv_ref, wout_ref,
    own_ref, send_ref, ar_ref, dqkv_ref, small_ref,
    where_scr, both_scr,
):
    frames, half = own_ref.shape[0], own_ref.shape[1]
    slot_places(slots_ref, where_scr, frames)
    small_ref[...] = jnp.zeros_like(small_ref)
    spread = lane_heads(BF16)
    steps = 4
    count = half // steps
    step_rows = count * GROUP_FRAMES
    gain = params_ref[2:3, 0:TILE]

    @pl.loop(0, steps)
    def _(i):
        span = rows_at(i, step_rows)
        place = rows_at(i, count)
        dxb = dxb_ref[span, :]
        ar = dxb.astype(BF16)
        ar_ref[span, :] = ar
        do = split_slots(dot_nt(ar, wout_ref[...]).astype(BF16))
        qs = split_slots(qkv_ref[span, 0:TILE])
        ks = split_slots(qkv_ref[span, TILE : 2 * TILE])
        vs = split_slots(qkv_ref[span, 2 * TILE :])
        probs = time_probs(time_scores(qs, ks, spread), count)
        dps = time_scores(do, vs, spread)
        dps = [dps[j * count : (j + 1) * count] for j in range(len(PAIRS))]
        dss = []
        at = 0
        for t in range(VIDEO_STEPS):
            centre = functools.reduce(
                lambda a, b: a + b, [probs[at + s] * dps[at + s] for s in range(t + 1)]
            )
            dss.extend([probs[at + s] * (dps[at + s] - centre) for s in range(t + 1)])
            at += t + 1
        wide_p = dot_nt(jnp.concatenate([p.astype(BF16) for p in probs], axis=0), spread)
        wide_ds = dot_nt(jnp.concatenate([d.astype(BF16) for d in dss], axis=0), spread)
        dq = [None] * GROUP_FRAMES
        dk = [None] * GROUP_FRAMES
        dv = [None] * GROUP_FRAMES

        def add(table, index, piece):
            table[index] = piece if table[index] is None else table[index] + piece

        for j, (t, s) in enumerate(PAIRS):
            rows = slice(j * count, (j + 1) * count)
            add(dq, t, wide_ds[rows] * ks[s])
            add(dk, s, wide_ds[rows] * qs[t])
            add(dv, s, wide_p[rows] * do[t])
        for t in range(VIDEO_STEPS, GROUP_FRAMES):
            dq[t] = jnp.zeros_like(do[t])
            dk[t] = jnp.zeros_like(do[t])
            dv[t] = do[t]
        dq = jnp.concatenate([(d * SCALE).astype(BF16) for d in dq], axis=0)
        dk = jnp.concatenate([d.astype(BF16) for d in dk], axis=0)
        dv = jnp.concatenate([d.astype(BF16) for d in dv], axis=0)
        dqkv_ref[span, 0:TILE] = dq
        dqkv_ref[span, TILE : 2 * TILE] = dk
        dqkv_ref[span, 2 * TILE :] = dv
        dh = dot_nt(dqkv_ref[span, :], wqkv_ref[...])
        unit, inv = norm(x_ref[span, :].astype(F32), gain, params_ref[6:7, 0:TILE])[1:]
        add_small(small_ref, [column_sum(dh * unit), column_sum(dh)], False)
        dxp = norm_back(dh, unit, inv, gain).astype(BF16).astype(F32)
        dx1 = (dxb + dxp).astype(BF16)
        for s in range(GROUP_FRAMES):
            both_scr[where_scr[s], place] = dx1[s * count : (s + 1) * count]

    own_ref[...] = both_scr[0:frames]
    send_ref[...] = both_scr[frames:]


def space_mlp_back_kernel(
    gr_ref, xa_ref, slope_ref, params_ref, wup_ref, wdown_ref,
    du_ref, dxa_ref, ar_ref, small_ref,
):
    small_ref[...] = jnp.zeros_like(small_ref)
    rows = 256
    gain = params_ref[1:2, 0:TILE]

    @pl.loop(0, gr_ref.shape[0] // rows, unroll=True)
    def _(f):
        span = rows_at(f, rows)
        grad_low = gr_ref[span, :]
        grad = grad_low.astype(F32)
        dh, sums = mlp_backward(grad_low, wup_ref.at[0], wdown_ref.at[0], span, slope_ref, du_ref)
        unit, inv = norm(xa_ref[span, :], gain, params_ref[5:6, 0:TILE])[1:]
        add_small(small_ref, [column_sum(dh * unit), column_sum(dh), column_sum(grad), None] + sums, False)
        dxa = grad + norm_back(dh, unit, inv, gain)
        dxa_ref[span, :] = dxa
        ar_ref[span, :] = dxa.astype(BF16)


def head_picker():
    h = lax.broadcasted_iota(jnp.int32, (HEADS, TILE), 0)
    c = lax.broadcasted_iota(jnp.int32, (HEADS, TILE), 1)
    return (c // HEAD == h).astype(BF16)


def attn_back_frame(f, ar_ref, qkv_ref, lse_ref, o_ref, wout_ref, pick, dqkv_ref):
    rows = lse_ref.shape[2]
    span = rows_at(f, rows)
    do = dot_nt(ar_ref[span, :], wout_ref[0]).astype(BF16)
    both = do.astype(F32) * o_ref[span, :].astype(F32)
    high = both.astype(BF16)
    rest = (both - high.astype(F32)).astype(BF16)
    centre = dot_nt(pick, high) + dot_nt(pick, rest)
    for pair in range(HEADS // 2):
        qp = qkv_ref[span, pair * 128 : (pair + 1) * 128]
        kp = qkv_ref[span, TILE + pair * 128 : TILE + (pair + 1) * 128]
        vp = qkv_ref[span, 2 * TILE + pair * 128 : 2 * TILE + (pair + 1) * 128]
        dop = do[:, pair * 128 : (pair + 1) * 128]
        zero = jnp.zeros_like(kp)
        mask = head_mask(kp, 0)
        st = dot_nt(jnp.concatenate([jnp.where(mask, kp, zero), jnp.where(mask, zero, kp)], axis=0), qp)
        dpt = dot_nt(jnp.concatenate([jnp.where(mask, vp, zero), jnp.where(mask, zero, vp)], axis=0), dop)
        pts, dsts, dqs = [], [], []
        for e in range(2):
            row = slice(2 * pair + e, 2 * pair + e + 1)
            keys = slice(e * rows, (e + 1) * rows)
            pt = jnp.exp(st[keys] - lse_ref[f, row, :])
            dst = (pt * (dpt[keys] - centre[row, :])).astype(BF16)
            pts.append(pt.astype(BF16))
            dsts.append(dst)
            dqs.append(dot_tn(dst, kp) * SCALE)
        dk = dot(jnp.concatenate(dsts, axis=0), qp)
        dv = dot(jnp.concatenate(pts, axis=0), dop)
        values = (
            jnp.where(mask, dqs[0], dqs[1]),
            jnp.where(mask, dk[:rows], dk[rows:]),
            jnp.where(mask, dv[:rows], dv[rows:]),
        )
        for index, value in enumerate(values):
            at = index * TILE + pair * 128
            dqkv_ref[span, at : at + 128] = value.astype(BF16)


def space_attn_back_kernel(ar_ref, qkv_ref, lse_ref, o_ref, wout_ref, dqkv_ref):
    pick = head_picker()

    @pl.loop(0, lse_ref.shape[0], unroll=True)
    def _(f):
        attn_back_frame(f, ar_ref, qkv_ref, lse_ref, o_ref, wout_ref, pick, dqkv_ref)


def qkv_weights_kernel(order, dqkv_ref, h_ref, keep_ref, send_ref):
    size = h_ref.shape[1] // lax.axis_size("sp")
    turned_columns(h_ref, dqkv_ref, 3, 0, 3 * size, size, order, keep_ref, send_ref)


def finish_kernel(
    dqkv_ref, tok_ref, dxa_ref, own_ref, recv_ref, params_ref, wqkv_ref, small1_ref,
    small2_ref, small3_ref, gtok_ref, out_ref, small_ref, sums_scr,
):
    part = lax.rem(lax.axis_index("sp"), 2)
    frames, half = own_ref.shape[0], own_ref.shape[1]
    rows = 2 * half
    gain = params_ref[0:1, 0:TILE]
    sums_scr[...] = jnp.zeros_like(sums_scr)

    @pl.loop(0, frames)
    def _(f):
        span = rows_at(f, rows)
        out_ref[f, half_rows(part, half), :] = own_ref[f]
        out_ref[f, half_rows(1 - part, half), :] = recv_ref[f]
        dh = dot_nt(dqkv_ref[span, :], wqkv_ref[0])
        unit, inv = norm(tok_ref[f].astype(F32), gain, params_ref[4:5, 0:TILE])[1:]
        add_small(sums_scr, [column_sum(dh * unit), column_sum(dh)], False)
        gtok_ref[f] = (dxa_ref[span, :] + norm_back(dh, unit, inv, gain)).astype(BF16)

    small = jnp.concatenate([sums_scr[...], small1_ref[...], small2_ref[...], small3_ref[...]], axis=0)
    small_ref[...] = small.astype(BF16)


def place_of(block, order, sp):
    bits = len(order)
    mixed = jnp.bitwise_xor(block, sp)
    slot = jnp.int32(0)
    for i, b in enumerate(order):
        bit = jnp.bitwise_and(lax.shift_right_logical(mixed, jnp.int32(b)), 1)
        slot = slot + lax.shift_left(bit, jnp.int32(bits - 1 - i))
    return slot


class Place:
    def __init__(self, base, rows, at):
        self.base, self.rows, self.at = base, rows, at


def put_blocks(result, first, size, place, order, keep_ref, send_ref):
    sp = lax.axis_index("sp")
    part = lax.rem(sp, 2)
    low = result.astype(BF16)
    for j in range(result.shape[0] // (2 * size)):
        even = low[2 * j * size : (2 * j + 1) * size]
        odd = low[(2 * j + 1) * size : (2 * j + 2) * size]
        slot = place_of(first + 2 * j, order[1:], sp)
        rows = pl.ds(pl.multiple_of(place.base + slot * place.rows + place.at, 16), size)
        keep_ref[rows, :] = jnp.where(part == 0, even, odd)
        send_ref[rows, :] = jnp.where(part == 0, odd, even)


def turned_columns(h_ref, wide_ref, chunks, base, rows, size, order, keep_ref, send_ref):
    turned = jnp.transpose(h_ref[...])
    for j in range(chunks):
        result = dot(turned, wide_ref[:, j * TILE : (j + 1) * TILE])
        put_blocks(result, jnp.int32(0), size, Place(base, rows, j * size), order, keep_ref, send_ref)


def put_up(h_ref, du_ref, base, rows, order, keep_ref, send_ref):
    size = h_ref.shape[1] // lax.axis_size("sp")
    turned_columns(h_ref, du_ref, du_ref.shape[1] // TILE, base, rows, size, order, keep_ref, send_ref)


def put_down(act_ref, gr_ref, base, order, keep_ref, send_ref):
    size = act_ref.shape[1] // lax.axis_size("sp")
    for j in range(act_ref.shape[1] // TILE):
        down = dot_tn(act_ref[:, j * TILE : (j + 1) * TILE], gr_ref[...])
        put_blocks(down, jnp.int32(j * (TILE // size)), size, Place(base, size, 0), order, keep_ref, send_ref)


def mlp_weights_kernel(orders, h_ref, du_ref, act_ref, gr_ref, keep_ref, send_ref):
    sp_size = lax.axis_size("sp")
    rows = du_ref.shape[1] // TILE * (h_ref.shape[1] // sp_size)
    put_up(h_ref, du_ref, 0, rows, orders[0], keep_ref, send_ref)
    put_down(act_ref, gr_ref, sp_size // 2 * rows, orders[1], keep_ref, send_ref)


def down_weights_kernel(order, act_ref, own_ref, recv_ref, gr_ref, keep_ref, send_ref):
    part = lax.rem(lax.axis_index("sp"), 2)
    frames, half = own_ref.shape[0], own_ref.shape[1]
    for f in range(frames):
        base = f * 2 * half
        gr_ref[pl.ds(pl.multiple_of(base + part * half, half), half), :] = own_ref[f]
        gr_ref[pl.ds(pl.multiple_of(base + (1 - part) * half, half), half), :] = recv_ref[f]
    put_down(act_ref, gr_ref, 0, order, keep_ref, send_ref)


def up_weights_kernel(order, h_ref, du_ref, o_ref, ar_ref, keep_ref, send_ref):
    size = h_ref.shape[1] // lax.axis_size("sp")
    at = du_ref.shape[1] // TILE * size
    put_up(h_ref, du_ref, 0, at + size, order, keep_ref, send_ref)
    out = dot_tn(o_ref[...], ar_ref[...])
    put_blocks(out, jnp.int32(0), size, Place(0, at + size, at), order, keep_ref, send_ref)


def attn_weights_kernel(order, h_ref, dqkv_ref, o_ref, ar_ref, keep_ref, send_ref):
    size = h_ref.shape[1] // lax.axis_size("sp")
    turned_columns(h_ref, dqkv_ref, 3, 0, 4 * size, size, order, keep_ref, send_ref)
    out = dot_tn(o_ref[...], ar_ref[...])
    put_blocks(out, jnp.int32(0), size, Place(0, 4 * size, 3 * size), order, keep_ref, send_ref)


def fold_kernel(moves, count, *refs):
    outs = refs[2 * count :]
    row_half = lax.rem(lax.axis_index("grp"), 2)
    for source, at, rows, slots, targets, to, split in moves:
        keep, recv = refs[2 * source], refs[2 * source + 1]
        if split == "none":
            span = slice(at, at + rows)
            total = keep[span, :] + recv[span, :]
            for target in targets:
                outs[target][to : to + rows, :] = total
        elif split == "slots":
            half = rows // 2
            for part, target in enumerate(targets):
                span = slice(at + part * half, at + (part + 1) * half)
                outs[target][to : to + half, :] = keep[span, :] + recv[span, :]
        else:
            half = rows // (2 * slots)
            for slot in range(slots):
                for part, target in enumerate(targets):
                    side = row_half if part == 0 else 1 - row_half
                    span = pl.ds(pl.multiple_of(at + 2 * slot * half + side * half, 16), half)
                    place = to + slot * half
                    outs[target][place : place + half, :] = keep[span, :] + recv[span, :]


class Group:
    def __init__(self, sizes, segments, apart=False):
        grp_size, sp_size = sizes
        bits = sp_size.bit_length() - 1
        grp_bits = grp_size.bit_length() - 1
        names = tuple(segments)
        self.halved = grp_bits > 0 and all(
            whole or (height // 2) % 16 == 0 for height, whole, path in segments.values()
        )
        self.segments = {}
        self.state = {}
        for name, (height, whole, path) in segments.items():
            path = [step for step in path if step != ROWS or self.halved] + list(range(4, bits))
            self.segments[name] = (height, whole, path)
            self.state[name] = [sp_size // 2, 1]
        self.stages = []
        for i in range(bits + (1 if self.halved else 0)):
            entries = {}
            for name in names:
                key = (self.segments[name][2][i], name if apart and i == 0 else None)
                entries.setdefault(key, []).append(name)
            stage = []
            for (step, _), who in entries.items():
                stage.append(("grp", grp_size, 0, who, "rows") if step == ROWS else ("sp", sp_size, step, who, "slots"))
            self.stages.append(stage)
        for b in range(1 if self.halved else 0, grp_bits):
            self.stages.append([("grp", grp_size, b, names, "none")])
        if self.halved:
            self.stages.append([("grp", grp_size, 0, names, "none")])
        self.stage = 0
        self.keeps, self.recvs = [], []

    def beside(self, other):
        group = Group.__new__(Group)
        group.halved, group.stage = self.halved, self.stage
        group.segments = {**self.segments, **other.segments}
        group.state = {**self.state, **other.state}
        group.keeps, group.recvs = self.keeps + other.keeps, self.recvs + other.recvs
        group.stages = []
        for mine, others in zip(self.stages, other.stages):
            entries = {}
            for entry in mine + others:
                entries.setdefault(entry[:3] + entry[4:], []).extend(entry[3])
            if len(group.stages) == group.stage:
                group.stages.append(mine + others)
            else:
                group.stages.append([key[:3] + (tuple(names),) + key[3:] for key, names in entries.items()])
        return group

    def height(self, name):
        height, whole, _ = self.segments[name]
        slots, cut = self.state[name]
        return height if whole else height // cut * slots

    def start(self, sends):
        self.sends = sends
        self.recvs = [swap(send, *entry[:3]) for send, entry in zip(sends, self.stages[self.stage])]

    def begin(self, keep, send):
        entry = self.stages[0][len(self.keeps)]
        self.keeps.append(keep)
        self.recvs.append(swap(send, *entry[:3]))

    def fold(self):
        places = {}
        for source, entry in enumerate(self.stages[self.stage]):
            at = 0
            for name in entry[3]:
                places[name] = (source, at, self.height(name), self.state[name][0])
                at += self.height(name)
        shapes, moves, keeps, sends = [], [], [], []
        for entry in self.stages[self.stage + 1]:
            split = entry[4]
            keeps.append(len(shapes))
            sends.append(len(shapes) + (0 if split == "none" else 1))
            targets = (keeps[-1],) if split == "none" else (keeps[-1], sends[-1])
            to = 0
            for name in entry[3]:
                whole = self.segments[name][1]
                if split == "slots":
                    self.state[name][0] //= 2
                elif split == "rows":
                    self.state[name][1] = 2
                moves.append(places[name] + (targets, to, "none" if whole else split))
                to += self.height(name)
            shapes += [sds((to, TILE), BF16)] * len(targets)
        args = [x for pair in zip(self.keeps, self.recvs) for x in pair]
        out = call(functools.partial(fold_kernel, moves, len(args) // 2), args, shapes, 0.5, limit=4)
        self.keeps = [out[i] for i in keeps]
        self.sends = [out[i] for i in sends]
        self.stage += 1

    def left(self):
        return len(self.stages) - 1 - self.stage

    def pair(self):
        return self.keeps[0], self.recvs[0]


def result_kernel(sp_size, halved, *refs):
    outs = refs[8:16]
    gain_scr, shift_scr, qkv_scr, out_scr, up_scr, bup_scr, down_scr, bdown_scr = refs[16:24]
    mlp1, both, up0, qkv0 = refs[24:28]
    small_scr, sems = refs[28:]
    size = TILE // sp_size
    chunks = up_scr.shape[2] // TILE
    down_size = chunks * size
    row_half = lax.rem(lax.axis_index("grp"), 2)
    segments = (
        (mlp1, (chunks * size, down_size)), (both, (4 * size, down_size)),
        (up0, (chunks * size + size,)), (qkv0, (3 * size,)),
    )
    for i, (scr, heights) in enumerate(segments):
        mine, other = refs[2 * i], refs[2 * i + 1]
        at = 0
        base = 0
        for height in heights:
            if halved[i]:
                half = height // 2
                for ref, side in ((mine, row_half), (other, 1 - row_half)):
                    place = pl.ds(pl.multiple_of(base + side * half, 16), half)
                    scr[place, :] = ref[at : at + half, :].astype(F32)
                at += half
            else:
                span = slice(at, at + height)
                scr[base : base + height, :] = mine[span, :].astype(F32) + other[span, :].astype(F32)
                at += height
            base += height
    mine, other = refs[6], refs[7]
    at = 3 * size // (2 if halved[3] else 1)
    small = mine[at : at + 32, :].astype(F32)
    small_scr[...] = small if halved[3] else small + other[at : at + 32, :].astype(F32)
    for layer, (qkv, up, down, out, first, last) in enumerate((
        (qkv0, up0, both, up0, 4 * size, chunks * size),
        (both, mlp1, mlp1, both, chunks * size, 3 * size),
    )):
        for j in range(3):
            qkv_scr[layer, :, j * TILE : (j + 1) * TILE] = qkv[j * size : (j + 1) * size, :]
        for j in range(chunks):
            up_scr[layer, :, j * TILE : (j + 1) * TILE] = up[j * size : (j + 1) * size, :]
        down_scr[layer] = down[first : first + down_size, :]
        out_scr[layer] = out[last : last + size, :]
    sp = lax.axis_index("sp")
    back = lax.rem(TILE - sp * size, TILE)
    turned = pltpu.roll(small_scr[...], back, 1)
    for i in range(4):
        gain_scr[i : i + 1, :] = turned[8 * i : 8 * i + 1, :size]
        shift_scr[i : i + 1, :] = turned[8 * i + 1 : 8 * i + 2, :size]
    start = sp * down_size
    line = start // TILE
    back = lax.rem(TILE - lax.rem(start, TILE), TILE)
    for layer in range(2):
        first = 8 + 16 * layer
        bdown_scr[layer : layer + 1, :] = turned[first + 2 : first + 3, :size]
        rows = small_scr[first : first + 8, :]
        lines = lax.broadcasted_iota(jnp.int32, rows.shape, 0)
        picked = jnp.sum(jnp.where(lines == 4 + line, rows, 0.0), axis=0, keepdims=True)
        picked = pltpu.roll(jnp.broadcast_to(picked, rows.shape), back, 1)
        bup_scr[layer : layer + 1, :] = picked[0:1, :down_size]
    scrs = (gain_scr, shift_scr, qkv_scr, out_scr, up_scr, bup_scr, down_scr, bdown_scr)
    copies = [pltpu.make_async_copy(scr, out, sems.at[i]) for i, (scr, out) in enumerate(zip(scrs, outs))]
    for copy in copies:
        copy.start()
    for copy in copies:
        copy.wait()


VMEM = pl.BlockSpec(memory_space=pltpu.VMEM)
SMEM = pl.BlockSpec(memory_space=pltpu.SMEM)
HBM = pl.BlockSpec(memory_space=pltpu.HBM)


def sds(shape, dtype):
    return jax.ShapeDtypeStruct(shape, dtype)


def call(kernel, args, outs, micros, scratch=(), specs=None, out_specs=None, limit=12):
    return pl.pallas_call(
        kernel,
        in_specs=[VMEM] * len(args) if specs is None else specs,
        out_specs=[VMEM] * len(outs) if out_specs is None else out_specs,
        out_shape=outs,
        scratch_shapes=list(scratch),
        compiler_params=pltpu.CompilerParams(vmem_limit_bytes=limit * MIB),
        cost_estimate=pl.CostEstimate(flops=int(micros * COST), bytes_accessed=0, transcendentals=0),
    )(*args)


def swap(array, axis, size, bit):
    return lax.ppermute(array, axis, [(i, i ^ (1 << bit)) for i in range(size)])


def shards(sizes, tokens, frame_slot, norm_gain, norm_shift, w_qkv, w_out, w_up, b_up, w_down, b_down, cotangent):
    grp_size, sp_size = sizes
    frames, patches, width = tokens.shape
    hidden = w_up.shape[2]
    assert GROUP_FRAMES == 2 * frames and sp_size >= 8
    half = patches // 2
    rows = frames * patches
    sp_bits = sp_size.bit_length() - 1
    core_swap = functools.partial(swap, axis="sp", size=sp_size, bit=0)
    slots = sp_size // 2
    size = width // sp_size
    down_size = hidden // sp_size
    def slots_of(path):
        return [step for step in path if step != ROWS] + list(range(4, sp_bits))

    path_up1, path_down1 = (0, 1, 2, ROWS, 3), (0, 2, 1, ROWS, 3)
    path_attn1, path_down0 = (0, ROWS, 2, 1, 3), (0, 2, 1, ROWS, 3)
    path_up0, path_qkv0 = (0, 1, ROWS, 2, 3), (0, ROWS, 2, 1, 3)

    def row_out(cols, dtype=BF16):
        return sds((rows, cols), dtype)

    half_out = sds((frames, half, width), BF16)
    small_out = sds((8, TILE), F32)
    fence = lambda *arrays: lax.optimization_barrier(arrays)

    token = []

    def meet(groups, *arrays):
        recvs = [r for g in groups for r in g.recvs]
        out = list(fence(*arrays, *recvs, *token))
        count = len(arrays)
        arrays, recvs = out[:count], out[count:]
        for g in groups:
            g.recvs = [recvs.pop(0) for _ in g.recvs]
            g.fold()
        sends = [x for g in groups for x in g.sends]
        out = list(fence(*arrays, *sends))
        arrays, sends = out[:count], out[count:]
        for g in groups:
            g.start([sends.pop(0) for _ in g.sends])
        token[:] = [groups[-1].sends[-1]] if groups else []
        return arrays

    def buffers(height):
        return [sds((slots * height, TILE), BF16)] * 2

    cot_recv = core_swap(cotangent)
    widen = lambda a: jnp.pad(a, ((0, 0), (0, hidden - width)))
    packed = jnp.concatenate([widen(norm_gain), widen(norm_shift), b_up, widen(b_down)], axis=0)
    weights = (w_qkv, w_out, w_up, w_down)
    shapes = [sds(w.shape[1:], BF16) for w in weights]
    out = call(
        space_forward_kernel,
        (tokens, packed) + weights,
        [
            half_out, half_out, row_out(width), row_out(3 * width), sds((frames, HEADS, patches), F32),
            row_out(width), row_out(width, F32), row_out(width), row_out(hidden), row_out(hidden),
        ],
        16,
        scratch=[pltpu.VMEM(tokens.shape, BF16)]
        + [pltpu.VMEM(x.shape, BF16) for x in shapes]
        + [
            pltpu.VMEM((2, patches, width), BF16), pltpu.VMEM((2, patches, 3 * width), BF16),
            pltpu.VMEM((2, patches, width), BF16), pltpu.VMEM((2, patches, width), F32),
            pltpu.VMEM((2, patches, width), BF16),
            pltpu.VMEM((2, patches, hidden), BF16), pltpu.VMEM((2, patches, hidden), BF16),
            pltpu.VMEM((patches, width), F32), pltpu.SemaphoreType.DMA((5,)),
            pltpu.SemaphoreType.DMA((14,)),
        ],
        specs=[HBM, VMEM] + [HBM] * 4,
        out_specs=[VMEM, VMEM, HBM, HBM, VMEM] + [HBM] * 5,
        limit=LIMIT1,
    )
    (x_keep, x_send, h0, qkv0, lse0, o0, xa, h1, act0, slope0) = out
    x_recv = core_swap(x_send)

    place_scratch = [
        pltpu.SMEM((GROUP_FRAMES,), jnp.int32),
        pltpu.VMEM((GROUP_FRAMES, half, width), BF16),
    ]
    (out_own, out_send, xt, h2, qkv1, o1, h3, act1, du1, gr1, dxb, small3, w_qkv1, w_out1) = call(
        time_forward_kernel,
        (frame_slot, x_keep, x_recv, cotangent, cot_recv, packed) + weights,
        [
            half_out, half_out, row_out(width), row_out(width), row_out(3 * width), row_out(width),
            row_out(width), row_out(hidden), row_out(hidden), row_out(width), row_out(width, F32),
            small_out,
        ] + shapes[:2],
        24,
        scratch=place_scratch
        + [pltpu.VMEM((rows // 4, hidden), BF16)]
        + [pltpu.VMEM(x.shape, BF16) for x in shapes[2:]]
        + [pltpu.SemaphoreType.DMA((4,))],
        specs=[SMEM] + [VMEM] * 5 + [HBM] * 4,
        limit=LIMIT2,
    )
    out_recv = core_swap(out_send)

    out = call(
        functools.partial(mlp_weights_kernel, (slots_of(path_up1), slots_of(path_down1))), (h3, du1, act1, gr1),
        buffers(4 * size + down_size), 4.5,
    )
    keep, send, dxb = fence(*out, dxb)
    mlp1 = Group(sizes, {"up": (4 * size, False, path_up1), "down": (down_size, False, path_down1)})
    mlp1.begin(keep, send)

    (dx_own, dx_send, ar1, dqkv1, small2) = call(
        time_backward_kernel,
        (frame_slot, xt, qkv1, dxb, packed, w_qkv1, w_out1),
        [half_out, half_out, row_out(width), row_out(3 * width), small_out],
        8,
        scratch=place_scratch,
        specs=[SMEM] + [VMEM] * 6,
    )
    dx_recv = core_swap(dx_send)
    keep, send = call(
        functools.partial(attn_weights_kernel, slots_of(path_attn1)), (h2, dqkv1, o1, ar1),
        buffers(4 * size), 2.4,
    )
    dx_own, dx_recv, keep, send, out_recv = meet((mlp1,), dx_own, dx_recv, keep, send, out_recv)
    attn1 = Group(sizes, {"attn": (4 * size, False, path_attn1)})
    attn1.begin(keep, send)
    gr0, keep_down, send_down = call(
        functools.partial(down_weights_kernel, slots_of(path_down0)), (act0, dx_own, dx_recv),
        [row_out(width)] + buffers(down_size), 2.4,
    )
    (du0, dxa, ar0, small1) = call(
        space_mlp_back_kernel,
        (gr0, xa, slope0, packed, w_up, w_down),
        [row_out(hidden), row_out(width, F32), row_out(width), small_out],
        6,
    )
    keep_up, send_up = call(
        functools.partial(up_weights_kernel, slots_of(path_up0)), (h1, du0, o0, ar0), buffers(5 * size), 3
    )
    keep_down, send_down, keep_up, send_up, ar0 = meet(
        (mlp1, attn1), keep_down, send_down, keep_up, send_up, ar0
    )
    down0 = Group(sizes, {"down": (down_size, False, path_down0)})
    down0.begin(keep_down, send_down)
    up0 = Group(sizes, {"up": (5 * size, False, path_up0)})
    up0.begin(keep_up, send_up)

    (dqkv0,) = call(
        space_attn_back_kernel, (ar0, qkv0, lse0, o0, w_out), [row_out(3 * width)], 10
    )
    keep, send = call(
        functools.partial(qkv_weights_kernel, slots_of(path_qkv0)), (dqkv0, h0), buffers(3 * size), 2
    )
    dqkv0, keep, send, *attn1.recvs = meet((up0, down0, mlp1), dqkv0, keep, send, *attn1.recvs)
    both = attn1.beside(down0)
    qkv = Group(
        sizes, {"qkv": (3 * size, False, path_qkv0), "small": (32, True, path_qkv0)}, apart=True
    )
    qkv.begin(keep, send)
    grad_tokens, output, small = call(
        finish_kernel,
        (
            dqkv0, tokens, dxa, out_own, out_recv, packed, w_qkv, small1, small2, small3,
        ),
        [sds(tokens.shape, BF16), sds(tokens.shape, BF16), sds((32, TILE), BF16)],
        4,
        scratch=[pltpu.VMEM((8, TILE), F32)],
    )
    (small,) = fence(small)
    qkv.begin(small, small)
    everyone = (mlp1, both, up0, qkv)
    for names in TAIL:
        groups = [g for g in (dict(zip("mbuq", everyone))[c] for c in names) if g.left()]
        if groups:
            meet(groups)
    while any(g.left() for g in everyone):
        meet([g for g in everyone if g.left()])
    finals = [
        sds((4, size), F32), sds((4, size), F32), sds((2, size, 3 * width), F32), sds((2, size, width), F32),
        sds((2, size, hidden), F32), sds((2, down_size), F32), sds((2, down_size, width), F32),
        sds((2, size), F32),
    ]
    heights = (4 * size + down_size, 4 * size + down_size, 5 * size, 3 * size)
    results = call(
        functools.partial(result_kernel, sp_size, tuple(g.halved for g in everyone)),
        [x for g in everyone for x in g.pair()], finals, 2,
        scratch=[pltpu.VMEM(f.shape, F32) for f in finals]
        + [pltpu.VMEM((h, TILE), F32) for h in heights]
        + [pltpu.VMEM((32, TILE), F32), pltpu.SemaphoreType.DMA((8,))],
        out_specs=[HBM] * 8,
    )
    return (output, grad_tokens, *results)


def solution(mesh):
    rows = P(("grp", "sp"), None, None)
    in_specs = (rows, P("grp", None), P(), P(), P(), P(), P(), P(), P(), P(), rows)
    out_specs = (
        rows, rows, P(None, "sp"), P(None, "sp"), P(None, "sp", None), P(None, "sp", None),
        P(None, "sp", None), P(None, "sp"), P(None, "sp", None), P(None, "sp"),
    )
    body = functools.partial(shards, (mesh.shape["grp"], mesh.shape["sp"]))
    return jax.shard_map(body, mesh=mesh, in_specs=in_specs, out_specs=out_specs, check_vma=False)
```

```python
import functools

import jax
import jax.numpy as jnp
from jax import lax
from jax.experimental import pallas as pl
from jax.experimental.pallas import tpu as pltpu
from jax.sharding import PartitionSpec as P

HEADS = 8
HEAD = 64
VIDEO_STEPS = 6
GROUP_FRAMES = 8
NORM_EPS = 1e-05
TILE = 512
STEP = 1024
SCALE = HEAD**-0.5
TANH_A = 0.7978845608028654
TANH_B = TANH_A * 0.044715
PAIRS = [(t, s) for t in range(VIDEO_STEPS) for s in range(t + 1)]
F32 = jnp.float32
BF16 = jnp.bfloat16
MIB = 1024 * 1024
ROWS = -1
COST = 1.15e9 * 0.02
TAIL = ("q", "m", "bu", "q", "m", "bu", "q", "bu", "q", "bu", "q")
LIMIT1 = 52
LIMIT2 = 24


def dot(left, right):
    return jnp.dot(left, right, preferred_element_type=F32)


def dot_nt(left, right):
    return lax.dot_general(left, right, (((1,), (1,)), ((), ())), preferred_element_type=F32)


def dot_tn(left, right):
    return lax.dot_general(left, right, (((0,), (0,)), ((), ())), preferred_element_type=F32)


def norm(rows, gain, shift):
    centred = rows - jnp.mean(rows, axis=-1, keepdims=True)
    inv = lax.rsqrt(jnp.mean(centred * centred, axis=-1, keepdims=True) + NORM_EPS)
    unit = centred * inv
    return unit * gain + shift, unit, inv


def norm_back(grad, unit, inv, gain):
    grad_unit = grad * gain
    mean_grad = jnp.mean(grad_unit, axis=-1, keepdims=True)
    mean_both = jnp.mean(grad_unit * unit, axis=-1, keepdims=True)
    return inv * (grad_unit - mean_grad - unit * mean_both)


def column_sum(rows):
    return jnp.sum(rows, axis=0, keepdims=True)


def gelu_pair(u):
    square = u * u
    sigma = 0.5 + 0.5 * jnp.tanh(u * (TANH_A + TANH_B * square))
    act = u * sigma
    slope = sigma + act * (1.0 - sigma) * (2.0 * TANH_A + 6.0 * TANH_B * square)
    return act.astype(BF16), slope.astype(BF16)


def head_mask(lanes, which):
    lane = lax.broadcasted_iota(jnp.int32, lanes.shape, 1)
    return (lane < HEAD) if which == 0 else (lane >= HEAD)


def qkv_rows(normed, weight):
    out = []
    for part in range(3):
        piece = dot(normed, weight[:, part * TILE : (part + 1) * TILE])
        if part == 0:
            out.append(piece.astype(BF16) * BF16(SCALE))
        else:
            out.append(piece.astype(BF16))
    return out


def mlp_forward(normed, w_up, b_up, w_down, rows, act_ref, slope_ref):
    chunks = w_up.shape[1] // STEP
    up = lambda j: dot(normed, w_up[:, j * STEP : (j + 1) * STEP])
    total = None
    u = up(0)
    for j in range(chunks):
        cols = slice(j * STEP, (j + 1) * STEP)
        later = up(j + 1) if j + 1 < chunks else None
        act, slope = gelu_pair(u + b_up[0:1, cols])
        act_ref[rows, cols] = act
        slope_ref[rows, cols] = slope
        piece = dot(act, w_down[cols, :])
        total = piece if total is None else total + piece
        u = later
    return total


def mlp_backward(grad_low, w_up, w_down, rows, slope_ref, du_ref):
    chunks = w_up.shape[1] // STEP
    down = lambda j: dot_nt(grad_low, w_down[j * STEP : (j + 1) * STEP, :])
    total = None
    sums = []
    da = down(0)
    for j in range(chunks):
        cols = slice(j * STEP, (j + 1) * STEP)
        later = down(j + 1) if j + 1 < chunks else None
        du = (da * slope_ref[rows, cols].astype(F32)).astype(BF16)
        du_ref[rows, cols] = du
        sums.append(column_sum(du.astype(F32)))
        piece = dot_nt(du, w_up[:, cols])
        total = piece if total is None else total + piece
        da = later
    return total, [x[:, k : k + TILE] for x in sums for k in range(0, STEP, TILE)]


def add_small(small_ref, values, first):
    for i, value in enumerate(values):
        row = slice(i, i + 1) if i < 4 else slice(i, i + 1)
        if value is None:
            continue
        if first:
            small_ref[row, :] = value
        else:
            small_ref[row, :] += value


def rows_at(index, count):
    return pl.ds(pl.multiple_of(index * count, count), count)


def half_rows(part, half):
    return pl.ds(pl.multiple_of(part * half, half), half)


def space_forward_kernel(
    tok_hbm, params_ref, wqkv_hbm, wout_hbm, wup_hbm, wdown_hbm,
    keep_ref, send_ref, h0_hbm, qkv_hbm, lse_ref, o_hbm, xa_hbm, h1_hbm, act_hbm, slope_hbm,
    tok_ref, wqkv_ref, wout_ref, wup_ref, wdown_ref, h0_scr, qkv_scr, o_scr, xa_scr, h1_scr, act_scr,
    slope_scr, x1_scr, in_sems, out_sems,
):
    pairs = [
        (tok_hbm, tok_ref), (wqkv_hbm.at[0], wqkv_ref), (wout_hbm.at[0], wout_ref),
        (wup_hbm.at[0], wup_ref), (wdown_hbm.at[0], wdown_ref),
    ]
    copies = [pltpu.make_async_copy(src, dst, in_sems.at[i]) for i, (src, dst) in enumerate(pairs)]
    for copy in copies[:2]:
        copy.start()
    gain_ref, shift_ref = params_ref.at[0:4, 0:TILE], params_ref.at[4:8, 0:TILE]
    part = lax.rem(lax.axis_index("sp"), 2)
    frames, rows = tok_ref.shape[0], tok_ref.shape[1]
    half = rows // 2
    lane = lax.broadcasted_iota(jnp.int32, (rows, 128), 1)
    places = (
        (h0_scr, h0_hbm), (qkv_scr, qkv_hbm), (o_scr, o_hbm), (xa_scr, xa_hbm), (h1_scr, h1_hbm),
        (act_scr, act_hbm), (slope_scr, slope_hbm),
    )

    def spills(f):
        now = lax.rem(f, 2)
        return [
            pltpu.make_async_copy(scr.at[now], hbm.at[rows_at(f, rows)], out_sems.at[7 * now + i])
            for i, (scr, hbm) in enumerate(places)
        ]

    def await_first(f, *which):
        @pl.when(f == 0)
        def _():
            for i in which:
                copies[i].wait()

    copies[0].wait()
    for copy in copies[2:]:
        copy.start()

    @pl.loop(0, frames)
    def _(f):
        now = lax.rem(f, 2)
        spill = spills(f)

        @pl.when(f >= 2)
        def _():
            for copy in spills(f - 2):
                copy.wait()

        x0 = tok_ref[f].astype(F32)
        h0 = norm(x0, gain_ref[0:1, :], shift_ref[0:1, :])[0].astype(BF16)
        h0_scr[now] = h0
        spill[0].start()
        await_first(f, 1)
        q, k, v = qkv_rows(h0, wqkv_ref)
        qkv_scr[now, :, 0:TILE] = q
        qkv_scr[now, :, TILE : 2 * TILE] = k
        qkv_scr[now, :, 2 * TILE :] = v
        spill[1].start()
        lse_all = jnp.zeros((rows, 128), F32)
        mixed = []
        for pair in range(HEADS // 2):
            cols = slice(pair * 128, (pair + 1) * 128)
            qp, kp, vp = q[:, cols], k[:, cols], v[:, cols]
            zero = jnp.zeros_like(qp)
            mask = head_mask(qp, 0)
            s = dot_nt(jnp.concatenate([jnp.where(mask, qp, zero), jnp.where(mask, zero, qp)], axis=0), kp)
            top = jnp.max(s, axis=-1, keepdims=True)
            p = jnp.exp(s - top)
            total = jnp.sum(p, axis=-1, keepdims=True)
            both = dot(p.astype(BF16), vp) * (1.0 / total)
            lse = top + jnp.log(total)
            lse_all = jnp.where(lane == 2 * pair, lse[:rows], lse_all)
            lse_all = jnp.where(lane == 2 * pair + 1, lse[rows:], lse_all)
            mixed.append(jnp.where(mask, both[:rows], both[rows:]).astype(BF16))
        lse_ref[f] = jnp.transpose(lse_all)[0:HEADS, :]
        o = jnp.concatenate(mixed, axis=1)
        o_scr[now] = o
        spill[2].start()
        await_first(f, 2)
        xa = x0 + dot(o, wout_ref[...])
        xa_scr[now] = xa
        spill[3].start()
        h1 = norm(xa, gain_ref[1:2, :], shift_ref[1:2, :])[0].astype(BF16)
        h1_scr[now] = h1
        spill[4].start()
        await_first(f, 3, 4)
        branch = mlp_forward(
            h1, wup_ref, params_ref.at[8:9], wdown_ref, slice(None), act_scr.at[now], slope_scr.at[now]
        )
        spill[5].start()
        spill[6].start()
        x1_scr[...] = xa + branch + params_ref[10:11, 0:TILE]
        keep_ref[f] = x1_scr[half_rows(part, half), :].astype(BF16)
        send_ref[f] = x1_scr[half_rows(1 - part, half), :].astype(BF16)

    for f in (frames - 2, frames - 1):
        for copy in spills(jnp.int32(f)):
            copy.wait()


def lane_heads(dtype):
    c = lax.broadcasted_iota(jnp.int32, (TILE, 128), 0)
    h = lax.broadcasted_iota(jnp.int32, (TILE, 128), 1)
    return (c // HEAD == h).astype(dtype)


def slot_places(slots_ref, where_scr, frames):
    sp = lax.axis_index("sp")
    group = (sp * frames) // GROUP_FRAMES
    part = lax.rem(sp, GROUP_FRAMES // frames)
    for t in range(GROUP_FRAMES):
        where_scr[slots_ref[group, t]] = lax.rem(t + GROUP_FRAMES - part * frames, GROUP_FRAMES)


def time_scores(q, k, spread):
    parts = []
    for t, s in PAIRS:
        parts.append((q[t] * k[s]).astype(BF16))
    return dot(jnp.concatenate(parts, axis=0), spread)


def time_probs(scores, count):
    blocks = [scores[i * count : (i + 1) * count] for i in range(len(PAIRS))]
    probs = []
    at = 0
    for t in range(VIDEO_STEPS):
        mine = blocks[at : at + t + 1]
        at += t + 1
        top = functools.reduce(jnp.maximum, mine)
        raw = [jnp.exp(b - top) for b in mine]
        inv = 1.0 / functools.reduce(lambda a, b: a + b, raw)
        probs.extend([r * inv for r in raw])
    return probs


def split_slots(rows):
    count = rows.shape[0] // GROUP_FRAMES
    return [rows[s * count : (s + 1) * count].astype(F32) for s in range(GROUP_FRAMES)]


def time_forward_kernel(
    slots_ref, keep_ref, recv_ref, cot_ref, cotr_ref, params_ref,
    wqkv_hbm, wout_hbm, wup_hbm, wdown_hbm,
    own_ref, send_ref, x_ref, h2_ref, qkv_ref, o_ref, h3_ref, act_ref, du_ref, gr_ref, dxb_ref,
    small_ref, wqkv_ref, wout_ref,
    where_scr, both_scr, slope_scr, wup_ref, wdown_ref, in_sems,
):
    pairs = [(wqkv_hbm, wqkv_ref), (wout_hbm, wout_ref), (wup_hbm, wup_ref), (wdown_hbm, wdown_ref)]
    copies = [pltpu.make_async_copy(src.at[1], dst, in_sems.at[i]) for i, (src, dst) in enumerate(pairs)]
    for copy in copies:
        copy.start()
    gain_ref, shift_ref = params_ref.at[0:4, 0:TILE], params_ref.at[4:8, 0:TILE]
    frames, half = keep_ref.shape[0], keep_ref.shape[1]
    part = lax.rem(lax.axis_index("sp"), GROUP_FRAMES // frames)
    slot_places(slots_ref, where_scr, frames)
    small_ref[...] = jnp.zeros_like(small_ref)
    both_scr[0:frames] = keep_ref[...]
    both_scr[frames:] = recv_ref[...]
    spread = lane_heads(BF16)
    steps = 4
    count = half // steps
    step_rows = count * GROUP_FRAMES

    def await_first(i, *which):
        @pl.when(i == 0)
        def _():
            for w in which:
                copies[w].wait()

    @pl.loop(0, steps)
    def _(i):
        span = rows_at(i, step_rows)
        place = rows_at(i, count)
        x_low = jnp.concatenate([both_scr[where_scr[s], place] for s in range(GROUP_FRAMES)], axis=0)
        x_ref[span, :] = x_low
        x = x_low.astype(F32)
        h2 = norm(x, gain_ref[2:3, :], shift_ref[2:3, :])[0].astype(BF16)
        h2_ref[span, :] = h2
        await_first(i, 0)
        q, k, v = qkv_rows(h2, wqkv_ref)
        qkv_ref[span, 0:TILE] = q
        qkv_ref[span, TILE : 2 * TILE] = k
        qkv_ref[span, 2 * TILE :] = v
        qs, ks, vs = split_slots(q), split_slots(k), split_slots(v)
        probs = time_probs(time_scores(qs, ks, spread), count)
        wide = dot_nt(jnp.concatenate([p.astype(BF16) for p in probs], axis=0), spread)
        mixed = []
        at = 0
        for t in range(VIDEO_STEPS):
            total = None
            for s in range(t + 1):
                piece = wide[at * count : (at + 1) * count] * vs[s]
                total = piece if total is None else total + piece
                at += 1
            mixed.append(total)
        mixed.extend(vs[VIDEO_STEPS:])
        o = jnp.concatenate([m.astype(BF16) for m in mixed], axis=0)
        o_ref[span, :] = o
        await_first(i, 1)
        xb = x + dot(o, wout_ref[...]).astype(BF16).astype(F32)
        h3, unit, inv = norm(xb, gain_ref[3:4, :], shift_ref[3:4, :])
        h3 = h3.astype(BF16)
        h3_ref[span, :] = h3
        slope = slope_scr
        await_first(i, 2, 3)
        branch = mlp_forward(h3, wup_ref, params_ref.at[9:10], wdown_ref, span, act_ref, SpanView(slope))
        out = (xb + branch + params_ref[11:12, 0:TILE]).astype(BF16)
        for s in range(GROUP_FRAMES):
            both_scr[where_scr[s], place] = out[s * count : (s + 1) * count]
        grad_low = jnp.concatenate(
            [cot_slot(cot_ref, cotr_ref, where_scr[s], part * half + i * count, count) for s in range(GROUP_FRAMES)],
            axis=0,
        )
        gr_ref[span, :] = grad_low
        grad = grad_low.astype(F32)
        dh, sums = mlp_backward(grad_low, wup_ref, wdown_ref, span, SpanView(slope), du_ref)
        add_small(small_ref, [column_sum(dh * unit), column_sum(dh), column_sum(grad), None] + sums, False)
        dxb_ref[span, :] = grad + norm_back(dh, unit, inv, gain_ref[3:4, :])

    own_ref[...] = both_scr[0:frames]
    send_ref[...] = both_scr[frames:]


class SpanView:
    def __init__(self, ref):
        self.ref = ref

    def __getitem__(self, index):
        return self.ref[:, index[1]]

    def __setitem__(self, index, value):
        self.ref[:, index[1]] = value


def cot_slot(cot_ref, cotr_ref, frame, start, count):
    frames = cot_ref.shape[0]
    places = pl.ds(pl.multiple_of(start, count), count)
    mine = cot_ref[lax.rem(frame, frames), places, :]
    other = cotr_ref[lax.rem(frame, frames), places, :]
    return jnp.where(frame < frames, mine, other)


def time_backward_kernel(
    slots_ref, x_ref, qkv_ref, dxb_ref, params_ref, wqkv_ref, wout_ref,
    own_ref, send_ref, ar_ref, dqkv_ref, small_ref,
    where_scr, both_scr,
):
    frames, half = own_ref.shape[0], own_ref.shape[1]
    slot_places(slots_ref, where_scr, frames)
    small_ref[...] = jnp.zeros_like(small_ref)
    spread = lane_heads(BF16)
    steps = 4
    count = half // steps
    step_rows = count * GROUP_FRAMES
    gain = params_ref[2:3, 0:TILE]

    @pl.loop(0, steps)
    def _(i):
        span = rows_at(i, step_rows)
        place = rows_at(i, count)
        dxb = dxb_ref[span, :]
        ar = dxb.astype(BF16)
        ar_ref[span, :] = ar
        do = split_slots(dot_nt(ar, wout_ref[...]).astype(BF16))
        qs = split_slots(qkv_ref[span, 0:TILE])
        ks = split_slots(qkv_ref[span, TILE : 2 * TILE])
        vs = split_slots(qkv_ref[span, 2 * TILE :])
        probs = time_probs(time_scores(qs, ks, spread), count)
        dps = time_scores(do, vs, spread)
        dps = [dps[j * count : (j + 1) * count] for j in range(len(PAIRS))]
        dss = []
        at = 0
        for t in range(VIDEO_STEPS):
            centre = functools.reduce(
                lambda a, b: a + b, [probs[at + s] * dps[at + s] for s in range(t + 1)]
            )
            dss.extend([probs[at + s] * (dps[at + s] - centre) for s in range(t + 1)])
            at += t + 1
        wide_p = dot_nt(jnp.concatenate([p.astype(BF16) for p in probs], axis=0), spread)
        wide_ds = dot_nt(jnp.concatenate([d.astype(BF16) for d in dss], axis=0), spread)
        dq = [None] * GROUP_FRAMES
        dk = [None] * GROUP_FRAMES
        dv = [None] * GROUP_FRAMES

        def add(table, index, piece):
            table[index] = piece if table[index] is None else table[index] + piece

        for j, (t, s) in enumerate(PAIRS):
            rows = slice(j * count, (j + 1) * count)
            add(dq, t, wide_ds[rows] * ks[s])
            add(dk, s, wide_ds[rows] * qs[t])
            add(dv, s, wide_p[rows] * do[t])
        for t in range(VIDEO_STEPS, GROUP_FRAMES):
            dq[t] = jnp.zeros_like(do[t])
            dk[t] = jnp.zeros_like(do[t])
            dv[t] = do[t]
        dq = jnp.concatenate([(d * SCALE).astype(BF16) for d in dq], axis=0)
        dk = jnp.concatenate([d.astype(BF16) for d in dk], axis=0)
        dv = jnp.concatenate([d.astype(BF16) for d in dv], axis=0)
        dqkv_ref[span, 0:TILE] = dq
        dqkv_ref[span, TILE : 2 * TILE] = dk
        dqkv_ref[span, 2 * TILE :] = dv
        dh = dot_nt(dqkv_ref[span, :], wqkv_ref[...])
        unit, inv = norm(x_ref[span, :].astype(F32), gain, params_ref[6:7, 0:TILE])[1:]
        add_small(small_ref, [column_sum(dh * unit), column_sum(dh)], False)
        dxp = norm_back(dh, unit, inv, gain).astype(BF16).astype(F32)
        dx1 = (dxb + dxp).astype(BF16)
        for s in range(GROUP_FRAMES):
            both_scr[where_scr[s], place] = dx1[s * count : (s + 1) * count]

    own_ref[...] = both_scr[0:frames]
    send_ref[...] = both_scr[frames:]


def space_mlp_back_kernel(
    gr_ref, xa_ref, slope_ref, params_ref, wup_ref, wdown_ref,
    du_ref, dxa_ref, ar_ref, small_ref,
):
    small_ref[...] = jnp.zeros_like(small_ref)
    rows = 256
    gain = params_ref[1:2, 0:TILE]

    @pl.loop(0, gr_ref.shape[0] // rows)
    def _(f):
        span = rows_at(f, rows)
        grad_low = gr_ref[span, :]
        grad = grad_low.astype(F32)
        dh, sums = mlp_backward(grad_low, wup_ref.at[0], wdown_ref.at[0], span, slope_ref, du_ref)
        unit, inv = norm(xa_ref[span, :], gain, params_ref[5:6, 0:TILE])[1:]
        add_small(small_ref, [column_sum(dh * unit), column_sum(dh), column_sum(grad), None] + sums, False)
        dxa = grad + norm_back(dh, unit, inv, gain)
        dxa_ref[span, :] = dxa
        ar_ref[span, :] = dxa.astype(BF16)


def head_picker():
    h = lax.broadcasted_iota(jnp.int32, (HEADS, TILE), 0)
    c = lax.broadcasted_iota(jnp.int32, (HEADS, TILE), 1)
    return (c // HEAD == h).astype(BF16)


def attn_back_frame(f, ar_ref, qkv_ref, lse_ref, o_ref, wout_ref, pick, dqkv_ref):
    rows = lse_ref.shape[2]
    span = rows_at(f, rows)
    do = dot_nt(ar_ref[span, :], wout_ref[0]).astype(BF16)
    both = do.astype(F32) * o_ref[span, :].astype(F32)
    high = both.astype(BF16)
    rest = (both - high.astype(F32)).astype(BF16)
    centre = dot_nt(pick, high) + dot_nt(pick, rest)
    for pair in range(HEADS // 2):
        qp = qkv_ref[span, pair * 128 : (pair + 1) * 128]
        kp = qkv_ref[span, TILE + pair * 128 : TILE + (pair + 1) * 128]
        vp = qkv_ref[span, 2 * TILE + pair * 128 : 2 * TILE + (pair + 1) * 128]
        dop = do[:, pair * 128 : (pair + 1) * 128]
        zero = jnp.zeros_like(kp)
        mask = head_mask(kp, 0)
        st = dot_nt(jnp.concatenate([jnp.where(mask, kp, zero), jnp.where(mask, zero, kp)], axis=0), qp)
        dpt = dot_nt(jnp.concatenate([jnp.where(mask, vp, zero), jnp.where(mask, zero, vp)], axis=0), dop)
        pts, dsts, dqs = [], [], []
        for e in range(2):
            row = slice(2 * pair + e, 2 * pair + e + 1)
            keys = slice(e * rows, (e + 1) * rows)
            pt = jnp.exp(st[keys] - lse_ref[f, row, :])
            dst = (pt * (dpt[keys] - centre[row, :])).astype(BF16)
            pts.append(pt.astype(BF16))
            dsts.append(dst)
            dqs.append(dot_tn(dst, kp) * SCALE)
        dk = dot(jnp.concatenate(dsts, axis=0), qp)
        dv = dot(jnp.concatenate(pts, axis=0), dop)
        values = (
            jnp.where(mask, dqs[0], dqs[1]),
            jnp.where(mask, dk[:rows], dk[rows:]),
            jnp.where(mask, dv[:rows], dv[rows:]),
        )
        for index, value in enumerate(values):
            at = index * TILE + pair * 128
            dqkv_ref[span, at : at + 128] = value.astype(BF16)


def space_attn_back_kernel(ar_ref, qkv_ref, lse_ref, o_ref, wout_ref, dqkv_ref):
    pick = head_picker()

    @pl.loop(0, lse_ref.shape[0])
    def _(f):
        attn_back_frame(f, ar_ref, qkv_ref, lse_ref, o_ref, wout_ref, pick, dqkv_ref)


def qkv_weights_kernel(order, dqkv_ref, h_ref, keep_ref, send_ref):
    size = h_ref.shape[1] // lax.axis_size("sp")
    turned_columns(h_ref, dqkv_ref, 3, 0, 3 * size, size, order, keep_ref, send_ref)


def finish_kernel(
    dqkv_ref, tok_ref, dxa_ref, own_ref, recv_ref, params_ref, wqkv_ref, small1_ref,
    small2_ref, small3_ref, gtok_ref, out_ref, small_ref, sums_scr,
):
    part = lax.rem(lax.axis_index("sp"), 2)
    frames, half = own_ref.shape[0], own_ref.shape[1]
    rows = 2 * half
    gain = params_ref[0:1, 0:TILE]
    sums_scr[...] = jnp.zeros_like(sums_scr)

    @pl.loop(0, frames)
    def _(f):
        span = rows_at(f, rows)
        out_ref[f, half_rows(part, half), :] = own_ref[f]
        out_ref[f, half_rows(1 - part, half), :] = recv_ref[f]
        dh = dot_nt(dqkv_ref[span, :], wqkv_ref[0])
        unit, inv = norm(tok_ref[f].astype(F32), gain, params_ref[4:5, 0:TILE])[1:]
        add_small(sums_scr, [column_sum(dh * unit), column_sum(dh)], False)
        gtok_ref[f] = (dxa_ref[span, :] + norm_back(dh, unit, inv, gain)).astype(BF16)

    small = jnp.concatenate([sums_scr[...], small1_ref[...], small2_ref[...], small3_ref[...]], axis=0)
    small_ref[...] = small.astype(BF16)


def place_of(block, order, sp):
    bits = len(order)
    mixed = jnp.bitwise_xor(block, sp)
    slot = jnp.int32(0)
    for i, b in enumerate(order):
        bit = jnp.bitwise_and(lax.shift_right_logical(mixed, jnp.int32(b)), 1)
        slot = slot + lax.shift_left(bit, jnp.int32(bits - 1 - i))
    return slot


class Place:
    def __init__(self, base, rows, at):
        self.base, self.rows, self.at = base, rows, at


def put_blocks(result, first, size, place, order, keep_ref, send_ref):
    sp = lax.axis_index("sp")
    part = lax.rem(sp, 2)
    low = result.astype(BF16)
    for j in range(result.shape[0] // (2 * size)):
        even = low[2 * j * size : (2 * j + 1) * size]
        odd = low[(2 * j + 1) * size : (2 * j + 2) * size]
        slot = place_of(first + 2 * j, order[1:], sp)
        rows = pl.ds(pl.multiple_of(place.base + slot * place.rows + place.at, 16), size)
        keep_ref[rows, :] = jnp.where(part == 0, even, odd)
        send_ref[rows, :] = jnp.where(part == 0, odd, even)


def turned_columns(h_ref, wide_ref, chunks, base, rows, size, order, keep_ref, send_ref):
    turned = jnp.transpose(h_ref[...])
    for j in range(chunks):
        result = dot(turned, wide_ref[:, j * TILE : (j + 1) * TILE])
        put_blocks(result, jnp.int32(0), size, Place(base, rows, j * size), order, keep_ref, send_ref)


def put_up(h_ref, du_ref, base, rows, order, keep_ref, send_ref):
    size = h_ref.shape[1] // lax.axis_size("sp")
    turned_columns(h_ref, du_ref, du_ref.shape[1] // TILE, base, rows, size, order, keep_ref, send_ref)


def put_down(act_ref, gr_ref, base, order, keep_ref, send_ref):
    size = act_ref.shape[1] // lax.axis_size("sp")
    for j in range(act_ref.shape[1] // TILE):
        down = dot_tn(act_ref[:, j * TILE : (j + 1) * TILE], gr_ref[...])
        put_blocks(down, jnp.int32(j * (TILE // size)), size, Place(base, size, 0), order, keep_ref, send_ref)


def mlp_weights_kernel(orders, h_ref, du_ref, act_ref, gr_ref, keep_ref, send_ref):
    sp_size = lax.axis_size("sp")
    rows = du_ref.shape[1] // TILE * (h_ref.shape[1] // sp_size)
    put_up(h_ref, du_ref, 0, rows, orders[0], keep_ref, send_ref)
    put_down(act_ref, gr_ref, sp_size // 2 * rows, orders[1], keep_ref, send_ref)


def down_weights_kernel(order, act_ref, own_ref, recv_ref, gr_ref, keep_ref, send_ref):
    part = lax.rem(lax.axis_index("sp"), 2)
    frames, half = own_ref.shape[0], own_ref.shape[1]
    for f in range(frames):
        base = f * 2 * half
        gr_ref[pl.ds(pl.multiple_of(base + part * half, half), half), :] = own_ref[f]
        gr_ref[pl.ds(pl.multiple_of(base + (1 - part) * half, half), half), :] = recv_ref[f]
    put_down(act_ref, gr_ref, 0, order, keep_ref, send_ref)


def up_weights_kernel(order, h_ref, du_ref, o_ref, ar_ref, keep_ref, send_ref):
    size = h_ref.shape[1] // lax.axis_size("sp")
    at = du_ref.shape[1] // TILE * size
    put_up(h_ref, du_ref, 0, at + size, order, keep_ref, send_ref)
    out = dot_tn(o_ref[...], ar_ref[...])
    put_blocks(out, jnp.int32(0), size, Place(0, at + size, at), order, keep_ref, send_ref)


def attn_weights_kernel(order, h_ref, dqkv_ref, o_ref, ar_ref, keep_ref, send_ref):
    size = h_ref.shape[1] // lax.axis_size("sp")
    turned_columns(h_ref, dqkv_ref, 3, 0, 4 * size, size, order, keep_ref, send_ref)
    out = dot_tn(o_ref[...], ar_ref[...])
    put_blocks(out, jnp.int32(0), size, Place(0, 4 * size, 3 * size), order, keep_ref, send_ref)


def in_pieces(rows, body):
    piece = next(p for p in (128, 96, 80, 64, 48, 32, 16, 8) if rows % p == 0)
    if rows <= 2 * piece:
        for start in range(0, rows, piece):
            body(start, piece)
    else:

        @pl.loop(0, rows // piece)
        def _(i):
            body(pl.multiple_of(i * piece, 8), piece)


def fold_kernel(moves, count, *refs):
    outs = refs[2 * count :]
    row_half = lax.rem(lax.axis_index("grp"), 2)

    def add(keep, recv, at, rows, places):
        def body(start, piece):
            span = pl.ds(pl.multiple_of(at + start, 8), piece)
            total = keep[span, :] + recv[span, :]
            for ref, to in places:
                ref[pl.ds(pl.multiple_of(to + start, 8), piece), :] = total

        in_pieces(rows, body)

    for source, at, rows, slots, targets, to, split in moves:
        keep, recv = refs[2 * source], refs[2 * source + 1]
        if split == "none":
            add(keep, recv, at, rows, [(outs[target], to) for target in targets])
        elif split == "slots":
            half = rows // 2
            for part, target in enumerate(targets):
                add(keep, recv, at + part * half, half, [(outs[target], to)])
        else:
            half = rows // (2 * slots)
            for slot in range(slots):
                for part, target in enumerate(targets):
                    side = row_half if part == 0 else 1 - row_half
                    add(keep, recv, at + 2 * slot * half + side * half, half, [(outs[target], to + slot * half)])


class Group:
    def __init__(self, sizes, segments, apart=False):
        grp_size, sp_size = sizes
        bits = sp_size.bit_length() - 1
        grp_bits = grp_size.bit_length() - 1
        names = tuple(segments)
        self.halved = grp_bits > 0 and all(
            whole or (height // 2) % 16 == 0 for height, whole, path in segments.values()
        )
        self.segments = {}
        self.state = {}
        for name, (height, whole, path) in segments.items():
            path = [step for step in path if step != ROWS or self.halved] + list(range(4, bits))
            self.segments[name] = (height, whole, path)
            self.state[name] = [sp_size // 2, 1]
        self.stages = []
        for i in range(bits + (1 if self.halved else 0)):
            entries = {}
            for name in names:
                key = (self.segments[name][2][i], name if apart and i == 0 else None)
                entries.setdefault(key, []).append(name)
            stage = []
            for (step, _), who in entries.items():
                stage.append(("grp", grp_size, 0, who, "rows") if step == ROWS else ("sp", sp_size, step, who, "slots"))
            self.stages.append(stage)
        for b in range(1 if self.halved else 0, grp_bits):
            self.stages.append([("grp", grp_size, b, names, "none")])
        if self.halved:
            self.stages.append([("grp", grp_size, 0, names, "none")])
        self.stage = 0
        self.keeps, self.recvs = [], []

    def beside(self, other):
        group = Group.__new__(Group)
        group.halved, group.stage = self.halved, self.stage
        group.segments = {**self.segments, **other.segments}
        group.state = {**self.state, **other.state}
        group.keeps, group.recvs = self.keeps + other.keeps, self.recvs + other.recvs
        group.stages = []
        for mine, others in zip(self.stages, other.stages):
            entries = {}
            for entry in mine + others:
                entries.setdefault(entry[:3] + entry[4:], []).extend(entry[3])
            if len(group.stages) == group.stage:
                group.stages.append(mine + others)
            else:
                group.stages.append([key[:3] + (tuple(names),) + key[3:] for key, names in entries.items()])
        return group

    def height(self, name):
        height, whole, _ = self.segments[name]
        slots, cut = self.state[name]
        return height if whole else height // cut * slots

    def start(self, sends):
        self.sends = sends
        self.recvs = [swap(send, *entry[:3]) for send, entry in zip(sends, self.stages[self.stage])]

    def begin(self, keep, send):
        entry = self.stages[0][len(self.keeps)]
        self.keeps.append(keep)
        self.recvs.append(swap(send, *entry[:3]))

    def fold(self):
        places = {}
        for source, entry in enumerate(self.stages[self.stage]):
            at = 0
            for name in entry[3]:
                places[name] = (source, at, self.height(name), self.state[name][0])
                at += self.height(name)
        shapes, moves, keeps, sends = [], [], [], []
        for entry in self.stages[self.stage + 1]:
            split = entry[4]
            keeps.append(len(shapes))
            sends.append(len(shapes) + (0 if split == "none" else 1))
            targets = (keeps[-1],) if split == "none" else (keeps[-1], sends[-1])
            to = 0
            for name in entry[3]:
                whole = self.segments[name][1]
                if split == "slots":
                    self.state[name][0] //= 2
                elif split == "rows":
                    self.state[name][1] = 2
                moves.append(places[name] + (targets, to, "none" if whole else split))
                to += self.height(name)
            shapes += [sds((to, TILE), BF16)] * len(targets)
        args = [x for pair in zip(self.keeps, self.recvs) for x in pair]
        out = call(functools.partial(fold_kernel, moves, len(args) // 2), args, shapes, 0.5, limit=4)
        self.keeps = [out[i] for i in keeps]
        self.sends = [out[i] for i in sends]
        self.stage += 1

    def left(self):
        return len(self.stages) - 1 - self.stage

    def pair(self):
        return self.keeps[0], self.recvs[0]


def result_kernel(sp_size, halved, *refs):
    outs = refs[8:16]
    gain_scr, shift_scr, qkv_scr, out_scr, up_scr, bup_scr, down_scr, bdown_scr = refs[16:24]
    mlp1, both, up0, qkv0 = refs[24:28]
    small_scr, sems = refs[28:]
    size = TILE // sp_size
    chunks = up_scr.shape[2] // TILE
    down_size = chunks * size
    row_half = lax.rem(lax.axis_index("grp"), 2)
    segments = (
        (mlp1, (chunks * size, down_size)), (both, (4 * size, down_size)),
        (up0, (chunks * size + size,)), (qkv0, (3 * size,)),
    )
    for i, (scr, heights) in enumerate(segments):
        mine, other = refs[2 * i], refs[2 * i + 1]
        at = 0
        base = 0
        for height in heights:
            if halved[i]:
                half = height // 2
                for ref, side in ((mine, row_half), (other, 1 - row_half)):
                    place = pl.ds(pl.multiple_of(base + side * half, 16), half)
                    scr[place, :] = ref[at : at + half, :].astype(F32)
                at += half
            else:
                span = slice(at, at + height)
                scr[base : base + height, :] = mine[span, :].astype(F32) + other[span, :].astype(F32)
                at += height
            base += height
    mine, other = refs[6], refs[7]
    at = 3 * size // (2 if halved[3] else 1)
    small = mine[at : at + 32, :].astype(F32)
    small_scr[...] = small if halved[3] else small + other[at : at + 32, :].astype(F32)
    for layer, (qkv, up, down, out, first, last) in enumerate((
        (qkv0, up0, both, up0, 4 * size, chunks * size),
        (both, mlp1, mlp1, both, chunks * size, 3 * size),
    )):
        for j in range(3):
            qkv_scr[layer, :, j * TILE : (j + 1) * TILE] = qkv[j * size : (j + 1) * size, :]
        for j in range(chunks):
            up_scr[layer, :, j * TILE : (j + 1) * TILE] = up[j * size : (j + 1) * size, :]
        down_scr[layer] = down[first : first + down_size, :]
        out_scr[layer] = out[last : last + size, :]
    sp = lax.axis_index("sp")
    back = lax.rem(TILE - sp * size, TILE)
    turned = pltpu.roll(small_scr[...], back, 1)
    for i in range(4):
        gain_scr[i : i + 1, :] = turned[8 * i : 8 * i + 1, :size]
        shift_scr[i : i + 1, :] = turned[8 * i + 1 : 8 * i + 2, :size]
    start = sp * down_size
    line = start // TILE
    back = lax.rem(TILE - lax.rem(start, TILE), TILE)
    for layer in range(2):
        first = 8 + 16 * layer
        bdown_scr[layer : layer + 1, :] = turned[first + 2 : first + 3, :size]
        rows = small_scr[first : first + 8, :]
        lines = lax.broadcasted_iota(jnp.int32, rows.shape, 0)
        picked = jnp.sum(jnp.where(lines == 4 + line, rows, 0.0), axis=0, keepdims=True)
        picked = pltpu.roll(jnp.broadcast_to(picked, rows.shape), back, 1)
        bup_scr[layer : layer + 1, :] = picked[0:1, :down_size]
    scrs = (gain_scr, shift_scr, qkv_scr, out_scr, up_scr, bup_scr, down_scr, bdown_scr)
    copies = [pltpu.make_async_copy(scr, out, sems.at[i]) for i, (scr, out) in enumerate(zip(scrs, outs))]
    for copy in copies:
        copy.start()
    for copy in copies:
        copy.wait()


VMEM = pl.BlockSpec(memory_space=pltpu.VMEM)
SMEM = pl.BlockSpec(memory_space=pltpu.SMEM)
HBM = pl.BlockSpec(memory_space=pltpu.HBM)


def sds(shape, dtype):
    return jax.ShapeDtypeStruct(shape, dtype)


def call(kernel, args, outs, micros, scratch=(), specs=None, out_specs=None, limit=12):
    return pl.pallas_call(
        kernel,
        in_specs=[VMEM] * len(args) if specs is None else specs,
        out_specs=[VMEM] * len(outs) if out_specs is None else out_specs,
        out_shape=outs,
        scratch_shapes=list(scratch),
        compiler_params=pltpu.CompilerParams(vmem_limit_bytes=limit * MIB),
        cost_estimate=pl.CostEstimate(flops=int(micros * COST), bytes_accessed=0, transcendentals=0),
    )(*args)


def swap(array, axis, size, bit):
    return lax.ppermute(array, axis, [(i, i ^ (1 << bit)) for i in range(size)])


def shards(sizes, tokens, frame_slot, norm_gain, norm_shift, w_qkv, w_out, w_up, b_up, w_down, b_down, cotangent):
    grp_size, sp_size = sizes
    frames, patches, width = tokens.shape
    hidden = w_up.shape[2]
    assert GROUP_FRAMES == 2 * frames and sp_size >= 8
    half = patches // 2
    rows = frames * patches
    sp_bits = sp_size.bit_length() - 1
    core_swap = functools.partial(swap, axis="sp", size=sp_size, bit=0)
    slots = sp_size // 2
    size = width // sp_size
    down_size = hidden // sp_size
    def slots_of(path):
        return [step for step in path if step != ROWS] + list(range(4, sp_bits))

    path_up1, path_down1 = (0, 1, 2, ROWS, 3), (0, 2, 1, ROWS, 3)
    path_attn1, path_down0 = (0, ROWS, 2, 1, 3), (0, 2, 1, ROWS, 3)
    path_up0, path_qkv0 = (0, 1, ROWS, 2, 3), (0, ROWS, 2, 1, 3)

    def row_out(cols, dtype=BF16):
        return sds((rows, cols), dtype)

    half_out = sds((frames, half, width), BF16)
    small_out = sds((8, TILE), F32)
    fence = lambda *arrays: lax.optimization_barrier(arrays)

    token = []

    def meet(groups, *arrays):
        recvs = [r for g in groups for r in g.recvs]
        out = list(fence(*arrays, *recvs, *token))
        count = len(arrays)
        arrays, recvs = out[:count], out[count:]
        for g in groups:
            g.recvs = [recvs.pop(0) for _ in g.recvs]
            g.fold()
        sends = [x for g in groups for x in g.sends]
        out = list(fence(*arrays, *sends))
        arrays, sends = out[:count], out[count:]
        for g in groups:
            g.start([sends.pop(0) for _ in g.sends])
        token[:] = [groups[-1].sends[-1]] if groups else []
        return arrays

    def buffers(height):
        return [sds((slots * height, TILE), BF16)] * 2

    cot_recv = core_swap(cotangent)
    widen = lambda a: jnp.pad(a, ((0, 0), (0, hidden - width)))
    packed = jnp.concatenate([widen(norm_gain), widen(norm_shift), b_up, widen(b_down)], axis=0)
    weights = (w_qkv, w_out, w_up, w_down)
    shapes = [sds(w.shape[1:], BF16) for w in weights]
    out = call(
        space_forward_kernel,
        (tokens, packed) + weights,
        [
            half_out, half_out, row_out(width), row_out(3 * width), sds((frames, HEADS, patches), F32),
            row_out(width), row_out(width, F32), row_out(width), row_out(hidden), row_out(hidden),
        ],
        16,
        scratch=[pltpu.VMEM(tokens.shape, BF16)]
        + [pltpu.VMEM(x.shape, BF16) for x in shapes]
        + [
            pltpu.VMEM((2, patches, width), BF16), pltpu.VMEM((2, patches, 3 * width), BF16),
            pltpu.VMEM((2, patches, width), BF16), pltpu.VMEM((2, patches, width), F32),
            pltpu.VMEM((2, patches, width), BF16),
            pltpu.VMEM((2, patches, hidden), BF16), pltpu.VMEM((2, patches, hidden), BF16),
            pltpu.VMEM((patches, width), F32), pltpu.SemaphoreType.DMA((5,)),
            pltpu.SemaphoreType.DMA((14,)),
        ],
        specs=[HBM, VMEM] + [HBM] * 4,
        out_specs=[VMEM, VMEM, HBM, HBM, VMEM] + [HBM] * 5,
        limit=LIMIT1,
    )
    (x_keep, x_send, h0, qkv0, lse0, o0, xa, h1, act0, slope0) = out
    x_recv = core_swap(x_send)

    place_scratch = [
        pltpu.SMEM((GROUP_FRAMES,), jnp.int32),
        pltpu.VMEM((GROUP_FRAMES, half, width), BF16),
    ]
    (out_own, out_send, xt, h2, qkv1, o1, h3, act1, du1, gr1, dxb, small3, w_qkv1, w_out1) = call(
        time_forward_kernel,
        (frame_slot, x_keep, x_recv, cotangent, cot_recv, packed) + weights,
        [
            half_out, half_out, row_out(width), row_out(width), row_out(3 * width), row_out(width),
            row_out(width), row_out(hidden), row_out(hidden), row_out(width), row_out(width, F32),
            small_out,
        ] + shapes[:2],
        24,
        scratch=place_scratch
        + [pltpu.VMEM((rows // 4, hidden), BF16)]
        + [pltpu.VMEM(x.shape, BF16) for x in shapes[2:]]
        + [pltpu.SemaphoreType.DMA((4,))],
        specs=[SMEM] + [VMEM] * 5 + [HBM] * 4,
        limit=LIMIT2,
    )
    out_recv = core_swap(out_send)

    out = call(
        functools.partial(mlp_weights_kernel, (slots_of(path_up1), slots_of(path_down1))), (h3, du1, act1, gr1),
        buffers(4 * size + down_size), 4.5,
    )
    keep, send, dxb = fence(*out, dxb)
    mlp1 = Group(sizes, {"up": (4 * size, False, path_up1), "down": (down_size, False, path_down1)})
    mlp1.begin(keep, send)

    (dx_own, dx_send, ar1, dqkv1, small2) = call(
        time_backward_kernel,
        (frame_slot, xt, qkv1, dxb, packed, w_qkv1, w_out1),
        [half_out, half_out, row_out(width), row_out(3 * width), small_out],
        8,
        scratch=place_scratch,
        specs=[SMEM] + [VMEM] * 6,
    )
    dx_recv = core_swap(dx_send)
    keep, send = call(
        functools.partial(attn_weights_kernel, slots_of(path_attn1)), (h2, dqkv1, o1, ar1),
        buffers(4 * size), 2.4,
    )
    dx_own, dx_recv, keep, send, out_recv = meet((mlp1,), dx_own, dx_recv, keep, send, out_recv)
    attn1 = Group(sizes, {"attn": (4 * size, False, path_attn1)})
    attn1.begin(keep, send)
    gr0, keep_down, send_down = call(
        functools.partial(down_weights_kernel, slots_of(path_down0)), (act0, dx_own, dx_recv),
        [row_out(width)] + buffers(down_size), 2.4,
    )
    (du0, dxa, ar0, small1) = call(
        space_mlp_back_kernel,
        (gr0, xa, slope0, packed, w_up, w_down),
        [row_out(hidden), row_out(width, F32), row_out(width), small_out],
        6,
    )
    keep_up, send_up = call(
        functools.partial(up_weights_kernel, slots_of(path_up0)), (h1, du0, o0, ar0), buffers(5 * size), 3
    )
    keep_down, send_down, keep_up, send_up, ar0 = meet(
        (mlp1, attn1), keep_down, send_down, keep_up, send_up, ar0
    )
    down0 = Group(sizes, {"down": (down_size, False, path_down0)})
    down0.begin(keep_down, send_down)
    up0 = Group(sizes, {"up": (5 * size, False, path_up0)})
    up0.begin(keep_up, send_up)

    (dqkv0,) = call(
        space_attn_back_kernel, (ar0, qkv0, lse0, o0, w_out), [row_out(3 * width)], 10
    )
    keep, send = call(
        functools.partial(qkv_weights_kernel, slots_of(path_qkv0)), (dqkv0, h0), buffers(3 * size), 2
    )
    dqkv0, keep, send, *attn1.recvs = meet((up0, down0, mlp1), dqkv0, keep, send, *attn1.recvs)
    both = attn1.beside(down0)
    qkv = Group(
        sizes, {"qkv": (3 * size, False, path_qkv0), "small": (32, True, path_qkv0)}, apart=True
    )
    qkv.begin(keep, send)
    grad_tokens, output, small = call(
        finish_kernel,
        (
            dqkv0, tokens, dxa, out_own, out_recv, packed, w_qkv, small1, small2, small3,
        ),
        [sds(tokens.shape, BF16), sds(tokens.shape, BF16), sds((32, TILE), BF16)],
        4,
        scratch=[pltpu.VMEM((8, TILE), F32)],
    )
    (small,) = fence(small)
    qkv.begin(small, small)
    everyone = (mlp1, both, up0, qkv)
    for names in TAIL:
        groups = [g for g in (dict(zip("mbuq", everyone))[c] for c in names) if g.left()]
        if groups:
            meet(groups)
    while any(g.left() for g in everyone):
        meet([g for g in everyone if g.left()])
    finals = [
        sds((4, size), F32), sds((4, size), F32), sds((2, size, 3 * width), F32), sds((2, size, width), F32),
        sds((2, size, hidden), F32), sds((2, down_size), F32), sds((2, down_size, width), F32),
        sds((2, size), F32),
    ]
    heights = (4 * size + down_size, 4 * size + down_size, 5 * size, 3 * size)
    results = call(
        functools.partial(result_kernel, sp_size, tuple(g.halved for g in everyone)),
        [x for g in everyone for x in g.pair()], finals, 2,
        scratch=[pltpu.VMEM(f.shape, F32) for f in finals]
        + [pltpu.VMEM((h, TILE), F32) for h in heights]
        + [pltpu.VMEM((32, TILE), F32), pltpu.SemaphoreType.DMA((8,))],
        out_specs=[HBM] * 8,
    )
    return (output, grad_tokens, *results)


def solution(mesh):
    rows = P(("grp", "sp"), None, None)
    in_specs = (rows, P("grp", None), P(), P(), P(), P(), P(), P(), P(), P(), rows)
    out_specs = (
        rows, rows, P(None, "sp"), P(None, "sp"), P(None, "sp", None), P(None, "sp", None),
        P(None, "sp", None), P(None, "sp"), P(None, "sp", None), P(None, "sp"),
    )
    body = functools.partial(shards, (mesh.shape["grp"], mesh.shape["sp"]))
    return jax.shard_map(body, mesh=mesh, in_specs=in_specs, out_specs=out_specs, check_vma=False)
```

```python
import functools

import jax
import jax.numpy as jnp
from jax import lax
from jax.experimental import pallas as pl
from jax.experimental.pallas import tpu as pltpu
from jax.sharding import PartitionSpec as P

HEADS = 8
HEAD = 64
VIDEO_STEPS = 6
GROUP_FRAMES = 8
NORM_EPS = 1e-05
TILE = 512
STEP = 1024
SCALE = HEAD**-0.5
TANH_A = 0.7978845608028654
TANH_B = TANH_A * 0.044715
PAIRS = [(t, s) for t in range(VIDEO_STEPS) for s in range(t + 1)]
F32 = jnp.float32
BF16 = jnp.bfloat16
MIB = 1024 * 1024
ROWS = -1
COST = 1.15e9 * 0.02
TAIL = ("q", "m", "bu", "q", "m", "bu", "q", "bu", "q", "bu", "q")
LIMIT1 = 52
LIMIT2 = 24


def dot(left, right):
    return jnp.dot(left, right, preferred_element_type=F32)


def dot_nt(left, right):
    return lax.dot_general(left, right, (((1,), (1,)), ((), ())), preferred_element_type=F32)


def dot_tn(left, right):
    return lax.dot_general(left, right, (((0,), (0,)), ((), ())), preferred_element_type=F32)


def norm(rows, gain, shift):
    centred = rows - jnp.mean(rows, axis=-1, keepdims=True)
    inv = lax.rsqrt(jnp.mean(centred * centred, axis=-1, keepdims=True) + NORM_EPS)
    unit = centred * inv
    return unit * gain + shift, unit, inv


def norm_back(grad, unit, inv, gain):
    grad_unit = grad * gain
    mean_grad = jnp.mean(grad_unit, axis=-1, keepdims=True)
    mean_both = jnp.mean(grad_unit * unit, axis=-1, keepdims=True)
    return inv * (grad_unit - mean_grad - unit * mean_both)


def column_sum(rows):
    return jnp.sum(rows, axis=0, keepdims=True)


def gelu_pair(u):
    square = u * u
    sigma = 0.5 + 0.5 * jnp.tanh(u * (TANH_A + TANH_B * square))
    act = u * sigma
    slope = sigma + act * (1.0 - sigma) * (2.0 * TANH_A + 6.0 * TANH_B * square)
    return act.astype(BF16), slope.astype(BF16)


def head_mask(lanes, which):
    lane = lax.broadcasted_iota(jnp.int32, lanes.shape, 1)
    return (lane < HEAD) if which == 0 else (lane >= HEAD)


def qkv_rows(normed, weight):
    out = []
    for part in range(3):
        piece = dot(normed, weight[:, part * TILE : (part + 1) * TILE])
        if part == 0:
            out.append(piece.astype(BF16) * BF16(SCALE))
        else:
            out.append(piece.astype(BF16))
    return out


def mlp_forward(normed, w_up, b_up, w_down, rows, act_ref, slope_ref):
    chunks = w_up.shape[1] // STEP
    up = lambda j: dot(normed, w_up[:, j * STEP : (j + 1) * STEP])
    total = None
    u = up(0)
    for j in range(chunks):
        cols = slice(j * STEP, (j + 1) * STEP)
        later = up(j + 1) if j + 1 < chunks else None
        act, slope = gelu_pair(u + b_up[0:1, cols])
        act_ref[rows, cols] = act
        slope_ref[rows, cols] = slope
        piece = dot(act, w_down[cols, :])
        total = piece if total is None else total + piece
        u = later
    return total


def mlp_backward(grad_low, w_up, w_down, rows, slope_ref, du_ref):
    chunks = w_up.shape[1] // STEP
    down = lambda j: dot_nt(grad_low, w_down[j * STEP : (j + 1) * STEP, :])
    total = None
    sums = []
    da = down(0)
    for j in range(chunks):
        cols = slice(j * STEP, (j + 1) * STEP)
        later = down(j + 1) if j + 1 < chunks else None
        du = (da * slope_ref[rows, cols].astype(F32)).astype(BF16)
        du_ref[rows, cols] = du
        sums.append(column_sum(du.astype(F32)))
        piece = dot_nt(du, w_up[:, cols])
        total = piece if total is None else total + piece
        da = later
    return total, [x[:, k : k + TILE] for x in sums for k in range(0, STEP, TILE)]


def add_small(small_ref, values, first):
    for i, value in enumerate(values):
        row = slice(i, i + 1) if i < 4 else slice(i, i + 1)
        if value is None:
            continue
        if first:
            small_ref[row, :] = value
        else:
            small_ref[row, :] += value


def rows_at(index, count):
    return pl.ds(pl.multiple_of(index * count, count), count)


def half_rows(part, half):
    return pl.ds(pl.multiple_of(part * half, half), half)


def space_forward_kernel(
    tok_hbm, params_ref, wqkv_hbm, wout_hbm, wup_hbm, wdown_hbm,
    keep_ref, send_ref, h0_hbm, qkv_hbm, lse_ref, o_hbm, xa_hbm, h1_hbm, act_hbm, slope_hbm,
    tok_ref, wqkv_ref, wout_ref, wup_ref, wdown_ref, h0_scr, qkv_scr, o_scr, xa_scr, h1_scr, act_scr,
    slope_scr, x1_scr, in_sems, out_sems,
):
    pairs = [
        (tok_hbm, tok_ref), (wqkv_hbm.at[0], wqkv_ref), (wout_hbm.at[0], wout_ref),
        (wup_hbm.at[0], wup_ref), (wdown_hbm.at[0], wdown_ref),
    ]
    copies = [pltpu.make_async_copy(src, dst, in_sems.at[i]) for i, (src, dst) in enumerate(pairs)]
    for copy in copies[:2]:
        copy.start()
    gain_ref, shift_ref = params_ref.at[0:4, 0:TILE], params_ref.at[4:8, 0:TILE]
    part = lax.rem(lax.axis_index("sp"), 2)
    frames, rows = tok_ref.shape[0], tok_ref.shape[1]
    half = rows // 2
    lane = lax.broadcasted_iota(jnp.int32, (rows, 128), 1)
    places = (
        (h0_scr, h0_hbm), (qkv_scr, qkv_hbm), (o_scr, o_hbm), (xa_scr, xa_hbm), (h1_scr, h1_hbm),
        (act_scr, act_hbm), (slope_scr, slope_hbm),
    )

    def spills(f):
        now = lax.rem(f, 2)
        return [
            pltpu.make_async_copy(scr.at[now], hbm.at[rows_at(f, rows)], out_sems.at[7 * now + i])
            for i, (scr, hbm) in enumerate(places)
        ]

    def await_first(f, *which):
        @pl.when(f == 0)
        def _():
            for i in which:
                copies[i].wait()

    copies[0].wait()
    for copy in copies[2:]:
        copy.start()

    @pl.loop(0, frames)
    def _(f):
        now = lax.rem(f, 2)
        spill = spills(f)

        @pl.when(f >= 2)
        def _():
            for copy in spills(f - 2):
                copy.wait()

        x0 = tok_ref[f].astype(F32)
        h0 = norm(x0, gain_ref[0:1, :], shift_ref[0:1, :])[0].astype(BF16)
        h0_scr[now] = h0
        spill[0].start()
        await_first(f, 1)
        q, k, v = qkv_rows(h0, wqkv_ref)
        qkv_scr[now, :, 0:TILE] = q
        qkv_scr[now, :, TILE : 2 * TILE] = k
        qkv_scr[now, :, 2 * TILE :] = v
        spill[1].start()
        lse_all = jnp.zeros((rows, 128), F32)
        mixed = []
        for pair in range(HEADS // 2):
            cols = slice(pair * 128, (pair + 1) * 128)
            qp, kp, vp = q[:, cols], k[:, cols], v[:, cols]
            zero = jnp.zeros_like(qp)
            mask = head_mask(qp, 0)
            s = dot_nt(jnp.concatenate([jnp.where(mask, qp, zero), jnp.where(mask, zero, qp)], axis=0), kp)
            top = jnp.max(s, axis=-1, keepdims=True)
            p = jnp.exp(s - top)
            total = jnp.sum(p, axis=-1, keepdims=True)
            both = dot(p.astype(BF16), vp) * (1.0 / total)
            lse = top + jnp.log(total)
            lse_all = jnp.where(lane == 2 * pair, lse[:rows], lse_all)
            lse_all = jnp.where(lane == 2 * pair + 1, lse[rows:], lse_all)
            mixed.append(jnp.where(mask, both[:rows], both[rows:]).astype(BF16))
        lse_ref[f] = jnp.transpose(lse_all)[0:HEADS, :]
        o = jnp.concatenate(mixed, axis=1)
        o_scr[now] = o
        spill[2].start()
        await_first(f, 2)
        xa = x0 + dot(o, wout_ref[...])
        xa_scr[now] = xa
        spill[3].start()
        h1 = norm(xa, gain_ref[1:2, :], shift_ref[1:2, :])[0].astype(BF16)
        h1_scr[now] = h1
        spill[4].start()
        await_first(f, 3, 4)
        branch = mlp_forward(
            h1, wup_ref, params_ref.at[8:9], wdown_ref, slice(None), act_scr.at[now], slope_scr.at[now]
        )
        spill[5].start()
        spill[6].start()
        x1_scr[...] = xa + branch + params_ref[10:11, 0:TILE]
        keep_ref[f] = x1_scr[half_rows(part, half), :].astype(BF16)
        send_ref[f] = x1_scr[half_rows(1 - part, half), :].astype(BF16)

    for f in (frames - 2, frames - 1):
        for copy in spills(jnp.int32(f)):
            copy.wait()


def lane_heads(dtype):
    c = lax.broadcasted_iota(jnp.int32, (TILE, 128), 0)
    h = lax.broadcasted_iota(jnp.int32, (TILE, 128), 1)
    return (c // HEAD == h).astype(dtype)


def slot_places(slots_ref, where_scr, frames):
    sp = lax.axis_index("sp")
    group = (sp * frames) // GROUP_FRAMES
    part = lax.rem(sp, GROUP_FRAMES // frames)
    for t in range(GROUP_FRAMES):
        where_scr[slots_ref[group, t]] = lax.rem(t + GROUP_FRAMES - part * frames, GROUP_FRAMES)


def time_scores(q, k, spread):
    parts = []
    for t, s in PAIRS:
        parts.append((q[t] * k[s]).astype(BF16))
    return dot(jnp.concatenate(parts, axis=0), spread)


def time_probs(scores, count):
    blocks = [scores[i * count : (i + 1) * count] for i in range(len(PAIRS))]
    probs = []
    at = 0
    for t in range(VIDEO_STEPS):
        mine = blocks[at : at + t + 1]
        at += t + 1
        top = functools.reduce(jnp.maximum, mine)
        raw = [jnp.exp(b - top) for b in mine]
        inv = 1.0 / functools.reduce(lambda a, b: a + b, raw)
        probs.extend([r * inv for r in raw])
    return probs


def split_slots(rows):
    count = rows.shape[0] // GROUP_FRAMES
    return [rows[s * count : (s + 1) * count].astype(F32) for s in range(GROUP_FRAMES)]


def time_forward_kernel(
    slots_ref, keep_ref, recv_ref, cot_ref, cotr_ref, params_ref,
    wqkv_hbm, wout_hbm, wup_hbm, wdown_hbm,
    own_ref, send_ref, x_ref, h2_ref, qkv_ref, o_ref, h3_ref, act_ref, du_ref, gr_ref, dxb_ref,
    small_ref, wqkv_ref, wout_ref,
    where_scr, both_scr, slope_scr, wup_ref, wdown_ref, in_sems,
):
    pairs = [(wqkv_hbm, wqkv_ref), (wout_hbm, wout_ref), (wup_hbm, wup_ref), (wdown_hbm, wdown_ref)]
    copies = [pltpu.make_async_copy(src.at[1], dst, in_sems.at[i]) for i, (src, dst) in enumerate(pairs)]
    for copy in copies:
        copy.start()
    gain_ref, shift_ref = params_ref.at[0:4, 0:TILE], params_ref.at[4:8, 0:TILE]
    frames, half = keep_ref.shape[0], keep_ref.shape[1]
    part = lax.rem(lax.axis_index("sp"), GROUP_FRAMES // frames)
    slot_places(slots_ref, where_scr, frames)
    small_ref[...] = jnp.zeros_like(small_ref)
    both_scr[0:frames] = keep_ref[...]
    both_scr[frames:] = recv_ref[...]
    spread = lane_heads(BF16)
    steps = 4
    count = half // steps
    step_rows = count * GROUP_FRAMES

    def await_first(i, *which):
        @pl.when(i == 0)
        def _():
            for w in which:
                copies[w].wait()

    @pl.loop(0, steps)
    def _(i):
        span = rows_at(i, step_rows)
        place = rows_at(i, count)
        x_low = jnp.concatenate([both_scr[where_scr[s], place] for s in range(GROUP_FRAMES)], axis=0)
        x_ref[span, :] = x_low
        x = x_low.astype(F32)
        h2 = norm(x, gain_ref[2:3, :], shift_ref[2:3, :])[0].astype(BF16)
        h2_ref[span, :] = h2
        await_first(i, 0)
        q, k, v = qkv_rows(h2, wqkv_ref)
        qkv_ref[span, 0:TILE] = q
        qkv_ref[span, TILE : 2 * TILE] = k
        qkv_ref[span, 2 * TILE :] = v
        qs, ks, vs = split_slots(q), split_slots(k), split_slots(v)
        probs = time_probs(time_scores(qs, ks, spread), count)
        wide = dot_nt(jnp.concatenate([p.astype(BF16) for p in probs], axis=0), spread)
        mixed = []
        at = 0
        for t in range(VIDEO_STEPS):
            total = None
            for s in range(t + 1):
                piece = wide[at * count : (at + 1) * count] * vs[s]
                total = piece if total is None else total + piece
                at += 1
            mixed.append(total)
        mixed.extend(vs[VIDEO_STEPS:])
        o = jnp.concatenate([m.astype(BF16) for m in mixed], axis=0)
        o_ref[span, :] = o
        await_first(i, 1)
        xb = x + dot(o, wout_ref[...]).astype(BF16).astype(F32)
        h3, unit, inv = norm(xb, gain_ref[3:4, :], shift_ref[3:4, :])
        h3 = h3.astype(BF16)
        h3_ref[span, :] = h3
        slope = slope_scr
        await_first(i, 2, 3)
        branch = mlp_forward(h3, wup_ref, params_ref.at[9:10], wdown_ref, span, act_ref, SpanView(slope))
        out = (xb + branch + params_ref[11:12, 0:TILE]).astype(BF16)
        for s in range(GROUP_FRAMES):
            both_scr[where_scr[s], place] = out[s * count : (s + 1) * count]
        grad_low = jnp.concatenate(
            [cot_slot(cot_ref, cotr_ref, where_scr[s], part * half + i * count, count) for s in range(GROUP_FRAMES)],
            axis=0,
        )
        gr_ref[span, :] = grad_low
        grad = grad_low.astype(F32)
        dh, sums = mlp_backward(grad_low, wup_ref, wdown_ref, span, SpanView(slope), du_ref)
        add_small(small_ref, [column_sum(dh * unit), column_sum(dh), column_sum(grad), None] + sums, False)
        dxb_ref[span, :] = grad + norm_back(dh, unit, inv, gain_ref[3:4, :])

    own_ref[...] = both_scr[0:frames]
    send_ref[...] = both_scr[frames:]


class SpanView:
    def __init__(self, ref):
        self.ref = ref

    def __getitem__(self, index):
        return self.ref[:, index[1]]

    def __setitem__(self, index, value):
        self.ref[:, index[1]] = value


def cot_slot(cot_ref, cotr_ref, frame, start, count):
    frames = cot_ref.shape[0]
    places = pl.ds(pl.multiple_of(start, count), count)
    mine = cot_ref[lax.rem(frame, frames), places, :]
    other = cotr_ref[lax.rem(frame, frames), places, :]
    return jnp.where(frame < frames, mine, other)


def time_backward_kernel(
    slots_ref, x_ref, qkv_ref, dxb_ref, params_ref, wqkv_ref, wout_ref,
    own_ref, send_ref, ar_ref, dqkv_ref, small_ref,
    where_scr, both_scr,
):
    frames, half = own_ref.shape[0], own_ref.shape[1]
    slot_places(slots_ref, where_scr, frames)
    small_ref[...] = jnp.zeros_like(small_ref)
    spread = lane_heads(BF16)
    steps = 4
    count = half // steps
    step_rows = count * GROUP_FRAMES
    gain = params_ref[2:3, 0:TILE]

    @pl.loop(0, steps)
    def _(i):
        span = rows_at(i, step_rows)
        place = rows_at(i, count)
        dxb = dxb_ref[span, :]
        ar = dxb.astype(BF16)
        ar_ref[span, :] = ar
        do = split_slots(dot_nt(ar, wout_ref[...]).astype(BF16))
        qs = split_slots(qkv_ref[span, 0:TILE])
        ks = split_slots(qkv_ref[span, TILE : 2 * TILE])
        vs = split_slots(qkv_ref[span, 2 * TILE :])
        probs = time_probs(time_scores(qs, ks, spread), count)
        dps = time_scores(do, vs, spread)
        dps = [dps[j * count : (j + 1) * count] for j in range(len(PAIRS))]
        dss = []
        at = 0
        for t in range(VIDEO_STEPS):
            centre = functools.reduce(
                lambda a, b: a + b, [probs[at + s] * dps[at + s] for s in range(t + 1)]
            )
            dss.extend([probs[at + s] * (dps[at + s] - centre) for s in range(t + 1)])
            at += t + 1
        wide_p = dot_nt(jnp.concatenate([p.astype(BF16) for p in probs], axis=0), spread)
        wide_ds = dot_nt(jnp.concatenate([d.astype(BF16) for d in dss], axis=0), spread)
        dq = [None] * GROUP_FRAMES
        dk = [None] * GROUP_FRAMES
        dv = [None] * GROUP_FRAMES

        def add(table, index, piece):
            table[index] = piece if table[index] is None else table[index] + piece

        for j, (t, s) in enumerate(PAIRS):
            rows = slice(j * count, (j + 1) * count)
            add(dq, t, wide_ds[rows] * ks[s])
            add(dk, s, wide_ds[rows] * qs[t])
            add(dv, s, wide_p[rows] * do[t])
        for t in range(VIDEO_STEPS, GROUP_FRAMES):
            dq[t] = jnp.zeros_like(do[t])
            dk[t] = jnp.zeros_like(do[t])
            dv[t] = do[t]
        dq = jnp.concatenate([(d * SCALE).astype(BF16) for d in dq], axis=0)
        dk = jnp.concatenate([d.astype(BF16) for d in dk], axis=0)
        dv = jnp.concatenate([d.astype(BF16) for d in dv], axis=0)
        dqkv_ref[span, 0:TILE] = dq
        dqkv_ref[span, TILE : 2 * TILE] = dk
        dqkv_ref[span, 2 * TILE :] = dv
        dh = dot_nt(dqkv_ref[span, :], wqkv_ref[...])
        unit, inv = norm(x_ref[span, :].astype(F32), gain, params_ref[6:7, 0:TILE])[1:]
        add_small(small_ref, [column_sum(dh * unit), column_sum(dh)], False)
        dxp = norm_back(dh, unit, inv, gain).astype(BF16).astype(F32)
        dx1 = (dxb + dxp).astype(BF16)
        for s in range(GROUP_FRAMES):
            both_scr[where_scr[s], place] = dx1[s * count : (s + 1) * count]

    own_ref[...] = both_scr[0:frames]
    send_ref[...] = both_scr[frames:]


def space_mlp_back_kernel(
    gr_ref, xa_ref, slope_ref, params_ref, wup_ref, wdown_ref,
    du_ref, dxa_ref, ar_ref, small_ref,
):
    small_ref[...] = jnp.zeros_like(small_ref)
    rows = 256
    gain = params_ref[1:2, 0:TILE]

    @pl.loop(0, gr_ref.shape[0] // rows)
    def _(f):
        span = rows_at(f, rows)
        grad_low = gr_ref[span, :]
        grad = grad_low.astype(F32)
        dh, sums = mlp_backward(grad_low, wup_ref.at[0], wdown_ref.at[0], span, slope_ref, du_ref)
        unit, inv = norm(xa_ref[span, :], gain, params_ref[5:6, 0:TILE])[1:]
        add_small(small_ref, [column_sum(dh * unit), column_sum(dh), column_sum(grad), None] + sums, False)
        dxa = grad + norm_back(dh, unit, inv, gain)
        dxa_ref[span, :] = dxa
        ar_ref[span, :] = dxa.astype(BF16)


def head_picker():
    h = lax.broadcasted_iota(jnp.int32, (HEADS, TILE), 0)
    c = lax.broadcasted_iota(jnp.int32, (HEADS, TILE), 1)
    return (c // HEAD == h).astype(BF16)


def attn_back_frame(f, ar_ref, qkv_ref, lse_ref, o_ref, wout_ref, pick, dqkv_ref):
    rows = lse_ref.shape[2]
    span = rows_at(f, rows)
    do = dot_nt(ar_ref[span, :], wout_ref[0]).astype(BF16)
    both = do.astype(F32) * o_ref[span, :].astype(F32)
    high = both.astype(BF16)
    rest = (both - high.astype(F32)).astype(BF16)
    centre = dot_nt(pick, high) + dot_nt(pick, rest)
    for pair in range(HEADS // 2):
        qp = qkv_ref[span, pair * 128 : (pair + 1) * 128]
        kp = qkv_ref[span, TILE + pair * 128 : TILE + (pair + 1) * 128]
        vp = qkv_ref[span, 2 * TILE + pair * 128 : 2 * TILE + (pair + 1) * 128]
        dop = do[:, pair * 128 : (pair + 1) * 128]
        zero = jnp.zeros_like(kp)
        mask = head_mask(kp, 0)
        st = dot_nt(jnp.concatenate([jnp.where(mask, kp, zero), jnp.where(mask, zero, kp)], axis=0), qp)
        dpt = dot_nt(jnp.concatenate([jnp.where(mask, vp, zero), jnp.where(mask, zero, vp)], axis=0), dop)
        pts, dsts, dqs = [], [], []
        for e in range(2):
            row = slice(2 * pair + e, 2 * pair + e + 1)
            keys = slice(e * rows, (e + 1) * rows)
            pt = jnp.exp(st[keys] - lse_ref[f, row, :])
            dst = (pt * (dpt[keys] - centre[row, :])).astype(BF16)
            pts.append(pt.astype(BF16))
            dsts.append(dst)
            dqs.append(dot_tn(dst, kp) * SCALE)
        dk = dot(jnp.concatenate(dsts, axis=0), qp)
        dv = dot(jnp.concatenate(pts, axis=0), dop)
        values = (
            jnp.where(mask, dqs[0], dqs[1]),
            jnp.where(mask, dk[:rows], dk[rows:]),
            jnp.where(mask, dv[:rows], dv[rows:]),
        )
        for index, value in enumerate(values):
            at = index * TILE + pair * 128
            dqkv_ref[span, at : at + 128] = value.astype(BF16)


def space_attn_back_kernel(ar_ref, qkv_ref, lse_ref, o_ref, wout_ref, dqkv_ref):
    pick = head_picker()

    @pl.loop(0, lse_ref.shape[0])
    def _(f):
        attn_back_frame(f, ar_ref, qkv_ref, lse_ref, o_ref, wout_ref, pick, dqkv_ref)


def qkv_weights_kernel(order, dqkv_ref, h_ref, keep_ref, send_ref):
    size = h_ref.shape[1] // lax.axis_size("sp")
    turned_columns(h_ref, dqkv_ref, 3, 0, 3 * size, size, order, keep_ref, send_ref)


def finish_kernel(
    dqkv_ref, tok_ref, dxa_ref, own_ref, recv_ref, params_ref, wqkv_ref, small1_ref,
    small2_ref, small3_ref, gtok_ref, out_ref, small_ref, sums_scr,
):
    part = lax.rem(lax.axis_index("sp"), 2)
    frames, half = own_ref.shape[0], own_ref.shape[1]
    rows = 2 * half
    gain = params_ref[0:1, 0:TILE]
    sums_scr[...] = jnp.zeros_like(sums_scr)

    @pl.loop(0, frames)
    def _(f):
        span = rows_at(f, rows)
        out_ref[f, half_rows(part, half), :] = own_ref[f]
        out_ref[f, half_rows(1 - part, half), :] = recv_ref[f]
        dh = dot_nt(dqkv_ref[span, :], wqkv_ref[0])
        unit, inv = norm(tok_ref[f].astype(F32), gain, params_ref[4:5, 0:TILE])[1:]
        add_small(sums_scr, [column_sum(dh * unit), column_sum(dh)], False)
        gtok_ref[f] = (dxa_ref[span, :] + norm_back(dh, unit, inv, gain)).astype(BF16)

    small = jnp.concatenate([sums_scr[...], small1_ref[...], small2_ref[...], small3_ref[...]], axis=0)
    small_ref[...] = small.astype(BF16)


def place_of(block, order, sp):
    bits = len(order)
    mixed = jnp.bitwise_xor(block, sp)
    slot = jnp.int32(0)
    for i, b in enumerate(order):
        bit = jnp.bitwise_and(lax.shift_right_logical(mixed, jnp.int32(b)), 1)
        slot = slot + lax.shift_left(bit, jnp.int32(bits - 1 - i))
    return slot


class Place:
    def __init__(self, base, rows, at):
        self.base, self.rows, self.at = base, rows, at


def put_blocks(result, first, size, place, order, keep_ref, send_ref):
    sp = lax.axis_index("sp")
    part = lax.rem(sp, 2)
    low = result.astype(BF16)
    for j in range(result.shape[0] // (2 * size)):
        even = low[2 * j * size : (2 * j + 1) * size]
        odd = low[(2 * j + 1) * size : (2 * j + 2) * size]
        slot = place_of(first + 2 * j, order[1:], sp)
        rows = pl.ds(pl.multiple_of(place.base + slot * place.rows + place.at, 16), size)
        keep_ref[rows, :] = jnp.where(part == 0, even, odd)
        send_ref[rows, :] = jnp.where(part == 0, odd, even)


def turned_columns(h_ref, wide_ref, chunks, base, rows, size, order, keep_ref, send_ref):
    turned = jnp.transpose(h_ref[...])
    for j in range(chunks):
        result = dot(turned, wide_ref[:, j * TILE : (j + 1) * TILE])
        put_blocks(result, jnp.int32(0), size, Place(base, rows, j * size), order, keep_ref, send_ref)


def put_up(h_ref, du_ref, base, rows, order, keep_ref, send_ref):
    size = h_ref.shape[1] // lax.axis_size("sp")
    turned_columns(h_ref, du_ref, du_ref.shape[1] // TILE, base, rows, size, order, keep_ref, send_ref)


def put_down(act_ref, gr_ref, base, order, keep_ref, send_ref):
    size = act_ref.shape[1] // lax.axis_size("sp")
    for j in range(act_ref.shape[1] // TILE):
        down = dot_tn(act_ref[:, j * TILE : (j + 1) * TILE], gr_ref[...])
        put_blocks(down, jnp.int32(j * (TILE // size)), size, Place(base, size, 0), order, keep_ref, send_ref)


def mlp_weights_kernel(orders, h_ref, du_ref, act_ref, gr_ref, keep_ref, send_ref):
    sp_size = lax.axis_size("sp")
    rows = du_ref.shape[1] // TILE * (h_ref.shape[1] // sp_size)
    put_up(h_ref, du_ref, 0, rows, orders[0], keep_ref, send_ref)
    put_down(act_ref, gr_ref, sp_size // 2 * rows, orders[1], keep_ref, send_ref)


def down_weights_kernel(order, act_ref, own_ref, recv_ref, gr_ref, keep_ref, send_ref):
    part = lax.rem(lax.axis_index("sp"), 2)
    frames, half = own_ref.shape[0], own_ref.shape[1]
    for f in range(frames):
        base = f * 2 * half
        gr_ref[pl.ds(pl.multiple_of(base + part * half, half), half), :] = own_ref[f]
        gr_ref[pl.ds(pl.multiple_of(base + (1 - part) * half, half), half), :] = recv_ref[f]
    put_down(act_ref, gr_ref, 0, order, keep_ref, send_ref)


def up_weights_kernel(order, h_ref, du_ref, o_ref, ar_ref, keep_ref, send_ref):
    size = h_ref.shape[1] // lax.axis_size("sp")
    at = du_ref.shape[1] // TILE * size
    put_up(h_ref, du_ref, 0, at + size, order, keep_ref, send_ref)
    out = dot_tn(o_ref[...], ar_ref[...])
    put_blocks(out, jnp.int32(0), size, Place(0, at + size, at), order, keep_ref, send_ref)


def attn_weights_kernel(order, h_ref, dqkv_ref, o_ref, ar_ref, keep_ref, send_ref):
    size = h_ref.shape[1] // lax.axis_size("sp")
    turned_columns(h_ref, dqkv_ref, 3, 0, 4 * size, size, order, keep_ref, send_ref)
    out = dot_tn(o_ref[...], ar_ref[...])
    put_blocks(out, jnp.int32(0), size, Place(0, 4 * size, 3 * size), order, keep_ref, send_ref)


def in_pieces(rows, body):
    piece = next(p for p in (128, 96, 80, 64, 48, 32, 16, 8) if rows % p == 0)
    if rows <= 2 * piece:
        for start in range(0, rows, piece):
            body(start, piece)
    else:

        @pl.loop(0, rows // piece)
        def _(i):
            body(pl.multiple_of(i * piece, 8), piece)


def fold_kernel(moves, count, *refs):
    outs = refs[2 * count :]
    row_half = lax.rem(lax.axis_index("grp"), 2)

    def add(keep, recv, at, rows, places):
        def body(start, piece):
            span = pl.ds(pl.multiple_of(at + start, 8), piece)
            total = keep[span, :] + recv[span, :]
            for ref, to in places:
                ref[pl.ds(pl.multiple_of(to + start, 8), piece), :] = total

        in_pieces(rows, body)

    for source, at, rows, slots, targets, to, split in moves:
        keep, recv = refs[2 * source], refs[2 * source + 1]
        if split == "none":
            add(keep, recv, at, rows, [(outs[target], to) for target in targets])
        elif split == "slots":
            half = rows // 2
            for part, target in enumerate(targets):
                add(keep, recv, at + part * half, half, [(outs[target], to)])
        else:
            half = rows // (2 * slots)
            for slot in range(slots):
                for part, target in enumerate(targets):
                    side = row_half if part == 0 else 1 - row_half
                    add(keep, recv, at + 2 * slot * half + side * half, half, [(outs[target], to + slot * half)])


class Group:
    def __init__(self, sizes, segments, apart=False):
        grp_size, sp_size = sizes
        bits = sp_size.bit_length() - 1
        grp_bits = grp_size.bit_length() - 1
        names = tuple(segments)
        self.halved = grp_bits > 0 and all(
            whole or (height // 2) % 16 == 0 for height, whole, path in segments.values()
        )
        self.segments = {}
        self.state = {}
        for name, (height, whole, path) in segments.items():
            path = [step for step in path if step != ROWS or self.halved] + list(range(4, bits))
            self.segments[name] = (height, whole, path)
            self.state[name] = [sp_size // 2, 1]
        self.stages = []
        for i in range(bits + (1 if self.halved else 0)):
            entries = {}
            for name in names:
                key = (self.segments[name][2][i], name if apart and i == 0 else None)
                entries.setdefault(key, []).append(name)
            stage = []
            for (step, _), who in entries.items():
                stage.append(("grp", grp_size, 0, who, "rows") if step == ROWS else ("sp", sp_size, step, who, "slots"))
            self.stages.append(stage)
        for b in range(1 if self.halved else 0, grp_bits):
            self.stages.append([("grp", grp_size, b, names, "none")])
        if self.halved:
            self.stages.append([("grp", grp_size, 0, names, "none")])
        self.stage = 0
        self.keeps, self.recvs = [], []

    def beside(self, other):
        group = Group.__new__(Group)
        group.halved, group.stage = self.halved, self.stage
        group.segments = {**self.segments, **other.segments}
        group.state = {**self.state, **other.state}
        group.keeps, group.recvs = self.keeps + other.keeps, self.recvs + other.recvs
        group.stages = []
        for mine, others in zip(self.stages, other.stages):
            entries = {}
            for entry in mine + others:
                entries.setdefault(entry[:3] + entry[4:], []).extend(entry[3])
            if len(group.stages) == group.stage:
                group.stages.append(mine + others)
            else:
                group.stages.append([key[:3] + (tuple(names),) + key[3:] for key, names in entries.items()])
        return group

    def height(self, name):
        height, whole, _ = self.segments[name]
        slots, cut = self.state[name]
        return height if whole else height // cut * slots

    def start(self, sends):
        self.sends = sends
        self.recvs = [swap(send, *entry[:3]) for send, entry in zip(sends, self.stages[self.stage])]

    def begin(self, keep, send):
        entry = self.stages[0][len(self.keeps)]
        self.keeps.append(keep)
        self.recvs.append(swap(send, *entry[:3]))

    def fold(self):
        places = {}
        for source, entry in enumerate(self.stages[self.stage]):
            at = 0
            for name in entry[3]:
                places[name] = (source, at, self.height(name), self.state[name][0])
                at += self.height(name)
        shapes, moves, keeps, sends = [], [], [], []
        for entry in self.stages[self.stage + 1]:
            split = entry[4]
            keeps.append(len(shapes))
            sends.append(len(shapes) + (0 if split == "none" else 1))
            targets = (keeps[-1],) if split == "none" else (keeps[-1], sends[-1])
            to = 0
            for name in entry[3]:
                whole = self.segments[name][1]
                if split == "slots":
                    self.state[name][0] //= 2
                elif split == "rows":
                    self.state[name][1] = 2
                moves.append(places[name] + (targets, to, "none" if whole else split))
                to += self.height(name)
            shapes += [sds((to, TILE), BF16)] * len(targets)
        args = [x for pair in zip(self.keeps, self.recvs) for x in pair]
        out = call(functools.partial(fold_kernel, moves, len(args) // 2), args, shapes, 0.5, limit=4)
        self.keeps = [out[i] for i in keeps]
        self.sends = [out[i] for i in sends]
        self.stage += 1

    def left(self):
        return len(self.stages) - 1 - self.stage

    def pair(self):
        return self.keeps[0], self.recvs[0]


def result_kernel(sp_size, halved, *refs):
    outs = refs[8:16]
    gain_scr, shift_scr, qkv_scr, out_scr, up_scr, bup_scr, down_scr, bdown_scr = refs[16:24]
    mlp1, both, up0, qkv0 = refs[24:28]
    small_scr, sems = refs[28:]
    size = TILE // sp_size
    chunks = up_scr.shape[2] // TILE
    down_size = chunks * size
    row_half = lax.rem(lax.axis_index("grp"), 2)
    segments = (
        (mlp1, (chunks * size, down_size)), (both, (4 * size, down_size)),
        (up0, (chunks * size + size,)), (qkv0, (3 * size,)),
    )
    for i, (scr, heights) in enumerate(segments):
        mine, other = refs[2 * i], refs[2 * i + 1]
        at = 0
        base = 0
        for height in heights:
            if halved[i]:
                half = height // 2
                for ref, side in ((mine, row_half), (other, 1 - row_half)):
                    place = pl.ds(pl.multiple_of(base + side * half, 16), half)
                    scr[place, :] = ref[at : at + half, :].astype(F32)
                at += half
            else:
                span = slice(at, at + height)
                scr[base : base + height, :] = mine[span, :].astype(F32) + other[span, :].astype(F32)
                at += height
            base += height
    mine, other = refs[6], refs[7]
    at = 3 * size // (2 if halved[3] else 1)
    small = mine[at : at + 32, :].astype(F32)
    small_scr[...] = small if halved[3] else small + other[at : at + 32, :].astype(F32)
    for layer, (qkv, up, down, out, first, last) in enumerate((
        (qkv0, up0, both, up0, 4 * size, chunks * size),
        (both, mlp1, mlp1, both, chunks * size, 3 * size),
    )):
        for j in range(3):
            qkv_scr[layer, :, j * TILE : (j + 1) * TILE] = qkv[j * size : (j + 1) * size, :]
        for j in range(chunks):
            up_scr[layer, :, j * TILE : (j + 1) * TILE] = up[j * size : (j + 1) * size, :]
        down_scr[layer] = down[first : first + down_size, :]
        out_scr[layer] = out[last : last + size, :]
    sp = lax.axis_index("sp")
    back = lax.rem(TILE - sp * size, TILE)
    turned = pltpu.roll(small_scr[...], back, 1)
    for i in range(4):
        gain_scr[i : i + 1, :] = turned[8 * i : 8 * i + 1, :size]
        shift_scr[i : i + 1, :] = turned[8 * i + 1 : 8 * i + 2, :size]
    start = sp * down_size
    line = start // TILE
    back = lax.rem(TILE - lax.rem(start, TILE), TILE)
    for layer in range(2):
        first = 8 + 16 * layer
        bdown_scr[layer : layer + 1, :] = turned[first + 2 : first + 3, :size]
        rows = small_scr[first : first + 8, :]
        lines = lax.broadcasted_iota(jnp.int32, rows.shape, 0)
        picked = jnp.sum(jnp.where(lines == 4 + line, rows, 0.0), axis=0, keepdims=True)
        picked = pltpu.roll(jnp.broadcast_to(picked, rows.shape), back, 1)
        bup_scr[layer : layer + 1, :] = picked[0:1, :down_size]
    scrs = (gain_scr, shift_scr, qkv_scr, out_scr, up_scr, bup_scr, down_scr, bdown_scr)
    copies = [pltpu.make_async_copy(scr, out, sems.at[i]) for i, (scr, out) in enumerate(zip(scrs, outs))]
    for copy in copies:
        copy.start()
    for copy in copies:
        copy.wait()


VMEM = pl.BlockSpec(memory_space=pltpu.VMEM)
SMEM = pl.BlockSpec(memory_space=pltpu.SMEM)
HBM = pl.BlockSpec(memory_space=pltpu.HBM)


def sds(shape, dtype):
    return jax.ShapeDtypeStruct(shape, dtype)


def call(kernel, args, outs, micros, scratch=(), specs=None, out_specs=None, limit=12):
    return pl.pallas_call(
        kernel,
        in_specs=[VMEM] * len(args) if specs is None else specs,
        out_specs=[VMEM] * len(outs) if out_specs is None else out_specs,
        out_shape=outs,
        scratch_shapes=list(scratch),
        compiler_params=pltpu.CompilerParams(vmem_limit_bytes=limit * MIB),
        cost_estimate=pl.CostEstimate(flops=int(micros * COST), bytes_accessed=0, transcendentals=0),
    )(*args)


def swap(array, axis, size, bit):
    return lax.ppermute(array, axis, [(i, i ^ (1 << bit)) for i in range(size)])


def shards(sizes, tokens, frame_slot, norm_gain, norm_shift, w_qkv, w_out, w_up, b_up, w_down, b_down, cotangent):
    grp_size, sp_size = sizes
    frames, patches, width = tokens.shape
    hidden = w_up.shape[2]
    assert GROUP_FRAMES == 2 * frames and sp_size >= 8
    half = patches // 2
    rows = frames * patches
    sp_bits = sp_size.bit_length() - 1
    core_swap = functools.partial(swap, axis="sp", size=sp_size, bit=0)
    slots = sp_size // 2
    size = width // sp_size
    down_size = hidden // sp_size
    def slots_of(path):
        return [step for step in path if step != ROWS] + list(range(4, sp_bits))

    path_up1, path_down1 = (0, 1, 2, ROWS, 3), (0, 2, 1, ROWS, 3)
    path_attn1, path_down0 = (0, ROWS, 2, 1, 3), (0, 2, 1, ROWS, 3)
    path_up0, path_qkv0 = (0, 1, ROWS, 3, 2), (0, ROWS, 2, 1, 3)

    def row_out(cols, dtype=BF16):
        return sds((rows, cols), dtype)

    half_out = sds((frames, half, width), BF16)
    small_out = sds((8, TILE), F32)
    fence = lambda *arrays: lax.optimization_barrier(arrays)

    token = []

    def meet(groups, *arrays):
        recvs = [r for g in groups for r in g.recvs]
        out = list(fence(*arrays, *recvs, *token))
        count = len(arrays)
        arrays, recvs = out[:count], out[count:]
        for g in groups:
            g.recvs = [recvs.pop(0) for _ in g.recvs]
            g.fold()
        sends = [x for g in groups for x in g.sends]
        out = list(fence(*arrays, *sends))
        arrays, sends = out[:count], out[count:]
        for g in groups:
            g.start([sends.pop(0) for _ in g.sends])
        token[:] = [groups[-1].sends[-1]] if groups else []
        return arrays

    def buffers(height):
        return [sds((slots * height, TILE), BF16)] * 2

    cot_recv = core_swap(cotangent)
    widen = lambda a: jnp.pad(a, ((0, 0), (0, hidden - width)))
    packed = jnp.concatenate([widen(norm_gain), widen(norm_shift), b_up, widen(b_down)], axis=0)
    weights = (w_qkv, w_out, w_up, w_down)
    shapes = [sds(w.shape[1:], BF16) for w in weights]
    out = call(
        space_forward_kernel,
        (tokens, packed) + weights,
        [
            half_out, half_out, row_out(width), row_out(3 * width), sds((frames, HEADS, patches), F32),
            row_out(width), row_out(width, F32), row_out(width), row_out(hidden), row_out(hidden),
        ],
        16,
        scratch=[pltpu.VMEM(tokens.shape, BF16)]
        + [pltpu.VMEM(x.shape, BF16) for x in shapes]
        + [
            pltpu.VMEM((2, patches, width), BF16), pltpu.VMEM((2, patches, 3 * width), BF16),
            pltpu.VMEM((2, patches, width), BF16), pltpu.VMEM((2, patches, width), F32),
            pltpu.VMEM((2, patches, width), BF16),
            pltpu.VMEM((2, patches, hidden), BF16), pltpu.VMEM((2, patches, hidden), BF16),
            pltpu.VMEM((patches, width), F32), pltpu.SemaphoreType.DMA((5,)),
            pltpu.SemaphoreType.DMA((14,)),
        ],
        specs=[HBM, VMEM] + [HBM] * 4,
        out_specs=[VMEM, VMEM, HBM, HBM, VMEM] + [HBM] * 5,
        limit=LIMIT1,
    )
    (x_keep, x_send, h0, qkv0, lse0, o0, xa, h1, act0, slope0) = out
    x_recv = core_swap(x_send)

    place_scratch = [
        pltpu.SMEM((GROUP_FRAMES,), jnp.int32),
        pltpu.VMEM((GROUP_FRAMES, half, width), BF16),
    ]
    (out_own, out_send, xt, h2, qkv1, o1, h3, act1, du1, gr1, dxb, small3, w_qkv1, w_out1) = call(
        time_forward_kernel,
        (frame_slot, x_keep, x_recv, cotangent, cot_recv, packed) + weights,
        [
            half_out, half_out, row_out(width), row_out(width), row_out(3 * width), row_out(width),
            row_out(width), row_out(hidden), row_out(hidden), row_out(width), row_out(width, F32),
            small_out,
        ] + shapes[:2],
        24,
        scratch=place_scratch
        + [pltpu.VMEM((rows // 4, hidden), BF16)]
        + [pltpu.VMEM(x.shape, BF16) for x in shapes[2:]]
        + [pltpu.SemaphoreType.DMA((4,))],
        specs=[SMEM] + [VMEM] * 5 + [HBM] * 4,
        limit=LIMIT2,
    )
    out_recv = core_swap(out_send)

    out = call(
        functools.partial(mlp_weights_kernel, (slots_of(path_up1), slots_of(path_down1))), (h3, du1, act1, gr1),
        buffers(4 * size + down_size), 4.5,
    )
    keep, send, dxb = fence(*out, dxb)
    mlp1 = Group(sizes, {"up": (4 * size, False, path_up1), "down": (down_size, False, path_down1)})
    mlp1.begin(keep, send)

    (dx_own, dx_send, ar1, dqkv1, small2) = call(
        time_backward_kernel,
        (frame_slot, xt, qkv1, dxb, packed, w_qkv1, w_out1),
        [half_out, half_out, row_out(width), row_out(3 * width), small_out],
        8,
        scratch=place_scratch,
        specs=[SMEM] + [VMEM] * 6,
    )
    dx_recv = core_swap(dx_send)
    keep, send = call(
        functools.partial(attn_weights_kernel, slots_of(path_attn1)), (h2, dqkv1, o1, ar1),
        buffers(4 * size), 2.4,
    )
    dx_own, dx_recv, keep, send, out_recv = meet((mlp1,), dx_own, dx_recv, keep, send, out_recv)
    attn1 = Group(sizes, {"attn": (4 * size, False, path_attn1)})
    attn1.begin(keep, send)
    gr0, keep_down, send_down = call(
        functools.partial(down_weights_kernel, slots_of(path_down0)), (act0, dx_own, dx_recv),
        [row_out(width)] + buffers(down_size), 2.4,
    )
    (du0, dxa, ar0, small1) = call(
        space_mlp_back_kernel,
        (gr0, xa, slope0, packed, w_up, w_down),
        [row_out(hidden), row_out(width, F32), row_out(width), small_out],
        6,
    )
    keep_up, send_up = call(
        functools.partial(up_weights_kernel, slots_of(path_up0)), (h1, du0, o0, ar0), buffers(5 * size), 3
    )
    keep_down, send_down, keep_up, send_up, ar0 = meet(
        (mlp1, attn1), keep_down, send_down, keep_up, send_up, ar0
    )
    down0 = Group(sizes, {"down": (down_size, False, path_down0)})
    down0.begin(keep_down, send_down)
    up0 = Group(sizes, {"up": (5 * size, False, path_up0)})
    up0.begin(keep_up, send_up)

    (dqkv0,) = call(
        space_attn_back_kernel, (ar0, qkv0, lse0, o0, w_out), [row_out(3 * width)], 10
    )
    keep, send = call(
        functools.partial(qkv_weights_kernel, slots_of(path_qkv0)), (dqkv0, h0), buffers(3 * size), 2
    )
    dqkv0, keep, send, *attn1.recvs = meet((up0, down0, mlp1), dqkv0, keep, send, *attn1.recvs)
    both = attn1.beside(down0)
    qkv = Group(
        sizes, {"qkv": (3 * size, False, path_qkv0), "small": (32, True, path_qkv0)}, apart=True
    )
    qkv.begin(keep, send)
    grad_tokens, output, small = call(
        finish_kernel,
        (
            dqkv0, tokens, dxa, out_own, out_recv, packed, w_qkv, small1, small2, small3,
        ),
        [sds(tokens.shape, BF16), sds(tokens.shape, BF16), sds((32, TILE), BF16)],
        4,
        scratch=[pltpu.VMEM((8, TILE), F32)],
    )
    (small,) = fence(small)
    qkv.begin(small, small)
    everyone = (mlp1, both, up0, qkv)
    for names in TAIL:
        groups = [g for g in (dict(zip("mbuq", everyone))[c] for c in names) if g.left()]
        if groups:
            meet(groups)
    while any(g.left() for g in everyone):
        meet([g for g in everyone if g.left()])
    finals = [
        sds((4, size), F32), sds((4, size), F32), sds((2, size, 3 * width), F32), sds((2, size, width), F32),
        sds((2, size, hidden), F32), sds((2, down_size), F32), sds((2, down_size, width), F32),
        sds((2, size), F32),
    ]
    heights = (4 * size + down_size, 4 * size + down_size, 5 * size, 3 * size)
    results = call(
        functools.partial(result_kernel, sp_size, tuple(g.halved for g in everyone)),
        [x for g in everyone for x in g.pair()], finals, 2,
        scratch=[pltpu.VMEM(f.shape, F32) for f in finals]
        + [pltpu.VMEM((h, TILE), F32) for h in heights]
        + [pltpu.VMEM((32, TILE), F32), pltpu.SemaphoreType.DMA((8,))],
        out_specs=[HBM] * 8,
    )
    return (output, grad_tokens, *results)


def solution(mesh):
    rows = P(("grp", "sp"), None, None)
    in_specs = (rows, P("grp", None), P(), P(), P(), P(), P(), P(), P(), P(), rows)
    out_specs = (
        rows, rows, P(None, "sp"), P(None, "sp"), P(None, "sp", None), P(None, "sp", None),
        P(None, "sp", None), P(None, "sp"), P(None, "sp", None), P(None, "sp"),
    )
    body = functools.partial(shards, (mesh.shape["grp"], mesh.shape["sp"]))
    return jax.shard_map(body, mesh=mesh, in_specs=in_specs, out_specs=out_specs, check_vma=False)
```

```python
import functools

import jax
import jax.numpy as jnp
from jax import lax
from jax.experimental import pallas as pl
from jax.experimental.pallas import tpu as pltpu
from jax.sharding import PartitionSpec as P

HEADS = 8
HEAD = 64
VIDEO_STEPS = 6
GROUP_FRAMES = 8
NORM_EPS = 1e-05
TILE = 512
STEP = 1024
SCALE = HEAD**-0.5
TANH_A = 0.7978845608028654
TANH_B = TANH_A * 0.044715
PAIRS = [(t, s) for t in range(VIDEO_STEPS) for s in range(t + 1)]
F32 = jnp.float32
BF16 = jnp.bfloat16
MIB = 1024 * 1024
ROWS = -1
COST = 1.15e9 * 0.02
TAIL = ("q", "m", "bu", "q", "m", "bu", "q", "bu", "q", "bu", "q")
LIMIT1 = 52
LIMIT2 = 24


def dot(left, right):
    return jnp.dot(left, right, preferred_element_type=F32)


def dot_nt(left, right):
    return lax.dot_general(left, right, (((1,), (1,)), ((), ())), preferred_element_type=F32)


def dot_tn(left, right):
    return lax.dot_general(left, right, (((0,), (0,)), ((), ())), preferred_element_type=F32)


def norm(rows, gain, shift):
    centred = rows - jnp.mean(rows, axis=-1, keepdims=True)
    inv = lax.rsqrt(jnp.mean(centred * centred, axis=-1, keepdims=True) + NORM_EPS)
    unit = centred * inv
    return unit * gain + shift, unit, inv


def norm_back(grad, unit, inv, gain):
    grad_unit = grad * gain
    mean_grad = jnp.mean(grad_unit, axis=-1, keepdims=True)
    mean_both = jnp.mean(grad_unit * unit, axis=-1, keepdims=True)
    return inv * (grad_unit - mean_grad - unit * mean_both)


def column_sum(rows):
    return jnp.sum(rows, axis=0, keepdims=True)


def gelu_pair(u):
    square = u * u
    sigma = 0.5 + 0.5 * jnp.tanh(u * (TANH_A + TANH_B * square))
    act = u * sigma
    slope = sigma + act * (1.0 - sigma) * (2.0 * TANH_A + 6.0 * TANH_B * square)
    return act.astype(BF16), slope.astype(BF16)


def head_mask(lanes, which):
    lane = lax.broadcasted_iota(jnp.int32, lanes.shape, 1)
    return (lane < HEAD) if which == 0 else (lane >= HEAD)


def qkv_rows(normed, weight):
    out = []
    for part in range(3):
        piece = dot(normed, weight[:, part * TILE : (part + 1) * TILE])
        if part == 0:
            out.append(piece.astype(BF16) * BF16(SCALE))
        else:
            out.append(piece.astype(BF16))
    return out


def mlp_forward(normed, w_up, b_up, w_down, rows, act_ref, slope_ref):
    chunks = w_up.shape[1] // STEP
    up = lambda j: dot(normed, w_up[:, j * STEP : (j + 1) * STEP])
    total = None
    u = up(0)
    for j in range(chunks):
        cols = slice(j * STEP, (j + 1) * STEP)
        later = up(j + 1) if j + 1 < chunks else None
        act, slope = gelu_pair(u + b_up[0:1, cols])
        act_ref[rows, cols] = act
        slope_ref[rows, cols] = slope
        piece = dot(act, w_down[cols, :])
        total = piece if total is None else total + piece
        u = later
    return total


def mlp_backward(grad_low, w_up, w_down, rows, slope_ref, du_ref):
    chunks = w_up.shape[1] // STEP
    down = lambda j: dot_nt(grad_low, w_down[j * STEP : (j + 1) * STEP, :])
    total = None
    sums = []
    da = down(0)
    for j in range(chunks):
        cols = slice(j * STEP, (j + 1) * STEP)
        later = down(j + 1) if j + 1 < chunks else None
        du = (da * slope_ref[rows, cols].astype(F32)).astype(BF16)
        du_ref[rows, cols] = du
        sums.append(column_sum(du.astype(F32)))
        piece = dot_nt(du, w_up[:, cols])
        total = piece if total is None else total + piece
        da = later
    return total, [x[:, k : k + TILE] for x in sums for k in range(0, STEP, TILE)]


def add_small(small_ref, values, first):
    for i, value in enumerate(values):
        row = slice(i, i + 1) if i < 4 else slice(i, i + 1)
        if value is None:
            continue
        if first:
            small_ref[row, :] = value
        else:
            small_ref[row, :] += value


def rows_at(index, count):
    return pl.ds(pl.multiple_of(index * count, count), count)


def half_rows(part, half):
    return pl.ds(pl.multiple_of(part * half, half), half)


def space_forward_kernel(
    tok_hbm, params_ref, wqkv_hbm, wout_hbm, wup_hbm, wdown_hbm,
    keep_ref, send_ref, h0_hbm, qkv_hbm, lse_ref, o_hbm, xa_hbm, h1_hbm, act_hbm, slope_hbm,
    tok_ref, wqkv_ref, wout_ref, wup_ref, wdown_ref, h0_scr, qkv_scr, o_scr, xa_scr, h1_scr, act_scr,
    slope_scr, x1_scr, in_sems, out_sems,
):
    pairs = [
        (tok_hbm, tok_ref), (wqkv_hbm.at[0], wqkv_ref), (wout_hbm.at[0], wout_ref),
        (wup_hbm.at[0], wup_ref), (wdown_hbm.at[0], wdown_ref),
    ]
    copies = [pltpu.make_async_copy(src, dst, in_sems.at[i]) for i, (src, dst) in enumerate(pairs)]
    for copy in copies[:2]:
        copy.start()
    gain_ref, shift_ref = params_ref.at[0:4, 0:TILE], params_ref.at[4:8, 0:TILE]
    part = lax.rem(lax.axis_index("sp"), 2)
    frames, rows = tok_ref.shape[0], tok_ref.shape[1]
    half = rows // 2
    lane = lax.broadcasted_iota(jnp.int32, (rows, 128), 1)
    places = (
        (h0_scr, h0_hbm), (qkv_scr, qkv_hbm), (o_scr, o_hbm), (xa_scr, xa_hbm), (h1_scr, h1_hbm),
        (act_scr, act_hbm), (slope_scr, slope_hbm),
    )

    def spills(f):
        now = lax.rem(f, 2)
        return [
            pltpu.make_async_copy(scr.at[now], hbm.at[rows_at(f, rows)], out_sems.at[7 * now + i])
            for i, (scr, hbm) in enumerate(places)
        ]

    def await_first(f, *which):
        @pl.when(f == 0)
        def _():
            for i in which:
                copies[i].wait()

    copies[0].wait()
    for copy in copies[2:]:
        copy.start()

    @pl.loop(0, frames)
    def _(f):
        now = lax.rem(f, 2)
        spill = spills(f)

        @pl.when(f >= 2)
        def _():
            for copy in spills(f - 2):
                copy.wait()

        x0 = tok_ref[f].astype(F32)
        h0 = norm(x0, gain_ref[0:1, :], shift_ref[0:1, :])[0].astype(BF16)
        h0_scr[now] = h0
        spill[0].start()
        await_first(f, 1)
        q, k, v = qkv_rows(h0, wqkv_ref)
        qkv_scr[now, :, 0:TILE] = q
        qkv_scr[now, :, TILE : 2 * TILE] = k
        qkv_scr[now, :, 2 * TILE :] = v
        spill[1].start()
        lse_all = jnp.zeros((rows, 128), F32)
        mixed = []
        for pair in range(HEADS // 2):
            cols = slice(pair * 128, (pair + 1) * 128)
            qp, kp, vp = q[:, cols], k[:, cols], v[:, cols]
            zero = jnp.zeros_like(qp)
            mask = head_mask(qp, 0)
            s = dot_nt(jnp.concatenate([jnp.where(mask, qp, zero), jnp.where(mask, zero, qp)], axis=0), kp)
            top = jnp.max(s, axis=-1, keepdims=True)
            p = jnp.exp(s - top)
            total = jnp.sum(p, axis=-1, keepdims=True)
            both = dot(p.astype(BF16), vp) * (1.0 / total)
            lse = top + jnp.log(total)
            lse_all = jnp.where(lane == 2 * pair, lse[:rows], lse_all)
            lse_all = jnp.where(lane == 2 * pair + 1, lse[rows:], lse_all)
            mixed.append(jnp.where(mask, both[:rows], both[rows:]).astype(BF16))
        lse_ref[f] = jnp.transpose(lse_all)[0:HEADS, :]
        o = jnp.concatenate(mixed, axis=1)
        o_scr[now] = o
        spill[2].start()
        await_first(f, 2)
        xa = x0 + dot(o, wout_ref[...])
        xa_scr[now] = xa
        spill[3].start()
        h1 = norm(xa, gain_ref[1:2, :], shift_ref[1:2, :])[0].astype(BF16)
        h1_scr[now] = h1
        spill[4].start()
        await_first(f, 3, 4)
        branch = mlp_forward(
            h1, wup_ref, params_ref.at[8:9], wdown_ref, slice(None), act_scr.at[now], slope_scr.at[now]
        )
        spill[5].start()
        spill[6].start()
        x1_scr[...] = xa + branch + params_ref[10:11, 0:TILE]
        keep_ref[f] = x1_scr[half_rows(part, half), :].astype(BF16)
        send_ref[f] = x1_scr[half_rows(1 - part, half), :].astype(BF16)

    for f in (frames - 2, frames - 1):
        for copy in spills(jnp.int32(f)):
            copy.wait()


def lane_heads(dtype):
    c = lax.broadcasted_iota(jnp.int32, (TILE, 128), 0)
    h = lax.broadcasted_iota(jnp.int32, (TILE, 128), 1)
    return (c // HEAD == h).astype(dtype)


def slot_places(slots_ref, where_scr, frames):
    sp = lax.axis_index("sp")
    group = (sp * frames) // GROUP_FRAMES
    part = lax.rem(sp, GROUP_FRAMES // frames)
    for t in range(GROUP_FRAMES):
        where_scr[slots_ref[group, t]] = lax.rem(t + GROUP_FRAMES - part * frames, GROUP_FRAMES)


def time_scores(q, k, spread):
    parts = []
    for t, s in PAIRS:
        parts.append((q[t] * k[s]).astype(BF16))
    return dot(jnp.concatenate(parts, axis=0), spread)


def time_probs(scores, count):
    blocks = [scores[i * count : (i + 1) * count] for i in range(len(PAIRS))]
    probs = []
    at = 0
    for t in range(VIDEO_STEPS):
        mine = blocks[at : at + t + 1]
        at += t + 1
        top = functools.reduce(jnp.maximum, mine)
        raw = [jnp.exp(b - top) for b in mine]
        inv = 1.0 / functools.reduce(lambda a, b: a + b, raw)
        probs.extend([r * inv for r in raw])
    return probs


def split_slots(rows):
    count = rows.shape[0] // GROUP_FRAMES
    return [rows[s * count : (s + 1) * count].astype(F32) for s in range(GROUP_FRAMES)]


def time_forward_kernel(
    slots_ref, keep_ref, recv_ref, cot_ref, cotr_ref, params_ref,
    wqkv_hbm, wout_hbm, wup_hbm, wdown_hbm,
    own_ref, send_ref, x_ref, h2_ref, qkv_ref, o_ref, h3_ref, act_ref, du_ref, gr_ref, dxb_ref,
    small_ref, wqkv_ref, wout_ref,
    where_scr, both_scr, slope_scr, wup_ref, wdown_ref, in_sems,
):
    pairs = [(wqkv_hbm, wqkv_ref), (wout_hbm, wout_ref), (wup_hbm, wup_ref), (wdown_hbm, wdown_ref)]
    copies = [pltpu.make_async_copy(src.at[1], dst, in_sems.at[i]) for i, (src, dst) in enumerate(pairs)]
    for copy in copies:
        copy.start()
    gain_ref, shift_ref = params_ref.at[0:4, 0:TILE], params_ref.at[4:8, 0:TILE]
    frames, half = keep_ref.shape[0], keep_ref.shape[1]
    part = lax.rem(lax.axis_index("sp"), GROUP_FRAMES // frames)
    slot_places(slots_ref, where_scr, frames)
    small_ref[...] = jnp.zeros_like(small_ref)
    both_scr[0:frames] = keep_ref[...]
    both_scr[frames:] = recv_ref[...]
    spread = lane_heads(BF16)
    steps = 4
    count = half // steps
    step_rows = count * GROUP_FRAMES

    def await_first(i, *which):
        @pl.when(i == 0)
        def _():
            for w in which:
                copies[w].wait()

    @pl.loop(0, steps)
    def _(i):
        span = rows_at(i, step_rows)
        place = rows_at(i, count)
        x_low = jnp.concatenate([both_scr[where_scr[s], place] for s in range(GROUP_FRAMES)], axis=0)
        x_ref[span, :] = x_low
        x = x_low.astype(F32)
        h2 = norm(x, gain_ref[2:3, :], shift_ref[2:3, :])[0].astype(BF16)
        h2_ref[span, :] = h2
        await_first(i, 0)
        q, k, v = qkv_rows(h2, wqkv_ref)
        qkv_ref[span, 0:TILE] = q
        qkv_ref[span, TILE : 2 * TILE] = k
        qkv_ref[span, 2 * TILE :] = v
        qs, ks, vs = split_slots(q), split_slots(k), split_slots(v)
        probs = time_probs(time_scores(qs, ks, spread), count)
        wide = dot_nt(jnp.concatenate([p.astype(BF16) for p in probs], axis=0), spread)
        mixed = []
        at = 0
        for t in range(VIDEO_STEPS):
            total = None
            for s in range(t + 1):
                piece = wide[at * count : (at + 1) * count] * vs[s]
                total = piece if total is None else total + piece
                at += 1
            mixed.append(total)
        mixed.extend(vs[VIDEO_STEPS:])
        o = jnp.concatenate([m.astype(BF16) for m in mixed], axis=0)
        o_ref[span, :] = o
        await_first(i, 1)
        xb = x + dot(o, wout_ref[...]).astype(BF16).astype(F32)
        h3, unit, inv = norm(xb, gain_ref[3:4, :], shift_ref[3:4, :])
        h3 = h3.astype(BF16)
        h3_ref[span, :] = h3
        slope = slope_scr
        await_first(i, 2, 3)
        branch = mlp_forward(h3, wup_ref, params_ref.at[9:10], wdown_ref, span, act_ref, SpanView(slope))
        out = (xb + branch + params_ref[11:12, 0:TILE]).astype(BF16)
        for s in range(GROUP_FRAMES):
            both_scr[where_scr[s], place] = out[s * count : (s + 1) * count]
        grad_low = jnp.concatenate(
            [cot_slot(cot_ref, cotr_ref, where_scr[s], part * half + i * count, count) for s in range(GROUP_FRAMES)],
            axis=0,
        )
        gr_ref[span, :] = grad_low
        grad = grad_low.astype(F32)
        dh, sums = mlp_backward(grad_low, wup_ref, wdown_ref, span, SpanView(slope), du_ref)
        add_small(small_ref, [column_sum(dh * unit), column_sum(dh), column_sum(grad), None] + sums, False)
        dxb_ref[span, :] = grad + norm_back(dh, unit, inv, gain_ref[3:4, :])

    own_ref[...] = both_scr[0:frames]
    send_ref[...] = both_scr[frames:]


class SpanView:
    def __init__(self, ref):
        self.ref = ref

    def __getitem__(self, index):
        return self.ref[:, index[1]]

    def __setitem__(self, index, value):
        self.ref[:, index[1]] = value


def cot_slot(cot_ref, cotr_ref, frame, start, count):
    frames = cot_ref.shape[0]
    places = pl.ds(pl.multiple_of(start, count), count)
    mine = cot_ref[lax.rem(frame, frames), places, :]
    other = cotr_ref[lax.rem(frame, frames), places, :]
    return jnp.where(frame < frames, mine, other)


def time_backward_kernel(
    slots_ref, x_ref, qkv_ref, dxb_ref, params_ref, wqkv_ref, wout_ref,
    own_ref, send_ref, ar_ref, dqkv_ref, small_ref,
    where_scr, both_scr,
):
    frames, half = own_ref.shape[0], own_ref.shape[1]
    slot_places(slots_ref, where_scr, frames)
    small_ref[...] = jnp.zeros_like(small_ref)
    spread = lane_heads(BF16)
    steps = 4
    count = half // steps
    step_rows = count * GROUP_FRAMES
    gain = params_ref[2:3, 0:TILE]

    @pl.loop(0, steps)
    def _(i):
        span = rows_at(i, step_rows)
        place = rows_at(i, count)
        dxb = dxb_ref[span, :]
        ar = dxb.astype(BF16)
        ar_ref[span, :] = ar
        do = split_slots(dot_nt(ar, wout_ref[...]).astype(BF16))
        qs = split_slots(qkv_ref[span, 0:TILE])
        ks = split_slots(qkv_ref[span, TILE : 2 * TILE])
        vs = split_slots(qkv_ref[span, 2 * TILE :])
        probs = time_probs(time_scores(qs, ks, spread), count)
        dps = time_scores(do, vs, spread)
        dps = [dps[j * count : (j + 1) * count] for j in range(len(PAIRS))]
        dss = []
        at = 0
        for t in range(VIDEO_STEPS):
            centre = functools.reduce(
                lambda a, b: a + b, [probs[at + s] * dps[at + s] for s in range(t + 1)]
            )
            dss.extend([probs[at + s] * (dps[at + s] - centre) for s in range(t + 1)])
            at += t + 1
        wide_p = dot_nt(jnp.concatenate([p.astype(BF16) for p in probs], axis=0), spread)
        wide_ds = dot_nt(jnp.concatenate([d.astype(BF16) for d in dss], axis=0), spread)
        dq = [None] * GROUP_FRAMES
        dk = [None] * GROUP_FRAMES
        dv = [None] * GROUP_FRAMES

        def add(table, index, piece):
            table[index] = piece if table[index] is None else table[index] + piece

        for j, (t, s) in enumerate(PAIRS):
            rows = slice(j * count, (j + 1) * count)
            add(dq, t, wide_ds[rows] * ks[s])
            add(dk, s, wide_ds[rows] * qs[t])
            add(dv, s, wide_p[rows] * do[t])
        for t in range(VIDEO_STEPS, GROUP_FRAMES):
            dq[t] = jnp.zeros_like(do[t])
            dk[t] = jnp.zeros_like(do[t])
            dv[t] = do[t]
        dq = jnp.concatenate([(d * SCALE).astype(BF16) for d in dq], axis=0)
        dk = jnp.concatenate([d.astype(BF16) for d in dk], axis=0)
        dv = jnp.concatenate([d.astype(BF16) for d in dv], axis=0)
        dqkv_ref[span, 0:TILE] = dq
        dqkv_ref[span, TILE : 2 * TILE] = dk
        dqkv_ref[span, 2 * TILE :] = dv
        dh = dot_nt(dqkv_ref[span, :], wqkv_ref[...])
        unit, inv = norm(x_ref[span, :].astype(F32), gain, params_ref[6:7, 0:TILE])[1:]
        add_small(small_ref, [column_sum(dh * unit), column_sum(dh)], False)
        dxp = norm_back(dh, unit, inv, gain).astype(BF16).astype(F32)
        dx1 = (dxb + dxp).astype(BF16)
        for s in range(GROUP_FRAMES):
            both_scr[where_scr[s], place] = dx1[s * count : (s + 1) * count]

    own_ref[...] = both_scr[0:frames]
    send_ref[...] = both_scr[frames:]


def space_mlp_back_kernel(
    gr_ref, xa_ref, slope_ref, params_ref, wup_ref, wdown_ref,
    du_ref, dxa_ref, ar_ref, small_ref,
):
    small_ref[...] = jnp.zeros_like(small_ref)
    rows = 256
    gain = params_ref[1:2, 0:TILE]

    @pl.loop(0, gr_ref.shape[0] // rows, unroll=2)
    def _(f):
        span = rows_at(f, rows)
        grad_low = gr_ref[span, :]
        grad = grad_low.astype(F32)
        dh, sums = mlp_backward(grad_low, wup_ref.at[0], wdown_ref.at[0], span, slope_ref, du_ref)
        unit, inv = norm(xa_ref[span, :], gain, params_ref[5:6, 0:TILE])[1:]
        add_small(small_ref, [column_sum(dh * unit), column_sum(dh), column_sum(grad), None] + sums, False)
        dxa = grad + norm_back(dh, unit, inv, gain)
        dxa_ref[span, :] = dxa
        ar_ref[span, :] = dxa.astype(BF16)


def head_picker():
    h = lax.broadcasted_iota(jnp.int32, (HEADS, TILE), 0)
    c = lax.broadcasted_iota(jnp.int32, (HEADS, TILE), 1)
    return (c // HEAD == h).astype(BF16)


def attn_back_frame(f, ar_ref, qkv_ref, lse_ref, o_ref, wout_ref, pick, dqkv_ref):
    rows = lse_ref.shape[2]
    span = rows_at(f, rows)
    do = dot_nt(ar_ref[span, :], wout_ref[0]).astype(BF16)
    both = do.astype(F32) * o_ref[span, :].astype(F32)
    high = both.astype(BF16)
    rest = (both - high.astype(F32)).astype(BF16)
    centre = dot_nt(pick, high) + dot_nt(pick, rest)
    for pair in range(HEADS // 2):
        qp = qkv_ref[span, pair * 128 : (pair + 1) * 128]
        kp = qkv_ref[span, TILE + pair * 128 : TILE + (pair + 1) * 128]
        vp = qkv_ref[span, 2 * TILE + pair * 128 : 2 * TILE + (pair + 1) * 128]
        dop = do[:, pair * 128 : (pair + 1) * 128]
        zero = jnp.zeros_like(kp)
        mask = head_mask(kp, 0)
        st = dot_nt(jnp.concatenate([jnp.where(mask, kp, zero), jnp.where(mask, zero, kp)], axis=0), qp)
        dpt = dot_nt(jnp.concatenate([jnp.where(mask, vp, zero), jnp.where(mask, zero, vp)], axis=0), dop)
        pts, dsts, dqs = [], [], []
        for e in range(2):
            row = slice(2 * pair + e, 2 * pair + e + 1)
            keys = slice(e * rows, (e + 1) * rows)
            pt = jnp.exp(st[keys] - lse_ref[f, row, :])
            dst = (pt * (dpt[keys] - centre[row, :])).astype(BF16)
            pts.append(pt.astype(BF16))
            dsts.append(dst)
            dqs.append(dot_tn(dst, kp) * SCALE)
        dk = dot(jnp.concatenate(dsts, axis=0), qp)
        dv = dot(jnp.concatenate(pts, axis=0), dop)
        values = (
            jnp.where(mask, dqs[0], dqs[1]),
            jnp.where(mask, dk[:rows], dk[rows:]),
            jnp.where(mask, dv[:rows], dv[rows:]),
        )
        for index, value in enumerate(values):
            at = index * TILE + pair * 128
            dqkv_ref[span, at : at + 128] = value.astype(BF16)


def space_attn_back_kernel(ar_ref, qkv_ref, lse_ref, o_ref, wout_ref, dqkv_ref):
    pick = head_picker()

    @pl.loop(0, lse_ref.shape[0])
    def _(f):
        attn_back_frame(f, ar_ref, qkv_ref, lse_ref, o_ref, wout_ref, pick, dqkv_ref)


def qkv_weights_kernel(order, dqkv_ref, h_ref, keep_ref, send_ref):
    size = h_ref.shape[1] // lax.axis_size("sp")
    turned_columns(h_ref, dqkv_ref, 3, 0, 3 * size, size, order, keep_ref, send_ref)


def finish_kernel(
    dqkv_ref, tok_ref, dxa_ref, own_ref, recv_ref, params_ref, wqkv_ref, small1_ref,
    small2_ref, small3_ref, gtok_ref, out_ref, small_ref, sums_scr,
):
    part = lax.rem(lax.axis_index("sp"), 2)
    frames, half = own_ref.shape[0], own_ref.shape[1]
    rows = 2 * half
    gain = params_ref[0:1, 0:TILE]
    sums_scr[...] = jnp.zeros_like(sums_scr)

    @pl.loop(0, frames)
    def _(f):
        span = rows_at(f, rows)
        out_ref[f, half_rows(part, half), :] = own_ref[f]
        out_ref[f, half_rows(1 - part, half), :] = recv_ref[f]
        dh = dot_nt(dqkv_ref[span, :], wqkv_ref[0])
        unit, inv = norm(tok_ref[f].astype(F32), gain, params_ref[4:5, 0:TILE])[1:]
        add_small(sums_scr, [column_sum(dh * unit), column_sum(dh)], False)
        gtok_ref[f] = (dxa_ref[span, :] + norm_back(dh, unit, inv, gain)).astype(BF16)

    small = jnp.concatenate([sums_scr[...], small1_ref[...], small2_ref[...], small3_ref[...]], axis=0)
    small_ref[...] = small.astype(BF16)


def place_of(block, order, sp):
    bits = len(order)
    mixed = jnp.bitwise_xor(block, sp)
    slot = jnp.int32(0)
    for i, b in enumerate(order):
        bit = jnp.bitwise_and(lax.shift_right_logical(mixed, jnp.int32(b)), 1)
        slot = slot + lax.shift_left(bit, jnp.int32(bits - 1 - i))
    return slot


class Place:
    def __init__(self, base, rows, at):
        self.base, self.rows, self.at = base, rows, at


def put_blocks(result, first, size, place, order, keep_ref, send_ref):
    sp = lax.axis_index("sp")
    part = lax.rem(sp, 2)
    low = result.astype(BF16)
    for j in range(result.shape[0] // (2 * size)):
        even = low[2 * j * size : (2 * j + 1) * size]
        odd = low[(2 * j + 1) * size : (2 * j + 2) * size]
        slot = place_of(first + 2 * j, order[1:], sp)
        rows = pl.ds(pl.multiple_of(place.base + slot * place.rows + place.at, 16), size)
        keep_ref[rows, :] = jnp.where(part == 0, even, odd)
        send_ref[rows, :] = jnp.where(part == 0, odd, even)


def turned_columns(h_ref, wide_ref, chunks, base, rows, size, order, keep_ref, send_ref):
    turned = jnp.transpose(h_ref[...])
    for j in range(chunks):
        result = dot(turned, wide_ref[:, j * TILE : (j + 1) * TILE])
        put_blocks(result, jnp.int32(0), size, Place(base, rows, j * size), order, keep_ref, send_ref)


def put_up(h_ref, du_ref, base, rows, order, keep_ref, send_ref):
    size = h_ref.shape[1] // lax.axis_size("sp")
    turned_columns(h_ref, du_ref, du_ref.shape[1] // TILE, base, rows, size, order, keep_ref, send_ref)


def put_down(act_ref, gr_ref, base, order, keep_ref, send_ref):
    size = act_ref.shape[1] // lax.axis_size("sp")
    for j in range(act_ref.shape[1] // TILE):
        down = dot_tn(act_ref[:, j * TILE : (j + 1) * TILE], gr_ref[...])
        put_blocks(down, jnp.int32(j * (TILE // size)), size, Place(base, size, 0), order, keep_ref, send_ref)


def mlp_weights_kernel(orders, h_ref, du_ref, act_ref, gr_ref, keep_ref, send_ref):
    sp_size = lax.axis_size("sp")
    rows = du_ref.shape[1] // TILE * (h_ref.shape[1] // sp_size)
    put_up(h_ref, du_ref, 0, rows, orders[0], keep_ref, send_ref)
    put_down(act_ref, gr_ref, sp_size // 2 * rows, orders[1], keep_ref, send_ref)


def down_weights_kernel(order, act_ref, own_ref, recv_ref, gr_ref, keep_ref, send_ref):
    part = lax.rem(lax.axis_index("sp"), 2)
    frames, half = own_ref.shape[0], own_ref.shape[1]
    for f in range(frames):
        base = f * 2 * half
        gr_ref[pl.ds(pl.multiple_of(base + part * half, half), half), :] = own_ref[f]
        gr_ref[pl.ds(pl.multiple_of(base + (1 - part) * half, half), half), :] = recv_ref[f]
    put_down(act_ref, gr_ref, 0, order, keep_ref, send_ref)


def up_weights_kernel(order, h_ref, du_ref, o_ref, ar_ref, keep_ref, send_ref):
    size = h_ref.shape[1] // lax.axis_size("sp")
    at = du_ref.shape[1] // TILE * size
    put_up(h_ref, du_ref, 0, at + size, order, keep_ref, send_ref)
    out = dot_tn(o_ref[...], ar_ref[...])
    put_blocks(out, jnp.int32(0), size, Place(0, at + size, at), order, keep_ref, send_ref)


def attn_weights_kernel(order, h_ref, dqkv_ref, o_ref, ar_ref, keep_ref, send_ref):
    size = h_ref.shape[1] // lax.axis_size("sp")
    turned_columns(h_ref, dqkv_ref, 3, 0, 4 * size, size, order, keep_ref, send_ref)
    out = dot_tn(o_ref[...], ar_ref[...])
    put_blocks(out, jnp.int32(0), size, Place(0, 4 * size, 3 * size), order, keep_ref, send_ref)


def in_pieces(rows, body):
    piece = next(p for p in (128, 96, 80, 64, 48, 32, 16, 8) if rows % p == 0)
    if rows <= 2 * piece:
        for start in range(0, rows, piece):
            body(start, piece)
    else:

        @pl.loop(0, rows // piece)
        def _(i):
            body(pl.multiple_of(i * piece, 8), piece)


def fold_kernel(moves, count, *refs):
    outs = refs[2 * count :]
    row_half = lax.rem(lax.axis_index("grp"), 2)

    def add(keep, recv, at, rows, places):
        def body(start, piece):
            span = pl.ds(pl.multiple_of(at + start, 8), piece)
            total = keep[span, :] + recv[span, :]
            for ref, to in places:
                ref[pl.ds(pl.multiple_of(to + start, 8), piece), :] = total

        in_pieces(rows, body)

    for source, at, rows, slots, targets, to, split in moves:
        keep, recv = refs[2 * source], refs[2 * source + 1]
        if split == "none":
            add(keep, recv, at, rows, [(outs[target], to) for target in targets])
        elif split == "slots":
            half = rows // 2
            for part, target in enumerate(targets):
                add(keep, recv, at + part * half, half, [(outs[target], to)])
        else:
            half = rows // (2 * slots)
            for slot in range(slots):
                for part, target in enumerate(targets):
                    side = row_half if part == 0 else 1 - row_half
                    add(keep, recv, at + 2 * slot * half + side * half, half, [(outs[target], to + slot * half)])


class Group:
    def __init__(self, sizes, segments, apart=False):
        grp_size, sp_size = sizes
        bits = sp_size.bit_length() - 1
        grp_bits = grp_size.bit_length() - 1
        names = tuple(segments)
        self.halved = grp_bits > 0 and all(
            whole or (height // 2) % 16 == 0 for height, whole, path in segments.values()
        )
        self.segments = {}
        self.state = {}
        for name, (height, whole, path) in segments.items():
            path = [step for step in path if step != ROWS or self.halved] + list(range(4, bits))
            self.segments[name] = (height, whole, path)
            self.state[name] = [sp_size // 2, 1]
        self.stages = []
        for i in range(bits + (1 if self.halved else 0)):
            entries = {}
            for name in names:
                key = (self.segments[name][2][i], name if apart and i == 0 else None)
                entries.setdefault(key, []).append(name)
            stage = []
            for (step, _), who in entries.items():
                stage.append(("grp", grp_size, 0, who, "rows") if step == ROWS else ("sp", sp_size, step, who, "slots"))
            self.stages.append(stage)
        for b in range(1 if self.halved else 0, grp_bits):
            self.stages.append([("grp", grp_size, b, names, "none")])
        if self.halved:
            self.stages.append([("grp", grp_size, 0, names, "none")])
        self.stage = 0
        self.keeps, self.recvs = [], []

    def beside(self, other):
        group = Group.__new__(Group)
        group.halved, group.stage = self.halved, self.stage
        group.segments = {**self.segments, **other.segments}
        group.state = {**self.state, **other.state}
        group.keeps, group.recvs = self.keeps + other.keeps, self.recvs + other.recvs
        group.stages = []
        for mine, others in zip(self.stages, other.stages):
            entries = {}
            for entry in mine + others:
                entries.setdefault(entry[:3] + entry[4:], []).extend(entry[3])
            if len(group.stages) == group.stage:
                group.stages.append(mine + others)
            else:
                group.stages.append([key[:3] + (tuple(names),) + key[3:] for key, names in entries.items()])
        return group

    def height(self, name):
        height, whole, _ = self.segments[name]
        slots, cut = self.state[name]
        return height if whole else height // cut * slots

    def start(self, sends):
        self.sends = sends
        self.recvs = [swap(send, *entry[:3]) for send, entry in zip(sends, self.stages[self.stage])]

    def begin(self, keep, send):
        entry = self.stages[0][len(self.keeps)]
        self.keeps.append(keep)
        self.recvs.append(swap(send, *entry[:3]))

    def fold(self):
        places = {}
        for source, entry in enumerate(self.stages[self.stage]):
            at = 0
            for name in entry[3]:
                places[name] = (source, at, self.height(name), self.state[name][0])
                at += self.height(name)
        shapes, moves, keeps, sends = [], [], [], []
        for entry in self.stages[self.stage + 1]:
            split = entry[4]
            keeps.append(len(shapes))
            sends.append(len(shapes) + (0 if split == "none" else 1))
            targets = (keeps[-1],) if split == "none" else (keeps[-1], sends[-1])
            to = 0
            for name in entry[3]:
                whole = self.segments[name][1]
                if split == "slots":
                    self.state[name][0] //= 2
                elif split == "rows":
                    self.state[name][1] = 2
                moves.append(places[name] + (targets, to, "none" if whole else split))
                to += self.height(name)
            shapes += [sds((to, TILE), BF16)] * len(targets)
        args = [x for pair in zip(self.keeps, self.recvs) for x in pair]
        out = call(functools.partial(fold_kernel, moves, len(args) // 2), args, shapes, 0.5, limit=4)
        self.keeps = [out[i] for i in keeps]
        self.sends = [out[i] for i in sends]
        self.stage += 1

    def left(self):
        return len(self.stages) - 1 - self.stage

    def pair(self):
        return self.keeps[0], self.recvs[0]


def result_kernel(sp_size, halved, *refs):
    outs = refs[8:16]
    gain_scr, shift_scr, qkv_scr, out_scr, up_scr, bup_scr, down_scr, bdown_scr = refs[16:24]
    mlp1, both, up0, qkv0 = refs[24:28]
    small_scr, sems = refs[28:]
    size = TILE // sp_size
    chunks = up_scr.shape[2] // TILE
    down_size = chunks * size
    row_half = lax.rem(lax.axis_index("grp"), 2)
    segments = (
        (mlp1, (chunks * size, down_size)), (both, (4 * size, down_size)),
        (up0, (chunks * size + size,)), (qkv0, (3 * size,)),
    )
    for i, (scr, heights) in enumerate(segments):
        mine, other = refs[2 * i], refs[2 * i + 1]
        at = 0
        base = 0
        for height in heights:
            if halved[i]:
                half = height // 2
                for ref, side in ((mine, row_half), (other, 1 - row_half)):
                    place = pl.ds(pl.multiple_of(base + side * half, 16), half)
                    scr[place, :] = ref[at : at + half, :].astype(F32)
                at += half
            else:
                span = slice(at, at + height)
                scr[base : base + height, :] = mine[span, :].astype(F32) + other[span, :].astype(F32)
                at += height
            base += height
    mine, other = refs[6], refs[7]
    at = 3 * size // (2 if halved[3] else 1)
    small = mine[at : at + 32, :].astype(F32)
    small_scr[...] = small if halved[3] else small + other[at : at + 32, :].astype(F32)
    for layer, (qkv, up, down, out, first, last) in enumerate((
        (qkv0, up0, both, up0, 4 * size, chunks * size),
        (both, mlp1, mlp1, both, chunks * size, 3 * size),
    )):
        for j in range(3):
            qkv_scr[layer, :, j * TILE : (j + 1) * TILE] = qkv[j * size : (j + 1) * size, :]
        for j in range(chunks):
            up_scr[layer, :, j * TILE : (j + 1) * TILE] = up[j * size : (j + 1) * size, :]
        down_scr[layer] = down[first : first + down_size, :]
        out_scr[layer] = out[last : last + size, :]
    sp = lax.axis_index("sp")
    back = lax.rem(TILE - sp * size, TILE)
    turned = pltpu.roll(small_scr[...], back, 1)
    for i in range(4):
        gain_scr[i : i + 1, :] = turned[8 * i : 8 * i + 1, :size]
        shift_scr[i : i + 1, :] = turned[8 * i + 1 : 8 * i + 2, :size]
    start = sp * down_size
    line = start // TILE
    back = lax.rem(TILE - lax.rem(start, TILE), TILE)
    for layer in range(2):
        first = 8 + 16 * layer
        bdown_scr[layer : layer + 1, :] = turned[first + 2 : first + 3, :size]
        rows = small_scr[first : first + 8, :]
        lines = lax.broadcasted_iota(jnp.int32, rows.shape, 0)
        picked = jnp.sum(jnp.where(lines == 4 + line, rows, 0.0), axis=0, keepdims=True)
        picked = pltpu.roll(jnp.broadcast_to(picked, rows.shape), back, 1)
        bup_scr[layer : layer + 1, :] = picked[0:1, :down_size]
    scrs = (gain_scr, shift_scr, qkv_scr, out_scr, up_scr, bup_scr, down_scr, bdown_scr)
    copies = [pltpu.make_async_copy(scr, out, sems.at[i]) for i, (scr, out) in enumerate(zip(scrs, outs))]
    for copy in copies:
        copy.start()
    for copy in copies:
        copy.wait()


VMEM = pl.BlockSpec(memory_space=pltpu.VMEM)
SMEM = pl.BlockSpec(memory_space=pltpu.SMEM)
HBM = pl.BlockSpec(memory_space=pltpu.HBM)


def sds(shape, dtype):
    return jax.ShapeDtypeStruct(shape, dtype)


def call(kernel, args, outs, micros, scratch=(), specs=None, out_specs=None, limit=12):
    return pl.pallas_call(
        kernel,
        in_specs=[VMEM] * len(args) if specs is None else specs,
        out_specs=[VMEM] * len(outs) if out_specs is None else out_specs,
        out_shape=outs,
        scratch_shapes=list(scratch),
        compiler_params=pltpu.CompilerParams(vmem_limit_bytes=limit * MIB),
        cost_estimate=pl.CostEstimate(flops=int(micros * COST), bytes_accessed=0, transcendentals=0),
    )(*args)


def swap(array, axis, size, bit):
    return lax.ppermute(array, axis, [(i, i ^ (1 << bit)) for i in range(size)])


def shards(sizes, tokens, frame_slot, norm_gain, norm_shift, w_qkv, w_out, w_up, b_up, w_down, b_down, cotangent):
    grp_size, sp_size = sizes
    frames, patches, width = tokens.shape
    hidden = w_up.shape[2]
    assert GROUP_FRAMES == 2 * frames and sp_size >= 8
    half = patches // 2
    rows = frames * patches
    sp_bits = sp_size.bit_length() - 1
    core_swap = functools.partial(swap, axis="sp", size=sp_size, bit=0)
    slots = sp_size // 2
    size = width // sp_size
    down_size = hidden // sp_size
    def slots_of(path):
        return [step for step in path if step != ROWS] + list(range(4, sp_bits))

    path_up1, path_down1 = (0, 1, 2, ROWS, 3), (0, 2, 1, ROWS, 3)
    path_attn1, path_down0 = (0, ROWS, 2, 1, 3), (0, 2, 1, ROWS, 3)
    path_up0, path_qkv0 = (0, 1, ROWS, 3, 2), (0, ROWS, 2, 1, 3)

    def row_out(cols, dtype=BF16):
        return sds((rows, cols), dtype)

    half_out = sds((frames, half, width), BF16)
    small_out = sds((8, TILE), F32)
    fence = lambda *arrays: lax.optimization_barrier(arrays)

    token = []

    def meet(groups, *arrays):
        recvs = [r for g in groups for r in g.recvs]
        out = list(fence(*arrays, *recvs, *token))
        count = len(arrays)
        arrays, recvs = out[:count], out[count:]
        for g in groups:
            g.recvs = [recvs.pop(0) for _ in g.recvs]
            g.fold()
        sends = [x for g in groups for x in g.sends]
        out = list(fence(*arrays, *sends))
        arrays, sends = out[:count], out[count:]
        for g in groups:
            g.start([sends.pop(0) for _ in g.sends])
        token[:] = [groups[-1].sends[-1]] if groups else []
        return arrays

    def buffers(height):
        return [sds((slots * height, TILE), BF16)] * 2

    cot_recv = core_swap(cotangent)
    widen = lambda a: jnp.pad(a, ((0, 0), (0, hidden - width)))
    packed = jnp.concatenate([widen(norm_gain), widen(norm_shift), b_up, widen(b_down)], axis=0)
    weights = (w_qkv, w_out, w_up, w_down)
    shapes = [sds(w.shape[1:], BF16) for w in weights]
    out = call(
        space_forward_kernel,
        (tokens, packed) + weights,
        [
            half_out, half_out, row_out(width), row_out(3 * width), sds((frames, HEADS, patches), F32),
            row_out(width), row_out(width, F32), row_out(width), row_out(hidden), row_out(hidden),
        ],
        16,
        scratch=[pltpu.VMEM(tokens.shape, BF16)]
        + [pltpu.VMEM(x.shape, BF16) for x in shapes]
        + [
            pltpu.VMEM((2, patches, width), BF16), pltpu.VMEM((2, patches, 3 * width), BF16),
            pltpu.VMEM((2, patches, width), BF16), pltpu.VMEM((2, patches, width), F32),
            pltpu.VMEM((2, patches, width), BF16),
            pltpu.VMEM((2, patches, hidden), BF16), pltpu.VMEM((2, patches, hidden), BF16),
            pltpu.VMEM((patches, width), F32), pltpu.SemaphoreType.DMA((5,)),
            pltpu.SemaphoreType.DMA((14,)),
        ],
        specs=[HBM, VMEM] + [HBM] * 4,
        out_specs=[VMEM, VMEM, HBM, HBM, VMEM] + [HBM] * 5,
        limit=LIMIT1,
    )
    (x_keep, x_send, h0, qkv0, lse0, o0, xa, h1, act0, slope0) = out
    x_recv = core_swap(x_send)

    place_scratch = [
        pltpu.SMEM((GROUP_FRAMES,), jnp.int32),
        pltpu.VMEM((GROUP_FRAMES, half, width), BF16),
    ]
    (out_own, out_send, xt, h2, qkv1, o1, h3, act1, du1, gr1, dxb, small3, w_qkv1, w_out1) = call(
        time_forward_kernel,
        (frame_slot, x_keep, x_recv, cotangent, cot_recv, packed) + weights,
        [
            half_out, half_out, row_out(width), row_out(width), row_out(3 * width), row_out(width),
            row_out(width), row_out(hidden), row_out(hidden), row_out(width), row_out(width, F32),
            small_out,
        ] + shapes[:2],
        24,
        scratch=place_scratch
        + [pltpu.VMEM((rows // 4, hidden), BF16)]
        + [pltpu.VMEM(x.shape, BF16) for x in shapes[2:]]
        + [pltpu.SemaphoreType.DMA((4,))],
        specs=[SMEM] + [VMEM] * 5 + [HBM] * 4,
        limit=LIMIT2,
    )
    out_recv = core_swap(out_send)

    out = call(
        functools.partial(mlp_weights_kernel, (slots_of(path_up1), slots_of(path_down1))), (h3, du1, act1, gr1),
        buffers(4 * size + down_size), 4.5,
    )
    keep, send, dxb = fence(*out, dxb)
    mlp1 = Group(sizes, {"up": (4 * size, False, path_up1), "down": (down_size, False, path_down1)})
    mlp1.begin(keep, send)

    (dx_own, dx_send, ar1, dqkv1, small2) = call(
        time_backward_kernel,
        (frame_slot, xt, qkv1, dxb, packed, w_qkv1, w_out1),
        [half_out, half_out, row_out(width), row_out(3 * width), small_out],
        8,
        scratch=place_scratch,
        specs=[SMEM] + [VMEM] * 6,
    )
    dx_recv = core_swap(dx_send)
    keep, send = call(
        functools.partial(attn_weights_kernel, slots_of(path_attn1)), (h2, dqkv1, o1, ar1),
        buffers(4 * size), 2.4,
    )
    dx_own, dx_recv, keep, send, out_recv = meet((mlp1,), dx_own, dx_recv, keep, send, out_recv)
    attn1 = Group(sizes, {"attn": (4 * size, False, path_attn1)})
    attn1.begin(keep, send)
    gr0, keep_down, send_down = call(
        functools.partial(down_weights_kernel, slots_of(path_down0)), (act0, dx_own, dx_recv),
        [row_out(width)] + buffers(down_size), 2.4,
    )
    (du0, dxa, ar0, small1) = call(
        space_mlp_back_kernel,
        (gr0, xa, slope0, packed, w_up, w_down),
        [row_out(hidden), row_out(width, F32), row_out(width), small_out],
        6,
    )
    keep_up, send_up = call(
        functools.partial(up_weights_kernel, slots_of(path_up0)), (h1, du0, o0, ar0), buffers(5 * size), 3
    )
    keep_down, send_down, keep_up, send_up, ar0 = meet(
        (mlp1, attn1), keep_down, send_down, keep_up, send_up, ar0
    )
    down0 = Group(sizes, {"down": (down_size, False, path_down0)})
    down0.begin(keep_down, send_down)
    up0 = Group(sizes, {"up": (5 * size, False, path_up0)})
    up0.begin(keep_up, send_up)

    (dqkv0,) = call(
        space_attn_back_kernel, (ar0, qkv0, lse0, o0, w_out), [row_out(3 * width)], 10
    )
    keep, send = call(
        functools.partial(qkv_weights_kernel, slots_of(path_qkv0)), (dqkv0, h0), buffers(3 * size), 2
    )
    dqkv0, keep, send, *attn1.recvs = meet((up0, down0, mlp1), dqkv0, keep, send, *attn1.recvs)
    both = attn1.beside(down0)
    qkv = Group(
        sizes, {"qkv": (3 * size, False, path_qkv0), "small": (32, True, path_qkv0)}, apart=True
    )
    qkv.begin(keep, send)
    grad_tokens, output, small = call(
        finish_kernel,
        (
            dqkv0, tokens, dxa, out_own, out_recv, packed, w_qkv, small1, small2, small3,
        ),
        [sds(tokens.shape, BF16), sds(tokens.shape, BF16), sds((32, TILE), BF16)],
        4,
        scratch=[pltpu.VMEM((8, TILE), F32)],
    )
    (small,) = fence(small)
    qkv.begin(small, small)
    everyone = (mlp1, both, up0, qkv)
    for names in TAIL:
        groups = [g for g in (dict(zip("mbuq", everyone))[c] for c in names) if g.left()]
        if groups:
            meet(groups)
    while any(g.left() for g in everyone):
        meet([g for g in everyone if g.left()])
    finals = [
        sds((4, size), F32), sds((4, size), F32), sds((2, size, 3 * width), F32), sds((2, size, width), F32),
        sds((2, size, hidden), F32), sds((2, down_size), F32), sds((2, down_size, width), F32),
        sds((2, size), F32),
    ]
    heights = (4 * size + down_size, 4 * size + down_size, 5 * size, 3 * size)
    results = call(
        functools.partial(result_kernel, sp_size, tuple(g.halved for g in everyone)),
        [x for g in everyone for x in g.pair()], finals, 2,
        scratch=[pltpu.VMEM(f.shape, F32) for f in finals]
        + [pltpu.VMEM((h, TILE), F32) for h in heights]
        + [pltpu.VMEM((32, TILE), F32), pltpu.SemaphoreType.DMA((8,))],
        out_specs=[HBM] * 8,
    )
    return (output, grad_tokens, *results)


def solution(mesh):
    rows = P(("grp", "sp"), None, None)
    in_specs = (rows, P("grp", None), P(), P(), P(), P(), P(), P(), P(), P(), rows)
    out_specs = (
        rows, rows, P(None, "sp"), P(None, "sp"), P(None, "sp", None), P(None, "sp", None),
        P(None, "sp", None), P(None, "sp"), P(None, "sp", None), P(None, "sp"),
    )
    body = functools.partial(shards, (mesh.shape["grp"], mesh.shape["sp"]))
    return jax.shard_map(body, mesh=mesh, in_specs=in_specs, out_specs=out_specs, check_vma=False)
```
